128 devices in a mesh: ctx: 16 (over y, z_hi, core), fsdp: 8 (over z_lo, x).
Axes of the slice: x: 4, y: 4, z: 4 (z_hi: 2, z_lo: 2; z = z_hi * 2 + z_lo), core: 2. Of those that a mesh axis runs over, the one named last changes fastest.
Arguments:
- decoder_in: bfloat16 [8, 2048, 768], P('fsdp', 'ctx'), may hold values from -6 to 6
- encoder_states: bfloat16 [8, 1024, 768], P('fsdp', 'ctx'), may hold values from -6 to 6
- out_grad: bfloat16 [8, 2048, 768], P('fsdp', 'ctx'), may hold values from -6 to 6
- block_pairs: int32 [16], replicated, may hold values from 0 to 15, each once
- bucket_table: int32 [128], replicated, may hold values from 0 to 31, as said below
- gain_self: bfloat16 [768], P('fsdp'), may hold values from 0.25 to 1.75
- self_query: bfloat16 [768, 768], P('fsdp'), may hold values from -0.078125 to 0.078125
- self_key: bfloat16 [768, 768], P('fsdp'), may hold values from -0.078125 to 0.078125
- self_value: bfloat16 [768, 768], P('fsdp'), may hold values from -0.21875 to 0.21875
- self_out: bfloat16 [768, 768], P('fsdp'), may hold values from -2.5 to 2.5
- position_bias: bfloat16 [32, 12], P('fsdp'), may hold values from -4 to 4
- gain_cross: bfloat16 [768], P('fsdp'), may hold values from 0.25 to 1.75
- cross_query: bfloat16 [768, 768], P('fsdp'), may hold values from -0.078125 to 0.078125
- cross_key: bfloat16 [768, 768], P('fsdp'), may hold values from -0.078125 to 0.078125
- cross_value: bfloat16 [768, 768], P('fsdp'), may hold values from -0.21875 to 0.21875
- cross_out: bfloat16 [768, 768], P('fsdp'), may hold values from -3.5 to 3.5
- gain_feed: bfloat16 [768], P('fsdp'), may hold values from 0.25 to 1.75
- feed_gate: bfloat16 [768, 2048], P('fsdp'), may hold values from -0.21875 to 0.21875
- feed_up: bfloat16 [768, 2048], P('fsdp'), may hold values from -0.21875 to 0.21875
- feed_down: bfloat16 [2048, 768], P('fsdp'), may hold values from -0.125 to 0.125
Outputs:
- block_out: float32 [8, 2048, 768], P('fsdp', 'ctx')
- grad_decoder: float32 [8, 2048, 768], P('fsdp', 'ctx')
- grad_encoder: float32 [8, 1024, 768], P('fsdp', 'ctx')
- grad_gain_self: float32 [768], P('fsdp')
- grad_self_query: float32 [768, 768], P('fsdp')
- grad_self_key: float32 [768, 768], P('fsdp')
- grad_self_value: float32 [768, 768], P('fsdp')
- grad_self_out: float32 [768, 768], P('fsdp')
- grad_position_bias: float32 [32, 12], P('fsdp')
- grad_gain_cross: float32 [768], P('fsdp')
- grad_cross_query: float32 [768, 768], P('fsdp')
- grad_cross_key: float32 [768, 768], P('fsdp')
- grad_cross_value: float32 [768, 768], P('fsdp')
- grad_cross_out: float32 [768, 768], P('fsdp')
- grad_gain_feed: float32 [768], P('fsdp')
- grad_feed_gate: float32 [768, 2048], P('fsdp')
- grad_feed_up: float32 [768, 2048], P('fsdp')
- grad_feed_down: float32 [2048, 768], P('fsdp')
The draws below stay inside these ranges and needn't reach their ends.
Inputs may be any that keep to these rules, and one draw needn't show every extreme that they name: block_pairs is a permutation of 0 to 15. `bucket_table`: entry n is the bucket of distance n (distances of 127 and more use the last entry); it never falls along n, is 0 at n = 0 and 31 at n = 127.
All inputs are finite; a program needn't handle non-finite values.
Results may differ from the reference program's by a relative error of at most 0.03.
Values may be sent and summed in bfloat16 or wider, within the bound.
A program may use at most 192 MiB of HBM per device.

```python
import jax
import jax.numpy as jnp
from jax import lax

D = 768
FF = 2048
HEADS = 12
BUCKETS = 32
RANGE = 128
TOK_DEV = 128
SEQS = 8
LENGTH = 2048
ENC_LEN = 1024
N_CTX = 16


def draw_bucket_table(key, part):
    key = jax.random.fold_in(key, 7)
    shuffled = jax.random.permutation(key, RANGE - 2) + 1
    bounds = shuffled[:BUCKETS - 1]
    distance = jnp.arange(RANGE, dtype=jnp.int32)
    return jnp.sum((bounds[None, :] <= distance[:, None]).astype(jnp.int32), axis=1).astype(jnp.int32)


def level_of(rng, shape, cuts, low, largest):
    level, own = 1.0, jax.random.fold_in(rng, 6)
    for dim, blocks in cuts:
        heights = jnp.exp(jax.random.uniform(jax.random.fold_in(own, dim), (blocks,), jnp.float32, low / len(cuts), largest / len(cuts)))
        level = level * jnp.repeat(heights, shape[dim] // blocks).reshape([-1 if axis == dim else 1 for axis in range(len(shape))])
    return level


def bell_draw(rng, dims, deviation, bound, cuts=(), kind=jnp.bfloat16):
    values = deviation * jax.random.normal(rng, dims, jnp.float32)
    if cuts:
        values = values * level_of(rng, dims, cuts, -0.22, 0.18)
    return jnp.clip(values, -bound, bound).astype(kind)


def setup_inputs(seed: int = 0) -> dict:
    streams_of = jax.random.split(jax.random.key(seed), 21)
    return {
        "decoder_in": bell_draw(streams_of[0], (SEQS, LENGTH, D), 1.0, 6.0, ((0, 8), (1, 16))),
        "encoder_states": bell_draw(streams_of[1], (SEQS, ENC_LEN, D), 1.0, 6.0, ((0, 8), (1, 16))),
        "out_grad": bell_draw(streams_of[2], (SEQS, LENGTH, D), 1.0, 6.0, ((0, 8), (1, 16))),
        "block_pairs": jax.random.permutation(streams_of[3], N_CTX).astype(jnp.int32),
        "bucket_table": draw_bucket_table(jax.random.fold_in(streams_of[20], 71), 0),
        "gain_self": jnp.clip(1.0 + 0.15 * jax.random.normal(streams_of[5], (D,), jnp.float32), 0.25, 1.75).astype(jnp.bfloat16),
        "self_query": bell_draw(streams_of[6], (D, D), (8 * D) ** -0.5, 0.078125, ((0, 8),)),
        "self_key": bell_draw(streams_of[7], (D, D), (8 * D) ** -0.5, 0.078125, ((0, 8),)),
        "self_value": bell_draw(streams_of[8], (D, D), D ** -0.5, 0.21875, ((0, 8),)),
        "self_out": bell_draw(streams_of[9], (D, D), (max(1, D // 128)) ** -0.5, 2.5, ((0, 8),)),
        "position_bias": bell_draw(streams_of[10], (BUCKETS, HEADS), 1.0, 4.0, ((0, 8),)),
        "gain_cross": jnp.clip(1.0 + 0.15 * jax.random.normal(streams_of[11], (D,), jnp.float32), 0.25, 1.75).astype(jnp.bfloat16),
        "cross_query": bell_draw(streams_of[12], (D, D), (8 * D) ** -0.5, 0.078125, ((0, 8),)),
        "cross_key": bell_draw(streams_of[13], (D, D), (8 * D) ** -0.5, 0.078125, ((0, 8),)),
        "cross_value": bell_draw(streams_of[14], (D, D), D ** -0.5, 0.21875, ((0, 8),)),
        "cross_out": bell_draw(streams_of[15], (D, D), (max(1, D // 256)) ** -0.5, 3.5, ((0, 8),)),
        "gain_feed": jnp.clip(1.0 + 0.15 * jax.random.normal(streams_of[16], (D,), jnp.float32), 0.25, 1.75).astype(jnp.bfloat16),
        "feed_gate": bell_draw(streams_of[17], (D, FF), D ** -0.5, 0.21875, ((0, 8),)),
        "feed_up": bell_draw(streams_of[18], (D, FF), D ** -0.5, 0.21875, ((0, 8),)),
        "feed_down": bell_draw(streams_of[19], (FF, D), FF ** -0.5, 0.125, ((0, 8),)),
    }


HIGHEST = lax.Precision.HIGHEST

@jax.custom_vjp
def low(v):
    return lax.optimization_barrier(v.astype(jnp.bfloat16)).astype(jnp.float32)

@jax.custom_vjp
def low_back(v):
    return v

def low_keep(v):
    return (low(v), None)

def low_pass(kept, grad):
    return (grad,)

def back_keep(v):
    return (v, None)

def back_low(kept, grad):
    return (low(grad),)
low.defvjp(low_keep, low_pass)
low_back.defvjp(back_keep, back_low)

def rms_scaled(values, gain):
    inverse = lax.rsqrt(lax.optimization_barrier(jnp.mean(values * values, axis=-1, keepdims=True)) + 1e-06)
    return values * inverse * gain

def product(left, right):
    return jnp.dot(left, right, precision=HIGHEST)

def place_rows(block_pairs, row_index, tok_dev, parts):
    half_block = tok_dev // 2
    owners = row_index // tok_dev
    within = row_index % tok_dev
    paired = jnp.take(block_pairs, owners)
    return jnp.where(within < half_block, paired * half_block + within, (2 * parts - 1 - paired) * half_block + within - half_block)

def self_block(queries, spots, keys_all, values_all, key_spots, bias_rows):
    heads = bias_rows.shape[0]
    count = queries.shape[0]
    scores = jnp.einsum('qhd,khd->hqk', queries.reshape(count, heads, -1), keys_all.reshape(keys_all.shape[0], heads, -1), precision=HIGHEST)
    scores = low_back(scores)
    distance = jnp.clip(spots[:, None] - key_spots[None, :], 0, bias_rows.shape[1] - 1)
    scores = scores + jnp.take(bias_rows, distance, axis=1)
    scores = jnp.where((key_spots[None, :] <= spots[:, None])[None], scores, -1e+30)
    shares = low(jax.nn.softmax(scores, axis=-1))
    mixture = jnp.einsum('hqk,khd->qhd', shares, values_all.reshape(values_all.shape[0], heads, -1), precision=HIGHEST)
    return mixture.reshape(count, -1)

def cross_block(queries, keys_all, values_all):
    count = queries.shape[0]
    scores = jnp.einsum('qhd,khd->hqk', queries.reshape(count, HEADS, -1), keys_all.reshape(keys_all.shape[0], HEADS, -1), precision=HIGHEST)
    scores = low_back(scores)
    shares = low(jax.nn.softmax(scores, axis=-1))
    mixture = jnp.einsum('hqk,khd->qhd', shares, values_all.reshape(values_all.shape[0], HEADS, -1), precision=HIGHEST)
    return mixture.reshape(count, -1)

def attend_self(queries, spots, keys_all, values_all, bias_rows):
    count = queries.shape[0]
    block_rows = min(512, count)
    blocks = queries.reshape(count // block_rows, block_rows, -1)
    places = spots.reshape(count // block_rows, block_rows)
    checked = jax.checkpoint(self_block)
    results = lax.map(lambda pieces: checked(pieces[0], pieces[1], keys_all, values_all, spots, bias_rows), (blocks, places))
    return results.reshape(count, -1)

def attend_cross(queries, keys_all, values_all):
    count = queries.shape[0]
    block_rows = min(512, count)
    blocks = queries.reshape(count // block_rows, block_rows, -1)
    checked = jax.checkpoint(cross_block)
    results = lax.map(lambda pieces: checked(pieces, keys_all, values_all), blocks)
    return results.reshape(count, -1)

def forward_sequence(decoder_row, encoder_row, spots, bucket_hot, weights):
    norm_one, query_one, key_one, value_one, out_one, table_full, norm_two, query_two, key_two, value_two, out_two, norm_three, gate_full, up_full, down_full = weights
    bias_rows = product(table_full.T, bucket_hot.T)
    normed_one = low(rms_scaled(decoder_row, norm_one))
    queries = low(low_back(product(normed_one, query_one)))
    keys_all = low(low_back(product(normed_one, key_one)))
    values_all = low(low_back(product(normed_one, value_one)))
    attended = low(low_back(attend_self(queries, spots, keys_all, values_all, bias_rows)))
    mid_one = decoder_row + low_back(product(attended, out_one))
    normed_two = low(rms_scaled(mid_one, norm_two))
    cross_queries = low(low_back(product(normed_two, query_two)))
    cross_keys = low(low_back(product(encoder_row, key_two)))
    cross_values = low(low_back(product(encoder_row, value_two)))
    cross_attended = low(low_back(attend_cross(cross_queries, cross_keys, cross_values)))
    mid_two = mid_one + low_back(product(cross_attended, out_two))
    normed_three = low(rms_scaled(mid_two, norm_three))
    gate_values = low(low_back(product(normed_three, gate_full)))
    up_values = low(low_back(product(normed_three, up_full)))
    hidden = low(jax.nn.gelu(gate_values, approximate=True) * up_values)
    return mid_two + low_back(product(hidden, down_full))

def reference(decoder_in, encoder_states, out_grad, block_pairs, bucket_table, gain_self, self_query, self_key, self_value, self_out, position_bias, gain_cross, cross_query, cross_key, cross_value, cross_out, gain_feed, feed_gate, feed_up, feed_down):
    weights = tuple((member.astype(jnp.float32) for member in (gain_self, self_query, self_key, self_value, self_out, position_bias, gain_cross, cross_query, cross_key, cross_value, cross_out, gain_feed, feed_gate, feed_up, feed_down)))
    spots = place_rows(block_pairs, jnp.arange(TOK_DEV * N_CTX, dtype=jnp.int32), TOK_DEV, N_CTX)
    bucket_hot = (bucket_table[:, None] == jnp.arange(BUCKETS, dtype=jnp.int32)[None, :]).astype(jnp.float32)

    def one_sequence(carried, inputs):
        decoder_row, encoder_row, grad_row = inputs
        result, pullback = jax.vjp(lambda first, second, third: forward_sequence(first, second, spots, bucket_hot, third), decoder_row.astype(jnp.float32), encoder_row.astype(jnp.float32), weights)
        grad_first, grad_second, grad_weights = pullback(grad_row.astype(jnp.float32))
        carried = tuple((left + right for left, right in zip(carried, grad_weights)))
        return (carried, (result, grad_first, grad_second))
    zeros_all = tuple((jnp.zeros_like(member) for member in weights))
    summed, stacked = lax.scan(one_sequence, zeros_all, (decoder_in, encoder_states, out_grad))
    return (stacked[0], stacked[1], stacked[2], summed[0], summed[1], summed[2], summed[3], summed[4], summed[5], summed[6], summed[7], summed[8], summed[9], summed[10], summed[11], summed[12], summed[13], summed[14])
```

```python
import functools

import jax
import jax.numpy as jnp
from jax import lax
from jax.experimental import pallas as pl
from jax.experimental.pallas import tpu as pltpu
from jax.sharding import PartitionSpec as P

D = 768
FF = 2048
HEADS = 12
HEAD_DIM = 64
PAIRS = HEADS // 2
N_CTX = 16
TOK = 128
ENC = 64
HALF = 64
REACH = 128
BF = jnp.bfloat16
F32 = jnp.float32
MIB = 1024 * 1024


def ctx_place():
    me = lax.axis_index("ctx")
    core = me % 2
    high = (me // 2) % 2
    y = me // 4
    return me, core, high, y


def slot_of(y, shift, high, core):
    return ((y + shift) % 4) * 4 + 2 * high + core


def greet(devices):
    barrier = pltpu.get_barrier_semaphore()
    for device in devices:
        pl.semaphore_signal(barrier, inc=1, device_id={"ctx": device})
    pl.semaphore_wait(barrier, len(devices))


def remote(src, dst, send_sem, recv_sem, device):
    return pltpu.make_async_remote_copy(
        src_ref=src, dst_ref=dst, send_sem=send_sem, recv_sem=recv_sem, device_id={"ctx": device}
    )


def gather_kernel(x_ref, out_ref, send_sem, recv_sem, local_sem):
    me, core, high, y = ctx_place()
    sibling = slot_of(y, 0, high, 1 - core)
    across = slot_of(y, 0, 1 - high, core)
    rows = [slot_of(y, shift, high, core) for shift in (1, 2, 3)]
    greet([sibling, across] + rows)
    sends = []

    def send(src, slot, device):
        copy = remote(src, out_ref.at[slot], send_sem.at[len(sends)], recv_sem.at[slot], device)
        copy.start()
        sends.append(copy)

    def arrived(slot):
        remote(x_ref, out_ref.at[slot], send_sem.at[0], recv_sem.at[slot], sibling).wait_recv()

    send(x_ref, me, across)
    for device in rows:
        send(x_ref, me, device)
    send(x_ref, me, sibling)
    own = pltpu.make_async_copy(x_ref, out_ref.at[me], local_sem)
    own.start()
    arrived(across)
    for device in rows:
        send(out_ref.at[across], across, device)
    send(out_ref.at[across], across, sibling)
    for shift in (1, 3, 2):
        slot = slot_of(y, shift, high, core)
        arrived(slot)
        send(out_ref.at[slot], slot, sibling)
    for shift in (1, 3, 2):
        slot = slot_of(y, shift, 1 - high, core)
        arrived(slot)
        send(out_ref.at[slot], slot, sibling)
    for shift in range(4):
        for other in range(2):
            arrived(slot_of(y, shift, other, 1 - core))
    own.wait()
    for copy in sends:
        copy.wait_send()


def ctx_gather(x, collective_id):
    return pl.pallas_call(
        gather_kernel,
        out_shape=jax.ShapeDtypeStruct((N_CTX,) + x.shape, x.dtype),
        in_specs=[pl.BlockSpec(memory_space=pl.ANY)],
        out_specs=pl.BlockSpec(memory_space=pl.ANY),
        scratch_shapes=[
            pltpu.SemaphoreType.DMA((15,)),
            pltpu.SemaphoreType.DMA((N_CTX,)),
            pltpu.SemaphoreType.DMA,
        ],
        compiler_params=pltpu.CompilerParams(collective_id=collective_id, has_side_effects=True),
        name="ctx_gather",
    )(x)


def scatter_kernel(
    x_ref, out_ref, from_core, kept, from_row, stage, from_high,
    send_a, recv_a, send_b, recv_b, send_c, recv_c,
):
    me, core, high, y = ctx_place()
    sibling = slot_of(y, 0, high, 1 - core)
    across = slot_of(y, 0, 1 - high, core)
    rows = [slot_of(y, shift, high, core) for shift in (1, 2, 3)]
    greet([sibling, across] + rows)
    order = [(shift, half) for shift in (2, 1, 3, 0) for half in range(2)]
    first = []
    for index, (shift, half) in enumerate(order):
        copy = remote(
            x_ref.at[slot_of(y, shift, half, 1 - core)],
            from_core.at[index],
            send_a.at[index],
            recv_a.at[index],
            sibling,
        )
        copy.start()
        first.append(copy)
    second = []
    for index, (shift, half) in enumerate(order):
        first[index].wait_recv()
        mine = x_ref[slot_of(y, shift, half, core)].astype(F32)
        kept[index] = (mine + from_core[index].astype(F32)).astype(BF)
        if half == 1 and shift:
            spot = index // 2
            copy = remote(
                kept.at[pl.ds(index - 1, 2)],
                from_row.at[spot],
                send_b.at[spot],
                recv_b.at[spot],
                rows[shift - 1],
            )
            copy.start()
            second.append(copy)
    for copy in second:
        copy.wait_recv()

    def total(half):
        result = kept[6 + half].astype(F32)
        for spot in range(3):
            result = result + from_row[spot, half].astype(F32)
        return result

    stage[...] = total(1 - high).astype(BF)
    last = remote(stage, from_high, send_c, recv_c, across)
    last.start()
    mine = total(high)
    last.wait_recv()
    out_ref[...] = (mine + from_high[...].astype(F32)).astype(BF)
    last.wait_send()
    for copy in first + second:
        copy.wait_send()


def ctx_scatter(x, collective_id):
    block = x.shape[1:]
    return pl.pallas_call(
        scatter_kernel,
        out_shape=jax.ShapeDtypeStruct(block, x.dtype),
        in_specs=[pl.BlockSpec(memory_space=pltpu.VMEM)],
        out_specs=pl.BlockSpec(memory_space=pltpu.VMEM),
        scratch_shapes=[
            pltpu.VMEM((8,) + block, BF),
            pltpu.VMEM((8,) + block, BF),
            pltpu.VMEM((3, 2) + block, BF),
            pltpu.VMEM(block, BF),
            pltpu.VMEM(block, BF),
            pltpu.SemaphoreType.DMA((8,)),
            pltpu.SemaphoreType.DMA((8,)),
            pltpu.SemaphoreType.DMA((3,)),
            pltpu.SemaphoreType.DMA((3,)),
            pltpu.SemaphoreType.DMA,
            pltpu.SemaphoreType.DMA,
        ],
        compiler_params=pltpu.CompilerParams(
            collective_id=collective_id, has_side_effects=True, vmem_limit_bytes=40 * MIB
        ),
        name="ctx_scatter",
    )(x)


def split_heads(block):
    lane = lax.broadcasted_iota(jnp.int32, block.shape, 1)
    nothing = jnp.zeros_like(block)
    return jnp.concatenate(
        [jnp.where(lane < HEAD_DIM, block, nothing), jnp.where(lane < HEAD_DIM, nothing, block)],
        axis=0,
    )


def join_heads(transposed):
    row = lax.broadcasted_iota(jnp.int32, (2 * HEAD_DIM, TOK), 0)
    return jnp.where(row < HEAD_DIM, transposed[:, :TOK], transposed[:, TOK:]).T


def contract(left, right, dims):
    return lax.dot_general(left, right, (dims, ((), ())), preferred_element_type=F32)


def key_chunk(ref, j):
    if ref.shape[2] == 2 * HALF:
        return ref[j, 0]
    return ref[pl.ds(2 * j, 2), 0].reshape(2 * HALF, 2 * HEAD_DIM)


def bias_chunk(class_ref, tile_ref, j):
    lane = lax.broadcasted_iota(jnp.int32, (HALF, TOK), 1)
    rows = []
    for half in range(2):
        spot = 2 * j + half
        near = class_ref[0, spot]
        far = class_ref[1, spot]
        rows.append(
            jnp.concatenate(
                [
                    jnp.where(lane < HALF, tile_ref[head, near], tile_ref[head, far])
                    for head in range(2)
                ],
                axis=1,
            )
        )
    return jnp.concatenate(rows, axis=0)


def fold(values, join):
    return join(values.reshape(-1, 8, values.shape[-1]), axis=0)


def forward_kernel(biased, *refs):
    if biased:
        class_ref, q_ref, k_ref, v_ref, tile_ref, out_ref, total_ref, score_ref, share_ref = refs
    else:
        q_ref, k_ref, v_ref, out_ref, total_ref, score_ref, share_ref = refs
    chunks = score_ref.shape[0]
    queries = split_heads(q_ref[...])
    highest = None
    for j in range(chunks):
        scores = contract(key_chunk(k_ref, j), queries, ((1,), (1,)))
        if biased:
            scores = scores + bias_chunk(class_ref, tile_ref, j)
        score_ref[j] = scores
        top = fold(scores, jnp.max)
        highest = top if highest is None else jnp.maximum(highest, top)
    highest = jnp.max(highest, axis=0, keepdims=True)
    summed = jnp.zeros((8, 2 * TOK), F32)
    for j in range(chunks):
        raised = jnp.exp(score_ref[j] - highest)
        summed = summed + fold(raised, jnp.sum)
        share_ref[j] = raised.astype(BF)
    summed = jnp.sum(summed, axis=0, keepdims=True)
    values = jnp.concatenate([key_chunk(v_ref, j) for j in range(chunks)], axis=0)
    mixed = contract(values, share_ref[...].reshape(-1, 2 * TOK), ((0,), (0,)))
    out_ref[...] = join_heads(mixed / summed).astype(BF)
    total_ref[0] = jnp.broadcast_to(highest + jnp.log(summed), (8, 2 * TOK))


def backward_kernel(biased, *refs):
    if biased:
        class_ref, near_ref, q_ref, k_ref, v_ref, g_ref, total_ref, tile_ref = refs[:8]
        dq_ref, dkv_ref, strip_ref, share_ref, slope_ref, share_low, slope_low = refs[8:]
    else:
        q_ref, k_ref, v_ref, g_ref, total_ref = refs[:5]
        dq_ref, dkv_ref, share_ref, slope_ref, share_low, slope_low = refs[5:]
    chunks = share_ref.shape[0]
    queries = split_heads(q_ref[...])
    grads = split_heads(g_ref[...])
    totals = total_ref[0, 0:1]
    inner = jnp.zeros((8, 2 * TOK), F32)
    for j in range(chunks):
        scores = contract(key_chunk(k_ref, j), queries, ((1,), (1,)))
        if biased:
            scores = scores + bias_chunk(class_ref, tile_ref, j)
        shares = jnp.exp(scores - totals)
        slopes = contract(key_chunk(v_ref, j), grads, ((1,), (1,)))
        inner = inner + fold(shares * slopes, jnp.sum)
        share_ref[j] = shares
        slope_ref[j] = slopes
        share_low[j] = shares.astype(BF)
    inner = jnp.sum(inner, axis=0, keepdims=True)
    for j in range(chunks):
        grad = share_ref[j] * (slope_ref[j] - inner)
        if biased:
            slope_ref[j] = grad
        slope_low[j] = grad.astype(BF)
    keys = jnp.concatenate([key_chunk(k_ref, j) for j in range(chunks)], axis=0)
    low = slope_low[...].reshape(-1, 2 * TOK)
    dq_ref[...] = join_heads(contract(keys, low, ((0,), (0,)))).astype(BF)
    shape = dkv_ref.shape
    block = (shape[0], shape[2], shape[3])
    dkv_ref[:, 0] = contract(low, queries, ((1,), (0,))).astype(BF).reshape(block)
    dkv_ref[:, 1] = (
        contract(share_low[...].reshape(-1, 2 * TOK), grads, ((1,), (0,))).astype(BF).reshape(block)
    )
    if biased:
        lane = lax.broadcasted_iota(jnp.int32, (HALF, TOK), 1)
        for gap in range(3):
            pieces = []
            for half in range(2):
                spot = near_ref[half, gap]
                held = slope_ref[jnp.maximum(spot, 0) // 2, pl.ds(
                    pl.multiple_of((jnp.maximum(spot, 0) % 2) * HALF, HALF), HALF)]
                pieces.append(jnp.where(spot >= 0, held, jnp.zeros_like(held)))
            for head in range(2):
                cut = slice(head * TOK, (head + 1) * TOK)
                strip_ref[head, gap] = jnp.where(lane < HALF, pieces[0][:, cut], pieces[1][:, cut])


def pair_columns(pair):
    return (0, pair)


def kv_spec(rows, row_block, part):
    return pl.BlockSpec(
        (N_CTX, 1, rows, 2 * HEAD_DIM), lambda pair: (0, part, row_block, pair)
    )


SMEM_SPEC = pl.BlockSpec(memory_space=pltpu.SMEM)
TILE_SPEC = pl.BlockSpec((2, 5, HALF, TOK), lambda pair: (pair, 0, 0, 0))
TOTAL_SPEC = pl.BlockSpec((1, 8, 2 * TOK), lambda pair: (pair, 0, 0))
ROW_SPEC = pl.BlockSpec((TOK, 2 * HEAD_DIM), pair_columns)
LOCAL = pltpu.CompilerParams(vmem_limit_bytes=48 * MIB)


def attend(queries, gathered, rows, row_block, classes=None, tiles=None):
    biased = classes is not None
    chunks = N_CTX * rows // TOK
    specs = [ROW_SPEC, kv_spec(rows, row_block, 0), kv_spec(rows, row_block, 1)]
    operands = [queries, gathered, gathered]
    if biased:
        specs = [SMEM_SPEC] + specs + [TILE_SPEC]
        operands = [classes] + operands + [tiles]
    return pl.pallas_call(
        functools.partial(forward_kernel, biased),
        grid=(PAIRS,),
        in_specs=specs,
        out_specs=[ROW_SPEC, TOTAL_SPEC],
        out_shape=[
            jax.ShapeDtypeStruct((TOK, D), BF),
            jax.ShapeDtypeStruct((PAIRS, 8, 2 * TOK), F32),
        ],
        scratch_shapes=[
            pltpu.VMEM((chunks, TOK, 2 * TOK), F32),
            pltpu.VMEM((chunks, TOK, 2 * TOK), BF),
        ],
        compiler_params=LOCAL,
        cost_estimate=pl.CostEstimate(flops=10**9, bytes_accessed=10**7, transcendentals=10**6),
        name="attend_self" if biased else "attend_cross",
    )(*operands)


def attend_back(queries, gathered, grads, totals, rows, row_block, classes=None, near=None, tiles=None):
    biased = classes is not None
    chunks = N_CTX * rows // TOK
    specs = [ROW_SPEC, kv_spec(rows, row_block, 0), kv_spec(rows, row_block, 1), ROW_SPEC, TOTAL_SPEC]
    operands = [queries, gathered, gathered, grads, totals]
    out_specs = [
        ROW_SPEC,
        pl.BlockSpec((N_CTX, 2, rows, 2 * HEAD_DIM), lambda pair: (0, 0, 0, pair)),
    ]
    out_shape = [
        jax.ShapeDtypeStruct((TOK, D), BF),
        jax.ShapeDtypeStruct((N_CTX, 2, rows, D), BF),
    ]
    if biased:
        specs = [SMEM_SPEC, SMEM_SPEC] + specs + [TILE_SPEC]
        operands = [classes, near] + operands + [tiles]
        out_specs.append(pl.BlockSpec((2, 3, HALF, TOK), lambda pair: (pair, 0, 0, 0)))
        out_shape.append(jax.ShapeDtypeStruct((HEADS, 3, HALF, TOK), F32))
    return pl.pallas_call(
        functools.partial(backward_kernel, biased),
        grid=(PAIRS,),
        in_specs=specs,
        out_specs=out_specs,
        out_shape=out_shape,
        scratch_shapes=[
            pltpu.VMEM((chunks, TOK, 2 * TOK), F32),
            pltpu.VMEM((chunks, TOK, 2 * TOK), F32),
            pltpu.VMEM((chunks, TOK, 2 * TOK), BF),
            pltpu.VMEM((chunks, TOK, 2 * TOK), BF),
        ],
        compiler_params=LOCAL,
        cost_estimate=pl.CostEstimate(flops=3 * 10**9, bytes_accessed=10**7, transcendentals=10**6),
        name="attend_self_back" if biased else "attend_cross_back",
    )(*operands)


def matmul(left, right):
    return jnp.dot(left, right, preferred_element_type=F32)


def transposed_left(left, right):
    return contract(left, right, ((0,), (0,)))


def transposed_right(left, right):
    return contract(left, right, ((1,), (1,)))


def rms_scaled(values, gain):
    inverse = lax.rsqrt(jnp.mean(values * values, axis=-1, keepdims=True) + 1e-06)
    return (values * inverse * gain).astype(BF)


def rms_back(values, gain, grad):
    inverse = lax.rsqrt(jnp.mean(values * values, axis=-1, keepdims=True) + 1e-06)
    scaled = gain * grad
    mixed = jnp.mean(values * scaled, axis=-1, keepdims=True)
    grad_values = inverse * scaled - values * (inverse * inverse * inverse * mixed)
    return grad_values, jnp.sum(values * inverse * grad, axis=0)


def gelu_product(gate_part, up_part):
    return jax.nn.gelu(gate_part, approximate=True) * up_part


def near_hot():
    shape = (REACH, 3 * HALF * HALF)
    spot = lax.broadcasted_iota(jnp.int32, shape, 1)
    gap = spot // (HALF * HALF)
    key = (spot // HALF) % HALF
    row = spot % HALF
    distance = jnp.clip(HALF * gap + row - key, 0, REACH - 1)
    return (distance == lax.broadcasted_iota(jnp.int32, shape, 0)).astype(BF)


def bias_tiles(bias_rows):
    near = matmul(bias_rows.astype(BF), near_hot()).reshape(HEADS, 3, HALF, HALF)
    key = jnp.arange(HALF, dtype=jnp.int32)[:, None]
    row = jnp.arange(HALF, dtype=jnp.int32)[None, :]
    barred = (jnp.arange(3) == 0)[None, :, None, None] & (key > row)[None, None]
    near = jnp.where(barred, -1e30, near)
    far = jnp.broadcast_to(bias_rows[:, -1][:, None, None, None], (HEADS, 1, HALF, HALF))
    none = jnp.full((HEADS, 1, HALF, HALF), -1e30, F32)
    tiles = jnp.concatenate([near, far, none], axis=1)
    return jnp.concatenate([tiles, tiles], axis=-1)


def bias_sums(strips):
    tiles = (strips[..., :HALF] + strips[..., HALF:]).reshape(HEADS, -1)
    high = tiles.astype(BF)
    low = (tiles - high.astype(F32)).astype(BF)
    hot = near_hot()
    sums = transposed_right(high, hot) + transposed_right(low, hot)
    far = -jnp.sum(sums[:, :-1], axis=1, keepdims=True)
    return jnp.concatenate([sums[:, :-1], far], axis=1)


def owned_rows(grad):
    return lax.psum_scatter(grad, "fsdp", scatter_dimension=0, tiled=True)


def body(
    decoder_in,
    encoder_states,
    out_grad,
    block_pairs,
    bucket_table,
    gain_self,
    self_query,
    self_key,
    self_value,
    self_out,
    position_bias,
    gain_cross,
    cross_query,
    cross_key,
    cross_value,
    cross_out,
    gain_feed,
    feed_gate,
    feed_up,
    feed_down,
):
    me = lax.axis_index("ctx")
    rows = self_query.shape[0]
    extra = jnp.concatenate(
        [
            gain_self[:, None],
            gain_cross[:, None],
            gain_feed[:, None],
            jnp.zeros((rows, 5), BF),
            jnp.pad(position_bias, ((0, rows - position_bias.shape[0]), (0, 0))),
            jnp.zeros((rows, 108), BF),
        ],
        axis=1,
    )
    early = lax.all_gather(
        jnp.concatenate([self_query, self_key, self_value, cross_key, cross_value, extra], axis=1),
        "fsdp",
        axis=0,
        tiled=True,
    )
    late = lax.all_gather(
        jnp.concatenate([self_out, cross_query, cross_out, feed_gate, feed_up], axis=1),
        "fsdp",
        axis=0,
        tiled=True,
    )
    down = lax.all_gather(feed_down, "fsdp", axis=0, tiled=True)
    qkv_one = early[:, : 3 * D]
    kv_two = early[:, 3 * D : 5 * D]
    gains = early[:, 5 * D : 5 * D + 3].astype(F32).T
    norm_one, norm_two, norm_three = gains[0:1], gains[1:2], gains[2:3]
    table = early.reshape(8, rows, -1)[:, :4, 5 * D + 8 : 5 * D + 20].reshape(32, HEADS)
    out_one = late[:, :D]
    query_two = late[:, D : 2 * D]
    out_two = late[:, 2 * D : 3 * D]
    gate_up = late[:, 3 * D :]

    bucket_hot = (bucket_table[:, None] == jnp.arange(32, dtype=jnp.int32)[None, :]).astype(BF)
    bias_rows = transposed_right(table.T, bucket_hot)
    tiles = bias_tiles(bias_rows)
    pair = block_pairs[me]
    query_blocks = jnp.stack([pair, 31 - pair])
    key_blocks = jnp.stack([block_pairs, 31 - block_pairs], axis=1).reshape(-1)
    gaps = query_blocks[:, None] - key_blocks[None, :]
    classes = jnp.where(gaps < 0, 4, jnp.minimum(gaps, 3)).astype(jnp.int32)
    wanted = query_blocks[:, None] - jnp.arange(3, dtype=jnp.int32)[None, :]
    near = jnp.max(
        jnp.where(
            wanted[:, :, None] == key_blocks[None, None, :],
            jnp.arange(32, dtype=jnp.int32)[None, None, :],
            -1,
        ),
        axis=-1,
    )

    tokens = decoder_in[0].astype(F32)
    states = encoder_states[0]
    upstream = out_grad[0]
    normed_one = rms_scaled(tokens, norm_one)
    qkv = matmul(normed_one, qkv_one).astype(BF)
    cross_kv = matmul(states, kv_two).astype(BF)
    queries = qkv[:, :D]
    local = jnp.stack(
        [
            jnp.concatenate([qkv[:, D : 2 * D], cross_kv[:, :D]], axis=0),
            jnp.concatenate([qkv[:, 2 * D :], cross_kv[:, D:]], axis=0),
        ]
    )
    gathered = ctx_gather(local, 0)
    attended, self_totals = attend(queries, gathered, TOK, 0, classes, tiles)
    mid_one = tokens + matmul(attended, out_one)
    normed_two = rms_scaled(mid_one, norm_two)
    cross_queries = matmul(normed_two, query_two).astype(BF)
    cross_attended, cross_totals = attend(cross_queries, gathered, ENC, 2)
    mid_two = mid_one + matmul(cross_attended, out_two)
    normed_three = rms_scaled(mid_two, norm_three)
    gate_up_values = matmul(normed_three, gate_up).astype(BF).astype(F32)
    gate_values, up_values = gate_up_values[:, :FF], gate_up_values[:, FF:]
    hidden, pull_feed = jax.vjp(gelu_product, gate_values, up_values)
    hidden = hidden.astype(BF)
    block_out = mid_two + matmul(hidden, down)

    d_hidden = transposed_right(upstream, down)
    d_gate_up = jnp.concatenate(pull_feed(d_hidden), axis=1).astype(BF)
    grad_down = owned_rows(transposed_left(hidden, upstream).astype(BF))
    grad_gate_up = owned_rows(transposed_left(normed_three, d_gate_up).astype(BF))
    d_normed_three = transposed_right(d_gate_up, gate_up)
    part_three, grad_norm_three = rms_back(mid_two, norm_three, d_normed_three)
    d_mid_two = upstream.astype(F32) + part_three
    cross_branch = d_mid_two.astype(BF)
    d_cross_attended = transposed_right(cross_branch, out_two).astype(BF)
    d_cross_queries, d_cross_kv_all = attend_back(
        cross_queries, gathered, d_cross_attended, cross_totals, ENC, 2
    )
    d_cross_kv = ctx_scatter(d_cross_kv_all, 1)
    d_cross_kv = jnp.concatenate([d_cross_kv[0], d_cross_kv[1]], axis=1)
    grad_encoder = transposed_right(d_cross_kv, kv_two)
    grad_cross = owned_rows(
        jnp.concatenate(
            [
                transposed_left(cross_attended, cross_branch),
                transposed_left(normed_two, d_cross_queries),
                transposed_left(states, d_cross_kv),
            ],
            axis=1,
        ).astype(BF)
    )
    d_normed_two = transposed_right(d_cross_queries, query_two)
    part_two, grad_norm_two = rms_back(mid_one, norm_two, d_normed_two)
    d_mid_one = d_mid_two + part_two
    self_branch = d_mid_one.astype(BF)
    d_attended = transposed_right(self_branch, out_one).astype(BF)
    d_queries, d_kv_all, strips = attend_back(
        queries, gathered, d_attended, self_totals, TOK, 0, classes, near, tiles
    )
    d_kv = ctx_scatter(d_kv_all, 2)
    d_qkv = jnp.concatenate([d_queries, d_kv[0], d_kv[1]], axis=1)
    d_normed_one = transposed_right(d_qkv, qkv_one)
    part_one, grad_norm_one = rms_back(tokens, norm_one, d_normed_one)
    grad_decoder = d_mid_one + part_one
    grad_table = matmul(bias_sums(strips), bucket_hot.astype(F32)).T.reshape(8, 4, HEADS)
    grad_extra = jnp.concatenate(
        [
            grad_norm_one[:, None],
            grad_norm_two[:, None],
            grad_norm_three[:, None],
            jnp.zeros((D, 5), F32),
            jnp.pad(grad_table, ((0, 0), (0, rows - 4), (0, 0))).reshape(D, HEADS),
            jnp.zeros((D, 108), F32),
        ],
        axis=1,
    )
    grad_self = owned_rows(
        jnp.concatenate(
            [transposed_left(attended, self_branch), transposed_left(normed_one, d_qkv), grad_extra],
            axis=1,
        ).astype(BF)
    )

    flat = jnp.concatenate(
        [grad_down.reshape(-1), grad_gate_up.reshape(-1), grad_cross.reshape(-1), grad_self.reshape(-1)]
    )
    length = flat.shape[0]
    unit = N_CTX * 16 * 128
    padded = -(-length // unit) * unit
    flat = jnp.pad(flat, (0, padded - length)).reshape(N_CTX, -1, 128)
    summed = ctx_gather(ctx_scatter(flat, 3), 4).reshape(-1)
    cuts = [grad_down.size, grad_gate_up.size, grad_cross.size, grad_self.size]
    spots = [sum(cuts[:k]) for k in range(5)]
    grad_down = summed[: spots[1]].reshape(grad_down.shape).astype(F32)
    grad_gate_up = summed[spots[1] : spots[2]].reshape(grad_gate_up.shape).astype(F32)
    grad_cross = summed[spots[2] : spots[3]].reshape(grad_cross.shape).astype(F32)
    grad_self = summed[spots[3] : spots[4]].reshape(grad_self.shape).astype(F32)
    extras = grad_self[:, 4 * D :]
    return (
        block_out[None],
        grad_decoder[None],
        grad_encoder[None],
        extras[:, 0],
        grad_self[:, D : 2 * D],
        grad_self[:, 2 * D : 3 * D],
        grad_self[:, 3 * D : 4 * D],
        grad_self[:, :D],
        extras[:4, 8:20],
        extras[:, 1],
        grad_cross[:, D : 2 * D],
        grad_cross[:, 2 * D : 3 * D],
        grad_cross[:, 3 * D :],
        grad_cross[:, :D],
        extras[:, 2],
        grad_gate_up[:, :FF],
        grad_gate_up[:, FF:],
        grad_down,
    )


def solution(mesh):
    tokens = P("fsdp", "ctx", None)
    matrix = P("fsdp", None)
    vector = P("fsdp")
    weights = (
        (vector,) + (matrix,) * 5 + (vector,) + (matrix,) * 4 + (vector,) + (matrix,) * 3
    )
    return jax.shard_map(
        body,
        mesh=mesh,
        in_specs=(tokens,) * 3 + (P(), P()) + weights,
        out_specs=(tokens,) * 3 + weights,
        check_vma=False,
    )
```

```python
import functools

import jax
import jax.numpy as jnp
from jax import lax
from jax.experimental import pallas as pl
from jax.experimental.pallas import tpu as pltpu
from jax.sharding import PartitionSpec as P

D = 768
FF = 2048
HEADS = 12
HEAD_DIM = 64
PAIRS = HEADS // 2
N_CTX = 16
TOK = 128
ENC = 64
HALF = 64
REACH = 128
BF = jnp.bfloat16
F32 = jnp.float32
MIB = 1024 * 1024


def ctx_place():
    me = lax.axis_index("ctx")
    core = me % 2
    high = (me // 2) % 2
    y = me // 4
    return me, core, high, y


def slot_of(y, shift, high, core):
    return ((y + shift) % 4) * 4 + 2 * high + core


def greet(devices):
    barrier = pltpu.get_barrier_semaphore()
    for device in devices:
        pl.semaphore_signal(barrier, inc=1, device_id={"ctx": device})
    pl.semaphore_wait(barrier, len(devices))


def remote(src, dst, send_sem, recv_sem, device):
    return pltpu.make_async_remote_copy(
        src_ref=src, dst_ref=dst, send_sem=send_sem, recv_sem=recv_sem, device_id={"ctx": device}
    )


def gather_kernel(x_ref, out_ref, send_sem, recv_sem, local_sem):
    me, core, high, y = ctx_place()
    sibling = slot_of(y, 0, high, 1 - core)
    across = slot_of(y, 0, 1 - high, core)
    rows = [slot_of(y, shift, high, core) for shift in (1, 2, 3)]
    greet([sibling, across] + rows)
    sends = []

    def send(src, slot, device):
        copy = remote(src, out_ref.at[slot], send_sem.at[len(sends)], recv_sem.at[slot], device)
        copy.start()
        sends.append(copy)

    def arrived(slot):
        remote(x_ref, out_ref.at[slot], send_sem.at[0], recv_sem.at[slot], sibling).wait_recv()

    send(x_ref, me, across)
    for device in rows:
        send(x_ref, me, device)
    send(x_ref, me, sibling)
    own = pltpu.make_async_copy(x_ref, out_ref.at[me], local_sem)
    own.start()
    arrived(across)
    for device in rows:
        send(out_ref.at[across], across, device)
    send(out_ref.at[across], across, sibling)
    for shift in (1, 3, 2):
        slot = slot_of(y, shift, high, core)
        arrived(slot)
        send(out_ref.at[slot], slot, sibling)
    for shift in (1, 3, 2):
        slot = slot_of(y, shift, 1 - high, core)
        arrived(slot)
        send(out_ref.at[slot], slot, sibling)
    for shift in range(4):
        for other in range(2):
            arrived(slot_of(y, shift, other, 1 - core))
    own.wait()
    for copy in sends:
        copy.wait_send()


def ctx_gather(x, collective_id):
    return pl.pallas_call(
        gather_kernel,
        out_shape=jax.ShapeDtypeStruct((N_CTX,) + x.shape, x.dtype),
        in_specs=[pl.BlockSpec(memory_space=pl.ANY)],
        out_specs=pl.BlockSpec(memory_space=pl.ANY),
        scratch_shapes=[
            pltpu.SemaphoreType.DMA((15,)),
            pltpu.SemaphoreType.DMA((N_CTX,)),
            pltpu.SemaphoreType.DMA,
        ],
        compiler_params=pltpu.CompilerParams(collective_id=collective_id, has_side_effects=True),
        name="ctx_gather",
    )(x)


def scatter_kernel(
    x_ref, out_ref, from_core, kept, from_row, stage, from_high,
    send_a, recv_a, send_b, recv_b, send_c, recv_c,
):
    me, core, high, y = ctx_place()
    sibling = slot_of(y, 0, high, 1 - core)
    across = slot_of(y, 0, 1 - high, core)
    rows = [slot_of(y, shift, high, core) for shift in (1, 2, 3)]
    greet([sibling, across] + rows)
    order = [(shift, half) for shift in (2, 1, 3, 0) for half in range(2)]
    first = []
    for index, (shift, half) in enumerate(order):
        copy = remote(
            x_ref.at[slot_of(y, shift, half, 1 - core)],
            from_core.at[index],
            send_a.at[index],
            recv_a.at[index],
            sibling,
        )
        copy.start()
        first.append(copy)
    second = []
    for index, (shift, half) in enumerate(order):
        first[index].wait_recv()
        mine = x_ref[slot_of(y, shift, half, core)].astype(F32)
        kept[index] = (mine + from_core[index].astype(F32)).astype(BF)
        if half == 1 and shift:
            spot = index // 2
            copy = remote(
                kept.at[pl.ds(index - 1, 2)],
                from_row.at[spot],
                send_b.at[spot],
                recv_b.at[spot],
                rows[shift - 1],
            )
            copy.start()
            second.append(copy)
    for copy in second:
        copy.wait_recv()

    def total(half):
        result = kept[6 + half].astype(F32)
        for spot in range(3):
            result = result + from_row[spot, half].astype(F32)
        return result

    stage[...] = total(1 - high).astype(BF)
    last = remote(stage, from_high, send_c, recv_c, across)
    last.start()
    mine = total(high)
    last.wait_recv()
    out_ref[...] = (mine + from_high[...].astype(F32)).astype(BF)
    last.wait_send()
    for copy in first + second:
        copy.wait_send()


def ctx_scatter(x, collective_id):
    block = x.shape[1:]
    return pl.pallas_call(
        scatter_kernel,
        out_shape=jax.ShapeDtypeStruct(block, x.dtype),
        in_specs=[pl.BlockSpec(memory_space=pltpu.VMEM)],
        out_specs=pl.BlockSpec(memory_space=pltpu.VMEM),
        scratch_shapes=[
            pltpu.VMEM((8,) + block, BF),
            pltpu.VMEM((8,) + block, BF),
            pltpu.VMEM((3, 2) + block, BF),
            pltpu.VMEM(block, BF),
            pltpu.VMEM(block, BF),
            pltpu.SemaphoreType.DMA((8,)),
            pltpu.SemaphoreType.DMA((8,)),
            pltpu.SemaphoreType.DMA((3,)),
            pltpu.SemaphoreType.DMA((3,)),
            pltpu.SemaphoreType.DMA,
            pltpu.SemaphoreType.DMA,
        ],
        compiler_params=pltpu.CompilerParams(
            collective_id=collective_id, has_side_effects=True, vmem_limit_bytes=40 * MIB
        ),
        name="ctx_scatter",
    )(x)


def torus_place():
    me, core, high, y = ctx_place()
    shard = lax.axis_index("fsdp")
    return me, core, high, y, shard // 4, shard % 4


def hop(src, dst, send_sem, recv_sem, ctx, fsdp):
    return pltpu.make_async_remote_copy(
        src_ref=src,
        dst_ref=dst,
        send_sem=send_sem,
        recv_sem=recv_sem,
        device_id={"ctx": ctx, "fsdp": fsdp},
    )


def greet_all(devices):
    barrier = pltpu.get_barrier_semaphore()
    for ctx, fsdp in devices:
        pl.semaphore_signal(barrier, inc=1, device_id={"ctx": ctx, "fsdp": fsdp})
    pl.semaphore_wait(barrier, len(devices))


def weights_kernel(count, *refs):
    sources = refs[:count]
    targets = refs[count : 2 * count]
    send_sem, x_sem, z_sem, core_sem, local_sem = refs[2 * count :]
    me, core, high, y, low, x = torus_place()
    shard = low * 4 + x
    sibling = (slot_of(y, 0, high, 1 - core), shard)
    inside = (me, (1 - low) * 4 + x)
    outside = (slot_of(y, 0, 1 - high, core), (1 - low) * 4 + x)
    others = [low * 4 + (x + shift) % 4 for shift in (1, 2, 3)]
    greet_all([sibling, inside, outside] + [(me, other) for other in others])

    def part(index, owner, whose, side=None):
        ref = targets[index]
        rows = ref.shape[1] // 2
        start = pl.multiple_of(whose * rows, 16)
        if side is None:
            return ref.at[owner, pl.ds(start, rows), :]
        width = ref.shape[2] // 2
        return ref.at[owner, pl.ds(start, rows), pl.ds(side * width, width)]

    def mine(index, side=None):
        ref = sources[index]
        rows = ref.shape[0] // 2
        start = pl.multiple_of(core * rows, 16)
        if side is None:
            return ref.at[pl.ds(start, rows), :]
        width = ref.shape[1] // 2
        return ref.at[pl.ds(start, rows), pl.ds(side * width, width)]

    sends = []

    def send(index, src, dst, recv_sem, device):
        copy = hop(src, dst, send_sem.at[len(sends)], recv_sem, *device)
        copy.start()
        sends.append(copy)

    def arrived(index, ref, recv_sem):
        hop(ref, ref, send_sem.at[0], recv_sem, *sibling).wait_recv()

    for index in range(count):
        for spot in (1, 0, 2):
            send(index, mine(index), part(index, shard, core), x_sem.at[index, spot], (me, others[spot]))
        for side, device in enumerate((inside, outside)):
            send(
                index, mine(index, side), part(index, shard, core, side), z_sem.at[index, 3, side], device
            )
    own = []
    for index in range(count):
        copy = pltpu.make_async_copy(sources[index], targets[index].at[shard], local_sem.at[index])
        copy.start()
        own.append(copy)
    for index in range(count):
        for spot in (0, 2, 1):
            owner = low * 4 + (x + 3 - spot) % 4
            block = part(index, owner, core)
            arrived(index, block, x_sem.at[index, spot])
            for side, device in enumerate((inside, outside)):
                piece = part(index, owner, core, side)
                send(index, piece, piece, z_sem.at[index, spot, side], device)
            send(index, block, block, core_sem.at[index, spot], sibling)
        for spot in (3, 0, 2, 1):
            owner = (1 - low) * 4 + (x + 3 - spot) % 4
            for side in range(2):
                piece = part(index, owner, core, side)
                arrived(index, piece, z_sem.at[index, spot, side])
                send(index, piece, piece, core_sem.at[index, 3 + 2 * spot + side], sibling)
    for index in range(count):
        for spot in range(3):
            owner = low * 4 + (x + 3 - spot) % 4
            arrived(index, part(index, owner, 1 - core), core_sem.at[index, spot])
        for spot in range(4):
            owner = (1 - low) * 4 + (x + 3 - spot) % 4
            for side in range(2):
                piece = part(index, owner, 1 - core, side)
                arrived(index, piece, core_sem.at[index, 3 + 2 * spot + side])
    for copy in own:
        copy.wait()
    for copy in sends:
        copy.wait_send()


def gather_weights(packs, collective_id):
    count = len(packs)
    return pl.pallas_call(
        functools.partial(weights_kernel, count),
        out_shape=[jax.ShapeDtypeStruct((8,) + pack.shape, pack.dtype) for pack in packs],
        in_specs=[pl.BlockSpec(memory_space=pl.ANY)] * count,
        out_specs=[pl.BlockSpec(memory_space=pl.ANY)] * count,
        scratch_shapes=[
            pltpu.SemaphoreType.DMA((22 * count,)),
            pltpu.SemaphoreType.DMA((count, 3)),
            pltpu.SemaphoreType.DMA((count, 4, 2)),
            pltpu.SemaphoreType.DMA((count, 11)),
            pltpu.SemaphoreType.DMA((count,)),
        ],
        compiler_params=pltpu.CompilerParams(collective_id=collective_id, has_side_effects=True),
        name="gather_weights",
    )(*packs)


PIECE = 48
ROOM = D + FF // 4 + FF // 8 + 128


def reduce_kernel(widths, *refs):
    count = len(widths)
    parts = refs[:count]
    wide_ref, down_ref, out_ref = refs[count : count + 3]
    (
        from_core, kept, from_z, held, from_x, wide_in, down_in, packed, from_ctx, total_ref,
        core_send, core_recv, z_send, z_recv, x_send, x_recv,
        ctx_send, ctx_recv, out_send, out_recv, pass_send, pass_recv, local_sem,
    ) = refs[count + 3 :]
    me, core, high, y, low, x = torus_place()
    shard = low * 4 + x
    rank = y * 2 + high
    sibling = (slot_of(y, 0, high, 1 - core), shard)
    inside = (me, (1 - low) * 4 + x)
    outside = (slot_of(y, 0, 1 - high, core), (1 - low) * 4 + x)
    others = [low * 4 + (x + shift) % 4 for shift in (1, 2, 3)]
    shifts = [(dy, dz) for dy in range(4) for dz in range(2)][1:]
    mates = [((y + dy) % 4) * 2 + (high + dz) % 2 for dy, dz in shifts]
    greet_all(
        [sibling, inside, outside]
        + [(me, other) for other in others]
        + [(mate * 2 + core, shard) for mate in mates]
    )
    mine = pl.ds(pl.multiple_of(core * PIECE, 16), PIECE)
    theirs = pl.ds(pl.multiple_of((1 - core) * PIECE, 16), PIECE)
    mine_down = pl.ds(pl.multiple_of(core * 128, 16), 128)
    theirs_down = pl.ds(pl.multiple_of((1 - core) * 128, 16), 128)
    starts = [sum(widths[:k]) for k in range(count)]
    cuts = [pl.ds(starts[k], widths[k]) for k in range(count)]
    sends = []

    def go(src, dst, send_sem, recv_sem, device):
        copy = hop(src, dst, send_sem, recv_sem, *device)
        copy.start()
        sends.append(copy)
        return copy

    over_core = [
        go(
            parts[k].at[:, theirs, :],
            from_core.at[:, :, cuts[k]],
            core_send.at[k],
            core_recv.at[k],
            sibling,
        )
        for k in range(count)
    ]
    wide_copy = go(wide_ref.at[theirs, :], wide_in, core_send.at[count], core_recv.at[count], sibling)
    down_copy = go(
        down_ref.at[theirs_down, :], down_in, core_send.at[count + 1], core_recv.at[count + 1], sibling
    )
    over_z = [None] * count
    over_x = [None] * count

    def step_core(k):
        over_core[k].wait_recv()
        half = widths[k] // 2
        away = pl.ds(4 * (1 - low), 4)
        for owner in range(8):
            kept[owner, :, cuts[k]] = (
                parts[k][owner, mine, :].astype(F32) + from_core[owner, :, cuts[k]].astype(F32)
            ).astype(BF)
        over_z[k] = [
            go(
                kept.at[away, :, pl.ds(starts[k] + side * half, half)],
                from_z.at[:, :, pl.ds(starts[k] + side * half, half)],
                z_send.at[k, side],
                z_recv.at[k, side],
                device,
            )
            for side, device in enumerate((inside, outside))
        ]

    def step_z(k):
        for copy in over_z[k]:
            copy.wait_recv()
        for column in range(4):
            held[column, :, cuts[k]] = (
                kept[4 * low + column, :, cuts[k]].astype(F32) + from_z[column, :, cuts[k]].astype(F32)
            ).astype(BF)
        over_x[k] = [
            go(
                held.at[(x + spot + 1) % 4, :, cuts[k]],
                from_x.at[spot, :, cuts[k]],
                x_send.at[k, spot],
                x_recv.at[k, spot],
                (me, others[spot]),
            )
            for spot in (1, 0, 2)
        ]

    def step_x(k):
        for copy in over_x[k]:
            copy.wait_recv()
        total = held[x, :, cuts[k]].astype(F32)
        for spot in range(3):
            total = total + from_x[spot, :, cuts[k]].astype(F32)
        total = total.astype(BF)
        if widths[k] % D:
            packed[0, :, ROOM - 128 :] = total[:, :128]
            for piece in range(1, 8):
                packed[piece, :, ROOM - 128 :] = jnp.zeros((PIECE, 128), BF)
            return
        for piece in range(widths[k] // D):
            packed[starts[k] // D + piece, :, :D] = total[:, piece * D : (piece + 1) * D]

    for k in range(count + 2):
        if k < count:
            step_core(k)
        if 0 <= k - 1 < count:
            step_z(k - 1)
        if k - 2 >= 0:
            step_x(k - 2)
        if k == 1:
            wide_copy.wait_recv()
            for piece in range(8):
                cut = slice(piece * 512, piece * 512 + 512)
                packed[piece, :, D : D + 512] = (
                    wide_ref[mine, cut].astype(F32) + wide_in[:, cut].astype(F32)
                ).astype(BF)
            down_copy.wait_recv()
            total = (down_ref[mine_down, :].astype(F32) + down_in[...].astype(F32)).astype(BF)
            for piece in range(8):
                for part in range(3):
                    packed[piece, part * 16 : part * 16 + 16, D + 512 : D + 768] = total[
                        piece * 16 : piece * 16 + 16, part * 256 : part * 256 + 256
                    ]

    over_ctx = [
        go(
            packed.at[mate],
            from_ctx.at[spot],
            ctx_send.at[spot],
            ctx_recv.at[spot],
            (mate * 2 + core, shard),
        )
        for spot, mate in enumerate(mates)
    ]
    total = packed[rank].astype(F32)
    for spot in range(7):
        over_ctx[spot].wait_recv()
        total = total + from_ctx[spot].astype(F32)
    total_ref[...] = total.astype(BF)
    for spot, mate in enumerate(mates):
        go(
            total_ref,
            out_ref.at[rank, mine, :],
            out_send.at[spot],
            out_recv.at[rank],
            (mate * 2 + core, shard),
        )
    go(total_ref, out_ref.at[rank, mine, :], pass_send.at[7], pass_recv.at[rank], sibling)
    own = pltpu.make_async_copy(total_ref, out_ref.at[rank, mine, :], local_sem)
    own.start()

    def landed(ref, recv_sem):
        hop(ref, ref, pass_send.at[0], recv_sem, *sibling).wait_recv()

    for spot, mate in enumerate(mates):
        block = out_ref.at[mate, mine, :]
        landed(block, out_recv.at[mate])
        go(block, block, pass_send.at[spot], pass_recv.at[mate], sibling)
    for mate in [rank] + mates:
        landed(out_ref.at[mate, theirs, :], pass_recv.at[mate])
    own.wait()
    for copy in sends:
        copy.wait_send()


def reduce_gradients(parts, wide, down, collective_id):
    widths = [part.shape[2] for part in parts]
    count = len(parts)
    span = sum(widths)
    dma = pltpu.SemaphoreType.DMA
    return pl.pallas_call(
        functools.partial(reduce_kernel, widths),
        out_shape=jax.ShapeDtypeStruct((8, 2 * PIECE, ROOM), BF),
        in_specs=[pl.BlockSpec(memory_space=pltpu.VMEM)] * (count + 2),
        out_specs=pl.BlockSpec(memory_space=pl.ANY),
        scratch_shapes=[
            pltpu.VMEM((8, PIECE, span), BF),
            pltpu.VMEM((8, PIECE, span), BF),
            pltpu.VMEM((4, PIECE, span), BF),
            pltpu.VMEM((4, PIECE, span), BF),
            pltpu.VMEM((3, PIECE, span), BF),
            pltpu.VMEM((PIECE, wide.shape[1]), BF),
            pltpu.VMEM((128, down.shape[1]), BF),
            pltpu.VMEM((8, PIECE, ROOM), BF),
            pltpu.VMEM((7, PIECE, ROOM), BF),
            pltpu.VMEM((PIECE, ROOM), BF),
            dma((count + 2,)),
            dma((count + 2,)),
            dma((count, 2)),
            dma((count, 2)),
            dma((count, 3)),
            dma((count, 3)),
            dma((7,)),
            dma((7,)),
            dma((7,)),
            dma((8,)),
            dma((8,)),
            dma((8,)),
            dma,
        ],
        compiler_params=pltpu.CompilerParams(
            collective_id=collective_id, has_side_effects=True, vmem_limit_bytes=56 * MIB
        ),
        name="reduce_gradients",
    )(*parts, wide, down)


def split_heads(block):
    lane = lax.broadcasted_iota(jnp.int32, block.shape, 1)
    nothing = jnp.zeros_like(block)
    return jnp.concatenate(
        [jnp.where(lane < HEAD_DIM, block, nothing), jnp.where(lane < HEAD_DIM, nothing, block)],
        axis=0,
    )


def join_heads(transposed):
    row = lax.broadcasted_iota(jnp.int32, (2 * HEAD_DIM, TOK), 0)
    return jnp.where(row < HEAD_DIM, transposed[:, :TOK], transposed[:, TOK:]).T


def contract(left, right, dims):
    return lax.dot_general(left, right, (dims, ((), ())), preferred_element_type=F32)


def key_chunk(ref, j):
    if ref.shape[2] == 2 * HALF:
        return ref[j, 0]
    return ref[pl.ds(2 * j, 2), 0].reshape(2 * HALF, 2 * HEAD_DIM)


def bias_chunk(class_ref, tile_ref, j):
    lane = lax.broadcasted_iota(jnp.int32, (HALF, TOK), 1)
    rows = []
    for half in range(2):
        spot = 2 * j + half
        near = class_ref[0, spot]
        far = class_ref[1, spot]
        rows.append(
            jnp.concatenate(
                [
                    jnp.where(lane < HALF, tile_ref[head, near], tile_ref[head, far])
                    for head in range(2)
                ],
                axis=1,
            )
        )
    return jnp.concatenate(rows, axis=0)


def fold(values, join):
    return join(values.reshape(-1, 8, values.shape[-1]), axis=0)


def forward_kernel(biased, *refs):
    if biased:
        class_ref, q_ref, k_ref, v_ref, tile_ref, out_ref, total_ref, score_ref, share_ref = refs
    else:
        q_ref, k_ref, v_ref, out_ref, total_ref, score_ref, share_ref = refs
    chunks = score_ref.shape[0]
    queries = split_heads(q_ref[...])
    highest = None
    for j in range(chunks):
        scores = contract(key_chunk(k_ref, j), queries, ((1,), (1,)))
        if biased:
            scores = scores + bias_chunk(class_ref, tile_ref, j)
        score_ref[j] = scores
        top = fold(scores, jnp.max)
        highest = top if highest is None else jnp.maximum(highest, top)
    highest = jnp.max(highest, axis=0, keepdims=True)
    summed = jnp.zeros((8, 2 * TOK), F32)
    for j in range(chunks):
        raised = jnp.exp(score_ref[j] - highest)
        summed = summed + fold(raised, jnp.sum)
        share_ref[j] = raised.astype(BF)
    summed = jnp.sum(summed, axis=0, keepdims=True)
    values = jnp.concatenate([key_chunk(v_ref, j) for j in range(chunks)], axis=0)
    mixed = contract(values, share_ref[...].reshape(-1, 2 * TOK), ((0,), (0,)))
    out_ref[...] = join_heads(mixed / summed).astype(BF)
    total_ref[0] = jnp.broadcast_to(highest + jnp.log(summed), (8, 2 * TOK))


def backward_kernel(biased, *refs):
    if biased:
        class_ref, near_ref, q_ref, k_ref, v_ref, g_ref, total_ref, tile_ref = refs[:8]
        dq_ref, dkv_ref, strip_ref, share_ref, slope_ref, share_low, slope_low = refs[8:]
    else:
        q_ref, k_ref, v_ref, g_ref, total_ref = refs[:5]
        dq_ref, dkv_ref, share_ref, slope_ref, share_low, slope_low = refs[5:]
    chunks = share_ref.shape[0]
    queries = split_heads(q_ref[...])
    grads = split_heads(g_ref[...])
    totals = total_ref[0, 0:1]
    inner = jnp.zeros((8, 2 * TOK), F32)
    for j in range(chunks):
        scores = contract(key_chunk(k_ref, j), queries, ((1,), (1,)))
        if biased:
            scores = scores + bias_chunk(class_ref, tile_ref, j)
        shares = jnp.exp(scores - totals)
        slopes = contract(key_chunk(v_ref, j), grads, ((1,), (1,)))
        inner = inner + fold(shares * slopes, jnp.sum)
        share_ref[j] = shares
        slope_ref[j] = slopes
        share_low[j] = shares.astype(BF)
    inner = jnp.sum(inner, axis=0, keepdims=True)
    for j in range(chunks):
        grad = share_ref[j] * (slope_ref[j] - inner)
        if biased:
            slope_ref[j] = grad
        slope_low[j] = grad.astype(BF)
    keys = jnp.concatenate([key_chunk(k_ref, j) for j in range(chunks)], axis=0)
    low = slope_low[...].reshape(-1, 2 * TOK)
    dq_ref[...] = join_heads(contract(keys, low, ((0,), (0,)))).astype(BF)
    shape = dkv_ref.shape
    block = (shape[0], shape[2], shape[3])
    dkv_ref[:, 0] = contract(low, queries, ((1,), (0,))).astype(BF).reshape(block)
    dkv_ref[:, 1] = (
        contract(share_low[...].reshape(-1, 2 * TOK), grads, ((1,), (0,))).astype(BF).reshape(block)
    )
    if biased:
        lane = lax.broadcasted_iota(jnp.int32, (HALF, TOK), 1)
        for gap in range(3):
            pieces = []
            for half in range(2):
                spot = near_ref[half, gap]
                held = slope_ref[jnp.maximum(spot, 0) // 2, pl.ds(
                    pl.multiple_of((jnp.maximum(spot, 0) % 2) * HALF, HALF), HALF)]
                pieces.append(jnp.where(spot >= 0, held, jnp.zeros_like(held)))
            for head in range(2):
                cut = slice(head * TOK, (head + 1) * TOK)
                strip_ref[head, gap] = jnp.where(lane < HALF, pieces[0][:, cut], pieces[1][:, cut])


def pair_columns(pair):
    return (0, pair)


def kv_spec(rows, row_block, part):
    return pl.BlockSpec(
        (N_CTX, 1, rows, 2 * HEAD_DIM), lambda pair: (0, part, row_block, pair)
    )


SMEM_SPEC = pl.BlockSpec(memory_space=pltpu.SMEM)
TILE_SPEC = pl.BlockSpec((2, 5, HALF, TOK), lambda pair: (pair, 0, 0, 0))
TOTAL_SPEC = pl.BlockSpec((1, 8, 2 * TOK), lambda pair: (pair, 0, 0))
ROW_SPEC = pl.BlockSpec((TOK, 2 * HEAD_DIM), pair_columns)
LOCAL = pltpu.CompilerParams(vmem_limit_bytes=48 * MIB)


def attend(queries, gathered, rows, row_block, classes=None, tiles=None):
    biased = classes is not None
    chunks = N_CTX * rows // TOK
    specs = [ROW_SPEC, kv_spec(rows, row_block, 0), kv_spec(rows, row_block, 1)]
    operands = [queries, gathered, gathered]
    if biased:
        specs = [SMEM_SPEC] + specs + [TILE_SPEC]
        operands = [classes] + operands + [tiles]
    return pl.pallas_call(
        functools.partial(forward_kernel, biased),
        grid=(PAIRS,),
        in_specs=specs,
        out_specs=[ROW_SPEC, TOTAL_SPEC],
        out_shape=[
            jax.ShapeDtypeStruct((TOK, D), BF),
            jax.ShapeDtypeStruct((PAIRS, 8, 2 * TOK), F32),
        ],
        scratch_shapes=[
            pltpu.VMEM((chunks, TOK, 2 * TOK), F32),
            pltpu.VMEM((chunks, TOK, 2 * TOK), BF),
        ],
        compiler_params=LOCAL,
        cost_estimate=pl.CostEstimate(flops=10**9, bytes_accessed=10**7, transcendentals=10**6),
        name="attend_self" if biased else "attend_cross",
    )(*operands)


def attend_back(queries, gathered, grads, totals, rows, row_block, classes=None, near=None, tiles=None):
    biased = classes is not None
    chunks = N_CTX * rows // TOK
    specs = [ROW_SPEC, kv_spec(rows, row_block, 0), kv_spec(rows, row_block, 1), ROW_SPEC, TOTAL_SPEC]
    operands = [queries, gathered, gathered, grads, totals]
    out_specs = [
        ROW_SPEC,
        pl.BlockSpec((N_CTX, 2, rows, 2 * HEAD_DIM), lambda pair: (0, 0, 0, pair)),
    ]
    out_shape = [
        jax.ShapeDtypeStruct((TOK, D), BF),
        jax.ShapeDtypeStruct((N_CTX, 2, rows, D), BF),
    ]
    if biased:
        specs = [SMEM_SPEC, SMEM_SPEC] + specs + [TILE_SPEC]
        operands = [classes, near] + operands + [tiles]
        out_specs.append(pl.BlockSpec((2, 3, HALF, TOK), lambda pair: (pair, 0, 0, 0)))
        out_shape.append(jax.ShapeDtypeStruct((HEADS, 3, HALF, TOK), F32))
    return pl.pallas_call(
        functools.partial(backward_kernel, biased),
        grid=(PAIRS,),
        in_specs=specs,
        out_specs=out_specs,
        out_shape=out_shape,
        scratch_shapes=[
            pltpu.VMEM((chunks, TOK, 2 * TOK), F32),
            pltpu.VMEM((chunks, TOK, 2 * TOK), F32),
            pltpu.VMEM((chunks, TOK, 2 * TOK), BF),
            pltpu.VMEM((chunks, TOK, 2 * TOK), BF),
        ],
        compiler_params=LOCAL,
        cost_estimate=pl.CostEstimate(flops=3 * 10**9, bytes_accessed=10**7, transcendentals=10**6),
        name="attend_self_back" if biased else "attend_cross_back",
    )(*operands)


def matmul(left, right):
    return jnp.dot(left, right, preferred_element_type=F32)


def transposed_left(left, right):
    return contract(left, right, ((0,), (0,)))


def transposed_right(left, right):
    return contract(left, right, ((1,), (1,)))


def rms_scaled(values, gain):
    inverse = lax.rsqrt(jnp.mean(values * values, axis=-1, keepdims=True) + 1e-06)
    return (values * inverse * gain).astype(BF)


def rms_back(values, gain, grad):
    inverse = lax.rsqrt(jnp.mean(values * values, axis=-1, keepdims=True) + 1e-06)
    scaled = gain * grad
    mixed = jnp.mean(values * scaled, axis=-1, keepdims=True)
    grad_values = inverse * scaled - values * (inverse * inverse * inverse * mixed)
    return grad_values, jnp.sum(values * inverse * grad, axis=0)


def gelu_product(gate_part, up_part):
    return jax.nn.gelu(gate_part, approximate=True) * up_part


def near_hot():
    shape = (REACH, 3 * HALF * HALF)
    spot = lax.broadcasted_iota(jnp.int32, shape, 1)
    gap = spot // (HALF * HALF)
    key = (spot // HALF) % HALF
    row = spot % HALF
    distance = jnp.clip(HALF * gap + row - key, 0, REACH - 1)
    return (distance == lax.broadcasted_iota(jnp.int32, shape, 0)).astype(BF)


def bias_tiles(bias_rows):
    near = matmul(bias_rows.astype(BF), near_hot()).reshape(HEADS, 3, HALF, HALF)
    key = jnp.arange(HALF, dtype=jnp.int32)[:, None]
    row = jnp.arange(HALF, dtype=jnp.int32)[None, :]
    barred = (jnp.arange(3) == 0)[None, :, None, None] & (key > row)[None, None]
    near = jnp.where(barred, -1e30, near)
    far = jnp.broadcast_to(bias_rows[:, -1][:, None, None, None], (HEADS, 1, HALF, HALF))
    none = jnp.full((HEADS, 1, HALF, HALF), -1e30, F32)
    tiles = jnp.concatenate([near, far, none], axis=1)
    return jnp.concatenate([tiles, tiles], axis=-1)


def bias_sums(strips):
    tiles = (strips[..., :HALF] + strips[..., HALF:]).reshape(HEADS, -1)
    high = tiles.astype(BF)
    low = (tiles - high.astype(F32)).astype(BF)
    hot = near_hot()
    sums = transposed_right(high, hot) + transposed_right(low, hot)
    far = -jnp.sum(sums[:, :-1], axis=1, keepdims=True)
    return jnp.concatenate([sums[:, :-1], far], axis=1)


def owned_rows(grad):
    return lax.psum_scatter(grad, "fsdp", scatter_dimension=0, tiled=True)


def body(
    decoder_in,
    encoder_states,
    out_grad,
    block_pairs,
    bucket_table,
    gain_self,
    self_query,
    self_key,
    self_value,
    self_out,
    position_bias,
    gain_cross,
    cross_query,
    cross_key,
    cross_value,
    cross_out,
    gain_feed,
    feed_gate,
    feed_up,
    feed_down,
):
    me = lax.axis_index("ctx")
    rows = self_query.shape[0]
    extra = jnp.concatenate(
        [
            gain_self[:, None],
            gain_cross[:, None],
            gain_feed[:, None],
            jnp.zeros((rows, 5), BF),
            jnp.pad(position_bias, ((0, rows - position_bias.shape[0]), (0, 0))),
            jnp.zeros((rows, 236), BF),
        ],
        axis=1,
    )
    early, late, down = gather_weights(
        [
            jnp.concatenate([self_query, self_key, self_value, cross_key, cross_value, extra], axis=1),
            jnp.concatenate([self_out, cross_query, cross_out, feed_gate, feed_up], axis=1),
            feed_down,
        ],
        5,
    )
    early = early.reshape(D, -1)
    late = late.reshape(D, -1)
    down = down.reshape(FF, D)
    qkv_one = early[:, : 3 * D]
    kv_two = early[:, 3 * D : 5 * D]
    gains = early[:, 5 * D : 5 * D + 3].astype(F32).T
    norm_one, norm_two, norm_three = gains[0:1], gains[1:2], gains[2:3]
    table = early.reshape(8, rows, -1)[:, :4, 5 * D + 8 : 5 * D + 20].reshape(32, HEADS)
    out_one = late[:, :D]
    query_two = late[:, D : 2 * D]
    out_two = late[:, 2 * D : 3 * D]
    gate_up = late[:, 3 * D :]

    bucket_hot = (bucket_table[:, None] == jnp.arange(32, dtype=jnp.int32)[None, :]).astype(BF)
    bias_rows = transposed_right(table.T, bucket_hot)
    tiles = bias_tiles(bias_rows)
    pair = block_pairs[me]
    query_blocks = jnp.stack([pair, 31 - pair])
    key_blocks = jnp.stack([block_pairs, 31 - block_pairs], axis=1).reshape(-1)
    gaps = query_blocks[:, None] - key_blocks[None, :]
    classes = jnp.where(gaps < 0, 4, jnp.minimum(gaps, 3)).astype(jnp.int32)
    wanted = query_blocks[:, None] - jnp.arange(3, dtype=jnp.int32)[None, :]
    near = jnp.max(
        jnp.where(
            wanted[:, :, None] == key_blocks[None, None, :],
            jnp.arange(32, dtype=jnp.int32)[None, None, :],
            -1,
        ),
        axis=-1,
    )

    tokens = decoder_in[0].astype(F32)
    states = encoder_states[0]
    upstream = out_grad[0]
    normed_one = rms_scaled(tokens, norm_one)
    qkv = matmul(normed_one, qkv_one).astype(BF)
    cross_kv = matmul(states, kv_two).astype(BF)
    queries = qkv[:, :D]
    local = jnp.stack(
        [
            jnp.concatenate([qkv[:, D : 2 * D], cross_kv[:, :D]], axis=0),
            jnp.concatenate([qkv[:, 2 * D :], cross_kv[:, D:]], axis=0),
        ]
    )
    gathered = ctx_gather(local, 0)
    attended, self_totals = attend(queries, gathered, TOK, 0, classes, tiles)
    mid_one = tokens + matmul(attended, out_one)
    normed_two = rms_scaled(mid_one, norm_two)
    cross_queries = matmul(normed_two, query_two).astype(BF)
    cross_attended, cross_totals = attend(cross_queries, gathered, ENC, 2)
    mid_two = mid_one + matmul(cross_attended, out_two)
    normed_three = rms_scaled(mid_two, norm_three)
    gate_up_values = matmul(normed_three, gate_up).astype(BF).astype(F32)
    gate_values, up_values = gate_up_values[:, :FF], gate_up_values[:, FF:]
    hidden, pull_feed = jax.vjp(gelu_product, gate_values, up_values)
    hidden = hidden.astype(BF)
    block_out = mid_two + matmul(hidden, down)

    d_hidden = transposed_right(upstream, down)
    d_gate_up = jnp.concatenate(pull_feed(d_hidden), axis=1).astype(BF)
    grad_down = owned_rows(transposed_left(hidden, upstream).astype(BF))
    grad_gate_up = owned_rows(transposed_left(normed_three, d_gate_up).astype(BF))
    d_normed_three = transposed_right(d_gate_up, gate_up)
    part_three, grad_norm_three = rms_back(mid_two, norm_three, d_normed_three)
    d_mid_two = upstream.astype(F32) + part_three
    cross_branch = d_mid_two.astype(BF)
    d_cross_attended = transposed_right(cross_branch, out_two).astype(BF)
    d_cross_queries, d_cross_kv_all = attend_back(
        cross_queries, gathered, d_cross_attended, cross_totals, ENC, 2
    )
    d_cross_kv = ctx_scatter(d_cross_kv_all, 1)
    d_cross_kv = jnp.concatenate([d_cross_kv[0], d_cross_kv[1]], axis=1)
    grad_encoder = transposed_right(d_cross_kv, kv_two)
    grad_out_two = transposed_left(cross_attended, cross_branch).astype(BF)
    grad_query_two = transposed_left(normed_two, d_cross_queries).astype(BF)
    grad_kv_two = transposed_left(states, d_cross_kv).astype(BF)
    d_normed_two = transposed_right(d_cross_queries, query_two)
    part_two, grad_norm_two = rms_back(mid_one, norm_two, d_normed_two)
    d_mid_one = d_mid_two + part_two
    self_branch = d_mid_one.astype(BF)
    d_attended = transposed_right(self_branch, out_one).astype(BF)
    d_queries, d_kv_all, strips = attend_back(
        queries, gathered, d_attended, self_totals, TOK, 0, classes, near, tiles
    )
    d_kv = ctx_scatter(d_kv_all, 2)
    d_qkv = jnp.concatenate([d_queries, d_kv[0], d_kv[1]], axis=1)
    d_normed_one = transposed_right(d_qkv, qkv_one)
    part_one, grad_norm_one = rms_back(tokens, norm_one, d_normed_one)
    grad_decoder = d_mid_one + part_one
    grad_table = matmul(bias_sums(strips), bucket_hot.astype(F32)).T.reshape(8, 4, HEADS)
    grad_extra = jnp.concatenate(
        [
            grad_norm_one[:, None],
            grad_norm_two[:, None],
            grad_norm_three[:, None],
            jnp.zeros((D, 5), F32),
            jnp.pad(grad_table, ((0, 0), (0, rows - 4), (0, 0))).reshape(D, HEADS),
            jnp.zeros((D, 236), F32),
        ],
        axis=1,
    )
    grad_out_one = transposed_left(attended, self_branch).astype(BF)
    grad_qkv_one = transposed_left(normed_one, d_qkv).astype(BF)
    summed = reduce_gradients(
        [
            part.astype(BF).reshape(8, rows, -1)
            for part in (
                grad_out_two, grad_query_two, grad_kv_two, grad_out_one, grad_qkv_one, grad_extra,
            )
        ],
        grad_gate_up,
        grad_down,
        3,
    )
    owned = summed[:, :, :D].astype(F32)
    wide = summed[:, :, D : D + 512].astype(F32)
    wide = jnp.transpose(wide, (1, 0, 2)).reshape(rows, 2 * FF)
    tall = summed[:, :, D + 512 : D + 768].astype(F32).reshape(8, 2, 3, 16, 256)
    tall = jnp.transpose(tall, (1, 0, 3, 2, 4)).reshape(256, D)
    extras = summed[0, :, D + 768 :].astype(F32)
    return (
        block_out[None],
        grad_decoder[None],
        grad_encoder[None],
        extras[:, 0],
        owned[5],
        owned[6],
        owned[7],
        owned[4],
        extras[:4, 8:20],
        extras[:, 1],
        owned[1],
        owned[2],
        owned[3],
        owned[0],
        extras[:, 2],
        wide[:, :FF],
        wide[:, FF:],
        tall,
    )


def solution(mesh):
    tokens = P("fsdp", "ctx", None)
    matrix = P("fsdp", None)
    vector = P("fsdp")
    weights = (
        (vector,) + (matrix,) * 5 + (vector,) + (matrix,) * 4 + (vector,) + (matrix,) * 3
    )
    return jax.shard_map(
        body,
        mesh=mesh,
        in_specs=(tokens,) * 3 + (P(), P()) + weights,
        out_specs=(tokens,) * 3 + weights,
        check_vma=False,
    )
```

```python
import functools

import jax
import jax.numpy as jnp
from jax import lax
from jax.experimental import pallas as pl
from jax.experimental.pallas import tpu as pltpu
from jax.sharding import PartitionSpec as P

D = 768
FF = 2048
HEADS = 12
HEAD_DIM = 64
PAIRS = HEADS // 2
N_CTX = 16
TOK = 128
ENC = 64
HALF = 64
REACH = 128
BF = jnp.bfloat16
F32 = jnp.float32
MIB = 1024 * 1024


def ctx_place():
    me = lax.axis_index("ctx")
    core = me % 2
    high = (me // 2) % 2
    y = me // 4
    return me, core, high, y


def slot_of(y, shift, high, core):
    return ((y + shift) % 4) * 4 + 2 * high + core


def greet(devices):
    barrier = pltpu.get_barrier_semaphore()
    for device in devices:
        pl.semaphore_signal(barrier, inc=1, device_id={"ctx": device})
    pl.semaphore_wait(barrier, len(devices))


def remote(src, dst, send_sem, recv_sem, device):
    return pltpu.make_async_remote_copy(
        src_ref=src, dst_ref=dst, send_sem=send_sem, recv_sem=recv_sem, device_id={"ctx": device}
    )


def gather_kernel(x_ref, out_ref, send_sem, recv_sem, local_sem):
    me, core, high, y = ctx_place()
    sibling = slot_of(y, 0, high, 1 - core)
    across = slot_of(y, 0, 1 - high, core)
    rows = [slot_of(y, shift, high, core) for shift in (1, 2, 3)]
    greet([sibling, across] + rows)
    sends = []

    def send(src, slot, device):
        copy = remote(src, out_ref.at[slot], send_sem.at[len(sends)], recv_sem.at[slot], device)
        copy.start()
        sends.append(copy)

    def arrived(slot):
        remote(x_ref, out_ref.at[slot], send_sem.at[0], recv_sem.at[slot], sibling).wait_recv()

    send(x_ref, me, across)
    for device in rows:
        send(x_ref, me, device)
    send(x_ref, me, sibling)
    own = pltpu.make_async_copy(x_ref, out_ref.at[me], local_sem)
    own.start()
    arrived(across)
    for device in rows:
        send(out_ref.at[across], across, device)
    send(out_ref.at[across], across, sibling)
    for shift in (1, 3, 2):
        slot = slot_of(y, shift, high, core)
        arrived(slot)
        send(out_ref.at[slot], slot, sibling)
    for shift in (1, 3, 2):
        slot = slot_of(y, shift, 1 - high, core)
        arrived(slot)
        send(out_ref.at[slot], slot, sibling)
    for shift in range(4):
        for other in range(2):
            arrived(slot_of(y, shift, other, 1 - core))
    own.wait()
    for copy in sends:
        copy.wait_send()


def ctx_gather(x, collective_id):
    return pl.pallas_call(
        gather_kernel,
        out_shape=jax.ShapeDtypeStruct((N_CTX,) + x.shape, x.dtype),
        in_specs=[pl.BlockSpec(memory_space=pl.ANY)],
        out_specs=pl.BlockSpec(memory_space=pl.ANY),
        scratch_shapes=[
            pltpu.SemaphoreType.DMA((15,)),
            pltpu.SemaphoreType.DMA((N_CTX,)),
            pltpu.SemaphoreType.DMA,
        ],
        compiler_params=pltpu.CompilerParams(collective_id=collective_id, has_side_effects=True),
        name="ctx_gather",
    )(x)


def torus_place():
    me, core, high, y = ctx_place()
    shard = lax.axis_index("fsdp")
    return me, core, high, y, shard // 4, shard % 4


def hop(src, dst, send_sem, recv_sem, ctx, fsdp):
    return pltpu.make_async_remote_copy(
        src_ref=src,
        dst_ref=dst,
        send_sem=send_sem,
        recv_sem=recv_sem,
        device_id={"ctx": ctx, "fsdp": fsdp},
    )


def greet_all(devices):
    barrier = pltpu.get_barrier_semaphore()
    for ctx, fsdp in devices:
        pl.semaphore_signal(barrier, inc=1, device_id={"ctx": ctx, "fsdp": fsdp})
    pl.semaphore_wait(barrier, len(devices))


def weights_kernel(count, *refs):
    sources = refs[:count]
    targets = refs[count : 2 * count]
    send_sem, x_sem, z_sem, core_sem, local_sem = refs[2 * count :]
    me, core, high, y, low, x = torus_place()
    shard = low * 4 + x
    sibling = (slot_of(y, 0, high, 1 - core), shard)
    inside = (me, (1 - low) * 4 + x)
    outside = (slot_of(y, 0, 1 - high, core), (1 - low) * 4 + x)
    others = [low * 4 + (x + shift) % 4 for shift in (1, 2, 3)]
    greet_all([sibling, inside, outside] + [(me, other) for other in others])

    def part(index, owner, whose, side=None):
        ref = targets[index]
        rows = ref.shape[1] // 2
        start = pl.multiple_of(whose * rows, 16)
        if side is None:
            return ref.at[owner, pl.ds(start, rows), :]
        width = ref.shape[2] // 2
        return ref.at[owner, pl.ds(start, rows), pl.ds(side * width, width)]

    def mine(index, side=None):
        ref = sources[index]
        rows = ref.shape[0] // 2
        start = pl.multiple_of(core * rows, 16)
        if side is None:
            return ref.at[pl.ds(start, rows), :]
        width = ref.shape[1] // 2
        return ref.at[pl.ds(start, rows), pl.ds(side * width, width)]

    sends = []

    def send(index, src, dst, recv_sem, device):
        copy = hop(src, dst, send_sem.at[len(sends)], recv_sem, *device)
        copy.start()
        sends.append(copy)

    def arrived(index, ref, recv_sem):
        hop(ref, ref, send_sem.at[0], recv_sem, *sibling).wait_recv()

    for index in range(count):
        for spot in (1, 0, 2):
            send(index, mine(index), part(index, shard, core), x_sem.at[index, spot], (me, others[spot]))
        for side, device in enumerate((inside, outside)):
            send(
                index, mine(index, side), part(index, shard, core, side), z_sem.at[index, 3, side], device
            )
    own = []
    for index in range(count):
        copy = pltpu.make_async_copy(sources[index], targets[index].at[shard], local_sem.at[index])
        copy.start()
        own.append(copy)
    for index in range(count):
        for spot in (0, 2, 1):
            owner = low * 4 + (x + 3 - spot) % 4
            block = part(index, owner, core)
            arrived(index, block, x_sem.at[index, spot])
            for side, device in enumerate((inside, outside)):
                piece = part(index, owner, core, side)
                send(index, piece, piece, z_sem.at[index, spot, side], device)
            send(index, block, block, core_sem.at[index, spot], sibling)
        for spot in (3, 0, 2, 1):
            owner = (1 - low) * 4 + (x + 3 - spot) % 4
            for side in range(2):
                piece = part(index, owner, core, side)
                arrived(index, piece, z_sem.at[index, spot, side])
                send(index, piece, piece, core_sem.at[index, 3 + 2 * spot + side], sibling)
    for index in range(count):
        for spot in range(3):
            owner = low * 4 + (x + 3 - spot) % 4
            arrived(index, part(index, owner, 1 - core), core_sem.at[index, spot])
        for spot in range(4):
            owner = (1 - low) * 4 + (x + 3 - spot) % 4
            for side in range(2):
                piece = part(index, owner, 1 - core, side)
                arrived(index, piece, core_sem.at[index, 3 + 2 * spot + side])
    for copy in own:
        copy.wait()
    for copy in sends:
        copy.wait_send()


def gather_weights(packs, collective_id):
    count = len(packs)
    return pl.pallas_call(
        functools.partial(weights_kernel, count),
        out_shape=[jax.ShapeDtypeStruct((8,) + pack.shape, pack.dtype) for pack in packs],
        in_specs=[pl.BlockSpec(memory_space=pl.ANY)] * count,
        out_specs=[pl.BlockSpec(memory_space=pl.ANY)] * count,
        scratch_shapes=[
            pltpu.SemaphoreType.DMA((22 * count,)),
            pltpu.SemaphoreType.DMA((count, 3)),
            pltpu.SemaphoreType.DMA((count, 4, 2)),
            pltpu.SemaphoreType.DMA((count, 11)),
            pltpu.SemaphoreType.DMA((count,)),
        ],
        compiler_params=pltpu.CompilerParams(collective_id=collective_id, has_side_effects=True),
        name="gather_weights",
    )(*packs)


PIECE = 48
ROOM = D + FF // 4 + FF // 8 + 128
EARLY = (2 * FF, D, D, D, D)
WIDTHS = EARLY + (2 * D, 2 * D, 256)
SPAN = sum(WIDTHS)
DOWN = len(WIDTHS)


def finish_kernel(*refs):
    (
        dckv_ref, dkv_ref, wide_ref, two_out_ref, two_query_ref, one_out_ref, one_query_ref, down_ref,
        normed_ref, states_ref, kv_ref, ckv_ref, dn_ref, dmid_ref, token_ref, gain_ref, extra_ref,
        out_ref, decoder_ref, encoder_ref,
        kept, from_core, from_z, from_x, d_kept, d_core, d_z, d_x,
        s_kept, s_core, s_row, s_stage, s_high, c_kept, c_core, c_row, c_stage, c_high,
        to_core, gain_cols, packed, from_ctx, total_ref,
        s_sem, c_sem, local_sem, core_send, core_recv, z_send, z_recv, x_send, x_recv,
        ctx_send, ctx_recv, out_send, out_recv, pass_send, pass_recv, own_sem,
    ) = refs
    me, core, high, y, low, x = torus_place()
    shard = low * 4 + x
    rank = y * 2 + high
    sibling = (slot_of(y, 0, high, 1 - core), shard)
    inside = (me, (1 - low) * 4 + x)
    outside = (slot_of(y, 0, 1 - high, core), (1 - low) * 4 + x)
    across = (slot_of(y, 0, 1 - high, core), shard)
    others = [low * 4 + (x + shift) % 4 for shift in (1, 2, 3)]
    shifts = [(dy, dz) for dy in range(4) for dz in range(2)][1:]
    mates = [((y + dy) % 4) * 2 + (high + dz) % 2 for dy, dz in shifts]
    greet_all(
        [sibling, inside, outside]
        + [(me, other) for other in others]
        + [(mate * 2 + core, shard) for mate in mates]
    )
    mine = pl.ds(pl.multiple_of(core * PIECE, 16), PIECE)
    theirs = pl.ds(pl.multiple_of((1 - core) * PIECE, 16), PIECE)
    mine_down = pl.ds(pl.multiple_of(core * 128, 16), 128)
    theirs_down = pl.ds(pl.multiple_of((1 - core) * 128, 16), 128)
    sends = []

    def go(src, dst, send_sem, recv_sem, device):
        copy = hop(src, dst, send_sem, recv_sem, *device)
        copy.start()
        sends.append(copy)
        return copy

    def bring(src, dst, sem):
        copy = pltpu.make_async_copy(src, dst, sem)
        copy.start()
        return copy


    def rows_start(source, held, arrived, sem, base):
        over = []
        local = []
        for spot, shift in enumerate((2, 1, 3, 0)):
            pair = pl.ds(((y + shift) % 4) * 2, 2)
            block = pl.ds(2 * spot, 2)
            over.append(
                go(
                    source.at[pair, 1 - core], arrived.at[block],
                    sem.at[0, spot], sem.at[1, spot], sibling,
                )
            )
            local.append(bring(source.at[pair, core], held.at[block], local_sem.at[base + spot]))
        return over, local

    def rows_send(copies, held, arrived, row, sem):
        over, local = copies
        onward = []
        for spot, shift in enumerate((2, 1, 3, 0)):
            local[spot].wait()
            over[spot].wait_recv()
            for block in (2 * spot, 2 * spot + 1):
                for part in range(2):
                    held[block, part] = held[block, part] + arrived[block, part]
            if shift:
                onward.append(
                    go(
                        held.at[pl.ds(2 * spot, 2)], row.at[spot],
                        sem.at[2, spot], sem.at[3, spot], (others_ctx[shift - 1], shard),
                    )
                )
        return onward

    others_ctx = [slot_of(y, shift, high, core) for shift in (1, 2, 3)]

    def rows_total(held, row, half, part):
        result = held[6 + half, part].astype(F32)
        for spot in range(3):
            result = result + row[spot, half, part].astype(F32)
        return result

    def rows_across(onward, held, row, stage, landing, sem):
        for copy in onward:
            copy.wait_recv()
        for part in range(2):
            stage[part] = rows_total(held, row, 1 - high, part).astype(BF)
        return go(stage, landing, sem.at[2, 3], sem.at[3, 3], across)

    def rows_sum(last, held, row, landing):
        totals = [rows_total(held, row, high, part) for part in range(2)]
        last.wait_recv()
        return jnp.concatenate(
            [(totals[part] + landing[part].astype(F32)).astype(BF) for part in range(2)], axis=1
        )


    starts = [sum(WIDTHS[:k]) for k in range(len(WIDTHS))]

    def buffers(k):
        if k == DOWN:
            return d_kept, d_core, d_z, d_x, 0, D
        return kept, from_core, from_z, from_x, starts[k], WIDTHS[k]

    over_core, over_z, over_x, brought = {}, {}, {}, {}

    def chunk_start(k, source):
        held, arrived, _, _, start, width = buffers(k)
        cut = pl.ds(start, width)
        rows, far_rows = (mine_down, theirs_down) if k == DOWN else (mine, theirs)
        over_core[k] = go(
            source.at[:, far_rows, :], arrived.at[:, :, cut], core_send.at[k], core_recv.at[k], sibling
        )
        brought[k] = bring(source.at[:, rows, :], held.at[:, :, cut], local_sem.at[8 + k])

    def chunk_send(k, offset):
        width = WIDTHS[k]
        over_core[k] = go(
            to_core.at[:, :, pl.ds(offset, width)],
            from_core.at[:, :, pl.ds(starts[k], width)],
            core_send.at[k],
            core_recv.at[k],
            sibling,
        )

    def step_core(k):
        held, arrived, landing, _, start, width = buffers(k)
        cut = pl.ds(start, width)
        if k in brought:
            brought[k].wait()
        over_core[k].wait_recv()
        for column in range(4):
            owner = 4 * (1 - low) + column
            held[owner, :, cut] = held[owner, :, cut] + arrived[owner, :, cut]
        half = width // 2
        over_z[k] = [
            go(
                held.at[pl.ds(4 * (1 - low), 4), :, pl.ds(start + side * half, half)],
                landing.at[:, :, pl.ds(start + side * half, half)],
                z_send.at[k, side],
                z_recv.at[k, side],
                device,
            )
            for side, device in enumerate((inside, outside))
        ]
        for column in range(4):
            owner = 4 * low + column
            held[owner, :, cut] = held[owner, :, cut] + arrived[owner, :, cut]

    def step_z(k):
        held, _, landing, spread, start, width = buffers(k)
        cut = pl.ds(start, width)
        for copy in over_z[k]:
            copy.wait_recv()
        for column in range(4):
            landing[column, :, cut] = landing[column, :, cut] + held[4 * low + column, :, cut]
        over_x[k] = [
            go(
                landing.at[(x + spot + 1) % 4, :, cut],
                spread.at[spot, :, cut],
                x_send.at[k, spot],
                x_recv.at[k, spot],
                (me, others[spot]),
            )
            for spot in (1, 0, 2)
        ]

    def step_x(k, first=None):
        _, _, landing, spread, start, width = buffers(k)
        cut = pl.ds(start, width)
        for copy in over_x[k]:
            copy.wait_recv()
        total = landing[x, :, cut].astype(F32)
        for spot in range(3):
            total = total + spread[spot, :, cut].astype(F32)
        total = total.astype(BF)
        if k == 0:
            for piece in range(8):
                packed[piece, :, D : D + 512] = total[:, piece * 512 : piece * 512 + 512]
        elif k == DOWN:
            for piece in range(8):
                for part in range(3):
                    packed[piece, part * 16 : part * 16 + 16, D + 512 : D + 768] = total[
                        piece * 16 : piece * 16 + 16, part * 256 : part * 256 + 256
                    ]
        elif k == len(WIDTHS) - 1:
            packed[0, :, ROOM - 128 :] = total[:, :128]
            for piece in range(1, 8):
                packed[piece, :, ROOM - 128 :] = jnp.zeros((PIECE, 128), BF)
        else:
            for piece in range(width // D):
                packed[first + piece, :, :D] = total[:, piece * D : (piece + 1) * D]

    def outer(left_ref, rows, right):
        left = left_ref[:, rows, :]
        return contract(left.reshape(8 * PIECE, left.shape[-1]), right, ((1,), (0,))).astype(BF).reshape(
            8, PIECE, right.shape[-1]
        )

    c_copies = rows_start(dckv_ref, c_kept, c_core, c_sem, 0)
    s_copies = rows_start(dkv_ref, s_kept, s_core, s_sem, 4)
    for k, source in enumerate((wide_ref, two_out_ref, two_query_ref, one_out_ref, one_query_ref)):
        chunk_start(k, source)
        if k == 0:
            chunk_start(DOWN, down_ref)
    c_onward = rows_send(c_copies, c_kept, c_core, c_row, c_sem)
    s_onward = rows_send(s_copies, s_kept, s_core, s_row, s_sem)
    for k in (0, DOWN, 1, 2, 3, 4):
        step_core(k)
    step_z(0)
    c_last = rows_across(c_onward, c_kept, c_row, c_stage, c_high, c_sem)
    step_z(DOWN)
    d_ckv = rows_sum(c_last, c_kept, c_row, c_high)
    to_core[:, :, : 2 * D] = outer(states_ref, theirs, d_ckv)
    chunk_send(5, 0)
    kept[:, :, starts[5] : starts[5] + 2 * D] = outer(states_ref, mine, d_ckv)
    encoder_ref[...] = contract(d_ckv, ckv_ref[...], ((1,), (1,)))
    for k in (1, 2, 3, 4):
        step_z(k)
    step_core(5)
    step_x(0)
    step_x(DOWN)
    s_last = rows_across(s_onward, s_kept, s_row, s_stage, s_high, s_sem)
    step_z(5)
    for k in (1, 2, 3, 4):
        step_x(k, k - 1)
    d_kv = rows_sum(s_last, s_kept, s_row, s_high)
    over_core[5].wait_send()
    to_core[:, :, : 2 * D] = outer(normed_ref, theirs, d_kv)
    chunk_send(6, 0)
    kept[:, :, starts[6] : starts[6] + 2 * D] = outer(normed_ref, mine, d_kv)
    tokens = token_ref[...].astype(F32)
    grad = dn_ref[...] + contract(d_kv, kv_ref[...], ((1,), (1,)))
    inverse = lax.rsqrt(jnp.mean(tokens * tokens, axis=-1, keepdims=True) + 1e-06)
    columns = contract(
        (tokens * inverse * grad).astype(BF), jnp.ones((TOK, 128), BF), ((0,), (0,))
    )
    lane = lax.broadcasted_iota(jnp.int32, (D, 128), 1)
    gain_cols[...] = jnp.where(lane == 0, columns, 0.0).astype(BF).reshape(8, 2 * PIECE, 128)
    to_core[:, :, 2 * D : 2 * D + 128] = gain_cols[:, theirs, :] + extra_ref[:, theirs, :128]
    to_core[:, :, 2 * D + 128 :] = extra_ref[:, theirs, 128:]
    chunk_send(7, 2 * D)
    kept[:, :, starts[7] : starts[7] + 128] = gain_cols[:, mine, :] + extra_ref[:, mine, :128]
    kept[:, :, starts[7] + 128 :] = extra_ref[:, mine, 128:]
    step_core(6)
    step_core(7)
    step_x(5, 4)
    step_z(6)
    step_z(7)
    scaled = gain_ref[...] * grad
    mixed = jnp.mean(tokens * scaled, axis=-1, keepdims=True)
    decoder_ref[...] = (
        dmid_ref[...] + inverse * scaled - tokens * (inverse * inverse * inverse * mixed)
    )
    step_x(6, 6)
    step_x(7)


    over_ctx = [
        go(
            packed.at[mate],
            from_ctx.at[spot],
            ctx_send.at[spot],
            ctx_recv.at[spot],
            (mate * 2 + core, shard),
        )
        for spot, mate in enumerate(mates)
    ]
    total = packed[rank].astype(F32)
    for spot in range(7):
        over_ctx[spot].wait_recv()
        total = total + from_ctx[spot].astype(F32)
    total_ref[...] = total.astype(BF)
    for spot, mate in enumerate(mates):
        go(
            total_ref,
            out_ref.at[rank, mine, :],
            out_send.at[spot],
            out_recv.at[rank],
            (mate * 2 + core, shard),
        )
    go(total_ref, out_ref.at[rank, mine, :], pass_send.at[7], pass_recv.at[rank], sibling)
    own = bring(total_ref, out_ref.at[rank, mine, :], own_sem)

    def landed(ref, recv_sem):
        hop(ref, ref, pass_send.at[0], recv_sem, *sibling).wait_recv()

    for spot, mate in enumerate(mates):
        block = out_ref.at[mate, mine, :]
        landed(block, out_recv.at[mate])
        go(block, block, pass_send.at[spot], pass_recv.at[mate], sibling)
    for mate in [rank] + mates:
        landed(out_ref.at[mate, theirs, :], pass_recv.at[mate])
    own.wait()
    for copy in sends:
        if copy is not over_core[5]:
            copy.wait_send()


def finish(far, near, collective_id):
    dma = pltpu.SemaphoreType.DMA
    chunks = len(WIDTHS) + 1

    def rows(count):
        return [
            pltpu.VMEM((8, 2, count, D), BF),
            pltpu.VMEM((8, 2, count, D), BF),
            pltpu.VMEM((3, 2, 2, count, D), BF),
            pltpu.VMEM((2, count, D), BF),
            pltpu.VMEM((2, count, D), BF),
        ]

    return pl.pallas_call(
        finish_kernel,
        out_shape=[
            jax.ShapeDtypeStruct((8, 2 * PIECE, ROOM), BF),
            jax.ShapeDtypeStruct((TOK, D), F32),
            jax.ShapeDtypeStruct((ENC, D), F32),
        ],
        in_specs=[pl.BlockSpec(memory_space=pl.ANY)] * len(far)
        + [pl.BlockSpec(memory_space=pltpu.VMEM)] * len(near),
        out_specs=[
            pl.BlockSpec(memory_space=pl.ANY),
            pl.BlockSpec(memory_space=pltpu.VMEM),
            pl.BlockSpec(memory_space=pltpu.VMEM),
        ],
        scratch_shapes=[
            pltpu.VMEM((8, PIECE, SPAN), BF),
            pltpu.VMEM((8, PIECE, SPAN), BF),
            pltpu.VMEM((4, PIECE, SPAN), BF),
            pltpu.VMEM((3, PIECE, SPAN), BF),
            pltpu.VMEM((8, 128, D), BF),
            pltpu.VMEM((8, 128, D), BF),
            pltpu.VMEM((4, 128, D), BF),
            pltpu.VMEM((3, 128, D), BF),
        ]
        + rows(TOK)
        + rows(ENC)
        + [
            pltpu.VMEM((8, PIECE, 2 * D + 256), BF),
            pltpu.VMEM((8, 2 * PIECE, 128), BF),
            pltpu.VMEM((8, PIECE, ROOM), BF),
            pltpu.VMEM((7, PIECE, ROOM), BF),
            pltpu.VMEM((PIECE, ROOM), BF),
            dma((4, 4)),
            dma((4, 4)),
            dma((8 + chunks,)),
            dma((chunks,)),
            dma((chunks,)),
            dma((chunks, 2)),
            dma((chunks, 2)),
            dma((chunks, 3)),
            dma((chunks, 3)),
            dma((7,)),
            dma((7,)),
            dma((7,)),
            dma((8,)),
            dma((8,)),
            dma((8,)),
            dma,
        ],
        compiler_params=pltpu.CompilerParams(
            collective_id=collective_id, has_side_effects=True, vmem_limit_bytes=60 * MIB
        ),
        name="finish_gradients",
    )(*far, *near)


def split_heads(block):
    lane = lax.broadcasted_iota(jnp.int32, block.shape, 1)
    nothing = jnp.zeros_like(block)
    return jnp.concatenate(
        [jnp.where(lane < HEAD_DIM, block, nothing), jnp.where(lane < HEAD_DIM, nothing, block)],
        axis=0,
    )


def join_heads(transposed):
    row = lax.broadcasted_iota(jnp.int32, (2 * HEAD_DIM, TOK), 0)
    return jnp.where(row < HEAD_DIM, transposed[:, :TOK], transposed[:, TOK:]).T


def contract(left, right, dims):
    return lax.dot_general(left, right, (dims, ((), ())), preferred_element_type=F32)


def key_chunk(ref, j):
    if ref.shape[2] == 2 * HALF:
        return ref[j, 0]
    return ref[pl.ds(2 * j, 2), 0].reshape(2 * HALF, 2 * HEAD_DIM)


def bias_chunk(class_ref, tile_ref, j):
    lane = lax.broadcasted_iota(jnp.int32, (HALF, TOK), 1)
    rows = []
    for half in range(2):
        spot = 2 * j + half
        near = class_ref[0, spot]
        far = class_ref[1, spot]
        rows.append(
            jnp.concatenate(
                [
                    jnp.where(lane < HALF, tile_ref[head, near], tile_ref[head, far])
                    for head in range(2)
                ],
                axis=1,
            )
        )
    return jnp.concatenate(rows, axis=0)


def fold(values, join):
    return join(values.reshape(-1, 8, values.shape[-1]), axis=0)


def forward_kernel(biased, *refs):
    if biased:
        class_ref, q_ref, k_ref, v_ref, tile_ref, out_ref, total_ref, score_ref, share_ref = refs
    else:
        q_ref, k_ref, v_ref, out_ref, total_ref, score_ref, share_ref = refs
    chunks = score_ref.shape[0]
    queries = split_heads(q_ref[...])
    highest = None
    for j in range(chunks):
        scores = contract(key_chunk(k_ref, j), queries, ((1,), (1,)))
        if biased:
            scores = scores + bias_chunk(class_ref, tile_ref, j)
        score_ref[j] = scores
        top = fold(scores, jnp.max)
        highest = top if highest is None else jnp.maximum(highest, top)
    highest = jnp.max(highest, axis=0, keepdims=True)
    summed = jnp.zeros((8, 2 * TOK), F32)
    for j in range(chunks):
        raised = jnp.exp(score_ref[j] - highest)
        summed = summed + fold(raised, jnp.sum)
        share_ref[j] = raised.astype(BF)
    summed = jnp.sum(summed, axis=0, keepdims=True)
    values = jnp.concatenate([key_chunk(v_ref, j) for j in range(chunks)], axis=0)
    mixed = contract(values, share_ref[...].reshape(-1, 2 * TOK), ((0,), (0,)))
    out_ref[...] = join_heads(mixed / summed).astype(BF)
    total_ref[0] = jnp.broadcast_to(highest + jnp.log(summed), (8, 2 * TOK))


def backward_kernel(biased, *refs):
    if biased:
        class_ref, near_ref, q_ref, k_ref, v_ref, g_ref, total_ref, tile_ref = refs[:8]
        dq_ref, dkv_ref, strip_ref, share_ref, slope_ref, share_low, slope_low = refs[8:]
    else:
        q_ref, k_ref, v_ref, g_ref, total_ref = refs[:5]
        dq_ref, dkv_ref, share_ref, slope_ref, share_low, slope_low = refs[5:]
    chunks = share_ref.shape[0]
    queries = split_heads(q_ref[...])
    grads = split_heads(g_ref[...])
    totals = total_ref[0, 0:1]
    inner = jnp.zeros((8, 2 * TOK), F32)
    for j in range(chunks):
        scores = contract(key_chunk(k_ref, j), queries, ((1,), (1,)))
        if biased:
            scores = scores + bias_chunk(class_ref, tile_ref, j)
        shares = jnp.exp(scores - totals)
        slopes = contract(key_chunk(v_ref, j), grads, ((1,), (1,)))
        inner = inner + fold(shares * slopes, jnp.sum)
        share_ref[j] = shares
        slope_ref[j] = slopes
        share_low[j] = shares.astype(BF)
    inner = jnp.sum(inner, axis=0, keepdims=True)
    for j in range(chunks):
        grad = share_ref[j] * (slope_ref[j] - inner)
        if biased:
            slope_ref[j] = grad
        slope_low[j] = grad.astype(BF)
    keys = jnp.concatenate([key_chunk(k_ref, j) for j in range(chunks)], axis=0)
    low = slope_low[...].reshape(-1, 2 * TOK)
    dq_ref[...] = join_heads(contract(keys, low, ((0,), (0,)))).astype(BF)
    shape = dkv_ref.shape
    block = (shape[0], shape[2], shape[3])
    dkv_ref[:, 0] = contract(low, queries, ((1,), (0,))).astype(BF).reshape(block)
    dkv_ref[:, 1] = (
        contract(share_low[...].reshape(-1, 2 * TOK), grads, ((1,), (0,))).astype(BF).reshape(block)
    )
    if biased:
        lane = lax.broadcasted_iota(jnp.int32, (HALF, TOK), 1)
        for gap in range(3):
            pieces = []
            for half in range(2):
                spot = near_ref[half, gap]
                held = slope_ref[jnp.maximum(spot, 0) // 2, pl.ds(
                    pl.multiple_of((jnp.maximum(spot, 0) % 2) * HALF, HALF), HALF)]
                pieces.append(jnp.where(spot >= 0, held, jnp.zeros_like(held)))
            for head in range(2):
                cut = slice(head * TOK, (head + 1) * TOK)
                strip_ref[head, gap] = jnp.where(lane < HALF, pieces[0][:, cut], pieces[1][:, cut])


def pair_columns(pair):
    return (0, pair)


def kv_spec(rows, row_block, part):
    return pl.BlockSpec(
        (N_CTX, 1, rows, 2 * HEAD_DIM), lambda pair: (0, part, row_block, pair)
    )


SMEM_SPEC = pl.BlockSpec(memory_space=pltpu.SMEM)
TILE_SPEC = pl.BlockSpec((2, 5, HALF, TOK), lambda pair: (pair, 0, 0, 0))
TOTAL_SPEC = pl.BlockSpec((1, 8, 2 * TOK), lambda pair: (pair, 0, 0))
ROW_SPEC = pl.BlockSpec((TOK, 2 * HEAD_DIM), pair_columns)
LOCAL = pltpu.CompilerParams(vmem_limit_bytes=48 * MIB)


def attend(queries, gathered, rows, row_block, classes=None, tiles=None):
    biased = classes is not None
    chunks = N_CTX * rows // TOK
    specs = [ROW_SPEC, kv_spec(rows, row_block, 0), kv_spec(rows, row_block, 1)]
    operands = [queries, gathered, gathered]
    if biased:
        specs = [SMEM_SPEC] + specs + [TILE_SPEC]
        operands = [classes] + operands + [tiles]
    return pl.pallas_call(
        functools.partial(forward_kernel, biased),
        grid=(PAIRS,),
        in_specs=specs,
        out_specs=[ROW_SPEC, TOTAL_SPEC],
        out_shape=[
            jax.ShapeDtypeStruct((TOK, D), BF),
            jax.ShapeDtypeStruct((PAIRS, 8, 2 * TOK), F32),
        ],
        scratch_shapes=[
            pltpu.VMEM((chunks, TOK, 2 * TOK), F32),
            pltpu.VMEM((chunks, TOK, 2 * TOK), BF),
        ],
        compiler_params=LOCAL,
        cost_estimate=pl.CostEstimate(flops=10**9, bytes_accessed=10**7, transcendentals=10**6),
        name="attend_self" if biased else "attend_cross",
    )(*operands)


def attend_back(queries, gathered, grads, totals, rows, row_block, classes=None, near=None, tiles=None):
    biased = classes is not None
    chunks = N_CTX * rows // TOK
    specs = [ROW_SPEC, kv_spec(rows, row_block, 0), kv_spec(rows, row_block, 1), ROW_SPEC, TOTAL_SPEC]
    operands = [queries, gathered, gathered, grads, totals]
    out_specs = [
        ROW_SPEC,
        pl.BlockSpec((N_CTX, 2, rows, 2 * HEAD_DIM), lambda pair: (0, 0, 0, pair)),
    ]
    out_shape = [
        jax.ShapeDtypeStruct((TOK, D), BF),
        jax.ShapeDtypeStruct((N_CTX, 2, rows, D), BF),
    ]
    if biased:
        specs = [SMEM_SPEC, SMEM_SPEC] + specs + [TILE_SPEC]
        operands = [classes, near] + operands + [tiles]
        out_specs.append(pl.BlockSpec((2, 3, HALF, TOK), lambda pair: (pair, 0, 0, 0)))
        out_shape.append(jax.ShapeDtypeStruct((HEADS, 3, HALF, TOK), F32))
    return pl.pallas_call(
        functools.partial(backward_kernel, biased),
        grid=(PAIRS,),
        in_specs=specs,
        out_specs=out_specs,
        out_shape=out_shape,
        scratch_shapes=[
            pltpu.VMEM((chunks, TOK, 2 * TOK), F32),
            pltpu.VMEM((chunks, TOK, 2 * TOK), F32),
            pltpu.VMEM((chunks, TOK, 2 * TOK), BF),
            pltpu.VMEM((chunks, TOK, 2 * TOK), BF),
        ],
        compiler_params=LOCAL,
        cost_estimate=pl.CostEstimate(flops=3 * 10**9, bytes_accessed=10**7, transcendentals=10**6),
        name="attend_self_back" if biased else "attend_cross_back",
    )(*operands)


def matmul(left, right):
    return jnp.dot(left, right, preferred_element_type=F32)


def transposed_left(left, right):
    return contract(left, right, ((0,), (0,)))


def transposed_right(left, right):
    return contract(left, right, ((1,), (1,)))


def rms_scaled(values, gain):
    inverse = lax.rsqrt(jnp.mean(values * values, axis=-1, keepdims=True) + 1e-06)
    return (values * inverse * gain).astype(BF)


def rms_back(values, gain, grad):
    inverse = lax.rsqrt(jnp.mean(values * values, axis=-1, keepdims=True) + 1e-06)
    scaled = gain * grad
    mixed = jnp.mean(values * scaled, axis=-1, keepdims=True)
    grad_values = inverse * scaled - values * (inverse * inverse * inverse * mixed)
    return grad_values, jnp.sum(values * inverse * grad, axis=0)


def gelu_product(gate_part, up_part):
    return jax.nn.gelu(gate_part, approximate=True) * up_part


def near_hot():
    shape = (REACH, 3 * HALF * HALF)
    spot = lax.broadcasted_iota(jnp.int32, shape, 1)
    gap = spot // (HALF * HALF)
    key = (spot // HALF) % HALF
    row = spot % HALF
    distance = jnp.clip(HALF * gap + row - key, 0, REACH - 1)
    return (distance == lax.broadcasted_iota(jnp.int32, shape, 0)).astype(BF)


def bias_tiles(bias_rows):
    near = matmul(bias_rows.astype(BF), near_hot()).reshape(HEADS, 3, HALF, HALF)
    key = jnp.arange(HALF, dtype=jnp.int32)[:, None]
    row = jnp.arange(HALF, dtype=jnp.int32)[None, :]
    barred = (jnp.arange(3) == 0)[None, :, None, None] & (key > row)[None, None]
    near = jnp.where(barred, -1e30, near)
    far = jnp.broadcast_to(bias_rows[:, -1][:, None, None, None], (HEADS, 1, HALF, HALF))
    none = jnp.full((HEADS, 1, HALF, HALF), -1e30, F32)
    tiles = jnp.concatenate([near, far, none], axis=1)
    return jnp.concatenate([tiles, tiles], axis=-1)


def bias_sums(strips):
    tiles = (strips[..., :HALF] + strips[..., HALF:]).reshape(HEADS, -1)
    high = tiles.astype(BF)
    low = (tiles - high.astype(F32)).astype(BF)
    hot = near_hot()
    sums = transposed_right(high, hot) + transposed_right(low, hot)
    far = -jnp.sum(sums[:, :-1], axis=1, keepdims=True)
    return jnp.concatenate([sums[:, :-1], far], axis=1)


def body(
    decoder_in,
    encoder_states,
    out_grad,
    block_pairs,
    bucket_table,
    gain_self,
    self_query,
    self_key,
    self_value,
    self_out,
    position_bias,
    gain_cross,
    cross_query,
    cross_key,
    cross_value,
    cross_out,
    gain_feed,
    feed_gate,
    feed_up,
    feed_down,
):
    me = lax.axis_index("ctx")
    rows = self_query.shape[0]
    extra = jnp.concatenate(
        [
            gain_self[:, None],
            gain_cross[:, None],
            gain_feed[:, None],
            jnp.zeros((rows, 5), BF),
            jnp.pad(position_bias, ((0, rows - position_bias.shape[0]), (0, 0))),
            jnp.zeros((rows, 236), BF),
        ],
        axis=1,
    )
    early, late, down = gather_weights(
        [
            jnp.concatenate([self_query, self_key, self_value, cross_key, cross_value, extra], axis=1),
            jnp.concatenate([self_out, cross_query, cross_out, feed_gate, feed_up], axis=1),
            feed_down,
        ],
        5,
    )
    early = early.reshape(D, -1)
    late = late.reshape(D, -1)
    down = down.reshape(FF, D)
    qkv_one = early[:, : 3 * D]
    kv_two = early[:, 3 * D : 5 * D]
    gains = early[:, 5 * D : 5 * D + 3].astype(F32).T
    norm_one, norm_two, norm_three = gains[0:1], gains[1:2], gains[2:3]
    table = early.reshape(8, rows, -1)[:, :4, 5 * D + 8 : 5 * D + 20].reshape(32, HEADS)
    out_one = late[:, :D]
    query_two = late[:, D : 2 * D]
    out_two = late[:, 2 * D : 3 * D]
    gate_up = late[:, 3 * D :]

    bucket_hot = (bucket_table[:, None] == jnp.arange(32, dtype=jnp.int32)[None, :]).astype(BF)
    bias_rows = transposed_right(table.T, bucket_hot)
    tiles = bias_tiles(bias_rows)
    pair = block_pairs[me]
    query_blocks = jnp.stack([pair, 31 - pair])
    key_blocks = jnp.stack([block_pairs, 31 - block_pairs], axis=1).reshape(-1)
    gaps = query_blocks[:, None] - key_blocks[None, :]
    classes = jnp.where(gaps < 0, 4, jnp.minimum(gaps, 3)).astype(jnp.int32)
    wanted = query_blocks[:, None] - jnp.arange(3, dtype=jnp.int32)[None, :]
    near = jnp.max(
        jnp.where(
            wanted[:, :, None] == key_blocks[None, None, :],
            jnp.arange(32, dtype=jnp.int32)[None, None, :],
            -1,
        ),
        axis=-1,
    )

    tokens = decoder_in[0].astype(F32)
    states = encoder_states[0]
    upstream = out_grad[0]
    normed_one = rms_scaled(tokens, norm_one)
    qkv = matmul(normed_one, qkv_one).astype(BF)
    cross_kv = matmul(states, kv_two).astype(BF)
    queries = qkv[:, :D]
    local = jnp.stack(
        [
            jnp.concatenate([qkv[:, D : 2 * D], cross_kv[:, :D]], axis=0),
            jnp.concatenate([qkv[:, 2 * D :], cross_kv[:, D:]], axis=0),
        ]
    )
    gathered = ctx_gather(local, 0)
    attended, self_totals = attend(queries, gathered, TOK, 0, classes, tiles)
    mid_one = tokens + matmul(attended, out_one)
    normed_two = rms_scaled(mid_one, norm_two)
    cross_queries = matmul(normed_two, query_two).astype(BF)
    cross_attended, cross_totals = attend(cross_queries, gathered, ENC, 2)
    mid_two = mid_one + matmul(cross_attended, out_two)
    normed_three = rms_scaled(mid_two, norm_three)
    gate_up_values = matmul(normed_three, gate_up).astype(BF).astype(F32)
    gate_values, up_values = gate_up_values[:, :FF], gate_up_values[:, FF:]
    hidden, pull_feed = jax.vjp(gelu_product, gate_values, up_values)
    hidden = hidden.astype(BF)
    block_out = mid_two + matmul(hidden, down)

    d_hidden = transposed_right(upstream, down)
    d_gate_up = jnp.concatenate(pull_feed(d_hidden), axis=1).astype(BF)
    grad_down = transposed_left(hidden, upstream).astype(BF)
    grad_gate_up = transposed_left(normed_three, d_gate_up).astype(BF)
    d_normed_three = transposed_right(d_gate_up, gate_up)
    part_three, grad_norm_three = rms_back(mid_two, norm_three, d_normed_three)
    d_mid_two = upstream.astype(F32) + part_three
    cross_branch = d_mid_two.astype(BF)
    d_cross_attended = transposed_right(cross_branch, out_two).astype(BF)
    d_cross_queries, d_cross_kv_all = attend_back(
        cross_queries, gathered, d_cross_attended, cross_totals, ENC, 2
    )
    grad_out_two = transposed_left(cross_attended, cross_branch).astype(BF)
    grad_query_two = transposed_left(normed_two, d_cross_queries).astype(BF)
    d_normed_two = transposed_right(d_cross_queries, query_two)
    part_two, grad_norm_two = rms_back(mid_one, norm_two, d_normed_two)
    d_mid_one = d_mid_two + part_two
    self_branch = d_mid_one.astype(BF)
    d_attended = transposed_right(self_branch, out_one).astype(BF)
    d_queries, d_kv_all, strips = attend_back(
        queries, gathered, d_attended, self_totals, TOK, 0, classes, near, tiles
    )
    grad_table = matmul(bias_sums(strips), bucket_hot.astype(F32)).T.reshape(8, 4, HEADS)
    grad_extra = jnp.concatenate(
        [
            jnp.zeros((D, 1), F32),
            grad_norm_two[:, None],
            grad_norm_three[:, None],
            jnp.zeros((D, 5), F32),
            jnp.pad(grad_table, ((0, 0), (0, rows - 4), (0, 0))).reshape(D, HEADS),
            jnp.zeros((D, 236), F32),
        ],
        axis=1,
    )
    grad_out_one = transposed_left(attended, self_branch).astype(BF)
    grad_query_one = transposed_left(normed_one, d_queries).astype(BF)
    summed, grad_decoder, grad_encoder = finish(
        [
            d_cross_kv_all.reshape(8, 2, 2, ENC, D),
            d_kv_all.reshape(8, 2, 2, TOK, D),
            grad_gate_up.reshape(8, rows, -1),
            grad_out_two.reshape(8, rows, D),
            grad_query_two.reshape(8, rows, D),
            grad_out_one.reshape(8, rows, D),
            grad_query_one.reshape(8, rows, D),
            grad_down.reshape(8, -1, D),
        ],
        [
            normed_one.T.reshape(8, rows, TOK),
            states.T.reshape(8, rows, ENC),
            qkv_one[:, D:],
            kv_two,
            transposed_right(d_queries, qkv_one[:, :D]),
            d_mid_one,
            decoder_in[0],
            norm_one,
            grad_extra.astype(BF).reshape(8, rows, 256),
        ],
        3,
    )
    owned = summed[:, :, :D].astype(F32)
    wide = summed[:, :, D : D + 512].astype(F32)
    wide = jnp.transpose(wide, (1, 0, 2)).reshape(rows, 2 * FF)
    tall = summed[:, :, D + 512 : D + 768].astype(F32).reshape(8, 2, 3, 16, 256)
    tall = jnp.transpose(tall, (1, 0, 3, 2, 4)).reshape(256, D)
    extras = summed[0, :, D + 768 :].astype(F32)
    return (
        block_out[None],
        grad_decoder[None],
        grad_encoder[None],
        extras[:, 0],
        owned[3],
        owned[6],
        owned[7],
        owned[2],
        extras[:4, 8:20],
        extras[:, 1],
        owned[1],
        owned[4],
        owned[5],
        owned[0],
        extras[:, 2],
        wide[:, :FF],
        wide[:, FF:],
        tall,
    )


def solution(mesh):
    tokens = P("fsdp", "ctx", None)
    matrix = P("fsdp", None)
    vector = P("fsdp")
    weights = (
        (vector,) + (matrix,) * 5 + (vector,) + (matrix,) * 4 + (vector,) + (matrix,) * 3
    )
    return jax.shard_map(
        body,
        mesh=mesh,
        in_specs=(tokens,) * 3 + (P(), P()) + weights,
        out_specs=(tokens,) * 3 + weights,
        check_vma=False,
    )
```

```python
import functools

import jax
import jax.numpy as jnp
from jax import lax
from jax.experimental import pallas as pl
from jax.experimental.pallas import tpu as pltpu
from jax.sharding import PartitionSpec as P

D = 768
FF = 2048
HEADS = 12
HEAD_DIM = 64
PAIRS = HEADS // 2
N_CTX = 16
TOK = 128
ENC = 64
HALF = 64
REACH = 128
BF = jnp.bfloat16
F32 = jnp.float32
MIB = 1024 * 1024


def ctx_place():
    me = lax.axis_index("ctx")
    core = me % 2
    high = (me // 2) % 2
    y = me // 4
    return me, core, high, y


def slot_of(y, shift, high, core):
    return ((y + shift) % 4) * 4 + 2 * high + core


def torus_place():
    me, core, high, y = ctx_place()
    shard = lax.axis_index("fsdp")
    return me, core, high, y, shard // 4, shard % 4


def hop(src, dst, send_sem, recv_sem, ctx, fsdp):
    return pltpu.make_async_remote_copy(
        src_ref=src,
        dst_ref=dst,
        send_sem=send_sem,
        recv_sem=recv_sem,
        device_id={"ctx": ctx, "fsdp": fsdp},
    )


def greet_all(devices):
    barrier = pltpu.get_barrier_semaphore()
    for ctx, fsdp in devices:
        pl.semaphore_signal(barrier, inc=1, device_id={"ctx": ctx, "fsdp": fsdp})
    pl.semaphore_wait(barrier, len(devices))


PACKS = ((0, 1), (2, 3), (4, 5, 6, 7), (8, 9), (10,))


def front_kernel(*refs):
    sources = refs[:11]
    small_ref, token_ref, state_ref = refs[11:14]
    targets = refs[14:19]
    small_out, normed_out, query_out, self_out_ref, cross_out_ref = refs[19:24]
    (
        landing, weight_ref, self_ref, cross_ref, send_sem, x_sem, z_sem, core_sem, fill_sem,
        small_sem, self_sem, cross_sem, local_sem,
    ) = refs[24:]
    me, core, high, y, low, x = torus_place()
    shard = low * 4 + x
    sibling = (slot_of(y, 0, high, 1 - core), shard)
    inside = (me, (1 - low) * 4 + x)
    outside = (slot_of(y, 0, 1 - high, core), (1 - low) * 4 + x)
    across = slot_of(y, 0, 1 - high, core)
    rows = [slot_of(y, shift, high, core) for shift in (1, 2, 3)]
    others = [low * 4 + (x + shift) % 4 for shift in (1, 2, 3)]
    peers = [(shard + shift) % 8 for shift in range(1, 8)]
    greet_all(
        [sibling, outside, (across, shard)]
        + [(me, peer) for peer in peers]
        + [(row, shard) for row in rows]
    )
    sends = []

    def send(src, dst, recv_sem, device):
        copy = hop(src, dst, send_sem.at[len(sends)], recv_sem, *device)
        copy.start()
        sends.append(copy)

    def arrived(ref, recv_sem):
        hop(ref, ref, send_sem.at[0], recv_sem, *sibling).wait_recv()

    def bring(src, dst, sem):
        copy = pltpu.make_async_copy(src, dst, sem)
        copy.start()
        return copy


    def part(k, owner, whose, side=None):
        ref = targets[k]
        count = ref.shape[1] // 2
        start = pl.multiple_of(whose * count, 16)
        if side is None:
            return ref.at[owner, pl.ds(start, count), :]
        width = ref.shape[2] // 2
        return ref.at[owner, pl.ds(start, count), pl.ds(side * width, width)]

    def fill(k):
        copies = []
        start = 0
        for source in PACKS[k]:
            width = sources[source].shape[1]
            copies.append(
                bring(
                    sources[source],
                    targets[k].at[shard, :, pl.ds(start, width)],
                    fill_sem.at[source],
                )
            )
            start += width
        return copies

    def send_own(k):
        for copy in fills[k]:
            copy.wait()
        for spot in (1, 0, 2):
            block = part(k, shard, core)
            send(block, block, x_sem.at[k, spot], (me, others[spot]))
        for side, device in enumerate((inside, outside)):
            piece = part(k, shard, core, side)
            send(piece, piece, z_sem.at[k, 3, side], device)


    def pass_x(k):
        for spot in (0, 2, 1):
            owner = low * 4 + (x + 3 - spot) % 4
            block = part(k, owner, core)
            arrived(block, x_sem.at[k, spot])
            for side, device in enumerate((inside, outside)):
                piece = part(k, owner, core, side)
                send(piece, piece, z_sem.at[k, spot, side], device)
            send(block, block, core_sem.at[k, spot], sibling)

    def pass_z(k):
        for spot in (3, 0, 2, 1):
            owner = (1 - low) * 4 + (x + 3 - spot) % 4
            for side in range(2):
                piece = part(k, owner, core, side)
                arrived(piece, z_sem.at[k, spot, side])
                send(piece, piece, core_sem.at[k, 3 + 2 * spot + side], sibling)

    def complete(k):
        for spot in range(3):
            owner = low * 4 + (x + 3 - spot) % 4
            arrived(part(k, owner, 1 - core), core_sem.at[k, spot])
        for spot in range(4):
            owner = (1 - low) * 4 + (x + 3 - spot) % 4
            for side in range(2):
                arrived(part(k, owner, 1 - core, side), core_sem.at[k, 3 + 2 * spot + side])


    def kv_start(src, out, sems):
        send(src, out.at[me], sems.at[me], (across, shard))
        for row in rows:
            send(src, out.at[me], sems.at[me], (row, shard))
        send(src, out.at[me], sems.at[me], sibling)

    def kv_across(out, sems):
        block = out.at[across]
        arrived(block, sems.at[across])
        for row in rows:
            send(block, block, sems.at[across], (row, shard))
        send(block, block, sems.at[across], sibling)

    def kv_rows(out, sems, flip):
        for shift in (1, 3, 2):
            slot = slot_of(y, shift, 1 - high if flip else high, core)
            block = out.at[slot]
            arrived(block, sems.at[slot])
            send(block, block, sems.at[slot], sibling)

    def kv_complete(out, sems):
        for shift in range(4):
            for half in range(2):
                slot = slot_of(y, shift, half, 1 - core)
                arrived(out.at[slot], sems.at[slot])

    fills = [fill(k) for k in range(5)]
    own_small = bring(small_ref, landing.at[shard], local_sem.at[0])
    for spot, peer in enumerate(peers):
        send(small_ref, landing.at[shard], small_sem.at[spot], (me, peer))
    send_own(0)
    send_own(1)
    own_small.wait()
    for spot in range(7):
        arrived(landing.at[(shard + 7 - spot) % 8], small_sem.at[spot])
    small = landing[...]
    small_out[...] = small
    gains = small.astype(F32)
    gain = jnp.concatenate([gains[owner, 0:1, :96] for owner in range(8)], axis=1)
    normed = rms_scaled(token_ref[...].astype(F32), gain)
    normed_out[...] = normed
    pass_x(0)
    send_own(2)
    pass_z(0)
    pass_x(1)
    send_own(3)
    complete(0)
    bring(targets[0], weight_ref, local_sem.at[1]).wait()
    for half in range(2):
        weight = weight_ref[:, :, half * D : half * D + D].reshape(D, D)
        self_ref[half] = matmul(normed, weight).astype(BF)
    kv_start(self_ref, self_out_ref, self_sem)
    own_self = bring(self_ref, self_out_ref.at[me], local_sem.at[2])
    pass_z(1)
    complete(1)
    bring(targets[1], weight_ref, local_sem.at[1]).wait()
    for half in range(2):
        weight = weight_ref[:, :, half * D : half * D + D].reshape(D, D)
        cross_ref[half] = matmul(state_ref[...], weight).astype(BF)
    kv_start(cross_ref, cross_out_ref, cross_sem)
    own_cross = bring(cross_ref, cross_out_ref.at[me], local_sem.at[3])
    pass_x(2)
    send_own(4)
    kv_across(self_out_ref, self_sem)
    pass_z(2)
    kv_across(cross_out_ref, cross_sem)
    pass_x(3)
    kv_rows(self_out_ref, self_sem, False)
    pass_z(3)
    pass_x(4)
    kv_rows(self_out_ref, self_sem, True)
    kv_rows(cross_out_ref, cross_sem, False)
    pass_z(4)
    kv_rows(cross_out_ref, cross_sem, True)
    complete(2)
    bring(targets[2].at[:, :, pl.ds(0, D)], weight_ref.at[:, :, pl.ds(0, D)], local_sem.at[1]).wait()
    query_out[...] = matmul(normed, weight_ref[:, :, :D].reshape(D, D)).astype(BF)
    complete(3)
    complete(4)
    kv_complete(self_out_ref, self_sem)
    kv_complete(cross_out_ref, cross_sem)
    own_self.wait()
    own_cross.wait()
    for copy in sends:
        copy.wait_send()


def front(weights, small, tokens, states, collective_id):
    dma = pltpu.SemaphoreType.DMA
    packs = [
        (8, weights[group[0]].shape[0], sum(weights[k].shape[1] for k in group)) for group in PACKS
    ]
    anywhere = pl.BlockSpec(memory_space=pl.ANY)
    inside = pl.BlockSpec(memory_space=pltpu.VMEM)
    return pl.pallas_call(
        front_kernel,
        out_shape=[jax.ShapeDtypeStruct(pack, BF) for pack in packs]
        + [
            jax.ShapeDtypeStruct((8, 16, 128), BF),
            jax.ShapeDtypeStruct((TOK, D), BF),
            jax.ShapeDtypeStruct((TOK, D), BF),
            jax.ShapeDtypeStruct((N_CTX, 2, TOK, D), BF),
            jax.ShapeDtypeStruct((N_CTX, 2, ENC, D), BF),
        ],
        in_specs=[anywhere] * 12 + [inside] * 2,
        out_specs=[anywhere] * 5 + [inside] * 3 + [anywhere] * 2,
        scratch_shapes=[
            pltpu.VMEM((8, 16, 128), BF),
            pltpu.VMEM((8, 96, 2 * D), BF),
            pltpu.VMEM((2, TOK, D), BF),
            pltpu.VMEM((2, ENC, D), BF),
            dma((5 * 22 + 7 + 30,)),
            dma((5, 3)),
            dma((5, 4, 2)),
            dma((5, 11)),
            dma((11,)),
            dma((7,)),
            dma((N_CTX,)),
            dma((N_CTX,)),
            dma((4,)),
        ],
        compiler_params=pltpu.CompilerParams(
            collective_id=collective_id, has_side_effects=True, vmem_limit_bytes=32 * MIB
        ),
        name="front",
    )(*weights, small, tokens, states)


PIECE = 48
ROOM = D + FF // 4 + FF // 8 + 128
EARLY = (2 * FF, D, D, D, D)
WIDTHS = EARLY + (2 * D, 2 * D, 256)
SPAN = sum(WIDTHS)
DOWN = len(WIDTHS)


def finish_kernel(*refs):
    (
        dckv_ref, dkv_ref, wide_ref, two_out_ref, two_query_ref, one_out_ref, one_query_ref, down_ref,
        normed_ref, states_ref, kv_ref, ckv_ref, dn_ref, dmid_ref, token_ref, gain_ref, extra_ref,
        out_ref, decoder_ref, encoder_ref,
        kept, from_core, from_z, from_x, d_kept, d_core, d_z, d_x,
        s_kept, s_core, s_row, s_stage, s_high, c_kept, c_core, c_row, c_stage, c_high,
        to_core, gain_cols, packed, from_ctx, total_ref,
        s_sem, c_sem, local_sem, core_send, core_recv, z_send, z_recv, x_send, x_recv,
        ctx_send, ctx_recv, out_send, out_recv, pass_send, pass_recv, own_sem,
    ) = refs
    me, core, high, y, low, x = torus_place()
    shard = low * 4 + x
    rank = y * 2 + high
    sibling = (slot_of(y, 0, high, 1 - core), shard)
    inside = (me, (1 - low) * 4 + x)
    outside = (slot_of(y, 0, 1 - high, core), (1 - low) * 4 + x)
    across = (slot_of(y, 0, 1 - high, core), shard)
    others = [low * 4 + (x + shift) % 4 for shift in (1, 2, 3)]
    shifts = [(dy, dz) for dy in range(4) for dz in range(2)][1:]
    mates = [((y + dy) % 4) * 2 + (high + dz) % 2 for dy, dz in shifts]
    greet_all(
        [sibling, inside, outside]
        + [(me, other) for other in others]
        + [(mate * 2 + core, shard) for mate in mates]
    )
    mine = pl.ds(pl.multiple_of(core * PIECE, 16), PIECE)
    theirs = pl.ds(pl.multiple_of((1 - core) * PIECE, 16), PIECE)
    mine_down = pl.ds(pl.multiple_of(core * 128, 16), 128)
    theirs_down = pl.ds(pl.multiple_of((1 - core) * 128, 16), 128)
    sends = []

    def go(src, dst, send_sem, recv_sem, device):
        copy = hop(src, dst, send_sem, recv_sem, *device)
        copy.start()
        sends.append(copy)
        return copy

    def bring(src, dst, sem):
        copy = pltpu.make_async_copy(src, dst, sem)
        copy.start()
        return copy


    def rows_start(source, held, arrived, sem, base):
        over = []
        local = []
        for spot, shift in enumerate((2, 1, 3, 0)):
            pair = pl.ds(((y + shift) % 4) * 2, 2)
            block = pl.ds(2 * spot, 2)
            over.append(
                go(
                    source.at[pair, 1 - core], arrived.at[block],
                    sem.at[0, spot], sem.at[1, spot], sibling,
                )
            )
            local.append(bring(source.at[pair, core], held.at[block], local_sem.at[base + spot]))
        return over, local

    def rows_send(copies, held, arrived, row, sem):
        over, local = copies
        onward = []
        for spot, shift in enumerate((2, 1, 3, 0)):
            local[spot].wait()
            over[spot].wait_recv()
            for block in (2 * spot, 2 * spot + 1):
                for part in range(2):
                    held[block, part] = held[block, part] + arrived[block, part]
            if shift:
                onward.append(
                    go(
                        held.at[pl.ds(2 * spot, 2)], row.at[spot],
                        sem.at[2, spot], sem.at[3, spot], (others_ctx[shift - 1], shard),
                    )
                )
        return onward

    others_ctx = [slot_of(y, shift, high, core) for shift in (1, 2, 3)]

    def rows_total(held, row, half, part):
        result = held[6 + half, part].astype(F32)
        for spot in range(3):
            result = result + row[spot, half, part].astype(F32)
        return result

    def rows_across(onward, held, row, stage, landing, sem):
        for copy in onward:
            copy.wait_recv()
        for part in range(2):
            stage[part] = rows_total(held, row, 1 - high, part).astype(BF)
        return go(stage, landing, sem.at[2, 3], sem.at[3, 3], across)

    def rows_sum(last, held, row, landing):
        totals = [rows_total(held, row, high, part) for part in range(2)]
        last.wait_recv()
        return jnp.concatenate(
            [(totals[part] + landing[part].astype(F32)).astype(BF) for part in range(2)], axis=1
        )


    starts = [sum(WIDTHS[:k]) for k in range(len(WIDTHS))]

    def buffers(k):
        if k == DOWN:
            return d_kept, d_core, d_z, d_x, 0, D
        return kept, from_core, from_z, from_x, starts[k], WIDTHS[k]

    over_core, over_z, over_x, brought = {}, {}, {}, {}

    def chunk_start(k, source):
        held, arrived, _, _, start, width = buffers(k)
        cut = pl.ds(start, width)
        rows, far_rows = (mine_down, theirs_down) if k == DOWN else (mine, theirs)
        over_core[k] = go(
            source.at[:, far_rows, :], arrived.at[:, :, cut], core_send.at[k], core_recv.at[k], sibling
        )
        brought[k] = bring(source.at[:, rows, :], held.at[:, :, cut], local_sem.at[8 + k])

    def chunk_send(k, offset):
        width = WIDTHS[k]
        over_core[k] = go(
            to_core.at[:, :, pl.ds(offset, width)],
            from_core.at[:, :, pl.ds(starts[k], width)],
            core_send.at[k],
            core_recv.at[k],
            sibling,
        )

    def step_core(k):
        held, arrived, landing, _, start, width = buffers(k)
        cut = pl.ds(start, width)
        if k in brought:
            brought[k].wait()
        over_core[k].wait_recv()
        for column in range(4):
            owner = 4 * (1 - low) + column
            held[owner, :, cut] = held[owner, :, cut] + arrived[owner, :, cut]
        half = width // 2
        over_z[k] = [
            go(
                held.at[pl.ds(4 * (1 - low), 4), :, pl.ds(start + side * half, half)],
                landing.at[:, :, pl.ds(start + side * half, half)],
                z_send.at[k, side],
                z_recv.at[k, side],
                device,
            )
            for side, device in enumerate((inside, outside))
        ]
        for column in range(4):
            owner = 4 * low + column
            held[owner, :, cut] = held[owner, :, cut] + arrived[owner, :, cut]

    def step_z(k):
        held, _, landing, spread, start, width = buffers(k)
        cut = pl.ds(start, width)
        for copy in over_z[k]:
            copy.wait_recv()
        for column in range(4):
            landing[column, :, cut] = landing[column, :, cut] + held[4 * low + column, :, cut]
        over_x[k] = [
            go(
                landing.at[(x + spot + 1) % 4, :, cut],
                spread.at[spot, :, cut],
                x_send.at[k, spot],
                x_recv.at[k, spot],
                (me, others[spot]),
            )
            for spot in (1, 0, 2)
        ]

    def step_x(k, first=None):
        _, _, landing, spread, start, width = buffers(k)
        cut = pl.ds(start, width)
        for copy in over_x[k]:
            copy.wait_recv()
        total = landing[x, :, cut].astype(F32)
        for spot in range(3):
            total = total + spread[spot, :, cut].astype(F32)
        total = total.astype(BF)
        if k == 0:
            for piece in range(8):
                packed[piece, :, D : D + 512] = total[:, piece * 512 : piece * 512 + 512]
        elif k == DOWN:
            for piece in range(8):
                for part in range(3):
                    packed[piece, part * 16 : part * 16 + 16, D + 512 : D + 768] = total[
                        piece * 16 : piece * 16 + 16, part * 256 : part * 256 + 256
                    ]
        elif k == len(WIDTHS) - 1:
            packed[0, :, ROOM - 128 :] = total[:, :128]
            for piece in range(1, 8):
                packed[piece, :, ROOM - 128 :] = jnp.zeros((PIECE, 128), BF)
        else:
            for piece in range(width // D):
                packed[first + piece, :, :D] = total[:, piece * D : (piece + 1) * D]

    def outer(left_ref, rows, right):
        left = left_ref[:, rows, :]
        return contract(left.reshape(8 * PIECE, left.shape[-1]), right, ((1,), (0,))).astype(BF).reshape(
            8, PIECE, right.shape[-1]
        )

    c_copies = rows_start(dckv_ref, c_kept, c_core, c_sem, 0)
    s_copies = rows_start(dkv_ref, s_kept, s_core, s_sem, 4)
    for k, source in enumerate((wide_ref, two_out_ref, two_query_ref, one_out_ref, one_query_ref)):
        chunk_start(k, source)
        if k == 0:
            chunk_start(DOWN, down_ref)
    c_onward = rows_send(c_copies, c_kept, c_core, c_row, c_sem)
    s_onward = rows_send(s_copies, s_kept, s_core, s_row, s_sem)
    for k in (0, DOWN, 1, 2, 3, 4):
        step_core(k)
    step_z(0)
    c_last = rows_across(c_onward, c_kept, c_row, c_stage, c_high, c_sem)
    step_z(DOWN)
    d_ckv = rows_sum(c_last, c_kept, c_row, c_high)
    to_core[:, :, : 2 * D] = outer(states_ref, theirs, d_ckv)
    chunk_send(5, 0)
    kept[:, :, starts[5] : starts[5] + 2 * D] = outer(states_ref, mine, d_ckv)
    encoder_ref[...] = contract(d_ckv, ckv_ref[...], ((1,), (1,)))
    for k in (1, 2, 3, 4):
        step_z(k)
    step_core(5)
    step_x(0)
    step_x(DOWN)
    s_last = rows_across(s_onward, s_kept, s_row, s_stage, s_high, s_sem)
    step_z(5)
    for k in (1, 2, 3, 4):
        step_x(k, k - 1)
    d_kv = rows_sum(s_last, s_kept, s_row, s_high)
    over_core[5].wait_send()
    to_core[:, :, : 2 * D] = outer(normed_ref, theirs, d_kv)
    chunk_send(6, 0)
    kept[:, :, starts[6] : starts[6] + 2 * D] = outer(normed_ref, mine, d_kv)
    tokens = token_ref[...].astype(F32)
    grad = dn_ref[...] + contract(d_kv, kv_ref[...], ((1,), (1,)))
    inverse = lax.rsqrt(jnp.mean(tokens * tokens, axis=-1, keepdims=True) + 1e-06)
    columns = contract(
        (tokens * inverse * grad).astype(BF), jnp.ones((TOK, 128), BF), ((0,), (0,))
    )
    lane = lax.broadcasted_iota(jnp.int32, (D, 128), 1)
    gain_cols[...] = jnp.where(lane == 0, columns, 0.0).astype(BF).reshape(8, 2 * PIECE, 128)
    to_core[:, :, 2 * D : 2 * D + 128] = gain_cols[:, theirs, :] + extra_ref[:, theirs, :128]
    to_core[:, :, 2 * D + 128 :] = extra_ref[:, theirs, 128:]
    chunk_send(7, 2 * D)
    kept[:, :, starts[7] : starts[7] + 128] = gain_cols[:, mine, :] + extra_ref[:, mine, :128]
    kept[:, :, starts[7] + 128 :] = extra_ref[:, mine, 128:]
    step_core(6)
    step_core(7)
    step_x(5, 4)
    step_z(6)
    step_z(7)
    scaled = gain_ref[...] * grad
    mixed = jnp.mean(tokens * scaled, axis=-1, keepdims=True)
    decoder_ref[...] = (
        dmid_ref[...] + inverse * scaled - tokens * (inverse * inverse * inverse * mixed)
    )
    step_x(6, 6)
    step_x(7)


    over_ctx = [
        go(
            packed.at[mate],
            from_ctx.at[spot],
            ctx_send.at[spot],
            ctx_recv.at[spot],
            (mate * 2 + core, shard),
        )
        for spot, mate in enumerate(mates)
    ]
    total = packed[rank].astype(F32)
    for spot in range(7):
        over_ctx[spot].wait_recv()
        total = total + from_ctx[spot].astype(F32)
    total_ref[...] = total.astype(BF)
    for spot, mate in enumerate(mates):
        go(
            total_ref,
            out_ref.at[rank, mine, :],
            out_send.at[spot],
            out_recv.at[rank],
            (mate * 2 + core, shard),
        )
    go(total_ref, out_ref.at[rank, mine, :], pass_send.at[7], pass_recv.at[rank], sibling)
    own = bring(total_ref, out_ref.at[rank, mine, :], own_sem)

    def landed(ref, recv_sem):
        hop(ref, ref, pass_send.at[0], recv_sem, *sibling).wait_recv()

    for spot, mate in enumerate(mates):
        block = out_ref.at[mate, mine, :]
        landed(block, out_recv.at[mate])
        go(block, block, pass_send.at[spot], pass_recv.at[mate], sibling)
    for mate in [rank] + mates:
        landed(out_ref.at[mate, theirs, :], pass_recv.at[mate])
    own.wait()
    for copy in sends:
        if copy is not over_core[5]:
            copy.wait_send()


def finish(far, near, collective_id):
    dma = pltpu.SemaphoreType.DMA
    chunks = len(WIDTHS) + 1

    def rows(count):
        return [
            pltpu.VMEM((8, 2, count, D), BF),
            pltpu.VMEM((8, 2, count, D), BF),
            pltpu.VMEM((3, 2, 2, count, D), BF),
            pltpu.VMEM((2, count, D), BF),
            pltpu.VMEM((2, count, D), BF),
        ]

    return pl.pallas_call(
        finish_kernel,
        out_shape=[
            jax.ShapeDtypeStruct((8, 2 * PIECE, ROOM), BF),
            jax.ShapeDtypeStruct((TOK, D), F32),
            jax.ShapeDtypeStruct((ENC, D), F32),
        ],
        in_specs=[pl.BlockSpec(memory_space=pl.ANY)] * len(far)
        + [pl.BlockSpec(memory_space=pltpu.VMEM)] * len(near),
        out_specs=[
            pl.BlockSpec(memory_space=pl.ANY),
            pl.BlockSpec(memory_space=pltpu.VMEM),
            pl.BlockSpec(memory_space=pltpu.VMEM),
        ],
        scratch_shapes=[
            pltpu.VMEM((8, PIECE, SPAN), BF),
            pltpu.VMEM((8, PIECE, SPAN), BF),
            pltpu.VMEM((4, PIECE, SPAN), BF),
            pltpu.VMEM((3, PIECE, SPAN), BF),
            pltpu.VMEM((8, 128, D), BF),
            pltpu.VMEM((8, 128, D), BF),
            pltpu.VMEM((4, 128, D), BF),
            pltpu.VMEM((3, 128, D), BF),
        ]
        + rows(TOK)
        + rows(ENC)
        + [
            pltpu.VMEM((8, PIECE, 2 * D + 256), BF),
            pltpu.VMEM((8, 2 * PIECE, 128), BF),
            pltpu.VMEM((8, PIECE, ROOM), BF),
            pltpu.VMEM((7, PIECE, ROOM), BF),
            pltpu.VMEM((PIECE, ROOM), BF),
            dma((4, 4)),
            dma((4, 4)),
            dma((8 + chunks,)),
            dma((chunks,)),
            dma((chunks,)),
            dma((chunks, 2)),
            dma((chunks, 2)),
            dma((chunks, 3)),
            dma((chunks, 3)),
            dma((7,)),
            dma((7,)),
            dma((7,)),
            dma((8,)),
            dma((8,)),
            dma((8,)),
            dma,
        ],
        compiler_params=pltpu.CompilerParams(
            collective_id=collective_id, has_side_effects=True, vmem_limit_bytes=60 * MIB
        ),
        name="finish_gradients",
    )(*far, *near)


def split_heads(block):
    lane = lax.broadcasted_iota(jnp.int32, block.shape, 1)
    nothing = jnp.zeros_like(block)
    return jnp.concatenate(
        [jnp.where(lane < HEAD_DIM, block, nothing), jnp.where(lane < HEAD_DIM, nothing, block)],
        axis=0,
    )


def join_heads(transposed):
    row = lax.broadcasted_iota(jnp.int32, (2 * HEAD_DIM, TOK), 0)
    return jnp.where(row < HEAD_DIM, transposed[:, :TOK], transposed[:, TOK:]).T


def contract(left, right, dims):
    return lax.dot_general(left, right, (dims, ((), ())), preferred_element_type=F32)


def key_chunk(ref, j):
    if ref.shape[2] == 2 * HALF:
        return ref[j, 0]
    return ref[pl.ds(2 * j, 2), 0].reshape(2 * HALF, 2 * HEAD_DIM)


def bias_chunk(class_ref, tile_ref, j):
    lane = lax.broadcasted_iota(jnp.int32, (HALF, TOK), 1)
    rows = []
    for half in range(2):
        spot = 2 * j + half
        near = class_ref[0, spot]
        far = class_ref[1, spot]
        rows.append(
            jnp.concatenate(
                [
                    jnp.where(lane < HALF, tile_ref[head, near], tile_ref[head, far])
                    for head in range(2)
                ],
                axis=1,
            )
        )
    return jnp.concatenate(rows, axis=0)


def fold(values, join):
    return join(values.reshape(-1, 8, values.shape[-1]), axis=0)


def forward_kernel(biased, *refs):
    if biased:
        class_ref, q_ref, k_ref, v_ref, tile_ref, out_ref, total_ref, score_ref, share_ref = refs
    else:
        q_ref, k_ref, v_ref, out_ref, total_ref, score_ref, share_ref = refs
    chunks = score_ref.shape[0]
    queries = split_heads(q_ref[...])
    highest = None
    for j in range(chunks):
        scores = contract(key_chunk(k_ref, j), queries, ((1,), (1,)))
        if biased:
            scores = scores + bias_chunk(class_ref, tile_ref, j)
        score_ref[j] = scores
        top = fold(scores, jnp.max)
        highest = top if highest is None else jnp.maximum(highest, top)
    highest = jnp.max(highest, axis=0, keepdims=True)
    summed = jnp.zeros((8, 2 * TOK), F32)
    for j in range(chunks):
        raised = jnp.exp(score_ref[j] - highest)
        summed = summed + fold(raised, jnp.sum)
        share_ref[j] = raised.astype(BF)
    summed = jnp.sum(summed, axis=0, keepdims=True)
    values = jnp.concatenate([key_chunk(v_ref, j) for j in range(chunks)], axis=0)
    mixed = contract(values, share_ref[...].reshape(-1, 2 * TOK), ((0,), (0,)))
    out_ref[...] = join_heads(mixed / summed).astype(BF)
    total_ref[0] = jnp.broadcast_to(highest + jnp.log(summed), (8, 2 * TOK))


def backward_kernel(biased, *refs):
    if biased:
        class_ref, near_ref, q_ref, k_ref, v_ref, g_ref, total_ref, tile_ref = refs[:8]
        dq_ref, dkv_ref, strip_ref, share_ref, slope_ref, share_low, slope_low = refs[8:]
    else:
        q_ref, k_ref, v_ref, g_ref, total_ref = refs[:5]
        dq_ref, dkv_ref, share_ref, slope_ref, share_low, slope_low = refs[5:]
    chunks = share_ref.shape[0]
    queries = split_heads(q_ref[...])
    grads = split_heads(g_ref[...])
    totals = total_ref[0, 0:1]
    inner = jnp.zeros((8, 2 * TOK), F32)
    for j in range(chunks):
        scores = contract(key_chunk(k_ref, j), queries, ((1,), (1,)))
        if biased:
            scores = scores + bias_chunk(class_ref, tile_ref, j)
        shares = jnp.exp(scores - totals)
        slopes = contract(key_chunk(v_ref, j), grads, ((1,), (1,)))
        inner = inner + fold(shares * slopes, jnp.sum)
        share_ref[j] = shares
        slope_ref[j] = slopes
        share_low[j] = shares.astype(BF)
    inner = jnp.sum(inner, axis=0, keepdims=True)
    for j in range(chunks):
        grad = share_ref[j] * (slope_ref[j] - inner)
        if biased:
            slope_ref[j] = grad
        slope_low[j] = grad.astype(BF)
    keys = jnp.concatenate([key_chunk(k_ref, j) for j in range(chunks)], axis=0)
    low = slope_low[...].reshape(-1, 2 * TOK)
    dq_ref[...] = join_heads(contract(keys, low, ((0,), (0,)))).astype(BF)
    shape = dkv_ref.shape
    block = (shape[0], shape[2], shape[3])
    dkv_ref[:, 0] = contract(low, queries, ((1,), (0,))).astype(BF).reshape(block)
    dkv_ref[:, 1] = (
        contract(share_low[...].reshape(-1, 2 * TOK), grads, ((1,), (0,))).astype(BF).reshape(block)
    )
    if biased:
        lane = lax.broadcasted_iota(jnp.int32, (HALF, TOK), 1)
        for gap in range(3):
            pieces = []
            for half in range(2):
                spot = near_ref[half, gap]
                held = slope_ref[jnp.maximum(spot, 0) // 2, pl.ds(
                    pl.multiple_of((jnp.maximum(spot, 0) % 2) * HALF, HALF), HALF)]
                pieces.append(jnp.where(spot >= 0, held, jnp.zeros_like(held)))
            for head in range(2):
                cut = slice(head * TOK, (head + 1) * TOK)
                strip_ref[head, gap] = jnp.where(lane < HALF, pieces[0][:, cut], pieces[1][:, cut])


def pair_columns(pair):
    return (0, pair)


def kv_spec(rows, row_block, part):
    return pl.BlockSpec(
        (N_CTX, 1, rows, 2 * HEAD_DIM), lambda pair: (0, part, row_block, pair)
    )


SMEM_SPEC = pl.BlockSpec(memory_space=pltpu.SMEM)
TILE_SPEC = pl.BlockSpec((2, 5, HALF, TOK), lambda pair: (pair, 0, 0, 0))
TOTAL_SPEC = pl.BlockSpec((1, 8, 2 * TOK), lambda pair: (pair, 0, 0))
ROW_SPEC = pl.BlockSpec((TOK, 2 * HEAD_DIM), pair_columns)
LOCAL = pltpu.CompilerParams(vmem_limit_bytes=48 * MIB)


def attend(queries, gathered, rows, row_block, classes=None, tiles=None):
    biased = classes is not None
    chunks = N_CTX * rows // TOK
    specs = [ROW_SPEC, kv_spec(rows, row_block, 0), kv_spec(rows, row_block, 1)]
    operands = [queries, gathered, gathered]
    if biased:
        specs = [SMEM_SPEC] + specs + [TILE_SPEC]
        operands = [classes] + operands + [tiles]
    return pl.pallas_call(
        functools.partial(forward_kernel, biased),
        grid=(PAIRS,),
        in_specs=specs,
        out_specs=[ROW_SPEC, TOTAL_SPEC],
        out_shape=[
            jax.ShapeDtypeStruct((TOK, D), BF),
            jax.ShapeDtypeStruct((PAIRS, 8, 2 * TOK), F32),
        ],
        scratch_shapes=[
            pltpu.VMEM((chunks, TOK, 2 * TOK), F32),
            pltpu.VMEM((chunks, TOK, 2 * TOK), BF),
        ],
        compiler_params=LOCAL,
        cost_estimate=pl.CostEstimate(flops=10**9, bytes_accessed=10**7, transcendentals=10**6),
        name="attend_self" if biased else "attend_cross",
    )(*operands)


def attend_back(queries, gathered, grads, totals, rows, row_block, classes=None, near=None, tiles=None):
    biased = classes is not None
    chunks = N_CTX * rows // TOK
    specs = [ROW_SPEC, kv_spec(rows, row_block, 0), kv_spec(rows, row_block, 1), ROW_SPEC, TOTAL_SPEC]
    operands = [queries, gathered, gathered, grads, totals]
    out_specs = [
        ROW_SPEC,
        pl.BlockSpec((N_CTX, 2, rows, 2 * HEAD_DIM), lambda pair: (0, 0, 0, pair)),
    ]
    out_shape = [
        jax.ShapeDtypeStruct((TOK, D), BF),
        jax.ShapeDtypeStruct((N_CTX, 2, rows, D), BF),
    ]
    if biased:
        specs = [SMEM_SPEC, SMEM_SPEC] + specs + [TILE_SPEC]
        operands = [classes, near] + operands + [tiles]
        out_specs.append(pl.BlockSpec((2, 3, HALF, TOK), lambda pair: (pair, 0, 0, 0)))
        out_shape.append(jax.ShapeDtypeStruct((HEADS, 3, HALF, TOK), F32))
    return pl.pallas_call(
        functools.partial(backward_kernel, biased),
        grid=(PAIRS,),
        in_specs=specs,
        out_specs=out_specs,
        out_shape=out_shape,
        scratch_shapes=[
            pltpu.VMEM((chunks, TOK, 2 * TOK), F32),
            pltpu.VMEM((chunks, TOK, 2 * TOK), F32),
            pltpu.VMEM((chunks, TOK, 2 * TOK), BF),
            pltpu.VMEM((chunks, TOK, 2 * TOK), BF),
        ],
        compiler_params=LOCAL,
        cost_estimate=pl.CostEstimate(flops=3 * 10**9, bytes_accessed=10**7, transcendentals=10**6),
        name="attend_self_back" if biased else "attend_cross_back",
    )(*operands)


def matmul(left, right):
    return jnp.dot(left, right, preferred_element_type=F32)


def transposed_left(left, right):
    return contract(left, right, ((0,), (0,)))


def transposed_right(left, right):
    return contract(left, right, ((1,), (1,)))


def rms_scaled(values, gain):
    inverse = lax.rsqrt(jnp.mean(values * values, axis=-1, keepdims=True) + 1e-06)
    return (values * inverse * gain).astype(BF)


def rms_back(values, gain, grad):
    inverse = lax.rsqrt(jnp.mean(values * values, axis=-1, keepdims=True) + 1e-06)
    scaled = gain * grad
    mixed = jnp.mean(values * scaled, axis=-1, keepdims=True)
    grad_values = inverse * scaled - values * (inverse * inverse * inverse * mixed)
    return grad_values, jnp.sum(values * inverse * grad, axis=0)


def gelu_product(gate_part, up_part):
    return jax.nn.gelu(gate_part, approximate=True) * up_part


def near_hot():
    shape = (REACH, 3 * HALF * HALF)
    spot = lax.broadcasted_iota(jnp.int32, shape, 1)
    gap = spot // (HALF * HALF)
    key = (spot // HALF) % HALF
    row = spot % HALF
    distance = jnp.clip(HALF * gap + row - key, 0, REACH - 1)
    return (distance == lax.broadcasted_iota(jnp.int32, shape, 0)).astype(BF)


def bias_tiles(bias_rows):
    near = matmul(bias_rows.astype(BF), near_hot()).reshape(HEADS, 3, HALF, HALF)
    key = jnp.arange(HALF, dtype=jnp.int32)[:, None]
    row = jnp.arange(HALF, dtype=jnp.int32)[None, :]
    barred = (jnp.arange(3) == 0)[None, :, None, None] & (key > row)[None, None]
    near = jnp.where(barred, -1e30, near)
    far = jnp.broadcast_to(bias_rows[:, -1][:, None, None, None], (HEADS, 1, HALF, HALF))
    none = jnp.full((HEADS, 1, HALF, HALF), -1e30, F32)
    tiles = jnp.concatenate([near, far, none], axis=1)
    return jnp.concatenate([tiles, tiles], axis=-1)


def bias_sums(strips):
    tiles = (strips[..., :HALF] + strips[..., HALF:]).reshape(HEADS, -1)
    high = tiles.astype(BF)
    low = (tiles - high.astype(F32)).astype(BF)
    hot = near_hot()
    sums = transposed_right(high, hot) + transposed_right(low, hot)
    far = -jnp.sum(sums[:, :-1], axis=1, keepdims=True)
    return jnp.concatenate([sums[:, :-1], far], axis=1)


def body(
    decoder_in,
    encoder_states,
    out_grad,
    block_pairs,
    bucket_table,
    gain_self,
    self_query,
    self_key,
    self_value,
    self_out,
    position_bias,
    gain_cross,
    cross_query,
    cross_key,
    cross_value,
    cross_out,
    gain_feed,
    feed_gate,
    feed_up,
    feed_down,
):
    me = lax.axis_index("ctx")
    rows = self_query.shape[0]
    small = jnp.concatenate(
        [
            jnp.pad(jnp.stack([gain_self, gain_cross, gain_feed]), ((0, 0), (0, 128 - rows))),
            jnp.pad(position_bias, ((0, 9), (0, 128 - HEADS))),
        ],
        axis=0,
    )
    kv_one, kv_two, square, gate_up, down, small, normed_one, queries, self_kv, cross_kv = front(
        [
            self_key, self_value, cross_key, cross_value,
            self_query, self_out, cross_query, cross_out,
            feed_gate, feed_up, feed_down,
        ],
        small,
        decoder_in[0],
        encoder_states[0],
        0,
    )
    kv_one = kv_one.reshape(D, 2 * D)
    kv_two = kv_two.reshape(D, 2 * D)
    square = square.reshape(D, 4 * D)
    gate_up = gate_up.reshape(D, 2 * FF)
    down = down.reshape(FF, D)
    query_one, out_one, query_two, out_two = (square[:, k * D : k * D + D] for k in range(4))
    gains = jnp.transpose(small[:, :3, :rows], (1, 0, 2)).reshape(3, D).astype(F32)
    norm_one, norm_two, norm_three = gains[0:1], gains[1:2], gains[2:3]
    table = small[:, 3:7, :HEADS].reshape(32, HEADS)

    bucket_hot = (bucket_table[:, None] == jnp.arange(32, dtype=jnp.int32)[None, :]).astype(BF)
    bias_rows = transposed_right(table.T, bucket_hot)
    tiles = bias_tiles(bias_rows)
    pair = block_pairs[me]
    query_blocks = jnp.stack([pair, 31 - pair])
    key_blocks = jnp.stack([block_pairs, 31 - block_pairs], axis=1).reshape(-1)
    gaps = query_blocks[:, None] - key_blocks[None, :]
    classes = jnp.where(gaps < 0, 4, jnp.minimum(gaps, 3)).astype(jnp.int32)
    wanted = query_blocks[:, None] - jnp.arange(3, dtype=jnp.int32)[None, :]
    near = jnp.max(
        jnp.where(
            wanted[:, :, None] == key_blocks[None, None, :],
            jnp.arange(32, dtype=jnp.int32)[None, None, :],
            -1,
        ),
        axis=-1,
    )

    tokens = decoder_in[0].astype(F32)
    states = encoder_states[0]
    upstream = out_grad[0]
    attended, self_totals = attend(queries, self_kv, TOK, 0, classes, tiles)
    mid_one = tokens + matmul(attended, out_one)
    normed_two = rms_scaled(mid_one, norm_two)
    cross_queries = matmul(normed_two, query_two).astype(BF)
    cross_attended, cross_totals = attend(cross_queries, cross_kv, ENC, 0)
    mid_two = mid_one + matmul(cross_attended, out_two)
    normed_three = rms_scaled(mid_two, norm_three)
    gate_up_values = matmul(normed_three, gate_up).astype(BF).astype(F32)
    gate_values, up_values = gate_up_values[:, :FF], gate_up_values[:, FF:]
    hidden, pull_feed = jax.vjp(gelu_product, gate_values, up_values)
    hidden = hidden.astype(BF)
    block_out = mid_two + matmul(hidden, down)

    d_hidden = transposed_right(upstream, down)
    d_gate_up = jnp.concatenate(pull_feed(d_hidden), axis=1).astype(BF)
    grad_down = transposed_left(hidden, upstream).astype(BF)
    grad_gate_up = transposed_left(normed_three, d_gate_up).astype(BF)
    d_normed_three = transposed_right(d_gate_up, gate_up)
    part_three, grad_norm_three = rms_back(mid_two, norm_three, d_normed_three)
    d_mid_two = upstream.astype(F32) + part_three
    cross_branch = d_mid_two.astype(BF)
    d_cross_attended = transposed_right(cross_branch, out_two).astype(BF)
    d_cross_queries, d_cross_kv_all = attend_back(
        cross_queries, cross_kv, d_cross_attended, cross_totals, ENC, 0
    )
    grad_out_two = transposed_left(cross_attended, cross_branch).astype(BF)
    grad_query_two = transposed_left(normed_two, d_cross_queries).astype(BF)
    d_normed_two = transposed_right(d_cross_queries, query_two)
    part_two, grad_norm_two = rms_back(mid_one, norm_two, d_normed_two)
    d_mid_one = d_mid_two + part_two
    self_branch = d_mid_one.astype(BF)
    d_attended = transposed_right(self_branch, out_one).astype(BF)
    d_queries, d_kv_all, strips = attend_back(
        queries, self_kv, d_attended, self_totals, TOK, 0, classes, near, tiles
    )
    grad_table = matmul(bias_sums(strips), bucket_hot.astype(F32)).T.reshape(8, 4, HEADS)
    grad_extra = jnp.concatenate(
        [
            jnp.zeros((D, 1), F32),
            grad_norm_two[:, None],
            grad_norm_three[:, None],
            jnp.zeros((D, 5), F32),
            jnp.pad(grad_table, ((0, 0), (0, rows - 4), (0, 0))).reshape(D, HEADS),
            jnp.zeros((D, 236), F32),
        ],
        axis=1,
    )
    grad_out_one = transposed_left(attended, self_branch).astype(BF)
    grad_query_one = transposed_left(normed_one, d_queries).astype(BF)
    summed, grad_decoder, grad_encoder = finish(
        [
            d_cross_kv_all.reshape(8, 2, 2, ENC, D),
            d_kv_all.reshape(8, 2, 2, TOK, D),
            grad_gate_up.reshape(8, rows, -1),
            grad_out_two.reshape(8, rows, D),
            grad_query_two.reshape(8, rows, D),
            grad_out_one.reshape(8, rows, D),
            grad_query_one.reshape(8, rows, D),
            grad_down.reshape(8, -1, D),
        ],
        [
            normed_one.T.reshape(8, rows, TOK),
            states.T.reshape(8, rows, ENC),
            kv_one,
            kv_two,
            transposed_right(d_queries, query_one),
            d_mid_one,
            decoder_in[0],
            norm_one,
            grad_extra.astype(BF).reshape(8, rows, 256),
        ],
        3,
    )
    owned = summed[:, :, :D].astype(F32)
    wide = summed[:, :, D : D + 512].astype(F32)
    wide = jnp.transpose(wide, (1, 0, 2)).reshape(rows, 2 * FF)
    tall = summed[:, :, D + 512 : D + 768].astype(F32).reshape(8, 2, 3, 16, 256)
    tall = jnp.transpose(tall, (1, 0, 3, 2, 4)).reshape(256, D)
    extras = summed[0, :, D + 768 :].astype(F32)
    return (
        block_out[None],
        grad_decoder[None],
        grad_encoder[None],
        extras[:, 0],
        owned[3],
        owned[6],
        owned[7],
        owned[2],
        extras[:4, 8:20],
        extras[:, 1],
        owned[1],
        owned[4],
        owned[5],
        owned[0],
        extras[:, 2],
        wide[:, :FF],
        wide[:, FF:],
        tall,
    )


def solution(mesh):
    tokens = P("fsdp", "ctx", None)
    matrix = P("fsdp", None)
    vector = P("fsdp")
    weights = (
        (vector,) + (matrix,) * 5 + (vector,) + (matrix,) * 4 + (vector,) + (matrix,) * 3
    )
    return jax.shard_map(
        body,
        mesh=mesh,
        in_specs=(tokens,) * 3 + (P(), P()) + weights,
        out_specs=(tokens,) * 3 + weights,
        check_vma=False,
    )
```

```python
import functools

import jax
import jax.numpy as jnp
from jax import lax
from jax.experimental import pallas as pl
from jax.experimental.pallas import tpu as pltpu
from jax.sharding import PartitionSpec as P

D = 768
FF = 2048
HEADS = 12
HEAD_DIM = 64
PAIRS = HEADS // 2
N_CTX = 16
TOK = 128
ENC = 64
HALF = 64
REACH = 128
BF = jnp.bfloat16
F32 = jnp.float32
MIB = 1024 * 1024


def ctx_place():
    me = lax.axis_index("ctx")
    core = me % 2
    high = (me // 2) % 2
    y = me // 4
    return me, core, high, y


def slot_of(y, shift, high, core):
    return ((y + shift) % 4) * 4 + 2 * high + core


def torus_place():
    me, core, high, y = ctx_place()
    shard = lax.axis_index("fsdp")
    return me, core, high, y, shard // 4, shard % 4


def hop(src, dst, send_sem, recv_sem, ctx, fsdp):
    return pltpu.make_async_remote_copy(
        src_ref=src,
        dst_ref=dst,
        send_sem=send_sem,
        recv_sem=recv_sem,
        device_id={"ctx": ctx, "fsdp": fsdp},
    )


def greet_all(devices):
    barrier = pltpu.get_barrier_semaphore()
    for ctx, fsdp in devices:
        pl.semaphore_signal(barrier, inc=1, device_id={"ctx": ctx, "fsdp": fsdp})
    pl.semaphore_wait(barrier, len(devices))


PACKS = ((0, 1), (2, 3), (4, 5, 6, 7), (8, 9), (10,))


def front_kernel(*refs):
    sources = refs[:11]
    small_ref, token_ref, state_ref = refs[11:14]
    targets = refs[14:19]
    small_out, normed_out, query_out, self_out_ref, cross_out_ref = refs[19:24]
    (
        landing, weight_ref, self_ref, cross_ref, send_sem, x_sem, z_sem, core_sem, fill_sem,
        small_sem, self_sem, cross_sem, local_sem,
    ) = refs[24:]
    me, core, high, y, low, x = torus_place()
    shard = low * 4 + x
    sibling = (slot_of(y, 0, high, 1 - core), shard)
    inside = (me, (1 - low) * 4 + x)
    outside = (slot_of(y, 0, 1 - high, core), (1 - low) * 4 + x)
    across = slot_of(y, 0, 1 - high, core)
    rows = [slot_of(y, shift, high, core) for shift in (1, 2, 3)]
    others = [low * 4 + (x + shift) % 4 for shift in (1, 2, 3)]
    peers = [(shard + shift) % 8 for shift in range(1, 8)]
    greet_all(
        [sibling, outside, (across, shard)]
        + [(me, peer) for peer in peers]
        + [(row, shard) for row in rows]
    )
    sends = []

    def send(src, dst, recv_sem, device):
        copy = hop(src, dst, send_sem.at[len(sends)], recv_sem, *device)
        copy.start()
        sends.append(copy)

    def arrived(ref, recv_sem):
        hop(ref, ref, send_sem.at[0], recv_sem, *sibling).wait_recv()

    def bring(src, dst, sem):
        copy = pltpu.make_async_copy(src, dst, sem)
        copy.start()
        return copy


    def part(k, owner, whose, side=None):
        ref = targets[k]
        count = ref.shape[1] // 2
        start = pl.multiple_of(whose * count, 16)
        if side is None:
            return ref.at[owner, pl.ds(start, count), :]
        width = ref.shape[2] // 2
        return ref.at[owner, pl.ds(start, count), pl.ds(side * width, width)]

    def fill(k):
        copies = []
        start = 0
        for source in PACKS[k]:
            width = sources[source].shape[1]
            copies.append(
                bring(
                    sources[source],
                    targets[k].at[shard, :, pl.ds(start, width)],
                    fill_sem.at[source],
                )
            )
            start += width
        return copies

    def send_own(k):
        for copy in fills[k]:
            copy.wait()
        for spot in (1, 0, 2):
            block = part(k, shard, core)
            send(block, block, x_sem.at[k, spot], (me, others[spot]))
        for side, device in enumerate((inside, outside)):
            piece = part(k, shard, core, side)
            send(piece, piece, z_sem.at[k, 3, side], device)


    def pass_x(k):
        for spot in (0, 2, 1):
            owner = low * 4 + (x + 3 - spot) % 4
            block = part(k, owner, core)
            arrived(block, x_sem.at[k, spot])
            for side, device in enumerate((inside, outside)):
                piece = part(k, owner, core, side)
                send(piece, piece, z_sem.at[k, spot, side], device)
            send(block, block, core_sem.at[k, spot], sibling)

    def pass_z(k):
        for spot in (3, 0, 2, 1):
            owner = (1 - low) * 4 + (x + 3 - spot) % 4
            for side in range(2):
                piece = part(k, owner, core, side)
                arrived(piece, z_sem.at[k, spot, side])
                send(piece, piece, core_sem.at[k, 3 + 2 * spot + side], sibling)

    def complete(k):
        for spot in range(3):
            owner = low * 4 + (x + 3 - spot) % 4
            arrived(part(k, owner, 1 - core), core_sem.at[k, spot])
        for spot in range(4):
            owner = (1 - low) * 4 + (x + 3 - spot) % 4
            for side in range(2):
                arrived(part(k, owner, 1 - core, side), core_sem.at[k, 3 + 2 * spot + side])


    def kv_start(src, out, sems):
        send(src, out.at[me], sems.at[me], (across, shard))
        for row in rows:
            send(src, out.at[me], sems.at[me], (row, shard))
        send(src, out.at[me], sems.at[me], sibling)

    def kv_across(out, sems):
        block = out.at[across]
        arrived(block, sems.at[across])
        for row in rows:
            send(block, block, sems.at[across], (row, shard))
        send(block, block, sems.at[across], sibling)

    def kv_rows(out, sems, flip):
        for shift in (1, 3, 2):
            slot = slot_of(y, shift, 1 - high if flip else high, core)
            block = out.at[slot]
            arrived(block, sems.at[slot])
            send(block, block, sems.at[slot], sibling)

    def kv_complete(out, sems):
        for shift in range(4):
            for half in range(2):
                slot = slot_of(y, shift, half, 1 - core)
                arrived(out.at[slot], sems.at[slot])

    fills = [fill(k) for k in range(5)]
    own_small = bring(small_ref, landing.at[shard], local_sem.at[0])
    for spot, peer in enumerate(peers):
        send(small_ref, landing.at[shard], small_sem.at[spot], (me, peer))
    send_own(0)
    send_own(1)
    own_small.wait()
    for spot in range(7):
        arrived(landing.at[(shard + 7 - spot) % 8], small_sem.at[spot])
    small = landing[...]
    small_out[...] = small
    gains = small.astype(F32)
    gain = jnp.concatenate([gains[owner, 0:1, :96] for owner in range(8)], axis=1)
    normed = rms_scaled(token_ref[...].astype(F32), gain)
    normed_out[...] = normed
    pass_x(0)
    send_own(2)
    pass_z(0)
    pass_x(1)
    send_own(3)
    complete(0)
    bring(targets[0], weight_ref, local_sem.at[1]).wait()
    for half in range(2):
        weight = weight_ref[:, :, half * D : half * D + D].reshape(D, D)
        self_ref[half] = matmul(normed, weight).astype(BF)
    kv_start(self_ref, self_out_ref, self_sem)
    own_self = bring(self_ref, self_out_ref.at[me], local_sem.at[2])
    pass_z(1)
    complete(1)
    bring(targets[1], weight_ref, local_sem.at[1]).wait()
    for half in range(2):
        weight = weight_ref[:, :, half * D : half * D + D].reshape(D, D)
        cross_ref[half] = matmul(state_ref[...], weight).astype(BF)
    kv_start(cross_ref, cross_out_ref, cross_sem)
    own_cross = bring(cross_ref, cross_out_ref.at[me], local_sem.at[3])
    pass_x(2)
    send_own(4)
    kv_across(self_out_ref, self_sem)
    pass_z(2)
    kv_across(cross_out_ref, cross_sem)
    pass_x(3)
    kv_rows(self_out_ref, self_sem, False)
    pass_z(3)
    pass_x(4)
    kv_rows(self_out_ref, self_sem, True)
    kv_rows(cross_out_ref, cross_sem, False)
    pass_z(4)
    kv_rows(cross_out_ref, cross_sem, True)
    complete(2)
    bring(targets[2].at[:, :, pl.ds(0, D)], weight_ref.at[:, :, pl.ds(0, D)], local_sem.at[1]).wait()
    query_out[...] = matmul(normed, weight_ref[:, :, :D].reshape(D, D)).astype(BF)
    complete(3)
    complete(4)
    kv_complete(self_out_ref, self_sem)
    kv_complete(cross_out_ref, cross_sem)
    own_self.wait()
    own_cross.wait()
    for copy in sends:
        copy.wait_send()


def front(weights, small, tokens, states, collective_id):
    dma = pltpu.SemaphoreType.DMA
    packs = [
        (8, weights[group[0]].shape[0], sum(weights[k].shape[1] for k in group)) for group in PACKS
    ]
    anywhere = pl.BlockSpec(memory_space=pl.ANY)
    inside = pl.BlockSpec(memory_space=pltpu.VMEM)
    return pl.pallas_call(
        front_kernel,
        out_shape=[jax.ShapeDtypeStruct(pack, BF) for pack in packs]
        + [
            jax.ShapeDtypeStruct((8, 16, 128), BF),
            jax.ShapeDtypeStruct((TOK, D), BF),
            jax.ShapeDtypeStruct((TOK, D), BF),
            jax.ShapeDtypeStruct((N_CTX, 2, TOK, D), BF),
            jax.ShapeDtypeStruct((N_CTX, 2, ENC, D), BF),
        ],
        in_specs=[anywhere] * 12 + [inside] * 2,
        out_specs=[anywhere] * 5 + [inside] * 3 + [anywhere] * 2,
        scratch_shapes=[
            pltpu.VMEM((8, 16, 128), BF),
            pltpu.VMEM((8, 96, 2 * D), BF),
            pltpu.VMEM((2, TOK, D), BF),
            pltpu.VMEM((2, ENC, D), BF),
            dma((5 * 22 + 7 + 30,)),
            dma((5, 3)),
            dma((5, 4, 2)),
            dma((5, 11)),
            dma((11,)),
            dma((7,)),
            dma((N_CTX,)),
            dma((N_CTX,)),
            dma((4,)),
        ],
        compiler_params=pltpu.CompilerParams(
            collective_id=collective_id, has_side_effects=True, vmem_limit_bytes=60 * MIB
        ),
        name="front",
    )(*weights, small, tokens, states)


PIECE = 96
ROOM = D // 2 + FF // 8 + FF // 16
WIDTHS = (FF, D // 2, D // 2, D // 2, D // 2, D, D)
SPAN = sum(WIDTHS)
DOWN = len(WIDTHS)
CHUNKS = DOWN + 1
CROSS_KV, SELF_KV = 5, 6
LEFT = (D, FF, D, D, D, D)
RIGHT = (FF, D // 2, D // 2, D // 2, D // 2, D // 2)


def finish_kernel(*refs):
    lefts = refs[:6]
    rights = refs[6:12]
    dkv_ref, dckv_ref = refs[12:14]
    state_ref, kv_ref, ckv_ref, dn_ref, dmid_ref, token_ref, gain_ref, small_ref = refs[14:22]
    decoder_ref, encoder_ref = refs[22:24]
    square_refs = refs[24:32]
    gate_ref, up_ref, down_ref, small_out = refs[32:36]
    (
        left_all, right_all, turned, turned_one, turned_state, state_all, s_right, c_right,
        kept, from_z, from_x, d_kept, d_z, d_x,
        s_kept, s_core, s_row, s_via, s_stage, s_high, s_fin,
        c_kept, c_core, c_row, c_via, c_stage, c_high, c_fin,
        small_f32, sm_own, sm_core, sm_z, sm_x, sm_ctx, sm_total, packed, from_ctx, land,
        s_sem, c_sem, fill_sem, act_send, act_recv, late_send, late_recv, z_send, z_recv,
        x_send, x_recv, ctx_send, ctx_recv, out_send, out_recv, pass_send, pass_recv,
        sm_send, sm_recv, local_sem,
    ) = refs[36:]
    me, core, high, y, low, x = torus_place()
    shard = low * 4 + x
    rank = y * 2 + high
    sibling = (slot_of(y, 0, high, 1 - core), shard)
    inside = (me, (1 - low) * 4 + x)
    outside = (slot_of(y, 0, 1 - high, core), (1 - low) * 4 + x)
    across = (slot_of(y, 0, 1 - high, core), shard)
    others = [low * 4 + (x + shift) % 4 for shift in (1, 2, 3)]
    ahead = (slot_of(y, 1, high, core), shard)
    behind = (slot_of(y, 3, high, core), shard)
    shifts = [(dy, dz) for dy in range(4) for dz in range(2)][1:]
    mates = [((y + dy) % 4) * 2 + (high + dz) % 2 for dy, dz in shifts]
    greet_all(
        [sibling, inside, outside]
        + [(me, other) for other in others]
        + [(mate * 2 + core, shard) for mate in mates]
    )
    sends = []

    def go(src, dst, send_sem, recv_sem, device):
        copy = hop(src, dst, send_sem, recv_sem, *device)
        copy.start()
        sends.append(copy)
        return copy

    def bring(src, dst, sem):
        copy = pltpu.make_async_copy(src, dst, sem)
        copy.start()
        return copy


    def rows_start(source, held, arrived, sem):
        over = []
        local = []
        for spot, shift in enumerate((2, 1, 3, 0)):
            pair = pl.ds(((y + shift) % 4) * 2, 2)
            block = pl.ds(2 * spot, 2)
            over.append(
                go(
                    source.at[pair, 1 - core], arrived.at[block],
                    sem.at[0, spot], sem.at[1, spot], sibling,
                )
            )
            local.append(bring(source.at[pair, core], held.at[block], sem.at[4, spot]))
        return over, local


    def rows_send(copies, held, arrived, via, row, sem):
        over, local = copies
        onward = []
        for spot in range(4):
            local[spot].wait()
            over[spot].wait_recv()
            for block in (2 * spot, 2 * spot + 1):
                for part in range(2):
                    held[block, part] = held[block, part] + arrived[block, part]
            if spot == 0:
                first = go(held.at[0], via.at[0], sem.at[2, 0], sem.at[3, 0], ahead)
                second = go(held.at[1], via.at[1], sem.at[2, 1], sem.at[3, 1], behind)
            elif spot == 1:
                onward.append(go(held.at[3], row.at[0, 1], sem.at[2, 2], sem.at[3, 2], ahead))
            elif spot == 2:
                onward.append(go(held.at[4], row.at[1, 0], sem.at[2, 3], sem.at[3, 3], behind))
        return first, second, onward

    def rows_via(state, held, via, row, sem):
        first, second, onward = state
        first.wait_recv()
        for part in range(2):
            held[2, part] = held[2, part] + via[0, part]
        onward.append(go(held.at[2], row.at[0, 0], sem.at[2, 4], sem.at[3, 4], ahead))
        second.wait_recv()
        for part in range(2):
            held[5, part] = held[5, part] + via[1, part]
        onward.append(go(held.at[5], row.at[1, 1], sem.at[2, 5], sem.at[3, 5], behind))
        return onward

    def rows_total(held, row, half, part):
        return (
            held[6 + half, part].astype(F32)
            + row[0, half, part].astype(F32)
            + row[1, half, part].astype(F32)
        )

    def rows_across(onward, held, row, stage, landing, sem):
        for copy in onward:
            copy.wait_recv()
        for part in range(2):
            stage[part] = rows_total(held, row, 1 - high, part).astype(BF)
        return go(stage, landing, sem.at[2, 6], sem.at[3, 6], across)

    def rows_sum(last, held, row, landing, final, right, which):
        totals = [rows_total(held, row, high, part) for part in range(2)]
        last.wait_recv()
        for part in range(2):
            final[part] = (totals[part] + landing[part].astype(F32)).astype(BF)
        count = final.shape[1]
        copy = go(
            final.at[1 - core], right.at[pl.ds(count, count)],
            late_send.at[which], late_recv.at[which], sibling,
        )
        right[:count] = final[core]
        return copy


    starts = [sum(WIDTHS[:k]) for k in range(len(WIDTHS))]
    left_starts = [sum(LEFT[:k]) for k in range(6)]
    right_starts = [sum(RIGHT[:k]) for k in range(6)]
    acts = {}
    over_z, over_x = {}, {}

    def buffers(k):
        if k == DOWN:
            return d_kept, d_z, d_x, pl.ds(0, D // 2)
        return kept, from_z, from_x, pl.ds(starts[k], WIDTHS[k])

    def acts_start(index):
        left = pl.ds(left_starts[index], LEFT[index])
        right = pl.ds(right_starts[index], RIGHT[index])
        near = pl.ds(pl.multiple_of(core * RIGHT[index], 128), RIGHT[index])
        far = pl.ds(pl.multiple_of((1 - core) * RIGHT[index], 128), RIGHT[index])
        mine = pl.ds(0, TOK)
        theirs = pl.ds(TOK, TOK)
        acts[index] = (
            bring(lefts[index], left_all.at[mine, left], fill_sem.at[index, 0]),
            bring(rights[index].at[:, near], right_all.at[mine, right], fill_sem.at[index, 1]),
            go(
                lefts[index], left_all.at[theirs, left],
                act_send.at[index, 0], act_recv.at[index, 0], sibling,
            ),
            go(
                rights[index].at[:, far], right_all.at[theirs, right],
                act_send.at[index, 1], act_recv.at[index, 1], sibling,
            ),
        )

    def multiply(k, left_ref, right):
        held, landing, _, cut = buffers(k)
        for column in range(8):
            owner = (4 * (1 - low) + column) % 8
            held[owner, :, cut] = contract(left_ref[owner], right, ((1,), (0,))).astype(BF)
            if column == 3:
                half = held.shape[1] // 2
                away = pl.ds(4 * (1 - low), 4)
                over_z[k] = [
                    go(
                        held.at[away, pl.ds(side * half, half), cut],
                        landing.at[:, pl.ds(side * half, half), cut],
                        z_send.at[k, side],
                        z_recv.at[k, side],
                        device,
                    )
                    for side, device in enumerate((inside, outside))
                ]

    def make(index, k):
        near_left, near_right, far_left, far_right = acts[index]
        near_left.wait()
        near_right.wait()
        far_left.wait_recv()
        far_right.wait_recv()
        left = left_all[:, left_starts[index] : left_starts[index] + LEFT[index]].T
        right = right_all[:, right_starts[index] : right_starts[index] + RIGHT[index]]
        target = turned_one if index == 5 else turned
        rows = LEFT[index] // 8
        target[:, :rows, :] = left.reshape(8, rows, 2 * TOK)
        multiply(k, target.at[:, pl.ds(0, rows), :], right)

    def step_z(k):
        held, landing, spread, cut = buffers(k)
        for copy in over_z[k]:
            copy.wait_recv()
        for column in range(4):
            landing[column, :, cut] = landing[column, :, cut] + held[4 * low + column, :, cut]
        over_x[k] = [
            go(
                landing.at[(x + spot + 1) % 4, :, cut],
                spread.at[spot, :, cut],
                x_send.at[k, spot],
                x_recv.at[k, spot],
                (me, others[spot]),
            )
            for spot in (1, 0, 2)
        ]

    def step_x(k):
        _, landing, spread, cut = buffers(k)
        for copy in over_x[k]:
            copy.wait_recv()
        total = landing[x, :, cut].astype(F32)
        for spot in range(3):
            total = total + spread[spot, :, cut].astype(F32)
        total = total.astype(BF)
        half = D // 2
        if k == 0:
            for piece in range(8):
                packed[piece, :, half : half + 256] = total[:, piece * 256 : piece * 256 + 256]
        elif k == DOWN:
            for piece in range(8):
                for part in range(3):
                    packed[piece, part * 32 : part * 32 + 32, half + 256 :] = total[
                        piece * 32 : piece * 32 + 32, part * 128 : part * 128 + 128
                    ]
        elif k == CROSS_KV or k == SELF_KV:
            for piece in range(2):
                packed[(4 if k == CROSS_KV else 6) + piece, :, :half] = total[
                    :, piece * half : piece * half + half
                ]
        else:
            packed[k - 1, :, :half] = total

    s_copies = rows_start(dkv_ref, s_kept, s_core, s_sem)
    c_copies = rows_start(dckv_ref, c_kept, c_core, c_sem)
    for index in range(6):
        acts_start(index)
    state_near = bring(state_ref, state_all.at[pl.ds(0, ENC)], local_sem.at[0])
    state_far = go(
        state_ref, state_all.at[pl.ds(ENC, ENC)], late_send.at[2], late_recv.at[2], sibling
    )
    s_state = rows_send(s_copies, s_kept, s_core, s_via, s_row, s_sem)
    c_state = rows_send(c_copies, c_kept, c_core, c_via, c_row, c_sem)
    make(0, 0)
    s_onward = rows_via(s_state, s_kept, s_via, s_row, s_sem)
    make(1, DOWN)
    c_onward = rows_via(c_state, c_kept, c_via, c_row, c_sem)
    for index in (2, 3, 4, 5):
        make(index, index - 1)
    step_z(0)
    step_z(DOWN)
    s_last = rows_across(s_onward, s_kept, s_row, s_stage, s_high, s_sem)
    for k in (1, 2, 3, 4):
        step_z(k)
    state_near.wait()
    state_far.wait_recv()
    turned_state[...] = state_all[...].T.reshape(8, PIECE, 2 * ENC)
    s_far = rows_sum(s_last, s_kept, s_row, s_high, s_fin, s_right, 0)
    step_x(0)
    s_far.wait_recv()
    multiply(SELF_KV, turned_one, s_right[...])
    c_last = rows_across(c_onward, c_kept, c_row, c_stage, c_high, c_sem)
    tokens = token_ref[...].astype(F32)
    d_kv = jnp.concatenate([s_fin[0], s_fin[1]], axis=1)
    grad = dn_ref[...] + contract(d_kv, kv_ref[...], ((1,), (1,)))
    inverse = lax.rsqrt(jnp.mean(tokens * tokens, axis=-1, keepdims=True) + 1e-06)
    small_f32[...] = small_ref[...]
    line = jnp.sum(tokens * inverse * grad, axis=0, keepdims=True)
    for owner in range(8):
        small_f32[owner, 0:1, :96] = line[:, owner * 96 : owner * 96 + 96]
    sm_own[...] = small_f32[...].astype(BF)
    sm_over = go(sm_own, sm_core, sm_send.at[0], sm_recv.at[0], sibling)
    c_far = rows_sum(c_last, c_kept, c_row, c_high, c_fin, c_right, 1)
    step_x(DOWN)
    c_far.wait_recv()
    multiply(CROSS_KV, turned_state, c_right[...])
    step_z(SELF_KV)
    sm_over.wait_recv()
    sm_own_sum = (sm_own[...].astype(F32) + sm_core[...].astype(F32)).astype(BF)
    sm_over.wait_send()
    sm_own[...] = sm_own_sum
    sm_inside = go(
        sm_own.at[pl.ds(4 * (1 - low), 4)], sm_z, sm_send.at[1], sm_recv.at[1], inside
    )
    for k in (1, 2, 3, 4):
        step_x(k)
    step_z(CROSS_KV)
    sm_inside.wait_recv()
    for column in range(4):
        sm_z[column] = sm_z[column] + sm_own[4 * low + column]
    sm_row = [
        go(
            sm_z.at[(x + spot + 1) % 4], sm_x.at[spot],
            sm_send.at[2 + spot], sm_recv.at[2 + spot], (me, others[spot]),
        )
        for spot in range(3)
    ]
    scaled = gain_ref[...] * grad
    mixed = jnp.mean(tokens * scaled, axis=-1, keepdims=True)
    decoder_ref[...] = (
        dmid_ref[...] + inverse * scaled - tokens * (inverse * inverse * inverse * mixed)
    )
    d_ckv = jnp.concatenate([c_fin[0], c_fin[1]], axis=1)
    encoder_ref[...] = contract(d_ckv, ckv_ref[...], ((1,), (1,)))
    step_x(SELF_KV)
    step_x(CROSS_KV)


    over_ctx = [
        go(
            packed.at[mate],
            from_ctx.at[spot],
            ctx_send.at[spot],
            ctx_recv.at[spot],
            (mate * 2 + core, shard),
        )
        for spot, mate in enumerate(mates)
    ]
    sm_sum = sm_z[x].astype(F32)
    for spot in range(3):
        sm_row[spot].wait_recv()
        sm_sum = sm_sum + sm_x[spot].astype(F32)
    sm_total[...] = sm_sum.astype(BF)
    sm_mates = [
        go(
            sm_total, sm_ctx.at[spot],
            sm_send.at[5 + spot], sm_recv.at[5 + spot], (mate * 2 + core, shard),
        )
        for spot, mate in enumerate(mates)
    ]
    total = packed[rank].astype(F32)
    for spot in range(7):
        over_ctx[spot].wait_recv()
        total = total + from_ctx[spot].astype(F32)
    land[rank, core] = total.astype(BF)
    own = land.at[rank, core]
    for spot, mate in enumerate(mates):
        go(own, own, out_send.at[spot], out_recv.at[rank], (mate * 2 + core, shard))
    go(own, own, pass_send.at[7], pass_recv.at[rank], sibling)

    def landed(ref, recv_sem):
        hop(ref, ref, pass_send.at[0], recv_sem, *sibling).wait_recv()

    sm_sum = sm_total[...].astype(F32)
    for spot in range(7):
        sm_mates[spot].wait_recv()
        sm_sum = sm_sum + sm_ctx[spot].astype(F32)
    small_out[...] = sm_sum
    for spot, mate in enumerate(mates):
        block = land.at[mate, core]
        landed(block, out_recv.at[mate])
        go(block, block, pass_send.at[spot], pass_recv.at[mate], sibling)
    for mate in [rank] + mates:
        landed(land.at[mate, 1 - core], pass_recv.at[mate])
    half = D // 2
    for side in range(2):
        for piece in range(4):
            square_refs[piece][:, side * half : side * half + half] = land[
                piece, side, :, :half
            ].astype(F32)
            square_refs[4 + 2 * (piece // 2) + side][
                :, (piece % 2) * half : (piece % 2) * half + half
            ] = land[4 + piece, side, :, :half].astype(F32)
        target = up_ref if side else gate_ref
        for piece in range(8):
            target[:, piece * 256 : piece * 256 + 256] = land[
                piece, side, :, half : half + 256
            ].astype(F32)
            for part in range(3):
                down_ref[
                    piece * 32 : piece * 32 + 32,
                    side * half + part * 128 : side * half + part * 128 + 128,
                ] = land[piece, side, part * 32 : part * 32 + 32, half + 256 :].astype(F32)
    for copy in sends:
        if copy is not sm_over:
            copy.wait_send()


def finish(far, near, collective_id):
    dma = pltpu.SemaphoreType.DMA

    def rows(count):
        return [
            pltpu.VMEM((8, 2, count, D), BF),
            pltpu.VMEM((8, 2, count, D), BF),
            pltpu.VMEM((2, 2, 2, count, D), BF),
            pltpu.VMEM((2, 2, count, D), BF),
            pltpu.VMEM((2, count, D), BF),
            pltpu.VMEM((2, count, D), BF),
            pltpu.VMEM((2, count, D), BF),
        ]

    outs = (
        [jax.ShapeDtypeStruct((TOK, D), F32), jax.ShapeDtypeStruct((ENC, D), F32)]
        + [jax.ShapeDtypeStruct((PIECE, D), F32)] * 8
        + [jax.ShapeDtypeStruct((PIECE, FF), F32)] * 2
        + [jax.ShapeDtypeStruct((FF // 8, D), F32), jax.ShapeDtypeStruct((16, 128), F32)]
    )
    return pl.pallas_call(
        finish_kernel,
        out_shape=outs,
        in_specs=[pl.BlockSpec(memory_space=pl.ANY)] * len(far)
        + [pl.BlockSpec(memory_space=pltpu.VMEM)] * len(near),
        out_specs=[pl.BlockSpec(memory_space=pltpu.VMEM)] * len(outs),
        scratch_shapes=[
            pltpu.VMEM((2 * TOK, sum(LEFT)), BF),
            pltpu.VMEM((2 * TOK, sum(RIGHT)), BF),
            pltpu.VMEM((8, FF // 8, 2 * TOK), BF),
            pltpu.VMEM((8, PIECE, 2 * TOK), BF),
            pltpu.VMEM((8, PIECE, 2 * ENC), BF),
            pltpu.VMEM((2 * ENC, D), BF),
            pltpu.VMEM((2 * TOK, D), BF),
            pltpu.VMEM((2 * ENC, D), BF),
            pltpu.VMEM((8, PIECE, SPAN), BF),
            pltpu.VMEM((4, PIECE, SPAN), BF),
            pltpu.VMEM((3, PIECE, SPAN), BF),
            pltpu.VMEM((8, FF // 8, D // 2), BF),
            pltpu.VMEM((4, FF // 8, D // 2), BF),
            pltpu.VMEM((3, FF // 8, D // 2), BF),
        ]
        + rows(TOK)
        + rows(ENC)
        + [
            pltpu.VMEM((8, 16, 128), F32),
            pltpu.VMEM((8, 16, 128), BF),
            pltpu.VMEM((8, 16, 128), BF),
            pltpu.VMEM((4, 16, 128), BF),
            pltpu.VMEM((3, 16, 128), BF),
            pltpu.VMEM((7, 16, 128), BF),
            pltpu.VMEM((16, 128), BF),
            pltpu.VMEM((8, PIECE, ROOM), BF),
            pltpu.VMEM((7, PIECE, ROOM), BF),
            pltpu.VMEM((8, 2, PIECE, ROOM), BF),
            dma((5, 7)),
            dma((5, 7)),
            dma((6, 2)),
            dma((6, 2)),
            dma((6, 2)),
            dma((3,)),
            dma((3,)),
            dma((CHUNKS, 2)),
            dma((CHUNKS, 2)),
            dma((CHUNKS, 3)),
            dma((CHUNKS, 3)),
            dma((7,)),
            dma((7,)),
            dma((7,)),
            dma((8,)),
            dma((8,)),
            dma((8,)),
            dma((12,)),
            dma((12,)),
            dma((1,)),
        ],
        compiler_params=pltpu.CompilerParams(
            collective_id=collective_id, has_side_effects=True, vmem_limit_bytes=62 * MIB
        ),
        name="finish_gradients",
    )(*far, *near)


def split_heads(block):
    lane = lax.broadcasted_iota(jnp.int32, block.shape, 1)
    nothing = jnp.zeros_like(block)
    return jnp.concatenate(
        [jnp.where(lane < HEAD_DIM, block, nothing), jnp.where(lane < HEAD_DIM, nothing, block)],
        axis=0,
    )


def join_heads(transposed):
    row = lax.broadcasted_iota(jnp.int32, (2 * HEAD_DIM, TOK), 0)
    return jnp.where(row < HEAD_DIM, transposed[:, :TOK], transposed[:, TOK:]).T


def contract(left, right, dims):
    return lax.dot_general(left, right, (dims, ((), ())), preferred_element_type=F32)


def key_chunk(ref, j):
    if ref.shape[2] == 2 * HALF:
        return ref[j, 0]
    return ref[pl.ds(2 * j, 2), 0].reshape(2 * HALF, 2 * HEAD_DIM)


def bias_chunk(class_ref, tile_ref, j):
    lane = lax.broadcasted_iota(jnp.int32, (HALF, TOK), 1)
    rows = []
    for half in range(2):
        spot = 2 * j + half
        near = class_ref[0, spot]
        far = class_ref[1, spot]
        rows.append(
            jnp.concatenate(
                [
                    jnp.where(lane < HALF, tile_ref[head, near], tile_ref[head, far])
                    for head in range(2)
                ],
                axis=1,
            )
        )
    return jnp.concatenate(rows, axis=0)


def fold(values, join):
    return join(values.reshape(-1, 8, values.shape[-1]), axis=0)


def forward_kernel(biased, *refs):
    if biased:
        class_ref, q_ref, k_ref, v_ref, tile_ref, out_ref, total_ref, score_ref, share_ref = refs
    else:
        q_ref, k_ref, v_ref, out_ref, total_ref, score_ref, share_ref = refs
    chunks = score_ref.shape[0]
    queries = split_heads(q_ref[...])
    highest = None
    for j in range(chunks):
        scores = contract(key_chunk(k_ref, j), queries, ((1,), (1,)))
        if biased:
            scores = scores + bias_chunk(class_ref, tile_ref, j)
        score_ref[j] = scores
        top = fold(scores, jnp.max)
        highest = top if highest is None else jnp.maximum(highest, top)
    highest = jnp.max(highest, axis=0, keepdims=True)
    summed = jnp.zeros((8, 2 * TOK), F32)
    for j in range(chunks):
        raised = jnp.exp(score_ref[j] - highest)
        summed = summed + fold(raised, jnp.sum)
        share_ref[j] = raised.astype(BF)
    summed = jnp.sum(summed, axis=0, keepdims=True)
    values = jnp.concatenate([key_chunk(v_ref, j) for j in range(chunks)], axis=0)
    mixed = contract(values, share_ref[...].reshape(-1, 2 * TOK), ((0,), (0,)))
    out_ref[...] = join_heads(mixed / summed).astype(BF)
    total_ref[0] = jnp.broadcast_to(highest + jnp.log(summed), (8, 2 * TOK))


def backward_kernel(biased, *refs):
    if biased:
        class_ref, near_ref, q_ref, k_ref, v_ref, g_ref, total_ref, tile_ref = refs[:8]
        dq_ref, dkv_ref, strip_ref, share_ref, slope_ref, share_low, slope_low = refs[8:]
    else:
        q_ref, k_ref, v_ref, g_ref, total_ref = refs[:5]
        dq_ref, dkv_ref, share_ref, slope_ref, share_low, slope_low = refs[5:]
    chunks = share_ref.shape[0]
    queries = split_heads(q_ref[...])
    grads = split_heads(g_ref[...])
    totals = total_ref[0, 0:1]
    inner = jnp.zeros((8, 2 * TOK), F32)
    for j in range(chunks):
        scores = contract(key_chunk(k_ref, j), queries, ((1,), (1,)))
        if biased:
            scores = scores + bias_chunk(class_ref, tile_ref, j)
        shares = jnp.exp(scores - totals)
        slopes = contract(key_chunk(v_ref, j), grads, ((1,), (1,)))
        inner = inner + fold(shares * slopes, jnp.sum)
        share_ref[j] = shares
        slope_ref[j] = slopes
        share_low[j] = shares.astype(BF)
    inner = jnp.sum(inner, axis=0, keepdims=True)
    for j in range(chunks):
        grad = share_ref[j] * (slope_ref[j] - inner)
        if biased:
            slope_ref[j] = grad
        slope_low[j] = grad.astype(BF)
    keys = jnp.concatenate([key_chunk(k_ref, j) for j in range(chunks)], axis=0)
    low = slope_low[...].reshape(-1, 2 * TOK)
    dq_ref[...] = join_heads(contract(keys, low, ((0,), (0,)))).astype(BF)
    shape = dkv_ref.shape
    block = (shape[0], shape[2], shape[3])
    dkv_ref[:, 0] = contract(low, queries, ((1,), (0,))).astype(BF).reshape(block)
    dkv_ref[:, 1] = (
        contract(share_low[...].reshape(-1, 2 * TOK), grads, ((1,), (0,))).astype(BF).reshape(block)
    )
    if biased:
        lane = lax.broadcasted_iota(jnp.int32, (HALF, TOK), 1)
        for gap in range(3):
            pieces = []
            for half in range(2):
                spot = near_ref[half, gap]
                held = slope_ref[jnp.maximum(spot, 0) // 2, pl.ds(
                    pl.multiple_of((jnp.maximum(spot, 0) % 2) * HALF, HALF), HALF)]
                pieces.append(jnp.where(spot >= 0, held, jnp.zeros_like(held)))
            for head in range(2):
                cut = slice(head * TOK, (head + 1) * TOK)
                strip_ref[head, gap] = jnp.where(lane < HALF, pieces[0][:, cut], pieces[1][:, cut])


def pair_columns(pair):
    return (0, pair)


def kv_spec(rows, row_block, part):
    return pl.BlockSpec(
        (N_CTX, 1, rows, 2 * HEAD_DIM), lambda pair: (0, part, row_block, pair)
    )


SMEM_SPEC = pl.BlockSpec(memory_space=pltpu.SMEM)
TILE_SPEC = pl.BlockSpec((2, 5, HALF, TOK), lambda pair: (pair, 0, 0, 0))
TOTAL_SPEC = pl.BlockSpec((1, 8, 2 * TOK), lambda pair: (pair, 0, 0))
ROW_SPEC = pl.BlockSpec((TOK, 2 * HEAD_DIM), pair_columns)
LOCAL = pltpu.CompilerParams(vmem_limit_bytes=48 * MIB)


def attend(queries, gathered, rows, row_block, classes=None, tiles=None):
    biased = classes is not None
    chunks = N_CTX * rows // TOK
    specs = [ROW_SPEC, kv_spec(rows, row_block, 0), kv_spec(rows, row_block, 1)]
    operands = [queries, gathered, gathered]
    if biased:
        specs = [SMEM_SPEC] + specs + [TILE_SPEC]
        operands = [classes] + operands + [tiles]
    return pl.pallas_call(
        functools.partial(forward_kernel, biased),
        grid=(PAIRS,),
        in_specs=specs,
        out_specs=[ROW_SPEC, TOTAL_SPEC],
        out_shape=[
            jax.ShapeDtypeStruct((TOK, D), BF),
            jax.ShapeDtypeStruct((PAIRS, 8, 2 * TOK), F32),
        ],
        scratch_shapes=[
            pltpu.VMEM((chunks, TOK, 2 * TOK), F32),
            pltpu.VMEM((chunks, TOK, 2 * TOK), BF),
        ],
        compiler_params=LOCAL,
        cost_estimate=pl.CostEstimate(flops=10**9, bytes_accessed=10**7, transcendentals=10**6),
        name="attend_self" if biased else "attend_cross",
    )(*operands)


def attend_back(queries, gathered, grads, totals, rows, row_block, classes=None, near=None, tiles=None):
    biased = classes is not None
    chunks = N_CTX * rows // TOK
    specs = [ROW_SPEC, kv_spec(rows, row_block, 0), kv_spec(rows, row_block, 1), ROW_SPEC, TOTAL_SPEC]
    operands = [queries, gathered, gathered, grads, totals]
    out_specs = [
        ROW_SPEC,
        pl.BlockSpec((N_CTX, 2, rows, 2 * HEAD_DIM), lambda pair: (0, 0, 0, pair)),
    ]
    out_shape = [
        jax.ShapeDtypeStruct((TOK, D), BF),
        jax.ShapeDtypeStruct((N_CTX, 2, rows, D), BF),
    ]
    if biased:
        specs = [SMEM_SPEC, SMEM_SPEC] + specs + [TILE_SPEC]
        operands = [classes, near] + operands + [tiles]
        out_specs.append(pl.BlockSpec((2, 3, HALF, TOK), lambda pair: (pair, 0, 0, 0)))
        out_shape.append(jax.ShapeDtypeStruct((HEADS, 3, HALF, TOK), F32))
    return pl.pallas_call(
        functools.partial(backward_kernel, biased),
        grid=(PAIRS,),
        in_specs=specs,
        out_specs=out_specs,
        out_shape=out_shape,
        scratch_shapes=[
            pltpu.VMEM((chunks, TOK, 2 * TOK), F32),
            pltpu.VMEM((chunks, TOK, 2 * TOK), F32),
            pltpu.VMEM((chunks, TOK, 2 * TOK), BF),
            pltpu.VMEM((chunks, TOK, 2 * TOK), BF),
        ],
        compiler_params=LOCAL,
        cost_estimate=pl.CostEstimate(flops=3 * 10**9, bytes_accessed=10**7, transcendentals=10**6),
        name="attend_self_back" if biased else "attend_cross_back",
    )(*operands)


def matmul(left, right):
    return jnp.dot(left, right, preferred_element_type=F32)


def transposed_left(left, right):
    return contract(left, right, ((0,), (0,)))


def transposed_right(left, right):
    return contract(left, right, ((1,), (1,)))


def rms_scaled(values, gain):
    inverse = lax.rsqrt(jnp.mean(values * values, axis=-1, keepdims=True) + 1e-06)
    return (values * inverse * gain).astype(BF)


def rms_back(values, gain, grad):
    inverse = lax.rsqrt(jnp.mean(values * values, axis=-1, keepdims=True) + 1e-06)
    scaled = gain * grad
    mixed = jnp.mean(values * scaled, axis=-1, keepdims=True)
    grad_values = inverse * scaled - values * (inverse * inverse * inverse * mixed)
    return grad_values, jnp.sum(values * inverse * grad, axis=0)


def gelu_product(gate_part, up_part):
    return jax.nn.gelu(gate_part, approximate=True) * up_part


def near_hot():
    shape = (REACH, 3 * HALF * HALF)
    spot = lax.broadcasted_iota(jnp.int32, shape, 1)
    gap = spot // (HALF * HALF)
    key = (spot // HALF) % HALF
    row = spot % HALF
    distance = jnp.clip(HALF * gap + row - key, 0, REACH - 1)
    return (distance == lax.broadcasted_iota(jnp.int32, shape, 0)).astype(BF)


def bias_tiles(bias_rows):
    near = matmul(bias_rows.astype(BF), near_hot()).reshape(HEADS, 3, HALF, HALF)
    key = jnp.arange(HALF, dtype=jnp.int32)[:, None]
    row = jnp.arange(HALF, dtype=jnp.int32)[None, :]
    barred = (jnp.arange(3) == 0)[None, :, None, None] & (key > row)[None, None]
    near = jnp.where(barred, -1e30, near)
    far = jnp.broadcast_to(bias_rows[:, -1][:, None, None, None], (HEADS, 1, HALF, HALF))
    none = jnp.full((HEADS, 1, HALF, HALF), -1e30, F32)
    tiles = jnp.concatenate([near, far, none], axis=1)
    return jnp.concatenate([tiles, tiles], axis=-1)


def bias_sums(strips):
    tiles = (strips[..., :HALF] + strips[..., HALF:]).reshape(HEADS, -1)
    high = tiles.astype(BF)
    low = (tiles - high.astype(F32)).astype(BF)
    hot = near_hot()
    sums = transposed_right(high, hot) + transposed_right(low, hot)
    far = -jnp.sum(sums[:, :-1], axis=1, keepdims=True)
    return jnp.concatenate([sums[:, :-1], far], axis=1)


def body(
    decoder_in,
    encoder_states,
    out_grad,
    block_pairs,
    bucket_table,
    gain_self,
    self_query,
    self_key,
    self_value,
    self_out,
    position_bias,
    gain_cross,
    cross_query,
    cross_key,
    cross_value,
    cross_out,
    gain_feed,
    feed_gate,
    feed_up,
    feed_down,
):
    me = lax.axis_index("ctx")
    rows = self_query.shape[0]
    small = jnp.concatenate(
        [
            jnp.pad(jnp.stack([gain_self, gain_cross, gain_feed]), ((0, 0), (0, 128 - rows))),
            jnp.pad(position_bias, ((0, 9), (0, 128 - HEADS))),
        ],
        axis=0,
    )
    kv_one, kv_two, square, gate_up, down, small, normed_one, queries, self_kv, cross_kv = front(
        [
            self_key, self_value, cross_key, cross_value,
            self_query, self_out, cross_query, cross_out,
            feed_gate, feed_up, feed_down,
        ],
        small,
        decoder_in[0],
        encoder_states[0],
        0,
    )
    kv_one = kv_one.reshape(D, 2 * D)
    kv_two = kv_two.reshape(D, 2 * D)
    square = square.reshape(D, 4 * D)
    gate_up = gate_up.reshape(D, 2 * FF)
    down = down.reshape(FF, D)
    query_one, out_one, query_two, out_two = (square[:, k * D : k * D + D] for k in range(4))
    gains = jnp.transpose(small[:, :3, :rows], (1, 0, 2)).reshape(3, D).astype(F32)
    norm_one, norm_two, norm_three = gains[0:1], gains[1:2], gains[2:3]
    table = small[:, 3:7, :HEADS].reshape(32, HEADS)

    bucket_hot = (bucket_table[:, None] == jnp.arange(32, dtype=jnp.int32)[None, :]).astype(BF)
    bias_rows = transposed_right(table.T, bucket_hot)
    tiles = bias_tiles(bias_rows)
    pair = block_pairs[me]
    query_blocks = jnp.stack([pair, 31 - pair])
    key_blocks = jnp.stack([block_pairs, 31 - block_pairs], axis=1).reshape(-1)
    gaps = query_blocks[:, None] - key_blocks[None, :]
    classes = jnp.where(gaps < 0, 4, jnp.minimum(gaps, 3)).astype(jnp.int32)
    wanted = query_blocks[:, None] - jnp.arange(3, dtype=jnp.int32)[None, :]
    near = jnp.max(
        jnp.where(
            wanted[:, :, None] == key_blocks[None, None, :],
            jnp.arange(32, dtype=jnp.int32)[None, None, :],
            -1,
        ),
        axis=-1,
    )

    tokens = decoder_in[0].astype(F32)
    states = encoder_states[0]
    upstream = out_grad[0]
    attended, self_totals = attend(queries, self_kv, TOK, 0, classes, tiles)
    mid_one = tokens + matmul(attended, out_one)
    normed_two = rms_scaled(mid_one, norm_two)
    cross_queries = matmul(normed_two, query_two).astype(BF)
    cross_attended, cross_totals = attend(cross_queries, cross_kv, ENC, 0)
    mid_two = mid_one + matmul(cross_attended, out_two)
    normed_three = rms_scaled(mid_two, norm_three)
    gate_up_values = matmul(normed_three, gate_up).astype(BF).astype(F32)
    gate_values, up_values = gate_up_values[:, :FF], gate_up_values[:, FF:]
    hidden, pull_feed = jax.vjp(gelu_product, gate_values, up_values)
    hidden = hidden.astype(BF)
    block_out = mid_two + matmul(hidden, down)

    d_hidden = transposed_right(upstream, down)
    d_gate_up = jnp.concatenate(pull_feed(d_hidden), axis=1).astype(BF)
    d_normed_three = transposed_right(d_gate_up, gate_up)
    part_three, grad_norm_three = rms_back(mid_two, norm_three, d_normed_three)
    d_mid_two = upstream.astype(F32) + part_three
    cross_branch = d_mid_two.astype(BF)
    d_cross_attended = transposed_right(cross_branch, out_two).astype(BF)
    d_cross_queries, d_cross_kv_all = attend_back(
        cross_queries, cross_kv, d_cross_attended, cross_totals, ENC, 0
    )
    d_normed_two = transposed_right(d_cross_queries, query_two)
    part_two, grad_norm_two = rms_back(mid_one, norm_two, d_normed_two)
    d_mid_one = d_mid_two + part_two
    self_branch = d_mid_one.astype(BF)
    d_attended = transposed_right(self_branch, out_one).astype(BF)
    d_queries, d_kv_all, strips = attend_back(
        queries, self_kv, d_attended, self_totals, TOK, 0, classes, near, tiles
    )
    grad_table = matmul(bias_sums(strips), bucket_hot.astype(F32)).T.reshape(8, 4, HEADS)
    grad_gains = jnp.stack([grad_norm_two, grad_norm_three]).reshape(2, 8, rows)
    grad_small = jnp.concatenate(
        [
            jnp.zeros((8, 1, 128), F32),
            jnp.pad(jnp.transpose(grad_gains, (1, 0, 2)), ((0, 0), (0, 0), (0, 128 - rows))),
            jnp.pad(grad_table, ((0, 0), (0, 9), (0, 128 - HEADS))),
        ],
        axis=1,
    )
    done = finish(
        [
            normed_three, hidden, cross_attended, normed_two, attended, normed_one,
            d_gate_up, upstream, cross_branch, d_cross_queries, self_branch, d_queries,
            d_kv_all.reshape(8, 2, 2, TOK, D),
            d_cross_kv_all.reshape(8, 2, 2, ENC, D),
        ],
        [
            states,
            kv_one,
            kv_two,
            transposed_right(d_queries, query_one),
            d_mid_one,
            decoder_in[0],
            norm_one,
            grad_small,
        ],
        3,
    )
    grad_decoder, grad_encoder = done[:2]
    (
        grad_out_two, grad_query_two, grad_out_one, grad_query_one,
        grad_key_two, grad_value_two, grad_key_one, grad_value_one,
        grad_gate, grad_up, grad_down, extras,
    ) = done[2:]
    return (
        block_out[None],
        grad_decoder[None],
        grad_encoder[None],
        extras[0, :rows],
        grad_query_one,
        grad_key_one,
        grad_value_one,
        grad_out_one,
        extras[3:7, :HEADS],
        extras[1, :rows],
        grad_query_two,
        grad_key_two,
        grad_value_two,
        grad_out_two,
        extras[2, :rows],
        grad_gate,
        grad_up,
        grad_down,
    )


def solution(mesh):
    tokens = P("fsdp", "ctx", None)
    matrix = P("fsdp", None)
    vector = P("fsdp")
    weights = (
        (vector,) + (matrix,) * 5 + (vector,) + (matrix,) * 4 + (vector,) + (matrix,) * 3
    )
    return jax.shard_map(
        body,
        mesh=mesh,
        in_specs=(tokens,) * 3 + (P(), P()) + weights,
        out_specs=(tokens,) * 3 + weights,
        check_vma=False,
    )
```

```python
import functools

import jax
import jax.numpy as jnp
from jax import lax
from jax.experimental import pallas as pl
from jax.experimental.pallas import tpu as pltpu
from jax.sharding import PartitionSpec as P

D = 768
FF = 2048
HEADS = 12
HEAD_DIM = 64
PAIRS = HEADS // 2
N_CTX = 16
TOK = 128
ENC = 64
HALF = 64
REACH = 128
BF = jnp.bfloat16
F32 = jnp.float32
MIB = 1024 * 1024


def ctx_place():
    me = lax.axis_index("ctx")
    core = me % 2
    high = (me // 2) % 2
    y = me // 4
    return me, core, high, y


def slot_of(y, shift, high, core):
    return ((y + shift) % 4) * 4 + 2 * high + core


def torus_place():
    me, core, high, y = ctx_place()
    shard = lax.axis_index("fsdp")
    return me, core, high, y, shard // 4, shard % 4


def hop(src, dst, send_sem, recv_sem, ctx, fsdp):
    return pltpu.make_async_remote_copy(
        src_ref=src,
        dst_ref=dst,
        send_sem=send_sem,
        recv_sem=recv_sem,
        device_id={"ctx": ctx, "fsdp": fsdp},
    )


def greet_all(devices):
    barrier = pltpu.get_barrier_semaphore()
    for ctx, fsdp in devices:
        pl.semaphore_signal(barrier, inc=1, device_id={"ctx": ctx, "fsdp": fsdp})
    pl.semaphore_wait(barrier, len(devices))


PACKS = ((0, 1), (2, 3), (4, 5, 6, 7), (8, 9), (10,))


def front_kernel(*refs):
    sources = refs[:11]
    small_ref, token_ref, state_ref = refs[11:14]
    results = refs[14:19]
    small_out, normed_out, query_out, self_result, cross_result = refs[19:24]
    targets = refs[24:29]
    (
        self_out_ref, cross_out_ref, landing, self_ref, cross_ref, send_sem, x_sem, z_sem, core_sem,
        fill_sem, small_sem, self_sem, cross_sem, local_sem,
    ) = refs[29:]
    me, core, high, y, low, x = torus_place()
    shard = low * 4 + x
    sibling = (slot_of(y, 0, high, 1 - core), shard)
    inside = (me, (1 - low) * 4 + x)
    outside = (slot_of(y, 0, 1 - high, core), (1 - low) * 4 + x)
    across = slot_of(y, 0, 1 - high, core)
    rows = [slot_of(y, shift, high, core) for shift in (1, 2, 3)]
    others = [low * 4 + (x + shift) % 4 for shift in (1, 2, 3)]
    peers = [(shard + shift) % 8 for shift in range(1, 8)]
    greet_all(
        [sibling, outside, (across, shard)]
        + [(me, peer) for peer in peers]
        + [(row, shard) for row in rows]
    )
    sends = []

    def send(src, dst, recv_sem, device):
        copy = hop(src, dst, send_sem.at[len(sends)], recv_sem, *device)
        copy.start()
        sends.append(copy)

    def arrived(ref, recv_sem):
        hop(ref, ref, send_sem.at[0], recv_sem, *sibling).wait_recv()

    def bring(src, dst, sem):
        copy = pltpu.make_async_copy(src, dst, sem)
        copy.start()
        return copy


    def part(k, owner, whose, side=None):
        ref = targets[k]
        count = ref.shape[1] // 2
        start = pl.multiple_of(whose * count, 16)
        if side is None:
            return ref.at[owner, pl.ds(start, count), :]
        width = ref.shape[2] // 2
        return ref.at[owner, pl.ds(start, count), pl.ds(side * width, width)]

    def fill(k):
        copies = []
        start = 0
        for source in PACKS[k]:
            width = sources[source].shape[1]
            copies.append(
                bring(
                    sources[source],
                    targets[k].at[shard, :, pl.ds(start, width)],
                    fill_sem.at[source],
                )
            )
            start += width
        return copies

    def send_own(k):
        for copy in fills[k]:
            copy.wait()
        for spot in (1, 0, 2):
            block = part(k, shard, core)
            send(block, block, x_sem.at[k, spot], (me, others[spot]))
        for side, device in enumerate((inside, outside)):
            piece = part(k, shard, core, side)
            send(piece, piece, z_sem.at[k, 3, side], device)


    def pass_x(k):
        for spot in (0, 2, 1):
            owner = low * 4 + (x + 3 - spot) % 4
            block = part(k, owner, core)
            arrived(block, x_sem.at[k, spot])
            for side, device in enumerate((inside, outside)):
                piece = part(k, owner, core, side)
                send(piece, piece, z_sem.at[k, spot, side], device)
            send(block, block, core_sem.at[k, spot], sibling)

    def pass_z(k):
        for spot in (3, 0, 2, 1):
            owner = (1 - low) * 4 + (x + 3 - spot) % 4
            for side in range(2):
                piece = part(k, owner, core, side)
                arrived(piece, z_sem.at[k, spot, side])
                send(piece, piece, core_sem.at[k, 3 + 2 * spot + side], sibling)

    def complete(k):
        for spot in range(3):
            owner = low * 4 + (x + 3 - spot) % 4
            arrived(part(k, owner, 1 - core), core_sem.at[k, spot])
        for spot in range(4):
            owner = (1 - low) * 4 + (x + 3 - spot) % 4
            for side in range(2):
                arrived(part(k, owner, 1 - core, side), core_sem.at[k, 3 + 2 * spot + side])


    def kv_start(src, out, sems):
        send(src, out.at[me], sems.at[me], (across, shard))
        for row in rows:
            send(src, out.at[me], sems.at[me], (row, shard))
        send(src, out.at[me], sems.at[me], sibling)

    def kv_across(out, sems):
        block = out.at[across]
        arrived(block, sems.at[across])
        for row in rows:
            send(block, block, sems.at[across], (row, shard))
        send(block, block, sems.at[across], sibling)

    def kv_rows(out, sems, flip):
        for shift in (1, 3, 2):
            slot = slot_of(y, shift, 1 - high if flip else high, core)
            block = out.at[slot]
            arrived(block, sems.at[slot])
            send(block, block, sems.at[slot], sibling)

    def kv_complete(out, sems):
        for shift in range(4):
            for half in range(2):
                slot = slot_of(y, shift, half, 1 - core)
                arrived(out.at[slot], sems.at[slot])

    fills = [fill(k) for k in range(5)]
    own_small = bring(small_ref, landing.at[shard], local_sem.at[0])
    for spot, peer in enumerate(peers):
        send(small_ref, landing.at[shard], small_sem.at[spot], (me, peer))
    send_own(0)
    send_own(1)
    own_small.wait()
    for spot in range(7):
        arrived(landing.at[(shard + 7 - spot) % 8], small_sem.at[spot])
    small = landing[...]
    small_out[...] = small
    gains = small.astype(F32)
    gain = jnp.concatenate([gains[owner, 0:1, :96] for owner in range(8)], axis=1)
    normed = rms_scaled(token_ref[...].astype(F32), gain)
    normed_out[...] = normed
    pass_x(0)
    send_own(2)
    pass_z(0)
    pass_x(1)
    send_own(3)
    complete(0)
    exits = [bring(targets[0], results[0], local_sem.at[1])]
    for half in range(2):
        weight = targets[0][:, :, half * D : half * D + D].reshape(D, D)
        self_ref[half] = matmul(normed, weight).astype(BF)
    kv_start(self_ref, self_out_ref, self_sem)
    own_self = bring(self_ref, self_out_ref.at[me], local_sem.at[2])
    pass_z(1)
    complete(1)
    exits.append(bring(targets[1], results[1], local_sem.at[4]))
    for half in range(2):
        weight = targets[1][:, :, half * D : half * D + D].reshape(D, D)
        cross_ref[half] = matmul(state_ref[...], weight).astype(BF)
    kv_start(cross_ref, cross_out_ref, cross_sem)
    own_cross = bring(cross_ref, cross_out_ref.at[me], local_sem.at[3])
    pass_x(2)
    send_own(4)
    kv_across(self_out_ref, self_sem)
    pass_z(2)
    kv_across(cross_out_ref, cross_sem)
    pass_x(3)
    kv_rows(self_out_ref, self_sem, False)
    pass_z(3)
    pass_x(4)
    kv_rows(self_out_ref, self_sem, True)
    kv_rows(cross_out_ref, cross_sem, False)
    pass_z(4)
    kv_rows(cross_out_ref, cross_sem, True)
    complete(2)
    exits.append(bring(targets[2], results[2], local_sem.at[5]))
    query_out[...] = matmul(normed, targets[2][:, :, :D].reshape(D, D)).astype(BF)
    own_self.wait()
    own_cross.wait()
    kv_complete(self_out_ref, self_sem)
    exits.append(bring(self_out_ref, self_result, local_sem.at[6]))
    kv_complete(cross_out_ref, cross_sem)
    exits.append(bring(cross_out_ref, cross_result, local_sem.at[7]))
    complete(3)
    exits.append(bring(targets[3], results[3], local_sem.at[8]))
    complete(4)
    exits.append(bring(targets[4], results[4], local_sem.at[9]))
    for copy in sends:
        copy.wait_send()
    for copy in exits:
        copy.wait()


def front(weights, small, tokens, states, collective_id):
    dma = pltpu.SemaphoreType.DMA
    packs = [
        (8, weights[group[0]].shape[0], sum(weights[k].shape[1] for k in group)) for group in PACKS
    ]
    anywhere = pl.BlockSpec(memory_space=pl.ANY)
    inside = pl.BlockSpec(memory_space=pltpu.VMEM)
    return pl.pallas_call(
        front_kernel,
        out_shape=[jax.ShapeDtypeStruct(pack, BF) for pack in packs]
        + [
            jax.ShapeDtypeStruct((8, 16, 128), BF),
            jax.ShapeDtypeStruct((TOK, D), BF),
            jax.ShapeDtypeStruct((TOK, D), BF),
            jax.ShapeDtypeStruct((N_CTX, 2, TOK, D), BF),
            jax.ShapeDtypeStruct((N_CTX, 2, ENC, D), BF),
        ],
        in_specs=[anywhere] * 12 + [inside] * 2,
        out_specs=[anywhere] * 5 + [inside] * 3 + [anywhere] * 2,
        scratch_shapes=[pltpu.VMEM(pack, BF) for pack in packs]
        + [
            pltpu.VMEM((N_CTX, 2, TOK, D), BF),
            pltpu.VMEM((N_CTX, 2, ENC, D), BF),
            pltpu.VMEM((8, 16, 128), BF),
            pltpu.VMEM((2, TOK, D), BF),
            pltpu.VMEM((2, ENC, D), BF),
            dma((5 * 22 + 7 + 30,)),
            dma((5, 3)),
            dma((5, 4, 2)),
            dma((5, 11)),
            dma((11,)),
            dma((7,)),
            dma((N_CTX,)),
            dma((N_CTX,)),
            dma((10,)),
        ],
        compiler_params=pltpu.CompilerParams(
            collective_id=collective_id, has_side_effects=True, vmem_limit_bytes=60 * MIB
        ),
        name="front",
    )(*weights, small, tokens, states)


PIECE = 96
ROOM = D // 2 + FF // 8 + FF // 16
WIDTHS = (D // 2, D // 2, D // 2, D // 2, D, D, FF)
SPAN = sum(WIDTHS)
DOWN = len(WIDTHS)
CHUNKS = DOWN + 1
CROSS_KV, SELF_KV, WIDE = 4, 5, 6
LEFT = (D,) * 4
RIGHT = (D // 2,) * 4


def finish_kernel(*refs):
    lefts = refs[:4]
    rights = refs[4:8]
    wide_ref, down_ref, dkv_ref, dckv_ref = refs[8:12]
    state_ref, kv_ref, ckv_ref, dn_ref, dmid_ref, token_ref, gain_ref, small_ref = refs[12:20]
    land_out, small_out, decoder_ref, encoder_ref = refs[20:24]
    (
        left_all, right_all, turned, turned_one, turned_state, state_all, s_right, c_right,
        kept, from_z, from_x, via_x, d_z, d_x, d_via,
        s_kept, s_core, s_row, s_via, s_stage, s_high, s_fin,
        c_kept, c_core, c_row, c_via, c_stage, c_high, c_fin,
        small_f32, sm_own, sm_core, sm_z, sm_x, sm_ctx, sm_total, packed, from_ctx, land,
        s_sem, c_sem, fill_sem, act_send, act_recv, late_send, late_recv, z_send, z_recv,
        x_send, x_recv, ctx_send, ctx_recv, out_send, out_recv, pass_send, pass_recv,
        sm_send, sm_recv, local_sem,
    ) = refs[24:]
    me, core, high, y, low, x = torus_place()
    shard = low * 4 + x
    rank = y * 2 + high
    sibling = (slot_of(y, 0, high, 1 - core), shard)
    inside = (me, (1 - low) * 4 + x)
    outside = (slot_of(y, 0, 1 - high, core), (1 - low) * 4 + x)
    across = (slot_of(y, 0, 1 - high, core), shard)
    others = [low * 4 + (x + shift) % 4 for shift in (1, 2, 3)]
    ahead = (slot_of(y, 1, high, core), shard)
    behind = (slot_of(y, 3, high, core), shard)
    shifts = [(dy, dz) for dy in range(4) for dz in range(2)][1:]
    mates = [((y + dy) % 4) * 2 + (high + dz) % 2 for dy, dz in shifts]
    greet_all(
        [sibling, inside, outside]
        + [(me, other) for other in others]
        + [(mate * 2 + core, shard) for mate in mates]
    )
    sends = []

    def go(src, dst, send_sem, recv_sem, device):
        copy = hop(src, dst, send_sem, recv_sem, *device)
        copy.start()
        sends.append(copy)
        return copy

    def bring(src, dst, sem):
        copy = pltpu.make_async_copy(src, dst, sem)
        copy.start()
        return copy


    def rows_start(source, held, arrived, sem):
        over = []
        local = []
        for spot, shift in enumerate((2, 1, 3, 0)):
            pair = pl.ds(((y + shift) % 4) * 2, 2)
            block = pl.ds(2 * spot, 2)
            over.append(
                go(
                    source.at[pair, 1 - core], arrived.at[block],
                    sem.at[0, spot], sem.at[1, spot], sibling,
                )
            )
            local.append(bring(source.at[pair, core], held.at[block], sem.at[4, spot]))
        return over, local


    def rows_send(copies, held, arrived, via, row, sem):
        over, local = copies
        onward = []
        for spot in range(4):
            local[spot].wait()
            over[spot].wait_recv()
            for block in (2 * spot, 2 * spot + 1):
                for part in range(2):
                    held[block, part] = held[block, part] + arrived[block, part]
            if spot == 0:
                first = go(held.at[0], via.at[0], sem.at[2, 0], sem.at[3, 0], ahead)
                second = go(held.at[1], via.at[1], sem.at[2, 1], sem.at[3, 1], behind)
            elif spot == 1:
                onward.append(go(held.at[3], row.at[0, 1], sem.at[2, 2], sem.at[3, 2], ahead))
            elif spot == 2:
                onward.append(go(held.at[4], row.at[1, 0], sem.at[2, 3], sem.at[3, 3], behind))
        return first, second, onward

    def rows_via(state, held, via, row, sem):
        first, second, onward = state
        first.wait_recv()
        for part in range(2):
            held[2, part] = held[2, part] + via[0, part]
        onward.append(go(held.at[2], row.at[0, 0], sem.at[2, 4], sem.at[3, 4], ahead))
        second.wait_recv()
        for part in range(2):
            held[5, part] = held[5, part] + via[1, part]
        onward.append(go(held.at[5], row.at[1, 1], sem.at[2, 5], sem.at[3, 5], behind))
        return onward

    def rows_total(held, row, half, part):
        return (
            held[6 + half, part].astype(F32)
            + row[0, half, part].astype(F32)
            + row[1, half, part].astype(F32)
        )

    def rows_across(onward, held, row, stage, landing, sem):
        for copy in onward:
            copy.wait_recv()
        for part in range(2):
            stage[part] = rows_total(held, row, 1 - high, part).astype(BF)
        return go(stage, landing, sem.at[2, 6], sem.at[3, 6], across)

    def rows_sum(last, held, row, landing, final, right, which):
        totals = [rows_total(held, row, high, part) for part in range(2)]
        last.wait_recv()
        for part in range(2):
            final[part] = (totals[part] + landing[part].astype(F32)).astype(BF)
        count = final.shape[1]
        copy = go(
            final.at[1 - core], right.at[pl.ds(count, count)],
            late_send.at[which], late_recv.at[which], sibling,
        )
        right[:count] = final[core]
        return copy


    starts = [sum(WIDTHS[:k]) for k in range(len(WIDTHS))]
    left_starts = [sum(LEFT[:k]) for k in range(4)]
    right_starts = [sum(RIGHT[:k]) for k in range(4)]
    acts = {}
    over_z, over_via, over_x = {}, {}, {}
    column_ahead = (me, low * 4 + (x + 1) % 4)
    column_behind = (me, low * 4 + (x + 3) % 4)

    def buffers(k):
        if k == DOWN:
            return d_z, d_x, d_via, pl.ds(0, D // 2)
        return from_z, from_x, via_x, pl.ds(starts[k], WIDTHS[k])

    def acts_start(index):
        left = pl.ds(left_starts[index], LEFT[index])
        right = pl.ds(right_starts[index], RIGHT[index])
        near = pl.ds(pl.multiple_of(core * RIGHT[index], 128), RIGHT[index])
        far = pl.ds(pl.multiple_of((1 - core) * RIGHT[index], 128), RIGHT[index])
        mine = pl.ds(0, TOK)
        theirs = pl.ds(TOK, TOK)
        acts[index] = (
            bring(lefts[index], left_all.at[mine, left], fill_sem.at[index, 0]),
            bring(rights[index].at[:, near], right_all.at[mine, right], fill_sem.at[index, 1]),
            go(
                lefts[index], left_all.at[theirs, left],
                act_send.at[index, 0], act_recv.at[index, 0], sibling,
            ),
            go(
                rights[index].at[:, far], right_all.at[theirs, right],
                act_send.at[index, 1], act_recv.at[index, 1], sibling,
            ),
        )

    def multiply(k, left_ref, right):
        landing, _, _, cut = buffers(k)
        for group in range(2):
            owners = pl.ds(4 * ((1 - low + group) % 2), 4)
            left = left_ref[owners].reshape(4 * PIECE, right.shape[0])
            kept[owners, :, cut] = (
                contract(left, right, ((1,), (0,))).astype(BF).reshape(4, PIECE, WIDTHS[k])
            )
            if group == 0:
                half = PIECE // 2
                over_z[k] = [
                    go(
                        kept.at[owners, pl.ds(side * half, half), cut],
                        landing.at[:, pl.ds(side * half, half), cut],
                        z_send.at[k, side],
                        z_recv.at[k, side],
                        device,
                    )
                    for side, device in enumerate((inside, outside))
                ]

    def make(index):
        near_left, near_right, far_left, far_right = acts[index]
        near_left.wait()
        near_right.wait()
        far_left.wait_recv()
        far_right.wait_recv()
        left = left_all[:, left_starts[index] : left_starts[index] + LEFT[index]].T
        right = right_all[:, right_starts[index] : right_starts[index] + RIGHT[index]]
        target = turned_one if index == 3 else turned
        target[...] = left.reshape(8, PIECE, 2 * TOK)
        multiply(index, target, right)

    def step_z(k):
        landing, _, _, cut = buffers(k)
        for copy in over_z[k]:
            copy.wait_recv()
        for column in range(4):
            landing[column, :, cut] = landing[column, :, cut] + kept[4 * low + column, :, cut]
        send_x(k)


    def send_x(k):
        landing, spread, via, cut = buffers(k)
        half = landing.shape[1] // 2
        upper, lower = pl.ds(0, half), pl.ds(half, half)
        away, front_column, back_column = (x + 2) % 4, (x + 1) % 4, (x + 3) % 4
        over_via[k] = (
            go(
                landing.at[away, upper, cut], via.at[0, :, cut],
                x_send.at[k, 0], x_recv.at[k, 0], column_ahead,
            ),
            go(
                landing.at[away, lower, cut], via.at[1, :, cut],
                x_send.at[k, 1], x_recv.at[k, 1], column_behind,
            ),
        )
        over_x[k] = [
            go(
                landing.at[front_column, lower, cut], spread.at[0, lower, cut],
                x_send.at[k, 2], x_recv.at[k, 2], column_ahead,
            ),
            go(
                landing.at[back_column, upper, cut], spread.at[1, upper, cut],
                x_send.at[k, 3], x_recv.at[k, 3], column_behind,
            ),
        ]

    def step_via(k):
        landing, spread, via, cut = buffers(k)
        half = landing.shape[1] // 2
        upper, lower = pl.ds(0, half), pl.ds(half, half)
        front_column, back_column = (x + 1) % 4, (x + 3) % 4
        over_via[k][0].wait_recv()
        landing[front_column, upper, cut] = landing[front_column, upper, cut] + via[0, :, cut]
        over_x[k].append(
            go(
                landing.at[front_column, upper, cut], spread.at[0, upper, cut],
                x_send.at[k, 4], x_recv.at[k, 4], column_ahead,
            )
        )
        over_via[k][1].wait_recv()
        landing[back_column, lower, cut] = landing[back_column, lower, cut] + via[1, :, cut]
        over_x[k].append(
            go(
                landing.at[back_column, lower, cut], spread.at[1, lower, cut],
                x_send.at[k, 5], x_recv.at[k, 5], column_behind,
            )
        )

    def step_x(k):
        landing, spread, _, cut = buffers(k)
        for copy in over_x[k]:
            copy.wait_recv()
        total = landing[x, :, cut].astype(F32)
        for spot in range(2):
            total = total + spread[spot, :, cut].astype(F32)
        total = total.astype(BF)
        half = D // 2
        if k == WIDE:
            for piece in range(8):
                packed[piece, :, half : half + 256] = total[:, piece * 256 : piece * 256 + 256]
        elif k == DOWN:
            for piece in range(8):
                for part in range(3):
                    packed[piece, part * 32 : part * 32 + 32, half + 256 :] = total[
                        piece * 32 : piece * 32 + 32, part * 128 : part * 128 + 128
                    ]
        elif k == CROSS_KV or k == SELF_KV:
            for piece in range(2):
                packed[k + (0 if k == CROSS_KV else 1) + piece, :, :half] = total[
                    :, piece * half : piece * half + half
                ]
        else:
            packed[k, :, :half] = total

    wide_copy = bring(wide_ref, from_z.at[:, :, pl.ds(starts[WIDE], FF)], local_sem.at[1])
    down_copy = bring(down_ref, d_z, local_sem.at[2])
    s_copies = rows_start(dkv_ref, s_kept, s_core, s_sem)
    c_copies = rows_start(dckv_ref, c_kept, c_core, c_sem)
    for index in range(4):
        acts_start(index)
    state_near = bring(state_ref, state_all.at[pl.ds(0, ENC)], local_sem.at[0])
    state_far = go(
        state_ref, state_all.at[pl.ds(ENC, ENC)], late_send.at[2], late_recv.at[2], sibling
    )
    down_copy.wait()
    send_x(DOWN)
    wide_copy.wait()
    send_x(WIDE)
    s_state = rows_send(s_copies, s_kept, s_core, s_via, s_row, s_sem)
    c_state = rows_send(c_copies, c_kept, c_core, c_via, c_row, c_sem)
    make(0)
    step_via(DOWN)
    make(1)
    s_onward = rows_via(s_state, s_kept, s_via, s_row, s_sem)
    make(2)
    make(3)
    step_via(WIDE)
    c_onward = rows_via(c_state, c_kept, c_via, c_row, c_sem)
    for k in range(4):
        step_z(k)
    state_near.wait()
    state_far.wait_recv()
    turned_state[...] = state_all[...].T.reshape(8, PIECE, 2 * ENC)
    s_last = rows_across(s_onward, s_kept, s_row, s_stage, s_high, s_sem)
    step_x(DOWN)
    step_via(0)
    s_far = rows_sum(s_last, s_kept, s_row, s_high, s_fin, s_right, 0)
    step_via(1)
    s_far.wait_recv()
    multiply(SELF_KV, turned_one, s_right[...])
    c_last = rows_across(c_onward, c_kept, c_row, c_stage, c_high, c_sem)
    step_via(2)
    step_via(3)
    tokens = token_ref[...].astype(F32)
    d_kv = jnp.concatenate([s_fin[0], s_fin[1]], axis=1)
    grad = dn_ref[...] + contract(d_kv, kv_ref[...], ((1,), (1,)))
    inverse = lax.rsqrt(jnp.mean(tokens * tokens, axis=-1, keepdims=True) + 1e-06)
    small_f32[...] = small_ref[...]
    line = jnp.sum(tokens * inverse * grad, axis=0, keepdims=True)
    for owner in range(8):
        small_f32[owner, 0:1, :96] = line[:, owner * 96 : owner * 96 + 96]
    sm_own[...] = small_f32[...].astype(BF)
    sm_over = go(sm_own, sm_core, sm_send.at[0], sm_recv.at[0], sibling)
    c_far = rows_sum(c_last, c_kept, c_row, c_high, c_fin, c_right, 1)
    step_x(WIDE)
    c_far.wait_recv()
    multiply(CROSS_KV, turned_state, c_right[...])
    step_z(SELF_KV)
    sm_over.wait_recv()
    sm_own_sum = (sm_own[...].astype(F32) + sm_core[...].astype(F32)).astype(BF)
    sm_over.wait_send()
    sm_own[...] = sm_own_sum
    sm_inside = go(
        sm_own.at[pl.ds(4 * (1 - low), 4)], sm_z, sm_send.at[1], sm_recv.at[1], inside
    )
    for k in range(4):
        step_x(k)
    step_z(CROSS_KV)
    sm_inside.wait_recv()
    for column in range(4):
        sm_z[column] = sm_z[column] + sm_own[4 * low + column]
    sm_row = [
        go(
            sm_z.at[(x + spot + 1) % 4], sm_x.at[spot],
            sm_send.at[2 + spot], sm_recv.at[2 + spot], (me, others[spot]),
        )
        for spot in range(3)
    ]
    step_via(SELF_KV)
    step_via(CROSS_KV)
    scaled = gain_ref[...] * grad
    mixed = jnp.mean(tokens * scaled, axis=-1, keepdims=True)
    decoder_ref[...] = (
        dmid_ref[...] + inverse * scaled - tokens * (inverse * inverse * inverse * mixed)
    )
    d_ckv = jnp.concatenate([c_fin[0], c_fin[1]], axis=1)
    encoder_ref[...] = contract(d_ckv, ckv_ref[...], ((1,), (1,)))
    step_x(SELF_KV)
    step_x(CROSS_KV)


    over_ctx = [
        go(
            packed.at[mate],
            from_ctx.at[spot],
            ctx_send.at[spot],
            ctx_recv.at[spot],
            (mate * 2 + core, shard),
        )
        for spot, mate in enumerate(mates)
    ]
    sm_sum = sm_z[x].astype(F32)
    for spot in range(3):
        sm_row[spot].wait_recv()
        sm_sum = sm_sum + sm_x[spot].astype(F32)
    sm_total[...] = sm_sum.astype(BF)
    sm_mates = [
        go(
            sm_total, sm_ctx.at[spot],
            sm_send.at[5 + spot], sm_recv.at[5 + spot], (mate * 2 + core, shard),
        )
        for spot, mate in enumerate(mates)
    ]
    total = packed[rank].astype(F32)
    for spot in range(7):
        over_ctx[spot].wait_recv()
        total = total + from_ctx[spot].astype(F32)
    land[rank, core] = total.astype(BF)
    own = land.at[rank, core]
    for spot, mate in enumerate(mates):
        go(own, own, out_send.at[spot], out_recv.at[rank], (mate * 2 + core, shard))
    go(own, own, pass_send.at[7], pass_recv.at[rank], sibling)

    def landed(ref, recv_sem):
        hop(ref, ref, pass_send.at[0], recv_sem, *sibling).wait_recv()

    sm_sum = sm_total[...].astype(F32)
    for spot in range(7):
        sm_mates[spot].wait_recv()
        sm_sum = sm_sum + sm_ctx[spot].astype(F32)
    small_out[...] = sm_sum
    for spot, mate in enumerate(mates):
        block = land.at[mate, core]
        landed(block, out_recv.at[mate])
        go(block, block, pass_send.at[spot], pass_recv.at[mate], sibling)
    for mate in [rank] + mates:
        landed(land.at[mate, 1 - core], pass_recv.at[mate])
    land_out[...] = land[...]
    for copy in sends:
        if copy is not sm_over:
            copy.wait_send()


def unpack_kernel(land, *refs):
    square_refs = refs[:8]
    gate_ref, up_ref, down_ref = refs[8:]
    half = D // 2
    for side in range(2):
        for piece in range(4):
            square_refs[piece][:, side * half : side * half + half] = land[
                piece, side, :, :half
            ].astype(F32)
            square_refs[4 + 2 * (piece // 2) + side][
                :, (piece % 2) * half : (piece % 2) * half + half
            ] = land[4 + piece, side, :, :half].astype(F32)
        target = up_ref if side else gate_ref
        for piece in range(8):
            target[:, piece * 256 : piece * 256 + 256] = land[
                piece, side, :, half : half + 256
            ].astype(F32)
            for part in range(3):
                down_ref[
                    piece * 32 : piece * 32 + 32,
                    side * half + part * 128 : side * half + part * 128 + 128,
                ] = land[piece, side, part * 32 : part * 32 + 32, half + 256 :].astype(F32)


def unpack(land):
    outs = (
        [jax.ShapeDtypeStruct((PIECE, D), F32)] * 8
        + [jax.ShapeDtypeStruct((PIECE, FF), F32)] * 2
        + [jax.ShapeDtypeStruct((FF // 8, D), F32)]
    )
    return pl.pallas_call(
        unpack_kernel,
        out_shape=outs,
        in_specs=[pl.BlockSpec(memory_space=pltpu.VMEM)],
        out_specs=[pl.BlockSpec(memory_space=pltpu.VMEM)] * len(outs),
        compiler_params=pltpu.CompilerParams(vmem_limit_bytes=24 * MIB),
        name="unpack",
    )(land)


def finish(far, near, collective_id):
    dma = pltpu.SemaphoreType.DMA

    def rows(count):
        return [
            pltpu.VMEM((8, 2, count, D), BF),
            pltpu.VMEM((8, 2, count, D), BF),
            pltpu.VMEM((2, 2, 2, count, D), BF),
            pltpu.VMEM((2, 2, count, D), BF),
            pltpu.VMEM((2, count, D), BF),
            pltpu.VMEM((2, count, D), BF),
            pltpu.VMEM((2, count, D), BF),
        ]

    outs = [
        jax.ShapeDtypeStruct((8, 2, PIECE, ROOM), BF),
        jax.ShapeDtypeStruct((16, 128), F32),
        jax.ShapeDtypeStruct((TOK, D), F32),
        jax.ShapeDtypeStruct((ENC, D), F32),
    ]
    return pl.pallas_call(
        finish_kernel,
        out_shape=outs,
        in_specs=[pl.BlockSpec(memory_space=pl.ANY)] * len(far)
        + [pl.BlockSpec(memory_space=pltpu.VMEM)] * len(near),
        out_specs=[pl.BlockSpec(memory_space=pltpu.VMEM)] * len(outs),
        scratch_shapes=[
            pltpu.VMEM((2 * TOK, sum(LEFT)), BF),
            pltpu.VMEM((2 * TOK, sum(RIGHT)), BF),
            pltpu.VMEM((8, PIECE, 2 * TOK), BF),
            pltpu.VMEM((8, PIECE, 2 * TOK), BF),
            pltpu.VMEM((8, PIECE, 2 * ENC), BF),
            pltpu.VMEM((2 * ENC, D), BF),
            pltpu.VMEM((2 * TOK, D), BF),
            pltpu.VMEM((2 * ENC, D), BF),
            pltpu.VMEM((8, PIECE, SPAN - FF), BF),
            pltpu.VMEM((4, PIECE, SPAN), BF),
            pltpu.VMEM((2, PIECE, SPAN), BF),
            pltpu.VMEM((2, PIECE // 2, SPAN), BF),
            pltpu.VMEM((4, FF // 8, D // 2), BF),
            pltpu.VMEM((2, FF // 8, D // 2), BF),
            pltpu.VMEM((2, FF // 16, D // 2), BF),
        ]
        + rows(TOK)
        + rows(ENC)
        + [
            pltpu.VMEM((8, 16, 128), F32),
            pltpu.VMEM((8, 16, 128), BF),
            pltpu.VMEM((8, 16, 128), BF),
            pltpu.VMEM((4, 16, 128), BF),
            pltpu.VMEM((3, 16, 128), BF),
            pltpu.VMEM((7, 16, 128), BF),
            pltpu.VMEM((16, 128), BF),
            pltpu.VMEM((8, PIECE, ROOM), BF),
            pltpu.VMEM((7, PIECE, ROOM), BF),
            pltpu.VMEM((8, 2, PIECE, ROOM), BF),
            dma((5, 7)),
            dma((5, 7)),
            dma((4, 2)),
            dma((4, 2)),
            dma((4, 2)),
            dma((3,)),
            dma((3,)),
            dma((CHUNKS, 2)),
            dma((CHUNKS, 2)),
            dma((CHUNKS, 6)),
            dma((CHUNKS, 6)),
            dma((7,)),
            dma((7,)),
            dma((7,)),
            dma((8,)),
            dma((8,)),
            dma((8,)),
            dma((12,)),
            dma((12,)),
            dma((3,)),
        ],
        compiler_params=pltpu.CompilerParams(
            collective_id=collective_id, has_side_effects=True, vmem_limit_bytes=62 * MIB
        ),
        name="finish_gradients",
    )(*far, *near)


def split_heads(block):
    lane = lax.broadcasted_iota(jnp.int32, block.shape, 1)
    nothing = jnp.zeros_like(block)
    return jnp.concatenate(
        [jnp.where(lane < HEAD_DIM, block, nothing), jnp.where(lane < HEAD_DIM, nothing, block)],
        axis=0,
    )


def join_heads(transposed):
    row = lax.broadcasted_iota(jnp.int32, (2 * HEAD_DIM, TOK), 0)
    return jnp.where(row < HEAD_DIM, transposed[:, :TOK], transposed[:, TOK:]).T


def contract(left, right, dims):
    return lax.dot_general(left, right, (dims, ((), ())), preferred_element_type=F32)


def key_chunk(ref, j):
    if ref.shape[2] == 2 * HALF:
        return ref[j, 0]
    return ref[pl.ds(2 * j, 2), 0].reshape(2 * HALF, 2 * HEAD_DIM)


def bias_chunk(class_ref, tile_ref, j):
    lane = lax.broadcasted_iota(jnp.int32, (HALF, TOK), 1)
    rows = []
    for half in range(2):
        spot = 2 * j + half
        near = class_ref[0, spot]
        far = class_ref[1, spot]
        rows.append(
            jnp.concatenate(
                [
                    jnp.where(lane < HALF, tile_ref[head, near], tile_ref[head, far])
                    for head in range(2)
                ],
                axis=1,
            )
        )
    return jnp.concatenate(rows, axis=0)


def fold(values, join):
    return join(values.reshape(-1, 8, values.shape[-1]), axis=0)


def forward_kernel(biased, *refs):
    if biased:
        class_ref, q_ref, k_ref, v_ref, tile_ref, out_ref, total_ref, score_ref, share_ref = refs
    else:
        q_ref, k_ref, v_ref, out_ref, total_ref, score_ref, share_ref = refs
    chunks = score_ref.shape[0]
    queries = split_heads(q_ref[...])
    highest = None
    for j in range(chunks):
        scores = contract(key_chunk(k_ref, j), queries, ((1,), (1,)))
        if biased:
            scores = scores + bias_chunk(class_ref, tile_ref, j)
        score_ref[j] = scores
        top = fold(scores, jnp.max)
        highest = top if highest is None else jnp.maximum(highest, top)
    highest = jnp.max(highest, axis=0, keepdims=True)
    summed = jnp.zeros((8, 2 * TOK), F32)
    for j in range(chunks):
        raised = jnp.exp(score_ref[j] - highest)
        summed = summed + fold(raised, jnp.sum)
        share_ref[j] = raised.astype(BF)
    summed = jnp.sum(summed, axis=0, keepdims=True)
    values = jnp.concatenate([key_chunk(v_ref, j) for j in range(chunks)], axis=0)
    mixed = contract(values, share_ref[...].reshape(-1, 2 * TOK), ((0,), (0,)))
    out_ref[...] = join_heads(mixed / summed).astype(BF)
    total_ref[0] = jnp.broadcast_to(highest + jnp.log(summed), (8, 2 * TOK))


def backward_kernel(biased, *refs):
    if biased:
        class_ref, near_ref, q_ref, k_ref, v_ref, g_ref, total_ref, tile_ref = refs[:8]
        dq_ref, dkv_ref, strip_ref, share_ref, slope_ref, share_low, slope_low = refs[8:]
    else:
        q_ref, k_ref, v_ref, g_ref, total_ref = refs[:5]
        dq_ref, dkv_ref, share_ref, slope_ref, share_low, slope_low = refs[5:]
    chunks = share_ref.shape[0]
    queries = split_heads(q_ref[...])
    grads = split_heads(g_ref[...])
    totals = total_ref[0, 0:1]
    inner = jnp.zeros((8, 2 * TOK), F32)
    for j in range(chunks):
        scores = contract(key_chunk(k_ref, j), queries, ((1,), (1,)))
        if biased:
            scores = scores + bias_chunk(class_ref, tile_ref, j)
        shares = jnp.exp(scores - totals)
        slopes = contract(key_chunk(v_ref, j), grads, ((1,), (1,)))
        inner = inner + fold(shares * slopes, jnp.sum)
        share_ref[j] = shares
        slope_ref[j] = slopes
        share_low[j] = shares.astype(BF)
    inner = jnp.sum(inner, axis=0, keepdims=True)
    for j in range(chunks):
        grad = share_ref[j] * (slope_ref[j] - inner)
        if biased:
            slope_ref[j] = grad
        slope_low[j] = grad.astype(BF)
    keys = jnp.concatenate([key_chunk(k_ref, j) for j in range(chunks)], axis=0)
    low = slope_low[...].reshape(-1, 2 * TOK)
    dq_ref[...] = join_heads(contract(keys, low, ((0,), (0,)))).astype(BF)
    shape = dkv_ref.shape
    block = (shape[0], shape[2], shape[3])
    dkv_ref[:, 0] = contract(low, queries, ((1,), (0,))).astype(BF).reshape(block)
    dkv_ref[:, 1] = (
        contract(share_low[...].reshape(-1, 2 * TOK), grads, ((1,), (0,))).astype(BF).reshape(block)
    )
    if biased:
        lane = lax.broadcasted_iota(jnp.int32, (HALF, TOK), 1)
        for gap in range(3):
            pieces = []
            for half in range(2):
                spot = near_ref[half, gap]
                held = slope_ref[jnp.maximum(spot, 0) // 2, pl.ds(
                    pl.multiple_of((jnp.maximum(spot, 0) % 2) * HALF, HALF), HALF)]
                pieces.append(jnp.where(spot >= 0, held, jnp.zeros_like(held)))
            for head in range(2):
                cut = slice(head * TOK, (head + 1) * TOK)
                strip_ref[head, gap] = jnp.where(lane < HALF, pieces[0][:, cut], pieces[1][:, cut])


def pair_columns(pair):
    return (0, pair)


def kv_spec(rows, row_block, part):
    return pl.BlockSpec(
        (N_CTX, 1, rows, 2 * HEAD_DIM), lambda pair: (0, part, row_block, pair)
    )


SMEM_SPEC = pl.BlockSpec(memory_space=pltpu.SMEM)
TILE_SPEC = pl.BlockSpec((2, 5, HALF, TOK), lambda pair: (pair, 0, 0, 0))
TOTAL_SPEC = pl.BlockSpec((1, 8, 2 * TOK), lambda pair: (pair, 0, 0))
ROW_SPEC = pl.BlockSpec((TOK, 2 * HEAD_DIM), pair_columns)
LOCAL = pltpu.CompilerParams(vmem_limit_bytes=48 * MIB)


def attend(queries, gathered, rows, row_block, classes=None, tiles=None):
    biased = classes is not None
    chunks = N_CTX * rows // TOK
    specs = [ROW_SPEC, kv_spec(rows, row_block, 0), kv_spec(rows, row_block, 1)]
    operands = [queries, gathered, gathered]
    if biased:
        specs = [SMEM_SPEC] + specs + [TILE_SPEC]
        operands = [classes] + operands + [tiles]
    return pl.pallas_call(
        functools.partial(forward_kernel, biased),
        grid=(PAIRS,),
        in_specs=specs,
        out_specs=[ROW_SPEC, TOTAL_SPEC],
        out_shape=[
            jax.ShapeDtypeStruct((TOK, D), BF),
            jax.ShapeDtypeStruct((PAIRS, 8, 2 * TOK), F32),
        ],
        scratch_shapes=[
            pltpu.VMEM((chunks, TOK, 2 * TOK), F32),
            pltpu.VMEM((chunks, TOK, 2 * TOK), BF),
        ],
        compiler_params=LOCAL,
        cost_estimate=pl.CostEstimate(flops=10**9, bytes_accessed=10**7, transcendentals=10**6),
        name="attend_self" if biased else "attend_cross",
    )(*operands)


def attend_back(queries, gathered, grads, totals, rows, row_block, classes=None, near=None, tiles=None):
    biased = classes is not None
    chunks = N_CTX * rows // TOK
    specs = [ROW_SPEC, kv_spec(rows, row_block, 0), kv_spec(rows, row_block, 1), ROW_SPEC, TOTAL_SPEC]
    operands = [queries, gathered, gathered, grads, totals]
    out_specs = [
        ROW_SPEC,
        pl.BlockSpec((N_CTX, 2, rows, 2 * HEAD_DIM), lambda pair: (0, 0, 0, pair)),
    ]
    out_shape = [
        jax.ShapeDtypeStruct((TOK, D), BF),
        jax.ShapeDtypeStruct((N_CTX, 2, rows, D), BF),
    ]
    if biased:
        specs = [SMEM_SPEC, SMEM_SPEC] + specs + [TILE_SPEC]
        operands = [classes, near] + operands + [tiles]
        out_specs.append(pl.BlockSpec((2, 3, HALF, TOK), lambda pair: (pair, 0, 0, 0)))
        out_shape.append(jax.ShapeDtypeStruct((HEADS, 3, HALF, TOK), F32))
    return pl.pallas_call(
        functools.partial(backward_kernel, biased),
        grid=(PAIRS,),
        in_specs=specs,
        out_specs=out_specs,
        out_shape=out_shape,
        scratch_shapes=[
            pltpu.VMEM((chunks, TOK, 2 * TOK), F32),
            pltpu.VMEM((chunks, TOK, 2 * TOK), F32),
            pltpu.VMEM((chunks, TOK, 2 * TOK), BF),
            pltpu.VMEM((chunks, TOK, 2 * TOK), BF),
        ],
        compiler_params=LOCAL,
        cost_estimate=pl.CostEstimate(flops=3 * 10**9, bytes_accessed=10**7, transcendentals=10**6),
        name="attend_self_back" if biased else "attend_cross_back",
    )(*operands)


def matmul(left, right):
    return jnp.dot(left, right, preferred_element_type=F32)


def transposed_left(left, right):
    return contract(left, right, ((0,), (0,)))


def transposed_right(left, right):
    return contract(left, right, ((1,), (1,)))


def rms_scaled(values, gain):
    inverse = lax.rsqrt(jnp.mean(values * values, axis=-1, keepdims=True) + 1e-06)
    return (values * inverse * gain).astype(BF)


def rms_back(values, gain, grad):
    inverse = lax.rsqrt(jnp.mean(values * values, axis=-1, keepdims=True) + 1e-06)
    scaled = gain * grad
    mixed = jnp.mean(values * scaled, axis=-1, keepdims=True)
    grad_values = inverse * scaled - values * (inverse * inverse * inverse * mixed)
    return grad_values, jnp.sum(values * inverse * grad, axis=0)


def gelu_product(gate_part, up_part):
    return jax.nn.gelu(gate_part, approximate=True) * up_part


def near_hot():
    shape = (REACH, 3 * HALF * HALF)
    spot = lax.broadcasted_iota(jnp.int32, shape, 1)
    gap = spot // (HALF * HALF)
    key = (spot // HALF) % HALF
    row = spot % HALF
    distance = jnp.clip(HALF * gap + row - key, 0, REACH - 1)
    return (distance == lax.broadcasted_iota(jnp.int32, shape, 0)).astype(BF)


def bias_tiles(bias_rows):
    near = matmul(bias_rows.astype(BF), near_hot()).reshape(HEADS, 3, HALF, HALF)
    key = jnp.arange(HALF, dtype=jnp.int32)[:, None]
    row = jnp.arange(HALF, dtype=jnp.int32)[None, :]
    barred = (jnp.arange(3) == 0)[None, :, None, None] & (key > row)[None, None]
    near = jnp.where(barred, -1e30, near)
    far = jnp.broadcast_to(bias_rows[:, -1][:, None, None, None], (HEADS, 1, HALF, HALF))
    none = jnp.full((HEADS, 1, HALF, HALF), -1e30, F32)
    tiles = jnp.concatenate([near, far, none], axis=1)
    return jnp.concatenate([tiles, tiles], axis=-1)


def bias_sums(strips):
    tiles = (strips[..., :HALF] + strips[..., HALF:]).reshape(HEADS, -1)
    high = tiles.astype(BF)
    low = (tiles - high.astype(F32)).astype(BF)
    hot = near_hot()
    sums = transposed_right(high, hot) + transposed_right(low, hot)
    far = -jnp.sum(sums[:, :-1], axis=1, keepdims=True)
    return jnp.concatenate([sums[:, :-1], far], axis=1)


def feed_gradients(normed, hidden, d_gate, d_up, upstream):
    first = lax.axis_index("ctx") % 2 == 0
    low = lax.axis_index("fsdp") // 4
    half = D // 2

    def swap(values, move):
        perm = []
        for ctx in range(N_CTX):
            for shard in range(8):
                there, owner = move(ctx, shard)
                perm.append((ctx * 8 + shard, there * 8 + owner))
        return lax.ppermute(values, ("ctx", "fsdp"), perm)

    near = jnp.where(first, d_gate, d_up)
    far = jnp.where(first, d_up, d_gate)
    near_grad = jnp.where(first, upstream[:, :half], upstream[:, half:])
    far_grad = jnp.where(first, upstream[:, half:], upstream[:, :half])
    other = swap(
        jnp.concatenate([normed, hidden, far, far_grad], axis=1), lambda ctx, shard: (ctx ^ 1, shard)
    )
    lefts = jnp.concatenate([normed, other[:, :D]], axis=0)
    rights = jnp.concatenate([near, other[:, D + FF : D + 2 * FF]], axis=0)
    wide = transposed_left(lefts, rights).astype(BF).reshape(8, PIECE, FF)
    lefts = jnp.concatenate([hidden, other[:, D : D + FF]], axis=0)
    rights = jnp.concatenate([near_grad, other[:, D + 2 * FF :]], axis=0)
    tall = transposed_left(lefts, rights).astype(BF).reshape(8, FF // 8, half)

    def over_z(part):
        middle = part.shape[1] // 2
        away = lax.dynamic_slice_in_dim(part, 4 * (1 - low), 4, 0)
        mine = lax.dynamic_slice_in_dim(part, 4 * low, 4, 0)
        inner = swap(away[:, :middle], lambda ctx, shard: (ctx, (shard + 4) % 8))
        outer = swap(away[:, middle:], lambda ctx, shard: (ctx ^ 2, (shard + 4) % 8))
        return mine + jnp.concatenate([inner, outer], axis=1)

    return over_z(wide), over_z(tall)


def body(
    decoder_in,
    encoder_states,
    out_grad,
    block_pairs,
    bucket_table,
    gain_self,
    self_query,
    self_key,
    self_value,
    self_out,
    position_bias,
    gain_cross,
    cross_query,
    cross_key,
    cross_value,
    cross_out,
    gain_feed,
    feed_gate,
    feed_up,
    feed_down,
):
    me = lax.axis_index("ctx")
    rows = self_query.shape[0]
    small = jnp.concatenate(
        [
            jnp.pad(jnp.stack([gain_self, gain_cross, gain_feed]), ((0, 0), (0, 128 - rows))),
            jnp.pad(position_bias, ((0, 9), (0, 128 - HEADS))),
        ],
        axis=0,
    )
    kv_one, kv_two, square, gate_up, down, small, normed_one, queries, self_kv, cross_kv = front(
        [
            self_key, self_value, cross_key, cross_value,
            self_query, self_out, cross_query, cross_out,
            feed_gate, feed_up, feed_down,
        ],
        small,
        decoder_in[0],
        encoder_states[0],
        0,
    )
    kv_one = kv_one.reshape(D, 2 * D)
    kv_two = kv_two.reshape(D, 2 * D)
    square = square.reshape(D, 4 * D)
    gate_up = gate_up.reshape(D, 2 * FF)
    down = down.reshape(FF, D)
    query_one, out_one, query_two, out_two = (square[:, k * D : k * D + D] for k in range(4))
    gains = jnp.transpose(small[:, :3, :rows], (1, 0, 2)).reshape(3, D).astype(F32)
    norm_one, norm_two, norm_three = gains[0:1], gains[1:2], gains[2:3]
    table = small[:, 3:7, :HEADS].reshape(32, HEADS)

    bucket_hot = (bucket_table[:, None] == jnp.arange(32, dtype=jnp.int32)[None, :]).astype(BF)
    bias_rows = transposed_right(table.T, bucket_hot)
    tiles = bias_tiles(bias_rows)
    pair = block_pairs[me]
    query_blocks = jnp.stack([pair, 31 - pair])
    key_blocks = jnp.stack([block_pairs, 31 - block_pairs], axis=1).reshape(-1)
    gaps = query_blocks[:, None] - key_blocks[None, :]
    classes = jnp.where(gaps < 0, 4, jnp.minimum(gaps, 3)).astype(jnp.int32)
    wanted = query_blocks[:, None] - jnp.arange(3, dtype=jnp.int32)[None, :]
    near = jnp.max(
        jnp.where(
            wanted[:, :, None] == key_blocks[None, None, :],
            jnp.arange(32, dtype=jnp.int32)[None, None, :],
            -1,
        ),
        axis=-1,
    )

    tokens = decoder_in[0].astype(F32)
    states = encoder_states[0]
    upstream = out_grad[0]
    attended, self_totals = attend(queries, self_kv, TOK, 0, classes, tiles)
    mid_one = tokens + matmul(attended, out_one)
    normed_two = rms_scaled(mid_one, norm_two)
    cross_queries = matmul(normed_two, query_two).astype(BF)
    cross_attended, cross_totals = attend(cross_queries, cross_kv, ENC, 0)
    mid_two = mid_one + matmul(cross_attended, out_two)
    normed_three = rms_scaled(mid_two, norm_three)
    gate_up_values = matmul(normed_three, gate_up).astype(BF).astype(F32)
    gate_values, up_values = gate_up_values[:, :FF], gate_up_values[:, FF:]
    hidden, pull_feed = jax.vjp(gelu_product, gate_values, up_values)
    hidden = hidden.astype(BF)
    block_out = mid_two + matmul(hidden, down)

    d_hidden = transposed_right(upstream, down)
    d_gate, d_up = (part.astype(BF) for part in pull_feed(d_hidden))
    d_gate_up = jnp.concatenate([d_gate, d_up], axis=1)
    wide, tall = feed_gradients(normed_three, hidden, d_gate, d_up, upstream)
    d_normed_three = transposed_right(d_gate_up, gate_up)
    part_three, grad_norm_three = rms_back(mid_two, norm_three, d_normed_three)
    d_mid_two = upstream.astype(F32) + part_three
    cross_branch = d_mid_two.astype(BF)
    d_cross_attended = transposed_right(cross_branch, out_two).astype(BF)
    d_cross_queries, d_cross_kv_all = attend_back(
        cross_queries, cross_kv, d_cross_attended, cross_totals, ENC, 0
    )
    d_normed_two = transposed_right(d_cross_queries, query_two)
    part_two, grad_norm_two = rms_back(mid_one, norm_two, d_normed_two)
    d_mid_one = d_mid_two + part_two
    self_branch = d_mid_one.astype(BF)
    d_attended = transposed_right(self_branch, out_one).astype(BF)
    d_queries, d_kv_all, strips = attend_back(
        queries, self_kv, d_attended, self_totals, TOK, 0, classes, near, tiles
    )
    grad_table = matmul(bias_sums(strips), bucket_hot.astype(F32)).T.reshape(8, 4, HEADS)
    grad_gains = jnp.stack([grad_norm_two, grad_norm_three]).reshape(2, 8, rows)
    grad_small = jnp.concatenate(
        [
            jnp.zeros((8, 1, 128), F32),
            jnp.pad(jnp.transpose(grad_gains, (1, 0, 2)), ((0, 0), (0, 0), (0, 128 - rows))),
            jnp.pad(grad_table, ((0, 0), (0, 9), (0, 128 - HEADS))),
        ],
        axis=1,
    )
    done = finish(
        [
            cross_attended, normed_two, attended, normed_one,
            cross_branch, d_cross_queries, self_branch, d_queries,
            wide, tall,
            d_kv_all.reshape(8, 2, 2, TOK, D),
            d_cross_kv_all.reshape(8, 2, 2, ENC, D),
        ],
        [
            states,
            kv_one,
            kv_two,
            transposed_right(d_queries, query_one),
            d_mid_one,
            decoder_in[0],
            norm_one,
            grad_small,
        ],
        3,
    )
    land, extras, grad_decoder, grad_encoder = done
    (
        grad_out_two, grad_query_two, grad_out_one, grad_query_one,
        grad_key_two, grad_value_two, grad_key_one, grad_value_one,
        grad_gate, grad_up, grad_down,
    ) = unpack(land)
    return (
        block_out[None],
        grad_decoder[None],
        grad_encoder[None],
        extras[0, :rows],
        grad_query_one,
        grad_key_one,
        grad_value_one,
        grad_out_one,
        extras[3:7, :HEADS],
        extras[1, :rows],
        grad_query_two,
        grad_key_two,
        grad_value_two,
        grad_out_two,
        extras[2, :rows],
        grad_gate,
        grad_up,
        grad_down,
    )


def solution(mesh):
    tokens = P("fsdp", "ctx", None)
    matrix = P("fsdp", None)
    vector = P("fsdp")
    weights = (
        (vector,) + (matrix,) * 5 + (vector,) + (matrix,) * 4 + (vector,) + (matrix,) * 3
    )
    return jax.shard_map(
        body,
        mesh=mesh,
        in_specs=(tokens,) * 3 + (P(), P()) + weights,
        out_specs=(tokens,) * 3 + weights,
        check_vma=False,
    )
```

```python
import functools

import jax
import jax.numpy as jnp
from jax import lax
from jax.experimental import pallas as pl
from jax.experimental.pallas import tpu as pltpu
from jax.sharding import PartitionSpec as P

D = 768
FF = 2048
HEADS = 12
HEAD_DIM = 64
PAIRS = HEADS // 2
N_CTX = 16
TOK = 128
ENC = 64
HALF = 64
REACH = 128
BF = jnp.bfloat16
F32 = jnp.float32
MIB = 1024 * 1024


def ctx_place():
    me = lax.axis_index("ctx")
    core = me % 2
    high = (me // 2) % 2
    y = me // 4
    return me, core, high, y


def slot_of(y, shift, high, core):
    return ((y + shift) % 4) * 4 + 2 * high + core


def torus_place():
    me, core, high, y = ctx_place()
    shard = lax.axis_index("fsdp")
    return me, core, high, y, shard // 4, shard % 4


def hop(src, dst, send_sem, recv_sem, ctx, fsdp):
    return pltpu.make_async_remote_copy(
        src_ref=src,
        dst_ref=dst,
        send_sem=send_sem,
        recv_sem=recv_sem,
        device_id={"ctx": ctx, "fsdp": fsdp},
    )


def greet_all(devices):
    barrier = pltpu.get_barrier_semaphore()
    for ctx, fsdp in devices:
        pl.semaphore_signal(barrier, inc=1, device_id={"ctx": ctx, "fsdp": fsdp})
    pl.semaphore_wait(barrier, len(devices))


PACKS = ((0, 1), (2, 3), (4, 5, 6, 7), (8, 9), (10,))


def front_kernel(*refs):
    sources = refs[:11]
    small_ref, token_ref, state_ref = refs[11:14]
    results = refs[14:19]
    small_out, normed_out, query_out, self_result, cross_result = refs[19:24]
    targets = refs[24:29]
    (
        self_out_ref, cross_out_ref, landing, self_ref, cross_ref, send_sem, x_sem, z_sem, core_sem,
        fill_sem, small_sem, self_sem, cross_sem, local_sem,
    ) = refs[29:]
    me, core, high, y, low, x = torus_place()
    shard = low * 4 + x
    sibling = (slot_of(y, 0, high, 1 - core), shard)
    inside = (me, (1 - low) * 4 + x)
    outside = (slot_of(y, 0, 1 - high, core), (1 - low) * 4 + x)
    across = slot_of(y, 0, 1 - high, core)
    rows = [slot_of(y, shift, high, core) for shift in (1, 2, 3)]
    others = [low * 4 + (x + shift) % 4 for shift in (1, 2, 3)]
    peers = [(shard + shift) % 8 for shift in range(1, 8)]
    greet_all(
        [sibling, outside, (across, shard)]
        + [(me, peer) for peer in peers]
        + [(row, shard) for row in rows]
    )
    sends = []

    def send(src, dst, recv_sem, device):
        copy = hop(src, dst, send_sem.at[len(sends)], recv_sem, *device)
        copy.start()
        sends.append(copy)

    def arrived(ref, recv_sem):
        hop(ref, ref, send_sem.at[0], recv_sem, *sibling).wait_recv()

    def bring(src, dst, sem):
        copy = pltpu.make_async_copy(src, dst, sem)
        copy.start()
        return copy


    def part(k, owner, whose, side=None):
        ref = targets[k]
        count = ref.shape[1] // 2
        start = pl.multiple_of(whose * count, 16)
        if side is None:
            return ref.at[owner, pl.ds(start, count), :]
        width = ref.shape[2] // 2
        return ref.at[owner, pl.ds(start, count), pl.ds(side * width, width)]

    def fill(k):
        copies = []
        start = 0
        for source in PACKS[k]:
            width = sources[source].shape[1]
            copies.append(
                bring(
                    sources[source],
                    targets[k].at[shard, :, pl.ds(start, width)],
                    fill_sem.at[source],
                )
            )
            start += width
        return copies

    def send_own(k):
        for copy in fills[k]:
            copy.wait()
        for spot in (1, 0, 2):
            block = part(k, shard, core)
            send(block, block, x_sem.at[k, spot], (me, others[spot]))
        for side, device in enumerate((inside, outside)):
            piece = part(k, shard, core, side)
            send(piece, piece, z_sem.at[k, 3, side], device)


    def pass_x(k):
        for spot in (0, 2, 1):
            owner = low * 4 + (x + 3 - spot) % 4
            block = part(k, owner, core)
            arrived(block, x_sem.at[k, spot])
            for side, device in enumerate((inside, outside)):
                piece = part(k, owner, core, side)
                send(piece, piece, z_sem.at[k, spot, side], device)
            send(block, block, core_sem.at[k, spot], sibling)

    def pass_z(k):
        for spot in (3, 0, 2, 1):
            owner = (1 - low) * 4 + (x + 3 - spot) % 4
            for side in range(2):
                piece = part(k, owner, core, side)
                arrived(piece, z_sem.at[k, spot, side])
                send(piece, piece, core_sem.at[k, 3 + 2 * spot + side], sibling)

    def complete(k):
        for spot in range(3):
            owner = low * 4 + (x + 3 - spot) % 4
            arrived(part(k, owner, 1 - core), core_sem.at[k, spot])
        for spot in range(4):
            owner = (1 - low) * 4 + (x + 3 - spot) % 4
            for side in range(2):
                arrived(part(k, owner, 1 - core, side), core_sem.at[k, 3 + 2 * spot + side])


    def kv_start(src, out, sems):
        send(src, out.at[me], sems.at[me], (across, shard))
        for row in rows:
            send(src, out.at[me], sems.at[me], (row, shard))
        send(src, out.at[me], sems.at[me], sibling)

    def kv_across(out, sems):
        block = out.at[across]
        arrived(block, sems.at[across])
        for row in rows:
            send(block, block, sems.at[across], (row, shard))
        send(block, block, sems.at[across], sibling)

    def kv_rows(out, sems, flip):
        for shift in (1, 3, 2):
            slot = slot_of(y, shift, 1 - high if flip else high, core)
            block = out.at[slot]
            arrived(block, sems.at[slot])
            send(block, block, sems.at[slot], sibling)

    def kv_complete(out, sems):
        for shift in range(4):
            for half in range(2):
                slot = slot_of(y, shift, half, 1 - core)
                arrived(out.at[slot], sems.at[slot])

    fills = [fill(k) for k in range(5)]
    own_small = bring(small_ref, landing.at[shard], local_sem.at[0])
    for spot, peer in enumerate(peers):
        send(small_ref, landing.at[shard], small_sem.at[spot], (me, peer))
    send_own(0)
    send_own(1)
    own_small.wait()
    for spot in range(7):
        arrived(landing.at[(shard + 7 - spot) % 8], small_sem.at[spot])
    small = landing[...]
    small_out[...] = small
    gains = small.astype(F32)
    gain = jnp.concatenate([gains[owner, 0:1, :96] for owner in range(8)], axis=1)
    normed = rms_scaled(token_ref[...].astype(F32), gain)
    normed_out[...] = normed
    pass_x(0)
    send_own(2)
    pass_z(0)
    pass_x(1)
    send_own(3)
    complete(0)
    exits = [bring(targets[0], results[0], local_sem.at[1])]
    for half in range(2):
        weight = targets[0][:, :, half * D : half * D + D].reshape(D, D)
        self_ref[half] = matmul(normed, weight).astype(BF)
    kv_start(self_ref, self_out_ref, self_sem)
    own_self = bring(self_ref, self_out_ref.at[me], local_sem.at[2])
    pass_z(1)
    complete(1)
    exits.append(bring(targets[1], results[1], local_sem.at[4]))
    for half in range(2):
        weight = targets[1][:, :, half * D : half * D + D].reshape(D, D)
        cross_ref[half] = matmul(state_ref[...], weight).astype(BF)
    kv_start(cross_ref, cross_out_ref, cross_sem)
    own_cross = bring(cross_ref, cross_out_ref.at[me], local_sem.at[3])
    pass_x(2)
    send_own(4)
    kv_across(self_out_ref, self_sem)
    pass_z(2)
    kv_across(cross_out_ref, cross_sem)
    pass_x(3)
    kv_rows(self_out_ref, self_sem, False)
    pass_z(3)
    pass_x(4)
    kv_rows(self_out_ref, self_sem, True)
    kv_rows(cross_out_ref, cross_sem, False)
    pass_z(4)
    kv_rows(cross_out_ref, cross_sem, True)
    complete(2)
    exits.append(bring(targets[2], results[2], local_sem.at[5]))
    query_out[...] = matmul(normed, targets[2][:, :, :D].reshape(D, D)).astype(BF)
    own_self.wait()
    own_cross.wait()
    kv_complete(self_out_ref, self_sem)
    exits.append(bring(self_out_ref, self_result, local_sem.at[6]))
    kv_complete(cross_out_ref, cross_sem)
    exits.append(bring(cross_out_ref, cross_result, local_sem.at[7]))
    complete(3)
    exits.append(bring(targets[3], results[3], local_sem.at[8]))
    complete(4)
    exits.append(bring(targets[4], results[4], local_sem.at[9]))
    for copy in sends:
        copy.wait_send()
    for copy in exits:
        copy.wait()


def front(weights, small, tokens, states, collective_id):
    dma = pltpu.SemaphoreType.DMA
    packs = [
        (8, weights[group[0]].shape[0], sum(weights[k].shape[1] for k in group)) for group in PACKS
    ]
    anywhere = pl.BlockSpec(memory_space=pl.ANY)
    inside = pl.BlockSpec(memory_space=pltpu.VMEM)
    return pl.pallas_call(
        front_kernel,
        out_shape=[jax.ShapeDtypeStruct(pack, BF) for pack in packs]
        + [
            jax.ShapeDtypeStruct((8, 16, 128), BF),
            jax.ShapeDtypeStruct((TOK, D), BF),
            jax.ShapeDtypeStruct((TOK, D), BF),
            jax.ShapeDtypeStruct((N_CTX, 2, TOK, D), BF),
            jax.ShapeDtypeStruct((N_CTX, 2, ENC, D), BF),
        ],
        in_specs=[anywhere] * 12 + [inside] * 2,
        out_specs=[anywhere] * 5 + [inside] * 3 + [anywhere] * 2,
        scratch_shapes=[pltpu.VMEM(pack, BF) for pack in packs]
        + [
            pltpu.VMEM((N_CTX, 2, TOK, D), BF),
            pltpu.VMEM((N_CTX, 2, ENC, D), BF),
            pltpu.VMEM((8, 16, 128), BF),
            pltpu.VMEM((2, TOK, D), BF),
            pltpu.VMEM((2, ENC, D), BF),
            dma((5 * 22 + 7 + 30,)),
            dma((5, 3)),
            dma((5, 4, 2)),
            dma((5, 11)),
            dma((11,)),
            dma((7,)),
            dma((N_CTX,)),
            dma((N_CTX,)),
            dma((10,)),
        ],
        compiler_params=pltpu.CompilerParams(
            collective_id=collective_id, has_side_effects=True, vmem_limit_bytes=60 * MIB
        ),
        name="front",
    )(*weights, small, tokens, states)


PIECE = 96
WIDTHS = (D // 2, D // 2, D // 2, D // 2, D, D, FF)
SPAN = sum(WIDTHS)
DOWN = len(WIDTHS)
CHUNKS = DOWN + 1
CROSS_KV, SELF_KV, WIDE = 4, 5, 6
LEFT = (D,) * 4
RIGHT = (D // 2,) * 4


def finish_kernel(*refs):
    lefts = refs[:4]
    rights = refs[4:8]
    wide_ref, down_ref, dkv_ref, dckv_ref = refs[8:12]
    state_ref, kv_ref, ckv_ref, dn_ref, dmid_ref, token_ref, gain_ref, small_ref = refs[12:20]
    early_out, late_out, small_out, decoder_ref, encoder_ref = refs[20:25]
    (
        left_all, right_all, turned, turned_one, turned_state, state_all, s_right, c_right,
        kept, from_z, from_x, via_x, d_z, d_x, d_via,
        s_kept, s_core, s_row, s_via, s_stage, s_high, s_fin,
        c_kept, c_core, c_row, c_via, c_stage, c_high, c_fin,
        small_f32, sm_own, sm_core, sm_z, sm_x, sm_ctx, sm_total,
        packed, from_ctx, land, late_packed, late_from, late_land,
        s_sem, c_sem, fill_sem, act_send, act_recv, late_send, late_recv, z_send, z_recv,
        x_send, x_recv, ctx_send, ctx_recv, pass_send, pass_recv, sm_send, sm_recv, local_sem,
    ) = refs[25:]
    me, core, high, y, low, x = torus_place()
    shard = low * 4 + x
    rank = y * 2 + high
    sibling = (slot_of(y, 0, high, 1 - core), shard)
    inside = (me, (1 - low) * 4 + x)
    outside = (slot_of(y, 0, 1 - high, core), (1 - low) * 4 + x)
    across = (slot_of(y, 0, 1 - high, core), shard)
    others = [low * 4 + (x + shift) % 4 for shift in (1, 2, 3)]
    ahead = (slot_of(y, 1, high, core), shard)
    behind = (slot_of(y, 3, high, core), shard)
    shifts = [(dy, dz) for dy in range(4) for dz in range(2)][1:]
    mates = [((y + dy) % 4) * 2 + (high + dz) % 2 for dy, dz in shifts]
    greet_all(
        [sibling, inside, outside]
        + [(me, other) for other in others]
        + [(mate * 2 + core, shard) for mate in mates]
    )
    sends = []

    def go(src, dst, send_sem, recv_sem, device):
        copy = hop(src, dst, send_sem, recv_sem, *device)
        copy.start()
        sends.append(copy)
        return copy

    def bring(src, dst, sem):
        copy = pltpu.make_async_copy(src, dst, sem)
        copy.start()
        return copy


    def rows_start(source, held, arrived, sem):
        over = []
        local = []
        for spot, shift in enumerate((2, 1, 3, 0)):
            pair = pl.ds(((y + shift) % 4) * 2, 2)
            block = pl.ds(2 * spot, 2)
            over.append(
                go(
                    source.at[pair, 1 - core], arrived.at[block],
                    sem.at[0, spot], sem.at[1, spot], sibling,
                )
            )
            local.append(bring(source.at[pair, core], held.at[block], sem.at[4, spot]))
        return over, local


    def rows_send(copies, held, arrived, via, row, sem):
        over, local = copies
        onward = []
        for spot in range(4):
            local[spot].wait()
            over[spot].wait_recv()
            for block in (2 * spot, 2 * spot + 1):
                for part in range(2):
                    held[block, part] = held[block, part] + arrived[block, part]
            if spot == 0:
                first = go(held.at[0], via.at[0], sem.at[2, 0], sem.at[3, 0], ahead)
                second = go(held.at[1], via.at[1], sem.at[2, 1], sem.at[3, 1], behind)
            elif spot == 1:
                onward.append(go(held.at[3], row.at[0, 1], sem.at[2, 2], sem.at[3, 2], ahead))
            elif spot == 2:
                onward.append(go(held.at[4], row.at[1, 0], sem.at[2, 3], sem.at[3, 3], behind))
        return first, second, onward

    def rows_via(state, held, via, row, sem):
        first, second, onward = state
        first.wait_recv()
        for part in range(2):
            held[2, part] = held[2, part] + via[0, part]
        onward.append(go(held.at[2], row.at[0, 0], sem.at[2, 4], sem.at[3, 4], ahead))
        second.wait_recv()
        for part in range(2):
            held[5, part] = held[5, part] + via[1, part]
        onward.append(go(held.at[5], row.at[1, 1], sem.at[2, 5], sem.at[3, 5], behind))
        return onward

    def rows_total(held, row, half, part):
        return (
            held[6 + half, part].astype(F32)
            + row[0, half, part].astype(F32)
            + row[1, half, part].astype(F32)
        )

    def rows_across(onward, held, row, stage, landing, sem):
        for copy in onward:
            copy.wait_recv()
        for part in range(2):
            stage[part] = rows_total(held, row, 1 - high, part).astype(BF)
        return go(stage, landing, sem.at[2, 6], sem.at[3, 6], across)

    def rows_sum(last, held, row, landing, final, right, which):
        totals = [rows_total(held, row, high, part) for part in range(2)]
        last.wait_recv()
        for part in range(2):
            final[part] = (totals[part] + landing[part].astype(F32)).astype(BF)
        count = final.shape[1]
        copy = go(
            final.at[1 - core], right.at[pl.ds(count, count)],
            late_send.at[which], late_recv.at[which], sibling,
        )
        right[:count] = final[core]
        return copy


    starts = [sum(WIDTHS[:k]) for k in range(len(WIDTHS))]
    left_starts = [sum(LEFT[:k]) for k in range(4)]
    right_starts = [sum(RIGHT[:k]) for k in range(4)]
    acts = {}
    over_z, over_via, over_x = {}, {}, {}
    column_ahead = (me, low * 4 + (x + 1) % 4)
    column_behind = (me, low * 4 + (x + 3) % 4)

    def buffers(k):
        if k == DOWN:
            return d_z, d_x, d_via, pl.ds(0, D // 2)
        return from_z, from_x, via_x, pl.ds(starts[k], WIDTHS[k])

    def acts_start(index):
        left = pl.ds(left_starts[index], LEFT[index])
        right = pl.ds(right_starts[index], RIGHT[index])
        near = pl.ds(pl.multiple_of(core * RIGHT[index], 128), RIGHT[index])
        far = pl.ds(pl.multiple_of((1 - core) * RIGHT[index], 128), RIGHT[index])
        mine = pl.ds(0, TOK)
        theirs = pl.ds(TOK, TOK)
        acts[index] = (
            bring(lefts[index], left_all.at[mine, left], fill_sem.at[index, 0]),
            bring(rights[index].at[:, near], right_all.at[mine, right], fill_sem.at[index, 1]),
            go(
                lefts[index], left_all.at[theirs, left],
                act_send.at[index, 0], act_recv.at[index, 0], sibling,
            ),
            go(
                rights[index].at[:, far], right_all.at[theirs, right],
                act_send.at[index, 1], act_recv.at[index, 1], sibling,
            ),
        )

    def multiply(k, left_ref, right):
        landing, _, _, cut = buffers(k)
        for group in range(2):
            owners = pl.ds(4 * ((1 - low + group) % 2), 4)
            left = left_ref[owners].reshape(4 * PIECE, right.shape[0])
            kept[owners, :, cut] = (
                contract(left, right, ((1,), (0,))).astype(BF).reshape(4, PIECE, WIDTHS[k])
            )
            if group == 0:
                half = PIECE // 2
                over_z[k] = [
                    go(
                        kept.at[owners, pl.ds(side * half, half), cut],
                        landing.at[:, pl.ds(side * half, half), cut],
                        z_send.at[k, side],
                        z_recv.at[k, side],
                        device,
                    )
                    for side, device in enumerate((inside, outside))
                ]

    def make(index):
        near_left, near_right, far_left, far_right = acts[index]
        near_left.wait()
        near_right.wait()
        far_left.wait_recv()
        far_right.wait_recv()
        left = left_all[:, left_starts[index] : left_starts[index] + LEFT[index]].T
        right = right_all[:, right_starts[index] : right_starts[index] + RIGHT[index]]
        target = turned_one if index == 3 else turned
        target[...] = left.reshape(8, PIECE, 2 * TOK)
        multiply(index, target, right)

    def step_z(k):
        landing, _, _, cut = buffers(k)
        for copy in over_z[k]:
            copy.wait_recv()
        for column in range(4):
            landing[column, :, cut] = landing[column, :, cut] + kept[4 * low + column, :, cut]
        send_x(k)


    def send_x(k):
        landing, spread, via, cut = buffers(k)
        half = landing.shape[1] // 2
        upper, lower = pl.ds(0, half), pl.ds(half, half)
        away, front_column, back_column = (x + 2) % 4, (x + 1) % 4, (x + 3) % 4
        over_via[k] = (
            go(
                landing.at[away, upper, cut], via.at[0, :, cut],
                x_send.at[k, 0], x_recv.at[k, 0], column_ahead,
            ),
            go(
                landing.at[away, lower, cut], via.at[1, :, cut],
                x_send.at[k, 1], x_recv.at[k, 1], column_behind,
            ),
        )
        over_x[k] = [
            go(
                landing.at[front_column, lower, cut], spread.at[0, lower, cut],
                x_send.at[k, 2], x_recv.at[k, 2], column_ahead,
            ),
            go(
                landing.at[back_column, upper, cut], spread.at[1, upper, cut],
                x_send.at[k, 3], x_recv.at[k, 3], column_behind,
            ),
        ]

    def step_via(k):
        landing, spread, via, cut = buffers(k)
        half = landing.shape[1] // 2
        upper, lower = pl.ds(0, half), pl.ds(half, half)
        front_column, back_column = (x + 1) % 4, (x + 3) % 4
        over_via[k][0].wait_recv()
        landing[front_column, upper, cut] = landing[front_column, upper, cut] + via[0, :, cut]
        over_x[k].append(
            go(
                landing.at[front_column, upper, cut], spread.at[0, upper, cut],
                x_send.at[k, 4], x_recv.at[k, 4], column_ahead,
            )
        )
        over_via[k][1].wait_recv()
        landing[back_column, lower, cut] = landing[back_column, lower, cut] + via[1, :, cut]
        over_x[k].append(
            go(
                landing.at[back_column, lower, cut], spread.at[1, lower, cut],
                x_send.at[k, 5], x_recv.at[k, 5], column_behind,
            )
        )

    def step_x(k):
        landing, spread, _, cut = buffers(k)
        for copy in over_x[k]:
            copy.wait_recv()
        total = landing[x, :, cut].astype(F32)
        for spot in range(2):
            total = total + spread[spot, :, cut].astype(F32)
        total = total.astype(BF)
        half = D // 2
        if k == WIDE:
            for piece in range(8):
                packed[piece, :PIECE, :256] = total[:, piece * 256 : piece * 256 + 256]
        elif k == DOWN:
            for piece in range(8):
                for part in range(3):
                    packed[piece, part * 32 : part * 32 + 32, 256:] = total[
                        piece * 32 : piece * 32 + 32, part * 128 : part * 128 + 128
                    ]
        else:
            middle = PIECE // 2
            for upper in range(2):
                rows = total[upper * middle : upper * middle + middle, :]
                if k == CROSS_KV or k == SELF_KV:
                    for piece in range(2):
                        late_packed[(0 if k == CROSS_KV else 4) + 2 * piece + upper] = rows[
                            :, piece * half : piece * half + half
                        ]
                else:
                    packed[2 * k + upper, PIECE:, :] = rows


    def mate_device(mate):
        return (mate * 2 + core, shard)

    def ctx_start(which, source, landing):
        return [
            go(
                source.at[mate], landing.at[spot],
                ctx_send.at[which, spot], ctx_recv.at[which, spot], mate_device(mate),
            )
            for spot, mate in enumerate(mates)
        ]

    def ctx_sum(which, over, source, landing, final):
        total = source[rank].astype(F32)
        for spot in range(7):
            over[spot].wait_recv()
            total = total + landing[spot].astype(F32)
        final[rank, core] = total.astype(BF)
        own = final.at[rank, core]
        for spot, mate in enumerate(mates):
            go(own, own, ctx_send.at[which, 7 + spot], ctx_recv.at[which, 7 + rank], mate_device(mate))
        go(own, own, pass_send.at[which, 7], pass_recv.at[which, rank], sibling)

    def landed(ref, recv_sem):
        hop(ref, ref, pass_send.at[0, 0], recv_sem, *sibling).wait_recv()

    def ctx_pass(which, final):
        for spot, mate in enumerate(mates):
            block = final.at[mate, core]
            landed(block, ctx_recv.at[which, 7 + mate])
            go(block, block, pass_send.at[which, spot], pass_recv.at[which, mate], sibling)

    def ctx_done(which, final):
        for mate in [rank] + mates:
            landed(final.at[mate, 1 - core], pass_recv.at[which, mate])

    wide_copy = bring(wide_ref, from_z.at[:, :, pl.ds(starts[WIDE], FF)], local_sem.at[1])
    down_copy = bring(down_ref, d_z, local_sem.at[2])
    s_copies = rows_start(dkv_ref, s_kept, s_core, s_sem)
    c_copies = rows_start(dckv_ref, c_kept, c_core, c_sem)
    for index in range(4):
        acts_start(index)
    state_near = bring(state_ref, state_all.at[pl.ds(0, ENC)], local_sem.at[0])
    state_far = go(
        state_ref, state_all.at[pl.ds(ENC, ENC)], late_send.at[2], late_recv.at[2], sibling
    )
    down_copy.wait()
    send_x(DOWN)
    wide_copy.wait()
    send_x(WIDE)
    s_state = rows_send(s_copies, s_kept, s_core, s_via, s_row, s_sem)
    make(0)
    make(1)
    s_onward = rows_via(s_state, s_kept, s_via, s_row, s_sem)
    c_state = rows_send(c_copies, c_kept, c_core, c_via, c_row, c_sem)
    make(2)
    make(3)
    step_via(DOWN)
    step_via(WIDE)
    for k in range(4):
        step_z(k)
    state_near.wait()
    state_far.wait_recv()
    turned_state[...] = state_all[...].T.reshape(8, PIECE, 2 * ENC)
    s_last = rows_across(s_onward, s_kept, s_row, s_stage, s_high, s_sem)
    c_onward = rows_via(c_state, c_kept, c_via, c_row, c_sem)
    for k in range(4):
        step_via(k)
    step_x(DOWN)
    step_x(WIDE)
    s_far = rows_sum(s_last, s_kept, s_row, s_high, s_fin, s_right, 0)
    for k in range(4):
        step_x(k)
    early = ctx_start(0, packed, from_ctx)
    s_far.wait_recv()
    multiply(SELF_KV, turned_one, s_right[...])
    c_last = rows_across(c_onward, c_kept, c_row, c_stage, c_high, c_sem)
    tokens = token_ref[...].astype(F32)
    d_kv = jnp.concatenate([s_fin[0], s_fin[1]], axis=1)
    grad = dn_ref[...] + contract(d_kv, kv_ref[...], ((1,), (1,)))
    inverse = lax.rsqrt(jnp.mean(tokens * tokens, axis=-1, keepdims=True) + 1e-06)
    small_f32[...] = small_ref[...]
    line = jnp.sum(tokens * inverse * grad, axis=0, keepdims=True)
    for owner in range(8):
        small_f32[owner, 0:1, :96] = line[:, owner * 96 : owner * 96 + 96]
    sm_own[...] = small_f32[...].astype(BF)
    sm_over = go(sm_own, sm_core, sm_send.at[0], sm_recv.at[0], sibling)
    c_far = rows_sum(c_last, c_kept, c_row, c_high, c_fin, c_right, 1)
    c_far.wait_recv()
    multiply(CROSS_KV, turned_state, c_right[...])
    step_z(SELF_KV)
    sm_over.wait_recv()
    sm_own_sum = (sm_own[...].astype(F32) + sm_core[...].astype(F32)).astype(BF)
    sm_over.wait_send()
    sm_own[...] = sm_own_sum
    sm_inside = go(
        sm_own.at[pl.ds(4 * (1 - low), 4)], sm_z, sm_send.at[1], sm_recv.at[1], inside
    )
    ctx_sum(0, early, packed, from_ctx, land)
    step_z(CROSS_KV)
    step_via(SELF_KV)
    sm_inside.wait_recv()
    for column in range(4):
        sm_z[column] = sm_z[column] + sm_own[4 * low + column]
    sm_row = [
        go(
            sm_z.at[(x + spot + 1) % 4], sm_x.at[spot],
            sm_send.at[2 + spot], sm_recv.at[2 + spot], (me, others[spot]),
        )
        for spot in range(3)
    ]
    step_via(CROSS_KV)
    scaled = gain_ref[...] * grad
    mixed = jnp.mean(tokens * scaled, axis=-1, keepdims=True)
    decoder_ref[...] = (
        dmid_ref[...] + inverse * scaled - tokens * (inverse * inverse * inverse * mixed)
    )
    step_x(SELF_KV)
    step_x(CROSS_KV)
    late = ctx_start(1, late_packed, late_from)
    sm_sum = sm_z[x].astype(F32)
    for spot in range(3):
        sm_row[spot].wait_recv()
        sm_sum = sm_sum + sm_x[spot].astype(F32)
    sm_total[...] = sm_sum.astype(BF)
    sm_mates = [
        go(sm_total, sm_ctx.at[spot], sm_send.at[5 + spot], sm_recv.at[5 + spot], mate_device(mate))
        for spot, mate in enumerate(mates)
    ]
    ctx_pass(0, land)
    ctx_sum(1, late, late_packed, late_from, late_land)
    d_ckv = jnp.concatenate([c_fin[0], c_fin[1]], axis=1)
    encoder_ref[...] = contract(d_ckv, ckv_ref[...], ((1,), (1,)))
    sm_sum = sm_total[...].astype(F32)
    for spot in range(7):
        sm_mates[spot].wait_recv()
        sm_sum = sm_sum + sm_ctx[spot].astype(F32)
    small_out[...] = sm_sum
    ctx_done(0, land)
    early_out[...] = land[...]
    ctx_pass(1, late_land)
    ctx_done(1, late_land)
    late_out[...] = late_land[...]
    for copy in sends:
        if copy is not sm_over:
            copy.wait_send()


def unpack_kernel(early, late, *refs):
    square_refs = refs[:8]
    gate_ref, up_ref, down_ref = refs[8:]
    half = D // 2
    middle = PIECE // 2
    for side in range(2):
        columns = slice(side * half, side * half + half)
        for upper in range(2):
            rows = slice(upper * middle, upper * middle + middle)
            for k in range(4):
                square_refs[k][rows, columns] = early[2 * k + upper, side, PIECE:, :].astype(F32)
            for k in range(2):
                for piece in range(2):
                    square_refs[4 + 2 * k + side][rows, piece * half : piece * half + half] = late[
                        4 * k + 2 * piece + upper, side
                    ].astype(F32)
        target = up_ref if side else gate_ref
        for piece in range(8):
            target[:, piece * 256 : piece * 256 + 256] = early[piece, side, :PIECE, :256].astype(F32)
            for part in range(3):
                down_ref[
                    piece * 32 : piece * 32 + 32,
                    side * half + part * 128 : side * half + part * 128 + 128,
                ] = early[piece, side, part * 32 : part * 32 + 32, 256:].astype(F32)


def unpack(early, late):
    outs = (
        [jax.ShapeDtypeStruct((PIECE, D), F32)] * 8
        + [jax.ShapeDtypeStruct((PIECE, FF), F32)] * 2
        + [jax.ShapeDtypeStruct((FF // 8, D), F32)]
    )
    return pl.pallas_call(
        unpack_kernel,
        out_shape=outs,
        in_specs=[pl.BlockSpec(memory_space=pltpu.VMEM)] * 2,
        out_specs=[pl.BlockSpec(memory_space=pltpu.VMEM)] * len(outs),
        compiler_params=pltpu.CompilerParams(vmem_limit_bytes=24 * MIB),
        name="unpack",
    )(early, late)


def finish(far, near, collective_id):
    dma = pltpu.SemaphoreType.DMA

    def rows(count):
        return [
            pltpu.VMEM((8, 2, count, D), BF),
            pltpu.VMEM((8, 2, count, D), BF),
            pltpu.VMEM((2, 2, 2, count, D), BF),
            pltpu.VMEM((2, 2, count, D), BF),
            pltpu.VMEM((2, count, D), BF),
            pltpu.VMEM((2, count, D), BF),
            pltpu.VMEM((2, count, D), BF),
        ]

    outs = [
        jax.ShapeDtypeStruct((8, 2, 3 * PIECE // 2, D // 2), BF),
        jax.ShapeDtypeStruct((8, 2, PIECE // 2, D // 2), BF),
        jax.ShapeDtypeStruct((16, 128), F32),
        jax.ShapeDtypeStruct((TOK, D), F32),
        jax.ShapeDtypeStruct((ENC, D), F32),
    ]
    return pl.pallas_call(
        finish_kernel,
        out_shape=outs,
        in_specs=[pl.BlockSpec(memory_space=pl.ANY)] * len(far)
        + [pl.BlockSpec(memory_space=pltpu.VMEM)] * len(near),
        out_specs=[pl.BlockSpec(memory_space=pltpu.VMEM)] * len(outs),
        scratch_shapes=[
            pltpu.VMEM((2 * TOK, sum(LEFT)), BF),
            pltpu.VMEM((2 * TOK, sum(RIGHT)), BF),
            pltpu.VMEM((8, PIECE, 2 * TOK), BF),
            pltpu.VMEM((8, PIECE, 2 * TOK), BF),
            pltpu.VMEM((8, PIECE, 2 * ENC), BF),
            pltpu.VMEM((2 * ENC, D), BF),
            pltpu.VMEM((2 * TOK, D), BF),
            pltpu.VMEM((2 * ENC, D), BF),
            pltpu.VMEM((8, PIECE, SPAN - FF), BF),
            pltpu.VMEM((4, PIECE, SPAN), BF),
            pltpu.VMEM((2, PIECE, SPAN), BF),
            pltpu.VMEM((2, PIECE // 2, SPAN), BF),
            pltpu.VMEM((4, FF // 8, D // 2), BF),
            pltpu.VMEM((2, FF // 8, D // 2), BF),
            pltpu.VMEM((2, FF // 16, D // 2), BF),
        ]
        + rows(TOK)
        + rows(ENC)
        + [
            pltpu.VMEM((8, 16, 128), F32),
            pltpu.VMEM((8, 16, 128), BF),
            pltpu.VMEM((8, 16, 128), BF),
            pltpu.VMEM((4, 16, 128), BF),
            pltpu.VMEM((3, 16, 128), BF),
            pltpu.VMEM((7, 16, 128), BF),
            pltpu.VMEM((16, 128), BF),
            pltpu.VMEM((8, 3 * PIECE // 2, D // 2), BF),
            pltpu.VMEM((7, 3 * PIECE // 2, D // 2), BF),
            pltpu.VMEM((8, 2, 3 * PIECE // 2, D // 2), BF),
            pltpu.VMEM((8, PIECE // 2, D // 2), BF),
            pltpu.VMEM((7, PIECE // 2, D // 2), BF),
            pltpu.VMEM((8, 2, PIECE // 2, D // 2), BF),
            dma((5, 7)),
            dma((5, 7)),
            dma((4, 2)),
            dma((4, 2)),
            dma((4, 2)),
            dma((3,)),
            dma((3,)),
            dma((CHUNKS, 2)),
            dma((CHUNKS, 2)),
            dma((CHUNKS, 6)),
            dma((CHUNKS, 6)),
            dma((2, 14)),
            dma((2, 15)),
            dma((2, 8)),
            dma((2, 8)),
            dma((12,)),
            dma((12,)),
            dma((3,)),
        ],
        compiler_params=pltpu.CompilerParams(
            collective_id=collective_id, has_side_effects=True, vmem_limit_bytes=62 * MIB
        ),
        name="finish_gradients",
    )(*far, *near)


def split_heads(block):
    lane = lax.broadcasted_iota(jnp.int32, block.shape, 1)
    nothing = jnp.zeros_like(block)
    return jnp.concatenate(
        [jnp.where(lane < HEAD_DIM, block, nothing), jnp.where(lane < HEAD_DIM, nothing, block)],
        axis=0,
    )


def join_heads(transposed):
    row = lax.broadcasted_iota(jnp.int32, (2 * HEAD_DIM, TOK), 0)
    return jnp.where(row < HEAD_DIM, transposed[:, :TOK], transposed[:, TOK:]).T


def contract(left, right, dims):
    return lax.dot_general(left, right, (dims, ((), ())), preferred_element_type=F32)


def key_chunk(ref, j):
    if ref.shape[2] == 2 * HALF:
        return ref[j, 0]
    return ref[pl.ds(2 * j, 2), 0].reshape(2 * HALF, 2 * HEAD_DIM)


def bias_chunk(class_ref, tile_ref, j):
    lane = lax.broadcasted_iota(jnp.int32, (HALF, TOK), 1)
    rows = []
    for half in range(2):
        spot = 2 * j + half
        near = class_ref[0, spot]
        far = class_ref[1, spot]
        rows.append(
            jnp.concatenate(
                [
                    jnp.where(lane < HALF, tile_ref[head, near], tile_ref[head, far])
                    for head in range(2)
                ],
                axis=1,
            )
        )
    return jnp.concatenate(rows, axis=0)


def fold(values, join):
    return join(values.reshape(-1, 8, values.shape[-1]), axis=0)


def forward_kernel(biased, *refs):
    if biased:
        class_ref, q_ref, k_ref, v_ref, tile_ref, out_ref, total_ref, score_ref, share_ref = refs
    else:
        q_ref, k_ref, v_ref, out_ref, total_ref, score_ref, share_ref = refs
    chunks = score_ref.shape[0]
    queries = split_heads(q_ref[...])
    highest = None
    for j in range(chunks):
        scores = contract(key_chunk(k_ref, j), queries, ((1,), (1,)))
        if biased:
            scores = scores + bias_chunk(class_ref, tile_ref, j)
        score_ref[j] = scores
        top = fold(scores, jnp.max)
        highest = top if highest is None else jnp.maximum(highest, top)
    highest = jnp.max(highest, axis=0, keepdims=True)
    summed = jnp.zeros((8, 2 * TOK), F32)
    for j in range(chunks):
        raised = jnp.exp(score_ref[j] - highest)
        summed = summed + fold(raised, jnp.sum)
        share_ref[j] = raised.astype(BF)
    summed = jnp.sum(summed, axis=0, keepdims=True)
    values = jnp.concatenate([key_chunk(v_ref, j) for j in range(chunks)], axis=0)
    mixed = contract(values, share_ref[...].reshape(-1, 2 * TOK), ((0,), (0,)))
    out_ref[...] = join_heads(mixed / summed).astype(BF)
    total_ref[0] = jnp.broadcast_to(highest + jnp.log(summed), (8, 2 * TOK))


def backward_kernel(biased, *refs):
    if biased:
        class_ref, near_ref, q_ref, k_ref, v_ref, g_ref, total_ref, tile_ref = refs[:8]
        dq_ref, dkv_ref, strip_ref, share_ref, slope_ref, share_low, slope_low = refs[8:]
    else:
        q_ref, k_ref, v_ref, g_ref, total_ref = refs[:5]
        dq_ref, dkv_ref, share_ref, slope_ref, share_low, slope_low = refs[5:]
    chunks = share_ref.shape[0]
    queries = split_heads(q_ref[...])
    grads = split_heads(g_ref[...])
    totals = total_ref[0, 0:1]
    inner = jnp.zeros((8, 2 * TOK), F32)
    for j in range(chunks):
        scores = contract(key_chunk(k_ref, j), queries, ((1,), (1,)))
        if biased:
            scores = scores + bias_chunk(class_ref, tile_ref, j)
        shares = jnp.exp(scores - totals)
        slopes = contract(key_chunk(v_ref, j), grads, ((1,), (1,)))
        inner = inner + fold(shares * slopes, jnp.sum)
        share_ref[j] = shares
        slope_ref[j] = slopes
        share_low[j] = shares.astype(BF)
    inner = jnp.sum(inner, axis=0, keepdims=True)
    for j in range(chunks):
        grad = share_ref[j] * (slope_ref[j] - inner)
        if biased:
            slope_ref[j] = grad
        slope_low[j] = grad.astype(BF)
    keys = jnp.concatenate([key_chunk(k_ref, j) for j in range(chunks)], axis=0)
    low = slope_low[...].reshape(-1, 2 * TOK)
    dq_ref[...] = join_heads(contract(keys, low, ((0,), (0,)))).astype(BF)
    shape = dkv_ref.shape
    block = (shape[0], shape[2], shape[3])
    dkv_ref[:, 0] = contract(low, queries, ((1,), (0,))).astype(BF).reshape(block)
    dkv_ref[:, 1] = (
        contract(share_low[...].reshape(-1, 2 * TOK), grads, ((1,), (0,))).astype(BF).reshape(block)
    )
    if biased:
        lane = lax.broadcasted_iota(jnp.int32, (HALF, TOK), 1)
        for gap in range(3):
            pieces = []
            for half in range(2):
                spot = near_ref[half, gap]
                held = slope_ref[jnp.maximum(spot, 0) // 2, pl.ds(
                    pl.multiple_of((jnp.maximum(spot, 0) % 2) * HALF, HALF), HALF)]
                pieces.append(jnp.where(spot >= 0, held, jnp.zeros_like(held)))
            for head in range(2):
                cut = slice(head * TOK, (head + 1) * TOK)
                strip_ref[head, gap] = jnp.where(lane < HALF, pieces[0][:, cut], pieces[1][:, cut])


def pair_columns(pair):
    return (0, pair)


def kv_spec(rows, row_block, part):
    return pl.BlockSpec(
        (N_CTX, 1, rows, 2 * HEAD_DIM), lambda pair: (0, part, row_block, pair)
    )


SMEM_SPEC = pl.BlockSpec(memory_space=pltpu.SMEM)
TILE_SPEC = pl.BlockSpec((2, 5, HALF, TOK), lambda pair: (pair, 0, 0, 0))
TOTAL_SPEC = pl.BlockSpec((1, 8, 2 * TOK), lambda pair: (pair, 0, 0))
ROW_SPEC = pl.BlockSpec((TOK, 2 * HEAD_DIM), pair_columns)
LOCAL = pltpu.CompilerParams(vmem_limit_bytes=48 * MIB)


def attend(queries, gathered, rows, row_block, classes=None, tiles=None):
    biased = classes is not None
    chunks = N_CTX * rows // TOK
    specs = [ROW_SPEC, kv_spec(rows, row_block, 0), kv_spec(rows, row_block, 1)]
    operands = [queries, gathered, gathered]
    if biased:
        specs = [SMEM_SPEC] + specs + [TILE_SPEC]
        operands = [classes] + operands + [tiles]
    return pl.pallas_call(
        functools.partial(forward_kernel, biased),
        grid=(PAIRS,),
        in_specs=specs,
        out_specs=[ROW_SPEC, TOTAL_SPEC],
        out_shape=[
            jax.ShapeDtypeStruct((TOK, D), BF),
            jax.ShapeDtypeStruct((PAIRS, 8, 2 * TOK), F32),
        ],
        scratch_shapes=[
            pltpu.VMEM((chunks, TOK, 2 * TOK), F32),
            pltpu.VMEM((chunks, TOK, 2 * TOK), BF),
        ],
        compiler_params=LOCAL,
        cost_estimate=pl.CostEstimate(flops=10**9, bytes_accessed=10**7, transcendentals=10**6),
        name="attend_self" if biased else "attend_cross",
    )(*operands)


def attend_back(queries, gathered, grads, totals, rows, row_block, classes=None, near=None, tiles=None):
    biased = classes is not None
    chunks = N_CTX * rows // TOK
    specs = [ROW_SPEC, kv_spec(rows, row_block, 0), kv_spec(rows, row_block, 1), ROW_SPEC, TOTAL_SPEC]
    operands = [queries, gathered, gathered, grads, totals]
    out_specs = [
        ROW_SPEC,
        pl.BlockSpec((N_CTX, 2, rows, 2 * HEAD_DIM), lambda pair: (0, 0, 0, pair)),
    ]
    out_shape = [
        jax.ShapeDtypeStruct((TOK, D), BF),
        jax.ShapeDtypeStruct((N_CTX, 2, rows, D), BF),
    ]
    if biased:
        specs = [SMEM_SPEC, SMEM_SPEC] + specs + [TILE_SPEC]
        operands = [classes, near] + operands + [tiles]
        out_specs.append(pl.BlockSpec((2, 3, HALF, TOK), lambda pair: (pair, 0, 0, 0)))
        out_shape.append(jax.ShapeDtypeStruct((HEADS, 3, HALF, TOK), F32))
    return pl.pallas_call(
        functools.partial(backward_kernel, biased),
        grid=(PAIRS,),
        in_specs=specs,
        out_specs=out_specs,
        out_shape=out_shape,
        scratch_shapes=[
            pltpu.VMEM((chunks, TOK, 2 * TOK), F32),
            pltpu.VMEM((chunks, TOK, 2 * TOK), F32),
            pltpu.VMEM((chunks, TOK, 2 * TOK), BF),
            pltpu.VMEM((chunks, TOK, 2 * TOK), BF),
        ],
        compiler_params=LOCAL,
        cost_estimate=pl.CostEstimate(flops=1000, bytes_accessed=1000, transcendentals=0),
        name="attend_self_back" if biased else "attend_cross_back",
    )(*operands)


def matmul(left, right):
    return jnp.dot(left, right, preferred_element_type=F32)


def transposed_left(left, right):
    return contract(left, right, ((0,), (0,)))


def transposed_right(left, right):
    return contract(left, right, ((1,), (1,)))


def rms_scaled(values, gain):
    inverse = lax.rsqrt(jnp.mean(values * values, axis=-1, keepdims=True) + 1e-06)
    return (values * inverse * gain).astype(BF)


def rms_back(values, gain, grad):
    inverse = lax.rsqrt(jnp.mean(values * values, axis=-1, keepdims=True) + 1e-06)
    scaled = gain * grad
    mixed = jnp.mean(values * scaled, axis=-1, keepdims=True)
    grad_values = inverse * scaled - values * (inverse * inverse * inverse * mixed)
    return grad_values, jnp.sum(values * inverse * grad, axis=0)


def gelu_product(gate_part, up_part):
    return jax.nn.gelu(gate_part, approximate=True) * up_part


def near_hot():
    shape = (REACH, 3 * HALF * HALF)
    spot = lax.broadcasted_iota(jnp.int32, shape, 1)
    gap = spot // (HALF * HALF)
    key = (spot // HALF) % HALF
    row = spot % HALF
    distance = jnp.clip(HALF * gap + row - key, 0, REACH - 1)
    return (distance == lax.broadcasted_iota(jnp.int32, shape, 0)).astype(BF)


def bias_tiles(bias_rows):
    near = matmul(bias_rows.astype(BF), near_hot()).reshape(HEADS, 3, HALF, HALF)
    key = jnp.arange(HALF, dtype=jnp.int32)[:, None]
    row = jnp.arange(HALF, dtype=jnp.int32)[None, :]
    barred = (jnp.arange(3) == 0)[None, :, None, None] & (key > row)[None, None]
    near = jnp.where(barred, -1e30, near)
    far = jnp.broadcast_to(bias_rows[:, -1][:, None, None, None], (HEADS, 1, HALF, HALF))
    none = jnp.full((HEADS, 1, HALF, HALF), -1e30, F32)
    tiles = jnp.concatenate([near, far, none], axis=1)
    return jnp.concatenate([tiles, tiles], axis=-1)


def bias_sums(strips):
    tiles = (strips[..., :HALF] + strips[..., HALF:]).reshape(HEADS, -1)
    high = tiles.astype(BF)
    low = (tiles - high.astype(F32)).astype(BF)
    hot = near_hot()
    sums = transposed_right(high, hot) + transposed_right(low, hot)
    far = -jnp.sum(sums[:, :-1], axis=1, keepdims=True)
    return jnp.concatenate([sums[:, :-1], far], axis=1)


def swap(values, move):
    perm = []
    for ctx in range(N_CTX):
        for shard in range(8):
            there, owner = move(ctx, shard)
            perm.append((ctx * 8 + shard, there * 8 + owner))
    return lax.ppermute(values, ("ctx", "fsdp"), perm)


def feed_gradients(normed, hidden, d_gate, d_up, upstream):
    first = lax.axis_index("ctx") % 2 == 0
    low = lax.axis_index("fsdp") // 4
    half = D // 2
    near = jnp.where(first, d_gate, d_up)
    far = jnp.where(first, d_up, d_gate)
    near_grad = jnp.where(first, upstream[:, :half], upstream[:, half:])
    far_grad = jnp.where(first, upstream[:, half:], upstream[:, :half])
    other = swap(
        jnp.concatenate([normed, hidden, far, far_grad], axis=1), lambda ctx, shard: (ctx ^ 1, shard)
    )
    lefts = jnp.concatenate([normed, other[:, :D]], axis=0)
    rights = jnp.concatenate([near, other[:, D + FF : D + 2 * FF]], axis=0)
    wide = transposed_left(lefts, rights).astype(BF).reshape(8, PIECE, FF)
    lefts = jnp.concatenate([hidden, other[:, D : D + FF]], axis=0)
    rights = jnp.concatenate([near_grad, other[:, D + 2 * FF :]], axis=0)
    tall = transposed_left(lefts, rights).astype(BF).reshape(8, FF // 8, half)

    def cut(part):
        middle = part.shape[1] // 2
        away = lax.dynamic_slice_in_dim(part, 4 * (1 - low), 4, 0)
        mine = lax.dynamic_slice_in_dim(part, 4 * low, 4, 0)
        return mine, away[:, :middle], away[:, middle:]

    return cut(wide), cut(tall)


def over_z(mine, upper, lower):
    inner = swap(upper, lambda ctx, shard: (ctx, (shard + 4) % 8))
    outer = swap(lower, lambda ctx, shard: (ctx ^ 2, (shard + 4) % 8))
    return mine, inner, outer


def body(
    decoder_in,
    encoder_states,
    out_grad,
    block_pairs,
    bucket_table,
    gain_self,
    self_query,
    self_key,
    self_value,
    self_out,
    position_bias,
    gain_cross,
    cross_query,
    cross_key,
    cross_value,
    cross_out,
    gain_feed,
    feed_gate,
    feed_up,
    feed_down,
):
    me = lax.axis_index("ctx")
    rows = self_query.shape[0]
    small = jnp.concatenate(
        [
            jnp.pad(jnp.stack([gain_self, gain_cross, gain_feed]), ((0, 0), (0, 128 - rows))),
            jnp.pad(position_bias, ((0, 9), (0, 128 - HEADS))),
        ],
        axis=0,
    )
    kv_one, kv_two, square, gate_up, down, small, normed_one, queries, self_kv, cross_kv = front(
        [
            self_key, self_value, cross_key, cross_value,
            self_query, self_out, cross_query, cross_out,
            feed_gate, feed_up, feed_down,
        ],
        small,
        decoder_in[0],
        encoder_states[0],
        0,
    )
    kv_one = kv_one.reshape(D, 2 * D)
    kv_two = kv_two.reshape(D, 2 * D)
    square = square.reshape(D, 4 * D)
    gate_up = gate_up.reshape(D, 2 * FF)
    down = down.reshape(FF, D)
    query_one, out_one, query_two, out_two = (square[:, k * D : k * D + D] for k in range(4))
    gains = jnp.transpose(small[:, :3, :rows], (1, 0, 2)).reshape(3, D).astype(F32)
    norm_one, norm_two, norm_three = gains[0:1], gains[1:2], gains[2:3]
    table = small[:, 3:7, :HEADS].reshape(32, HEADS)

    bucket_hot = (bucket_table[:, None] == jnp.arange(32, dtype=jnp.int32)[None, :]).astype(BF)
    bias_rows = transposed_right(table.T, bucket_hot)
    tiles = bias_tiles(bias_rows)
    pair = block_pairs[me]
    query_blocks = jnp.stack([pair, 31 - pair])
    key_blocks = jnp.stack([block_pairs, 31 - block_pairs], axis=1).reshape(-1)
    gaps = query_blocks[:, None] - key_blocks[None, :]
    classes = jnp.where(gaps < 0, 4, jnp.minimum(gaps, 3)).astype(jnp.int32)
    wanted = query_blocks[:, None] - jnp.arange(3, dtype=jnp.int32)[None, :]
    near = jnp.max(
        jnp.where(
            wanted[:, :, None] == key_blocks[None, None, :],
            jnp.arange(32, dtype=jnp.int32)[None, None, :],
            -1,
        ),
        axis=-1,
    )

    tokens = decoder_in[0].astype(F32)
    states = encoder_states[0]
    upstream = out_grad[0]
    attended, self_totals = attend(queries, self_kv, TOK, 0, classes, tiles)
    mid_one = tokens + matmul(attended, out_one)
    normed_two = rms_scaled(mid_one, norm_two)
    cross_queries = matmul(normed_two, query_two).astype(BF)
    cross_attended, cross_totals = attend(cross_queries, cross_kv, ENC, 0)
    mid_two = mid_one + matmul(cross_attended, out_two)
    normed_three = rms_scaled(mid_two, norm_three)
    gate_up_values = matmul(normed_three, gate_up).astype(BF).astype(F32)
    gate_values, up_values = gate_up_values[:, :FF], gate_up_values[:, FF:]
    hidden, pull_feed = jax.vjp(gelu_product, gate_values, up_values)
    hidden = hidden.astype(BF)
    block_out = mid_two + matmul(hidden, down)

    d_hidden = transposed_right(upstream, down)
    d_gate, d_up = (part.astype(BF) for part in pull_feed(d_hidden))
    d_gate_up = jnp.concatenate([d_gate, d_up], axis=1)
    feed_parts = feed_gradients(normed_three, hidden, d_gate, d_up, upstream)
    d_normed_three = transposed_right(d_gate_up, gate_up)
    part_three, grad_norm_three = rms_back(mid_two, norm_three, d_normed_three)
    d_mid_two = upstream.astype(F32) + part_three
    cross_branch = d_mid_two.astype(BF)
    d_cross_attended = transposed_right(cross_branch, out_two).astype(BF)
    feed_parts, d_cross_attended = lax.optimization_barrier((feed_parts, d_cross_attended))
    feed_parts = [over_z(*parts) for parts in feed_parts]
    d_cross_queries, d_cross_kv_all = attend_back(
        cross_queries, cross_kv, d_cross_attended, cross_totals, ENC, 0
    )
    d_normed_two = transposed_right(d_cross_queries, query_two)
    part_two, grad_norm_two = rms_back(mid_one, norm_two, d_normed_two)
    d_mid_one = d_mid_two + part_two
    self_branch = d_mid_one.astype(BF)
    d_attended = transposed_right(self_branch, out_one).astype(BF)
    feed_parts[1], d_attended = lax.optimization_barrier((feed_parts[1], d_attended))
    d_queries, d_kv_all, strips = attend_back(
        queries, self_kv, d_attended, self_totals, TOK, 0, classes, near, tiles
    )
    feed_parts, d_queries, d_kv_all, strips = lax.optimization_barrier(
        (feed_parts, d_queries, d_kv_all, strips)
    )
    wide, tall = (
        mine + jnp.concatenate([inner, outer], axis=1) for mine, inner, outer in feed_parts
    )
    grad_table = matmul(bias_sums(strips), bucket_hot.astype(F32)).T.reshape(8, 4, HEADS)
    grad_gains = jnp.stack([grad_norm_two, grad_norm_three]).reshape(2, 8, rows)
    grad_small = jnp.concatenate(
        [
            jnp.zeros((8, 1, 128), F32),
            jnp.pad(jnp.transpose(grad_gains, (1, 0, 2)), ((0, 0), (0, 0), (0, 128 - rows))),
            jnp.pad(grad_table, ((0, 0), (0, 9), (0, 128 - HEADS))),
        ],
        axis=1,
    )
    done = finish(
        [
            cross_attended, normed_two, attended, normed_one,
            cross_branch, d_cross_queries, self_branch, d_queries,
            wide, tall,
            d_kv_all.reshape(8, 2, 2, TOK, D),
            d_cross_kv_all.reshape(8, 2, 2, ENC, D),
        ],
        [
            states,
            kv_one,
            kv_two,
            transposed_right(d_queries, query_one),
            d_mid_one,
            decoder_in[0],
            norm_one,
            grad_small,
        ],
        3,
    )
    early, late, extras, grad_decoder, grad_encoder = done
    (
        grad_out_two, grad_query_two, grad_out_one, grad_query_one,
        grad_key_two, grad_value_two, grad_key_one, grad_value_one,
        grad_gate, grad_up, grad_down,
    ) = unpack(early, late)
    return (
        block_out[None],
        grad_decoder[None],
        grad_encoder[None],
        extras[0, :rows],
        grad_query_one,
        grad_key_one,
        grad_value_one,
        grad_out_one,
        extras[3:7, :HEADS],
        extras[1, :rows],
        grad_query_two,
        grad_key_two,
        grad_value_two,
        grad_out_two,
        extras[2, :rows],
        grad_gate,
        grad_up,
        grad_down,
    )


def solution(mesh):
    tokens = P("fsdp", "ctx", None)
    matrix = P("fsdp", None)
    vector = P("fsdp")
    weights = (
        (vector,) + (matrix,) * 5 + (vector,) + (matrix,) * 4 + (vector,) + (matrix,) * 3
    )
    return jax.shard_map(
        body,
        mesh=mesh,
        in_specs=(tokens,) * 3 + (P(), P()) + weights,
        out_specs=(tokens,) * 3 + weights,
        check_vma=False,
    )
```

```python
import functools

import jax
import jax.numpy as jnp
from jax import lax
from jax.experimental import pallas as pl
from jax.experimental.pallas import tpu as pltpu
from jax.sharding import PartitionSpec as P

D = 768
FF = 2048
HEADS = 12
HEAD_DIM = 64
PAIRS = HEADS // 2
N_CTX = 16
TOK = 128
ENC = 64
HALF = 64
REACH = 128
BF = jnp.bfloat16
F32 = jnp.float32
MIB = 1024 * 1024


def ctx_place():
    me = lax.axis_index("ctx")
    core = me % 2
    high = (me // 2) % 2
    y = me // 4
    return me, core, high, y


def slot_of(y, shift, high, core):
    return ((y + shift) % 4) * 4 + 2 * high + core


def split_heads(block):
    lane = lax.broadcasted_iota(jnp.int32, block.shape, 1)
    nothing = jnp.zeros_like(block)
    return jnp.concatenate(
        [jnp.where(lane < HEAD_DIM, block, nothing), jnp.where(lane < HEAD_DIM, nothing, block)],
        axis=0,
    )


def join_heads(transposed):
    row = lax.broadcasted_iota(jnp.int32, (2 * HEAD_DIM, TOK), 0)
    return jnp.where(row < HEAD_DIM, transposed[:, :TOK], transposed[:, TOK:]).T


def contract(left, right, dims):
    return lax.dot_general(left, right, (dims, ((), ())), preferred_element_type=F32)


def key_chunk(ref, j):
    if ref.shape[2] == 2 * HALF:
        return ref[j, 0]
    return ref[pl.ds(2 * j, 2), 0].reshape(2 * HALF, 2 * HEAD_DIM)


def bias_chunk(class_ref, tile_ref, j, first=0):
    lane = lax.broadcasted_iota(jnp.int32, (HALF, TOK), 1)
    rows = []
    for half in range(2):
        spot = 2 * j + half
        near = class_ref[0, spot]
        far = class_ref[1, spot]
        rows.append(
            jnp.concatenate(
                [
                    jnp.where(lane < HALF, tile_ref[first + head, near], tile_ref[first + head, far])
                    for head in range(2)
                ],
                axis=1,
            )
        )
    return jnp.concatenate(rows, axis=0)


def fold(values, join):
    return join(values.reshape(-1, 8, values.shape[-1]), axis=0)


def attend_pair(queries, keys, values, bias, score_ref, share_ref, chunks):
    queries = split_heads(queries)
    highest = None
    for j in range(chunks):
        scores = contract(keys(j), queries, ((1,), (1,)))
        if bias is not None:
            scores = scores + bias(j)
        score_ref[j] = scores
        top = fold(scores, jnp.max)
        highest = top if highest is None else jnp.maximum(highest, top)
    highest = jnp.max(highest, axis=0, keepdims=True)
    summed = jnp.zeros((8, 2 * TOK), F32)
    for j in range(chunks):
        raised = jnp.exp(score_ref[j] - highest)
        summed = summed + fold(raised, jnp.sum)
        share_ref[j] = raised.astype(BF)
    summed = jnp.sum(summed, axis=0, keepdims=True)
    gathered = jnp.concatenate([values(j) for j in range(chunks)], axis=0)
    mixed = contract(gathered, share_ref[:chunks].reshape(-1, 2 * TOK), ((0,), (0,)))
    return join_heads(mixed / summed).astype(BF), highest + jnp.log(summed)


def attend_pairs(first, last, kv_ref, query_ref, out_ref, total_ref, score_ref, share_ref, bias=None):
    rows = kv_ref.shape[2]
    chunks = N_CTX * rows // TOK

    def step(pair, carry):
        cut = pl.ds(pl.multiple_of(pair * TOK, TOK), TOK)

        def chunk(part, j):
            if rows == TOK:
                return kv_ref[j, part, :, cut]
            return kv_ref[2 * j : 2 * j + 2, part, :, cut].reshape(TOK, TOK)

        mixed, total = attend_pair(
            query_ref[:, cut],
            functools.partial(chunk, 0),
            functools.partial(chunk, 1),
            None if bias is None else functools.partial(bias, pair),
            score_ref,
            share_ref,
            chunks,
        )
        out_ref[:, cut] = mixed
        total_ref[pair] = jnp.broadcast_to(total, (8, 2 * TOK))
        return carry

    lax.fori_loop(first, last, step, 0)


def build_tiles(bias_rows, strips, tile_ref):
    lane = lax.broadcasted_iota(jnp.int32, (HALF, TOK), 1)
    key = lax.broadcasted_iota(jnp.int32, (HALF, TOK), 0)
    row = jnp.where(lane < HALF, lane, lane - HALF)
    for head in range(HEADS):
        for gap in range(3):
            strip = strips[head : head + 1, gap * TOK : gap * TOK + TOK]
            turned = pltpu.roll(
                jnp.broadcast_to(strip, (HALF, TOK)), 65, 1, stride=1, stride_axis=0
            )
            tile = jnp.where(lane < HALF, turned, pltpu.roll(turned, HALF, 1))
            if gap == 0:
                tile = jnp.where(key > row, -1e30, tile)
            tile_ref[head, gap] = tile
        tile_ref[head, 3] = jnp.broadcast_to(bias_rows[head : head + 1, REACH - 1 :], (HALF, TOK))
        tile_ref[head, 4] = jnp.full((HALF, TOK), -1e30, F32)


def torus_place():
    me, core, high, y = ctx_place()
    shard = lax.axis_index("fsdp")
    return me, core, high, y, shard // 4, shard % 4


def hop(src, dst, send_sem, recv_sem, ctx, fsdp):
    return pltpu.make_async_remote_copy(
        src_ref=src,
        dst_ref=dst,
        send_sem=send_sem,
        recv_sem=recv_sem,
        device_id={"ctx": ctx, "fsdp": fsdp},
    )


def greet_all(devices):
    barrier = pltpu.get_barrier_semaphore()
    for ctx, fsdp in devices:
        pl.semaphore_signal(barrier, inc=1, device_id={"ctx": ctx, "fsdp": fsdp})
    pl.semaphore_wait(barrier, len(devices))


PACKS = ((0, 1), (2, 3), (4, 5, 6, 7), (8, 9), (10,))


def front_kernel(*refs):
    sources = refs[:11]
    small_ref, token_ref, state_ref, hot_ref, strip_ref, class_ref = refs[11:17]
    results = refs[17:22]
    (
        gain_out, normed_out, query_out, tile_ref, attended_ref, total_ref, mid_one_ref,
        normed_two_ref, cross_query_ref, cross_attended_ref, cross_total_ref, mid_two_ref,
        normed_three_ref, self_result, cross_result,
    ) = refs[22:37]
    targets = refs[37:42]
    (
        self_out_ref, cross_out_ref, landing, self_ref, cross_ref, score_ref, share_ref,
        send_sem, x_sem, z_sem, core_sem,
        fill_sem, small_sem, self_sem, cross_sem, local_sem,
    ) = refs[42:]
    me, core, high, y, low, x = torus_place()
    shard = low * 4 + x
    sibling = (slot_of(y, 0, high, 1 - core), shard)
    inside = (me, (1 - low) * 4 + x)
    outside = (slot_of(y, 0, 1 - high, core), (1 - low) * 4 + x)
    across = slot_of(y, 0, 1 - high, core)
    ahead, behind = (slot_of(y, shift, high, core) for shift in (1, 3))
    others = [low * 4 + (x + shift) % 4 for shift in (1, 2, 3)]
    peers = [(shard + shift) % 8 for shift in range(1, 8)]
    greet_all(
        [sibling, outside, (across, shard), (ahead, shard), (behind, shard)]
        + [(me, peer) for peer in peers]
    )
    sends = []

    def send(src, dst, recv_sem, device):
        copy = hop(src, dst, send_sem.at[len(sends)], recv_sem, *device)
        copy.start()
        sends.append(copy)

    def arrived(ref, recv_sem):
        hop(ref, ref, send_sem.at[0], recv_sem, *sibling).wait_recv()

    def bring(src, dst, sem):
        copy = pltpu.make_async_copy(src, dst, sem)
        copy.start()
        return copy


    def part(k, owner, whose, side=None):
        ref = targets[k]
        count = ref.shape[1] // 2
        start = pl.multiple_of(whose * count, 16)
        if side is None:
            return ref.at[owner, pl.ds(start, count), :]
        width = ref.shape[2] // 2
        return ref.at[owner, pl.ds(start, count), pl.ds(side * width, width)]

    def fill(k):
        copies = []
        start = 0
        for source in PACKS[k]:
            width = sources[source].shape[1]
            copies.append(
                bring(
                    sources[source],
                    targets[k].at[shard, :, pl.ds(start, width)],
                    fill_sem.at[source],
                )
            )
            start += width
        return copies

    def send_own(k):
        for copy in fills[k]:
            copy.wait()
        for spot in (1, 0, 2):
            block = part(k, shard, core)
            send(block, block, x_sem.at[k, spot], (me, others[spot]))
        for side, device in enumerate((inside, outside)):
            piece = part(k, shard, core, side)
            send(piece, piece, z_sem.at[k, 3, side], device)


    def pass_x(k):
        for spot in (0, 2, 1):
            owner = low * 4 + (x + 3 - spot) % 4
            block = part(k, owner, core)
            arrived(block, x_sem.at[k, spot])
            for side, device in enumerate((inside, outside)):
                piece = part(k, owner, core, side)
                send(piece, piece, z_sem.at[k, spot, side], device)
            send(block, block, core_sem.at[k, spot], sibling)

    def pass_z(k):
        for spot in (3, 0, 2, 1):
            owner = (1 - low) * 4 + (x + 3 - spot) % 4
            for side in range(2):
                piece = part(k, owner, core, side)
                arrived(piece, z_sem.at[k, spot, side])
                send(piece, piece, core_sem.at[k, 3 + 2 * spot + side], sibling)

    def complete(k):
        for spot in range(3):
            owner = low * 4 + (x + 3 - spot) % 4
            arrived(part(k, owner, 1 - core), core_sem.at[k, spot])
        for spot in range(4):
            owner = (1 - low) * 4 + (x + 3 - spot) % 4
            for side in range(2):
                arrived(part(k, owner, 1 - core, side), core_sem.at[k, 3 + 2 * spot + side])


    def kv_start(src, out, sems):
        send(src, out.at[me], sems.at[me, 0], (across, shard))
        send(src, out.at[me], sems.at[me, 0], (ahead, shard))
        send(src, out.at[me], sems.at[me, 0], (behind, shard))
        send(src, out.at[me], sems.at[me, 0], sibling)

    def kv_across(out, sems):
        block = out.at[across]
        arrived(block, sems.at[across, 0])
        send(block, block, sems.at[across, 0], (ahead, shard))
        send(block, block, sems.at[across, 0], (behind, shard))
        send(block, block, sems.at[across, 0], sibling)

    def kv_near(out, sems, flip):
        half = 1 - high if flip else high
        slot = slot_of(y, 1, half, core)
        block = out.at[slot]
        arrived(block, sems.at[slot, 0])
        send(block.at[0], block.at[0], sems.at[slot, 0], (behind, shard))
        send(block, block, sems.at[slot, 0], sibling)
        slot = slot_of(y, 3, half, core)
        block = out.at[slot]
        arrived(block, sems.at[slot, 0])
        send(block.at[1], block.at[1], sems.at[slot, 1], (ahead, shard))
        send(block, block, sems.at[slot, 0], sibling)

    def kv_far(out, sems, flip):
        slot = slot_of(y, 2, 1 - high if flip else high, core)
        for part in range(2):
            arrived(out.at[slot, part], sems.at[slot, part])
        send(out.at[slot], out.at[slot], sems.at[slot, 0], sibling)

    def kv_complete(out, sems):
        for shift in range(4):
            for half in range(2):
                slot = slot_of(y, shift, half, 1 - core)
                arrived(out.at[slot], sems.at[slot, 0])

    fills = [fill(k) for k in range(5)]
    own_small = bring(small_ref, landing.at[shard], local_sem.at[0])
    for spot, peer in enumerate(peers):
        send(small_ref, landing.at[shard], small_sem.at[spot], (me, peer))
    send_own(0)
    send_own(1)
    own_small.wait()
    for spot in range(7):
        arrived(landing.at[(shard + 7 - spot) % 8], small_sem.at[spot])
    gains = landing[...].astype(F32)
    gain = [
        jnp.concatenate([gains[owner, k : k + 1, :96] for owner in range(8)], axis=1)
        for k in range(3)
    ]
    for k in range(3):
        gain_out[k : k + 1, :] = gain[k]
    tokens = token_ref[...].astype(F32)
    normed = rms_scaled(tokens, gain[0])
    normed_out[...] = normed
    pass_x(0)
    send_own(2)
    pass_z(0)
    pass_x(1)
    send_own(3)
    complete(0)
    exits = [bring(targets[0], results[0], local_sem.at[1])]
    for half in range(2):
        weight = targets[0][:, :, half * D : half * D + D].reshape(D, D)
        self_ref[half] = matmul(normed, weight).astype(BF)
    kv_start(self_ref, self_out_ref, self_sem)
    own_self = bring(self_ref, self_out_ref.at[me], local_sem.at[2])
    pass_z(1)
    complete(1)
    exits.append(bring(targets[1], results[1], local_sem.at[4]))
    for half in range(2):
        weight = targets[1][:, :, half * D : half * D + D].reshape(D, D)
        cross_ref[half] = matmul(state_ref[...], weight).astype(BF)
    kv_start(cross_ref, cross_out_ref, cross_sem)
    own_cross = bring(cross_ref, cross_out_ref.at[me], local_sem.at[3])
    bias_rows = contract(landing[...].reshape(128, 128), hot_ref[...], ((0,), (0,)))[:16]
    build_tiles(bias_rows, matmul(bias_rows.astype(BF), strip_ref[...]), tile_ref)
    kv_across(self_out_ref, self_sem)
    pass_x(2)
    send_own(4)
    kv_near(self_out_ref, self_sem, False)
    pass_z(2)
    kv_across(cross_out_ref, cross_sem)
    kv_near(self_out_ref, self_sem, True)
    pass_x(3)
    complete(2)
    exits.append(bring(targets[2], results[2], local_sem.at[5]))

    def square(k):
        return targets[2][:, :, k * D : k * D + D].reshape(D, D)

    query_out[...] = matmul(normed, square(0)).astype(BF)
    kv_far(self_out_ref, self_sem, False)
    kv_far(self_out_ref, self_sem, True)
    kv_near(cross_out_ref, cross_sem, False)
    own_self.wait()
    own_cross.wait()
    kv_complete(self_out_ref, self_sem)
    exits.append(bring(self_out_ref, self_result, local_sem.at[6]))

    def attend_self(first, last):
        attend_pairs(
            first, last, self_out_ref, query_out, attended_ref, total_ref, score_ref, share_ref,
            lambda pair, j: bias_chunk(class_ref, tile_ref, j, 2 * pair),
        )

    def attend_cross(first, last):
        attend_pairs(
            first, last, cross_out_ref, cross_query_ref, cross_attended_ref, cross_total_ref,
            score_ref, share_ref,
        )

    attend_self(0, 2)
    pass_x(4)
    kv_near(cross_out_ref, cross_sem, True)
    kv_far(cross_out_ref, cross_sem, False)
    attend_self(2, 4)
    pass_z(3)
    kv_far(cross_out_ref, cross_sem, True)
    attend_self(4, 6)
    mid_one = tokens + matmul(attended_ref[...], square(1))
    mid_one_ref[...] = mid_one
    normed_two = rms_scaled(mid_one, gain[1])
    normed_two_ref[...] = normed_two
    cross_query_ref[...] = matmul(normed_two, square(2)).astype(BF)
    pass_z(4)
    kv_complete(cross_out_ref, cross_sem)
    exits.append(bring(cross_out_ref, cross_result, local_sem.at[7]))
    attend_cross(0, 3)
    complete(3)
    exits.append(bring(targets[3], results[3], local_sem.at[8]))
    attend_cross(3, 6)
    complete(4)
    exits.append(bring(targets[4], results[4], local_sem.at[9]))
    mid_two = mid_one_ref[...] + matmul(cross_attended_ref[...], square(3))
    mid_two_ref[...] = mid_two
    normed_three_ref[...] = rms_scaled(mid_two, gain[2])
    for copy in sends:
        copy.wait_send()
    for copy in exits:
        copy.wait()


def front(weights, others, collective_id):
    dma = pltpu.SemaphoreType.DMA
    packs = [
        (8, weights[group[0]].shape[0], sum(weights[k].shape[1] for k in group)) for group in PACKS
    ]
    anywhere = pl.BlockSpec(memory_space=pl.ANY)
    inside = pl.BlockSpec(memory_space=pltpu.VMEM)
    return pl.pallas_call(
        front_kernel,
        out_shape=[jax.ShapeDtypeStruct(pack, BF) for pack in packs]
        + [
            jax.ShapeDtypeStruct((3, D), F32),
            jax.ShapeDtypeStruct((TOK, D), BF),
            jax.ShapeDtypeStruct((TOK, D), BF),
            jax.ShapeDtypeStruct((HEADS, 5, HALF, TOK), F32),
            jax.ShapeDtypeStruct((TOK, D), BF),
            jax.ShapeDtypeStruct((PAIRS, 8, 2 * TOK), F32),
            jax.ShapeDtypeStruct((TOK, D), F32),
            jax.ShapeDtypeStruct((TOK, D), BF),
            jax.ShapeDtypeStruct((TOK, D), BF),
            jax.ShapeDtypeStruct((TOK, D), BF),
            jax.ShapeDtypeStruct((PAIRS, 8, 2 * TOK), F32),
            jax.ShapeDtypeStruct((TOK, D), F32),
            jax.ShapeDtypeStruct((TOK, D), BF),
            jax.ShapeDtypeStruct((N_CTX, 2, TOK, D), BF),
            jax.ShapeDtypeStruct((N_CTX, 2, ENC, D), BF),
        ],
        in_specs=[anywhere] * 12 + [inside] * 4 + [pl.BlockSpec(memory_space=pltpu.SMEM)],
        out_specs=[anywhere] * 5 + [inside] * 13 + [anywhere] * 2,
        scratch_shapes=[pltpu.VMEM(pack, BF) for pack in packs]
        + [
            pltpu.VMEM((N_CTX, 2, TOK, D), BF),
            pltpu.VMEM((N_CTX, 2, ENC, D), BF),
            pltpu.VMEM((8, 16, 128), BF),
            pltpu.VMEM((2, TOK, D), BF),
            pltpu.VMEM((2, ENC, D), BF),
            pltpu.VMEM((N_CTX, TOK, 2 * TOK), F32),
            pltpu.VMEM((N_CTX, TOK, 2 * TOK), BF),
            dma((5 * 22 + 7 + 2 * 18,)),
            dma((5, 3)),
            dma((5, 4, 2)),
            dma((5, 11)),
            dma((11,)),
            dma((7,)),
            dma((N_CTX, 2)),
            dma((N_CTX, 2)),
            dma((10,)),
        ],
        compiler_params=pltpu.CompilerParams(
            collective_id=collective_id, has_side_effects=True, vmem_limit_bytes=60 * MIB
        ),
        name="front",
    )(*weights, *others)


PIECE = 96
WIDTHS = (D // 2, D // 2, D // 2, D // 2, D, D, FF)
SPAN = sum(WIDTHS)
DOWN = len(WIDTHS)
CHUNKS = DOWN + 1
CROSS_KV, SELF_KV, WIDE = 4, 5, 6
LEFT = (D,) * 4
RIGHT = (D // 2,) * 4


def finish_kernel(*refs):
    lefts = refs[:4]
    rights = refs[4:8]
    wide_ref, down_ref, dkv_ref, dckv_ref = refs[8:12]
    state_ref, kv_ref, ckv_ref, dn_ref, dmid_ref, token_ref, gain_ref, small_ref = refs[12:20]
    early_out, late_out, small_out, decoder_ref, encoder_ref = refs[20:25]
    (
        left_all, right_all, turned, turned_one, turned_state, state_all, s_right, c_right,
        kept, from_z, from_x, via_x, d_z, d_x, d_via,
        s_kept, s_core, s_row, s_via, s_stage, s_high, s_fin,
        c_kept, c_core, c_row, c_via, c_stage, c_high, c_fin,
        small_f32, sm_own, sm_core, sm_z, sm_x, sm_ctx, sm_total,
        packed, from_ctx, land, late_packed, late_from, late_land,
        s_sem, c_sem, fill_sem, act_send, act_recv, late_send, late_recv, z_send, z_recv,
        x_send, x_recv, ctx_send, ctx_recv, pass_send, pass_recv, sm_send, sm_recv, local_sem,
    ) = refs[25:]
    me, core, high, y, low, x = torus_place()
    shard = low * 4 + x
    rank = y * 2 + high
    sibling = (slot_of(y, 0, high, 1 - core), shard)
    inside = (me, (1 - low) * 4 + x)
    outside = (slot_of(y, 0, 1 - high, core), (1 - low) * 4 + x)
    across = (slot_of(y, 0, 1 - high, core), shard)
    others = [low * 4 + (x + shift) % 4 for shift in (1, 2, 3)]
    ahead = (slot_of(y, 1, high, core), shard)
    behind = (slot_of(y, 3, high, core), shard)
    shifts = [(dy, dz) for dy in range(4) for dz in range(2)][1:]
    mates = [((y + dy) % 4) * 2 + (high + dz) % 2 for dy, dz in shifts]
    greet_all(
        [sibling, inside, outside]
        + [(me, other) for other in others]
        + [(mate * 2 + core, shard) for mate in mates]
    )
    sends = []

    def go(src, dst, send_sem, recv_sem, device):
        copy = hop(src, dst, send_sem, recv_sem, *device)
        copy.start()
        sends.append(copy)
        return copy

    def bring(src, dst, sem):
        copy = pltpu.make_async_copy(src, dst, sem)
        copy.start()
        return copy


    def rows_start(source, held, arrived, sem):
        over = []
        local = []
        for spot, shift in enumerate((2, 1, 3, 0)):
            pair = pl.ds(((y + shift) % 4) * 2, 2)
            block = pl.ds(2 * spot, 2)
            over.append(
                go(
                    source.at[pair, 1 - core], arrived.at[block],
                    sem.at[0, spot], sem.at[1, spot], sibling,
                )
            )
            local.append(bring(source.at[pair, core], held.at[block], sem.at[4, spot]))
        return over, local


    def rows_send(copies, held, arrived, via, row, sem):
        over, local = copies
        onward = []
        for spot in range(4):
            local[spot].wait()
            over[spot].wait_recv()
            for block in (2 * spot, 2 * spot + 1):
                for part in range(2):
                    held[block, part] = held[block, part] + arrived[block, part]
            if spot == 0:
                first = go(held.at[0], via.at[0], sem.at[2, 0], sem.at[3, 0], ahead)
                second = go(held.at[1], via.at[1], sem.at[2, 1], sem.at[3, 1], behind)
            elif spot == 1:
                onward.append(go(held.at[3], row.at[0, 1], sem.at[2, 2], sem.at[3, 2], ahead))
            elif spot == 2:
                onward.append(go(held.at[4], row.at[1, 0], sem.at[2, 3], sem.at[3, 3], behind))
        return first, second, onward

    def rows_via(state, held, via, row, sem):
        first, second, onward = state
        first.wait_recv()
        for part in range(2):
            held[2, part] = held[2, part] + via[0, part]
        onward.append(go(held.at[2], row.at[0, 0], sem.at[2, 4], sem.at[3, 4], ahead))
        second.wait_recv()
        for part in range(2):
            held[5, part] = held[5, part] + via[1, part]
        onward.append(go(held.at[5], row.at[1, 1], sem.at[2, 5], sem.at[3, 5], behind))
        return onward

    def rows_total(held, row, half, part):
        return (
            held[6 + half, part].astype(F32)
            + row[0, half, part].astype(F32)
            + row[1, half, part].astype(F32)
        )

    def rows_across(onward, held, row, stage, landing, sem):
        for copy in onward:
            copy.wait_recv()
        for part in range(2):
            stage[part] = rows_total(held, row, 1 - high, part).astype(BF)
        return go(stage, landing, sem.at[2, 6], sem.at[3, 6], across)

    def rows_sum(last, held, row, landing, final, right, which):
        totals = [rows_total(held, row, high, part) for part in range(2)]
        last.wait_recv()
        for part in range(2):
            final[part] = (totals[part] + landing[part].astype(F32)).astype(BF)
        count = final.shape[1]
        copy = go(
            final.at[1 - core], right.at[pl.ds(count, count)],
            late_send.at[which], late_recv.at[which], sibling,
        )
        right[:count] = final[core]
        return copy


    starts = [sum(WIDTHS[:k]) for k in range(len(WIDTHS))]
    left_starts = [sum(LEFT[:k]) for k in range(4)]
    right_starts = [sum(RIGHT[:k]) for k in range(4)]
    acts = {}
    over_z, over_via, over_x = {}, {}, {}
    column_ahead = (me, low * 4 + (x + 1) % 4)
    column_behind = (me, low * 4 + (x + 3) % 4)

    def buffers(k):
        if k == DOWN:
            return d_z, d_x, d_via, pl.ds(0, D // 2)
        return from_z, from_x, via_x, pl.ds(starts[k], WIDTHS[k])

    def acts_start(index):
        left = pl.ds(left_starts[index], LEFT[index])
        right = pl.ds(right_starts[index], RIGHT[index])
        near = pl.ds(pl.multiple_of(core * RIGHT[index], 128), RIGHT[index])
        far = pl.ds(pl.multiple_of((1 - core) * RIGHT[index], 128), RIGHT[index])
        mine = pl.ds(0, TOK)
        theirs = pl.ds(TOK, TOK)
        acts[index] = (
            bring(lefts[index], left_all.at[mine, left], fill_sem.at[index, 0]),
            bring(rights[index].at[:, near], right_all.at[mine, right], fill_sem.at[index, 1]),
            go(
                lefts[index], left_all.at[theirs, left],
                act_send.at[index, 0], act_recv.at[index, 0], sibling,
            ),
            go(
                rights[index].at[:, far], right_all.at[theirs, right],
                act_send.at[index, 1], act_recv.at[index, 1], sibling,
            ),
        )

    def multiply(k, left_ref, right):
        landing, _, _, cut = buffers(k)
        for group in range(2):
            owners = pl.ds(4 * ((1 - low + group) % 2), 4)
            left = left_ref[owners].reshape(4 * PIECE, right.shape[0])
            kept[owners, :, cut] = (
                contract(left, right, ((1,), (0,))).astype(BF).reshape(4, PIECE, WIDTHS[k])
            )
            if group == 0:
                half = PIECE // 2
                over_z[k] = [
                    go(
                        kept.at[owners, pl.ds(side * half, half), cut],
                        landing.at[:, pl.ds(side * half, half), cut],
                        z_send.at[k, side],
                        z_recv.at[k, side],
                        device,
                    )
                    for side, device in enumerate((inside, outside))
                ]

    def make(index):
        near_left, near_right, far_left, far_right = acts[index]
        near_left.wait()
        near_right.wait()
        far_left.wait_recv()
        far_right.wait_recv()
        left = left_all[:, left_starts[index] : left_starts[index] + LEFT[index]].T
        right = right_all[:, right_starts[index] : right_starts[index] + RIGHT[index]]
        target = turned_one if index == 3 else turned
        target[...] = left.reshape(8, PIECE, 2 * TOK)
        multiply(index, target, right)

    def step_z(k):
        landing, _, _, cut = buffers(k)
        for copy in over_z[k]:
            copy.wait_recv()
        for column in range(4):
            landing[column, :, cut] = landing[column, :, cut] + kept[4 * low + column, :, cut]
        send_x(k)


    def send_x(k):
        landing, spread, via, cut = buffers(k)
        half = landing.shape[1] // 2
        upper, lower = pl.ds(0, half), pl.ds(half, half)
        away, front_column, back_column = (x + 2) % 4, (x + 1) % 4, (x + 3) % 4
        over_via[k] = (
            go(
                landing.at[away, upper, cut], via.at[0, :, cut],
                x_send.at[k, 0], x_recv.at[k, 0], column_ahead,
            ),
            go(
                landing.at[away, lower, cut], via.at[1, :, cut],
                x_send.at[k, 1], x_recv.at[k, 1], column_behind,
            ),
        )
        over_x[k] = [
            go(
                landing.at[front_column, lower, cut], spread.at[0, lower, cut],
                x_send.at[k, 2], x_recv.at[k, 2], column_ahead,
            ),
            go(
                landing.at[back_column, upper, cut], spread.at[1, upper, cut],
                x_send.at[k, 3], x_recv.at[k, 3], column_behind,
            ),
        ]

    def step_via(k):
        landing, spread, via, cut = buffers(k)
        half = landing.shape[1] // 2
        upper, lower = pl.ds(0, half), pl.ds(half, half)
        front_column, back_column = (x + 1) % 4, (x + 3) % 4
        over_via[k][0].wait_recv()
        landing[front_column, upper, cut] = landing[front_column, upper, cut] + via[0, :, cut]
        over_x[k].append(
            go(
                landing.at[front_column, upper, cut], spread.at[0, upper, cut],
                x_send.at[k, 4], x_recv.at[k, 4], column_ahead,
            )
        )
        over_via[k][1].wait_recv()
        landing[back_column, lower, cut] = landing[back_column, lower, cut] + via[1, :, cut]
        over_x[k].append(
            go(
                landing.at[back_column, lower, cut], spread.at[1, lower, cut],
                x_send.at[k, 5], x_recv.at[k, 5], column_behind,
            )
        )

    def step_x(k):
        landing, spread, _, cut = buffers(k)
        for copy in over_x[k]:
            copy.wait_recv()
        total = landing[x, :, cut].astype(F32)
        for spot in range(2):
            total = total + spread[spot, :, cut].astype(F32)
        total = total.astype(BF)
        half = D // 2
        if k == WIDE:
            for piece in range(8):
                packed[piece, :PIECE, :256] = total[:, piece * 256 : piece * 256 + 256]
        elif k == DOWN:
            for piece in range(8):
                for part in range(3):
                    packed[piece, part * 32 : part * 32 + 32, 256:] = total[
                        piece * 32 : piece * 32 + 32, part * 128 : part * 128 + 128
                    ]
        else:
            middle = PIECE // 2
            for upper in range(2):
                rows = total[upper * middle : upper * middle + middle, :]
                if k == CROSS_KV or k == SELF_KV:
                    for piece in range(2):
                        late_packed[(0 if k == CROSS_KV else 4) + 2 * piece + upper] = rows[
                            :, piece * half : piece * half + half
                        ]
                else:
                    packed[2 * k + upper, PIECE:, :] = rows


    def mate_device(mate):
        return (mate * 2 + core, shard)

    def ctx_start(which, source, landing):
        return [
            go(
                source.at[mate], landing.at[spot],
                ctx_send.at[which, spot], ctx_recv.at[which, spot], mate_device(mate),
            )
            for spot, mate in enumerate(mates)
        ]

    def ctx_sum(which, over, source, landing, final):
        total = source[rank].astype(F32)
        for spot in range(7):
            over[spot].wait_recv()
            total = total + landing[spot].astype(F32)
        final[rank, core] = total.astype(BF)
        own = final.at[rank, core]
        for spot, mate in enumerate(mates):
            go(own, own, ctx_send.at[which, 7 + spot], ctx_recv.at[which, 7 + rank], mate_device(mate))
        go(own, own, pass_send.at[which, 7], pass_recv.at[which, rank], sibling)

    def landed(ref, recv_sem):
        hop(ref, ref, pass_send.at[0, 0], recv_sem, *sibling).wait_recv()

    def ctx_pass(which, final):
        for spot, mate in enumerate(mates):
            block = final.at[mate, core]
            landed(block, ctx_recv.at[which, 7 + mate])
            go(block, block, pass_send.at[which, spot], pass_recv.at[which, mate], sibling)

    def ctx_done(which, final):
        for mate in [rank] + mates:
            landed(final.at[mate, 1 - core], pass_recv.at[which, mate])

    wide_copy = bring(wide_ref, from_z.at[:, :, pl.ds(starts[WIDE], FF)], local_sem.at[1])
    down_copy = bring(down_ref, d_z, local_sem.at[2])
    s_copies = rows_start(dkv_ref, s_kept, s_core, s_sem)
    c_copies = rows_start(dckv_ref, c_kept, c_core, c_sem)
    for index in range(4):
        acts_start(index)
    state_near = bring(state_ref, state_all.at[pl.ds(0, ENC)], local_sem.at[0])
    state_far = go(
        state_ref, state_all.at[pl.ds(ENC, ENC)], late_send.at[2], late_recv.at[2], sibling
    )
    down_copy.wait()
    send_x(DOWN)
    wide_copy.wait()
    send_x(WIDE)
    s_state = rows_send(s_copies, s_kept, s_core, s_via, s_row, s_sem)
    make(0)
    make(1)
    s_onward = rows_via(s_state, s_kept, s_via, s_row, s_sem)
    c_state = rows_send(c_copies, c_kept, c_core, c_via, c_row, c_sem)
    make(2)
    make(3)
    step_via(DOWN)
    step_via(WIDE)
    for k in range(4):
        step_z(k)
    state_near.wait()
    state_far.wait_recv()
    turned_state[...] = state_all[...].T.reshape(8, PIECE, 2 * ENC)
    s_last = rows_across(s_onward, s_kept, s_row, s_stage, s_high, s_sem)
    c_onward = rows_via(c_state, c_kept, c_via, c_row, c_sem)
    for k in range(4):
        step_via(k)
    step_x(DOWN)
    step_x(WIDE)
    s_far = rows_sum(s_last, s_kept, s_row, s_high, s_fin, s_right, 0)
    for k in range(4):
        step_x(k)
    early = ctx_start(0, packed, from_ctx)
    s_far.wait_recv()
    multiply(SELF_KV, turned_one, s_right[...])
    c_last = rows_across(c_onward, c_kept, c_row, c_stage, c_high, c_sem)
    tokens = token_ref[...].astype(F32)
    d_kv = jnp.concatenate([s_fin[0], s_fin[1]], axis=1)
    grad = dn_ref[...] + contract(d_kv, kv_ref[...], ((1,), (1,)))
    inverse = lax.rsqrt(jnp.mean(tokens * tokens, axis=-1, keepdims=True) + 1e-06)
    small_f32[...] = small_ref[...]
    line = jnp.sum(tokens * inverse * grad, axis=0, keepdims=True)
    for owner in range(8):
        small_f32[owner, 0:1, :96] = line[:, owner * 96 : owner * 96 + 96]
    sm_own[...] = small_f32[...].astype(BF)
    sm_over = go(sm_own, sm_core, sm_send.at[0], sm_recv.at[0], sibling)
    c_far = rows_sum(c_last, c_kept, c_row, c_high, c_fin, c_right, 1)
    c_far.wait_recv()
    multiply(CROSS_KV, turned_state, c_right[...])
    step_z(SELF_KV)
    sm_over.wait_recv()
    sm_own_sum = (sm_own[...].astype(F32) + sm_core[...].astype(F32)).astype(BF)
    sm_over.wait_send()
    sm_own[...] = sm_own_sum
    sm_inside = go(
        sm_own.at[pl.ds(4 * (1 - low), 4)], sm_z, sm_send.at[1], sm_recv.at[1], inside
    )
    ctx_sum(0, early, packed, from_ctx, land)
    step_z(CROSS_KV)
    step_via(SELF_KV)
    sm_inside.wait_recv()
    for column in range(4):
        sm_z[column] = sm_z[column] + sm_own[4 * low + column]
    sm_row = [
        go(
            sm_z.at[(x + spot + 1) % 4], sm_x.at[spot],
            sm_send.at[2 + spot], sm_recv.at[2 + spot], (me, others[spot]),
        )
        for spot in range(3)
    ]
    step_via(CROSS_KV)
    scaled = gain_ref[...] * grad
    mixed = jnp.mean(tokens * scaled, axis=-1, keepdims=True)
    decoder_ref[...] = (
        dmid_ref[...] + inverse * scaled - tokens * (inverse * inverse * inverse * mixed)
    )
    step_x(SELF_KV)
    step_x(CROSS_KV)
    late = ctx_start(1, late_packed, late_from)
    sm_sum = sm_z[x].astype(F32)
    for spot in range(3):
        sm_row[spot].wait_recv()
        sm_sum = sm_sum + sm_x[spot].astype(F32)
    sm_total[...] = sm_sum.astype(BF)
    sm_mates = [
        go(sm_total, sm_ctx.at[spot], sm_send.at[5 + spot], sm_recv.at[5 + spot], mate_device(mate))
        for spot, mate in enumerate(mates)
    ]
    ctx_pass(0, land)
    ctx_sum(1, late, late_packed, late_from, late_land)
    d_ckv = jnp.concatenate([c_fin[0], c_fin[1]], axis=1)
    encoder_ref[...] = contract(d_ckv, ckv_ref[...], ((1,), (1,)))
    sm_sum = sm_total[...].astype(F32)
    for spot in range(7):
        sm_mates[spot].wait_recv()
        sm_sum = sm_sum + sm_ctx[spot].astype(F32)
    small_out[...] = sm_sum
    ctx_done(0, land)
    early_out[...] = land[...]
    ctx_pass(1, late_land)
    ctx_done(1, late_land)
    late_out[...] = late_land[...]
    for copy in sends:
        if copy is not sm_over:
            copy.wait_send()


def unpack_kernel(early, late, *refs):
    square_refs = refs[:8]
    gate_ref, up_ref, down_ref = refs[8:]
    half = D // 2
    middle = PIECE // 2
    for side in range(2):
        columns = slice(side * half, side * half + half)
        for upper in range(2):
            rows = slice(upper * middle, upper * middle + middle)
            for k in range(4):
                square_refs[k][rows, columns] = early[2 * k + upper, side, PIECE:, :].astype(F32)
            for k in range(2):
                for piece in range(2):
                    square_refs[4 + 2 * k + side][rows, piece * half : piece * half + half] = late[
                        4 * k + 2 * piece + upper, side
                    ].astype(F32)
        target = up_ref if side else gate_ref
        for piece in range(8):
            target[:, piece * 256 : piece * 256 + 256] = early[piece, side, :PIECE, :256].astype(F32)
            for part in range(3):
                down_ref[
                    piece * 32 : piece * 32 + 32,
                    side * half + part * 128 : side * half + part * 128 + 128,
                ] = early[piece, side, part * 32 : part * 32 + 32, 256:].astype(F32)


def unpack(early, late):
    outs = (
        [jax.ShapeDtypeStruct((PIECE, D), F32)] * 8
        + [jax.ShapeDtypeStruct((PIECE, FF), F32)] * 2
        + [jax.ShapeDtypeStruct((FF // 8, D), F32)]
    )
    return pl.pallas_call(
        unpack_kernel,
        out_shape=outs,
        in_specs=[pl.BlockSpec(memory_space=pltpu.VMEM)] * 2,
        out_specs=[pl.BlockSpec(memory_space=pltpu.VMEM)] * len(outs),
        compiler_params=pltpu.CompilerParams(vmem_limit_bytes=24 * MIB),
        name="unpack",
    )(early, late)


def finish(far, near, collective_id):
    dma = pltpu.SemaphoreType.DMA

    def rows(count):
        return [
            pltpu.VMEM((8, 2, count, D), BF),
            pltpu.VMEM((8, 2, count, D), BF),
            pltpu.VMEM((2, 2, 2, count, D), BF),
            pltpu.VMEM((2, 2, count, D), BF),
            pltpu.VMEM((2, count, D), BF),
            pltpu.VMEM((2, count, D), BF),
            pltpu.VMEM((2, count, D), BF),
        ]

    outs = [
        jax.ShapeDtypeStruct((8, 2, 3 * PIECE // 2, D // 2), BF),
        jax.ShapeDtypeStruct((8, 2, PIECE // 2, D // 2), BF),
        jax.ShapeDtypeStruct((16, 128), F32),
        jax.ShapeDtypeStruct((TOK, D), F32),
        jax.ShapeDtypeStruct((ENC, D), F32),
    ]
    return pl.pallas_call(
        finish_kernel,
        out_shape=outs,
        in_specs=[pl.BlockSpec(memory_space=pl.ANY)] * len(far)
        + [pl.BlockSpec(memory_space=pltpu.VMEM)] * len(near),
        out_specs=[pl.BlockSpec(memory_space=pltpu.VMEM)] * len(outs),
        scratch_shapes=[
            pltpu.VMEM((2 * TOK, sum(LEFT)), BF),
            pltpu.VMEM((2 * TOK, sum(RIGHT)), BF),
            pltpu.VMEM((8, PIECE, 2 * TOK), BF),
            pltpu.VMEM((8, PIECE, 2 * TOK), BF),
            pltpu.VMEM((8, PIECE, 2 * ENC), BF),
            pltpu.VMEM((2 * ENC, D), BF),
            pltpu.VMEM((2 * TOK, D), BF),
            pltpu.VMEM((2 * ENC, D), BF),
            pltpu.VMEM((8, PIECE, SPAN - FF), BF),
            pltpu.VMEM((4, PIECE, SPAN), BF),
            pltpu.VMEM((2, PIECE, SPAN), BF),
            pltpu.VMEM((2, PIECE // 2, SPAN), BF),
            pltpu.VMEM((4, FF // 8, D // 2), BF),
            pltpu.VMEM((2, FF // 8, D // 2), BF),
            pltpu.VMEM((2, FF // 16, D // 2), BF),
        ]
        + rows(TOK)
        + rows(ENC)
        + [
            pltpu.VMEM((8, 16, 128), F32),
            pltpu.VMEM((8, 16, 128), BF),
            pltpu.VMEM((8, 16, 128), BF),
            pltpu.VMEM((4, 16, 128), BF),
            pltpu.VMEM((3, 16, 128), BF),
            pltpu.VMEM((7, 16, 128), BF),
            pltpu.VMEM((16, 128), BF),
            pltpu.VMEM((8, 3 * PIECE // 2, D // 2), BF),
            pltpu.VMEM((7, 3 * PIECE // 2, D // 2), BF),
            pltpu.VMEM((8, 2, 3 * PIECE // 2, D // 2), BF),
            pltpu.VMEM((8, PIECE // 2, D // 2), BF),
            pltpu.VMEM((7, PIECE // 2, D // 2), BF),
            pltpu.VMEM((8, 2, PIECE // 2, D // 2), BF),
            dma((5, 7)),
            dma((5, 7)),
            dma((4, 2)),
            dma((4, 2)),
            dma((4, 2)),
            dma((3,)),
            dma((3,)),
            dma((CHUNKS, 2)),
            dma((CHUNKS, 2)),
            dma((CHUNKS, 6)),
            dma((CHUNKS, 6)),
            dma((2, 14)),
            dma((2, 15)),
            dma((2, 8)),
            dma((2, 8)),
            dma((12,)),
            dma((12,)),
            dma((3,)),
        ],
        compiler_params=pltpu.CompilerParams(
            collective_id=collective_id, has_side_effects=True, vmem_limit_bytes=62 * MIB
        ),
        name="finish_gradients",
    )(*far, *near)


def backward_kernel(biased, *refs):
    if biased:
        class_ref, near_ref, q_ref, k_ref, v_ref, g_ref, total_ref, tile_ref = refs[:8]
        dq_ref, dkv_ref, strip_ref, share_ref, slope_ref, share_low, slope_low = refs[8:]
    else:
        q_ref, k_ref, v_ref, g_ref, total_ref = refs[:5]
        dq_ref, dkv_ref, share_ref, slope_ref, share_low, slope_low = refs[5:]
    chunks = share_ref.shape[0]
    queries = split_heads(q_ref[...])
    grads = split_heads(g_ref[...])
    totals = total_ref[0, 0:1]
    inner = jnp.zeros((8, 2 * TOK), F32)
    for j in range(chunks):
        scores = contract(key_chunk(k_ref, j), queries, ((1,), (1,)))
        if biased:
            scores = scores + bias_chunk(class_ref, tile_ref, j)
        shares = jnp.exp(scores - totals)
        slopes = contract(key_chunk(v_ref, j), grads, ((1,), (1,)))
        inner = inner + fold(shares * slopes, jnp.sum)
        share_ref[j] = shares
        slope_ref[j] = slopes
        share_low[j] = shares.astype(BF)
    inner = jnp.sum(inner, axis=0, keepdims=True)
    for j in range(chunks):
        grad = share_ref[j] * (slope_ref[j] - inner)
        if biased:
            slope_ref[j] = grad
        slope_low[j] = grad.astype(BF)
    keys = jnp.concatenate([key_chunk(k_ref, j) for j in range(chunks)], axis=0)
    low = slope_low[...].reshape(-1, 2 * TOK)
    dq_ref[...] = join_heads(contract(keys, low, ((0,), (0,)))).astype(BF)
    shape = dkv_ref.shape
    block = (shape[0], shape[2], shape[3])
    dkv_ref[:, 0] = contract(low, queries, ((1,), (0,))).astype(BF).reshape(block)
    dkv_ref[:, 1] = (
        contract(share_low[...].reshape(-1, 2 * TOK), grads, ((1,), (0,))).astype(BF).reshape(block)
    )
    if biased:
        lane = lax.broadcasted_iota(jnp.int32, (HALF, TOK), 1)
        for gap in range(3):
            pieces = []
            for half in range(2):
                spot = near_ref[half, gap]
                held = slope_ref[jnp.maximum(spot, 0) // 2, pl.ds(
                    pl.multiple_of((jnp.maximum(spot, 0) % 2) * HALF, HALF), HALF)]
                pieces.append(jnp.where(spot >= 0, held, jnp.zeros_like(held)))
            for head in range(2):
                cut = slice(head * TOK, (head + 1) * TOK)
                strip_ref[head, gap] = jnp.where(lane < HALF, pieces[0][:, cut], pieces[1][:, cut])


def pair_columns(pair):
    return (0, pair)


def kv_spec(rows, row_block, part):
    return pl.BlockSpec(
        (N_CTX, 1, rows, 2 * HEAD_DIM), lambda pair: (0, part, row_block, pair)
    )


SMEM_SPEC = pl.BlockSpec(memory_space=pltpu.SMEM)
TILE_SPEC = pl.BlockSpec((2, 5, HALF, TOK), lambda pair: (pair, 0, 0, 0))
TOTAL_SPEC = pl.BlockSpec((1, 8, 2 * TOK), lambda pair: (pair, 0, 0))
ROW_SPEC = pl.BlockSpec((TOK, 2 * HEAD_DIM), pair_columns)
LOCAL = pltpu.CompilerParams(vmem_limit_bytes=48 * MIB)


def attend_back(queries, gathered, grads, totals, rows, row_block, classes=None, near=None, tiles=None):
    biased = classes is not None
    chunks = N_CTX * rows // TOK
    specs = [ROW_SPEC, kv_spec(rows, row_block, 0), kv_spec(rows, row_block, 1), ROW_SPEC, TOTAL_SPEC]
    operands = [queries, gathered, gathered, grads, totals]
    out_specs = [
        ROW_SPEC,
        pl.BlockSpec((N_CTX, 2, rows, 2 * HEAD_DIM), lambda pair: (0, 0, 0, pair)),
    ]
    out_shape = [
        jax.ShapeDtypeStruct((TOK, D), BF),
        jax.ShapeDtypeStruct((N_CTX, 2, rows, D), BF),
    ]
    if biased:
        specs = [SMEM_SPEC, SMEM_SPEC] + specs + [TILE_SPEC]
        operands = [classes, near] + operands + [tiles]
        out_specs.append(pl.BlockSpec((2, 3, HALF, TOK), lambda pair: (pair, 0, 0, 0)))
        out_shape.append(jax.ShapeDtypeStruct((HEADS, 3, HALF, TOK), F32))
    return pl.pallas_call(
        functools.partial(backward_kernel, biased),
        grid=(PAIRS,),
        in_specs=specs,
        out_specs=out_specs,
        out_shape=out_shape,
        scratch_shapes=[
            pltpu.VMEM((chunks, TOK, 2 * TOK), F32),
            pltpu.VMEM((chunks, TOK, 2 * TOK), F32),
            pltpu.VMEM((chunks, TOK, 2 * TOK), BF),
            pltpu.VMEM((chunks, TOK, 2 * TOK), BF),
        ],
        compiler_params=LOCAL,
        cost_estimate=pl.CostEstimate(flops=1000, bytes_accessed=1000, transcendentals=0),
        name="attend_self_back" if biased else "attend_cross_back",
    )(*operands)


def matmul(left, right):
    return jnp.dot(left, right, preferred_element_type=F32)


def transposed_left(left, right):
    return contract(left, right, ((0,), (0,)))


def transposed_right(left, right):
    return contract(left, right, ((1,), (1,)))


def rms_scaled(values, gain):
    inverse = lax.rsqrt(jnp.mean(values * values, axis=-1, keepdims=True) + 1e-06)
    return (values * inverse * gain).astype(BF)


def rms_back(values, gain, grad):
    inverse = lax.rsqrt(jnp.mean(values * values, axis=-1, keepdims=True) + 1e-06)
    scaled = gain * grad
    mixed = jnp.mean(values * scaled, axis=-1, keepdims=True)
    grad_values = inverse * scaled - values * (inverse * inverse * inverse * mixed)
    return grad_values, jnp.sum(values * inverse * grad, axis=0)


def gelu_product(gate_part, up_part):
    return jax.nn.gelu(gate_part, approximate=True) * up_part


def near_hot():
    shape = (REACH, 3 * HALF * HALF)
    spot = lax.broadcasted_iota(jnp.int32, shape, 1)
    gap = spot // (HALF * HALF)
    key = (spot // HALF) % HALF
    row = spot % HALF
    distance = jnp.clip(HALF * gap + row - key, 0, REACH - 1)
    return (distance == lax.broadcasted_iota(jnp.int32, shape, 0)).astype(BF)


def strip_hot():
    shape = (REACH, 3 * TOK)
    spot = lax.broadcasted_iota(jnp.int32, shape, 1)
    distance = jnp.clip(HALF * (spot // TOK) + spot % TOK - (HALF - 1), 0, REACH - 1)
    return (distance == lax.broadcasted_iota(jnp.int32, shape, 0)).astype(BF)


def bias_sums(strips):
    tiles = (strips[..., :HALF] + strips[..., HALF:]).reshape(HEADS, -1)
    high = tiles.astype(BF)
    low = (tiles - high.astype(F32)).astype(BF)
    hot = near_hot()
    sums = transposed_right(high, hot) + transposed_right(low, hot)
    far = -jnp.sum(sums[:, :-1], axis=1, keepdims=True)
    return jnp.concatenate([sums[:, :-1], far], axis=1)


def swap(values, move):
    perm = []
    for ctx in range(N_CTX):
        for shard in range(8):
            there, owner = move(ctx, shard)
            perm.append((ctx * 8 + shard, there * 8 + owner))
    return lax.ppermute(values, ("ctx", "fsdp"), perm)


def feed_gradients(normed, hidden, d_gate, d_up, upstream):
    first = lax.axis_index("ctx") % 2 == 0
    low = lax.axis_index("fsdp") // 4
    half = D // 2
    near = jnp.where(first, d_gate, d_up)
    far = jnp.where(first, d_up, d_gate)
    near_grad = jnp.where(first, upstream[:, :half], upstream[:, half:])
    far_grad = jnp.where(first, upstream[:, half:], upstream[:, :half])
    other = swap(
        jnp.concatenate([normed, hidden, far, far_grad], axis=1), lambda ctx, shard: (ctx ^ 1, shard)
    )
    lefts = jnp.concatenate([normed, other[:, :D]], axis=0)
    rights = jnp.concatenate([near, other[:, D + FF : D + 2 * FF]], axis=0)
    wide = transposed_left(lefts, rights).astype(BF).reshape(8, PIECE, FF)
    lefts = jnp.concatenate([hidden, other[:, D : D + FF]], axis=0)
    rights = jnp.concatenate([near_grad, other[:, D + 2 * FF :]], axis=0)
    tall = transposed_left(lefts, rights).astype(BF).reshape(8, FF // 8, half)

    def cut(part):
        middle = part.shape[1] // 2
        away = lax.dynamic_slice_in_dim(part, 4 * (1 - low), 4, 0)
        mine = lax.dynamic_slice_in_dim(part, 4 * low, 4, 0)
        return mine, away[:, :middle], away[:, middle:]

    return cut(wide), cut(tall)


def over_z(mine, upper, lower):
    inner = swap(upper, lambda ctx, shard: (ctx, (shard + 4) % 8))
    outer = swap(lower, lambda ctx, shard: (ctx ^ 2, (shard + 4) % 8))
    return mine, inner, outer


def body(
    decoder_in,
    encoder_states,
    out_grad,
    block_pairs,
    bucket_table,
    gain_self,
    self_query,
    self_key,
    self_value,
    self_out,
    position_bias,
    gain_cross,
    cross_query,
    cross_key,
    cross_value,
    cross_out,
    gain_feed,
    feed_gate,
    feed_up,
    feed_down,
):
    me = lax.axis_index("ctx")
    rows = self_query.shape[0]
    small = jnp.concatenate(
        [
            jnp.pad(jnp.stack([gain_self, gain_cross, gain_feed]), ((0, 0), (0, 128 - rows))),
            jnp.pad(position_bias, ((0, 9), (0, 128 - HEADS))),
        ],
        axis=0,
    )
    pair = block_pairs[me]
    query_blocks = jnp.stack([pair, 31 - pair])
    key_blocks = jnp.stack([block_pairs, 31 - block_pairs], axis=1).reshape(-1)
    gaps = query_blocks[:, None] - key_blocks[None, :]
    classes = jnp.where(gaps < 0, 4, jnp.minimum(gaps, 3)).astype(jnp.int32)
    wanted = query_blocks[:, None] - jnp.arange(3, dtype=jnp.int32)[None, :]
    near = jnp.max(
        jnp.where(
            wanted[:, :, None] == key_blocks[None, None, :],
            jnp.arange(32, dtype=jnp.int32)[None, None, :],
            -1,
        ),
        axis=-1,
    )

    slab = jnp.arange(128, dtype=jnp.int32)
    bucket = 4 * (slab // 16) + slab % 16 - 3
    held = (slab % 16 >= 3) & (slab % 16 < 7)
    hot = (held[:, None] & (bucket[:, None] == bucket_table[None, :])).astype(BF)
    (
        kv_one, kv_two, square, gate_up, down, gains, normed_one, queries, tiles, attended,
        self_totals, mid_one, normed_two, cross_queries, cross_attended, cross_totals, mid_two,
        normed_three, self_kv, cross_kv,
    ) = front(
        [
            self_key, self_value, cross_key, cross_value,
            self_query, self_out, cross_query, cross_out,
            feed_gate, feed_up, feed_down,
        ],
        [small, decoder_in[0], encoder_states[0], hot, strip_hot(), classes],
        0,
    )
    kv_one = kv_one.reshape(D, 2 * D)
    kv_two = kv_two.reshape(D, 2 * D)
    square = square.reshape(D, 4 * D)
    gate_up = gate_up.reshape(D, 2 * FF)
    down = down.reshape(FF, D)
    query_one, out_one, query_two, out_two = (square[:, k * D : k * D + D] for k in range(4))
    norm_one, norm_two, norm_three = gains[0:1], gains[1:2], gains[2:3]
    bucket_hot = (bucket_table[:, None] == jnp.arange(32, dtype=jnp.int32)[None, :]).astype(BF)
    tokens = decoder_in[0].astype(F32)
    states = encoder_states[0]
    upstream = out_grad[0]
    gate_up_values = matmul(normed_three, gate_up).astype(BF).astype(F32)
    gate_values, up_values = gate_up_values[:, :FF], gate_up_values[:, FF:]
    hidden, pull_feed = jax.vjp(gelu_product, gate_values, up_values)
    hidden = hidden.astype(BF)
    block_out = mid_two + matmul(hidden, down)

    d_hidden = transposed_right(upstream, down)
    d_gate, d_up = (part.astype(BF) for part in pull_feed(d_hidden))
    d_gate_up = jnp.concatenate([d_gate, d_up], axis=1)
    feed_parts = feed_gradients(normed_three, hidden, d_gate, d_up, upstream)
    d_normed_three = transposed_right(d_gate_up, gate_up)
    part_three, grad_norm_three = rms_back(mid_two, norm_three, d_normed_three)
    d_mid_two = upstream.astype(F32) + part_three
    cross_branch = d_mid_two.astype(BF)
    d_cross_attended = transposed_right(cross_branch, out_two).astype(BF)
    feed_parts, d_cross_attended = lax.optimization_barrier((feed_parts, d_cross_attended))
    feed_parts = [over_z(*parts) for parts in feed_parts]
    d_cross_queries, d_cross_kv_all = attend_back(
        cross_queries, cross_kv, d_cross_attended, cross_totals, ENC, 0
    )
    d_normed_two = transposed_right(d_cross_queries, query_two)
    part_two, grad_norm_two = rms_back(mid_one, norm_two, d_normed_two)
    d_mid_one = d_mid_two + part_two
    self_branch = d_mid_one.astype(BF)
    d_attended = transposed_right(self_branch, out_one).astype(BF)
    feed_parts[1], d_attended = lax.optimization_barrier((feed_parts[1], d_attended))
    d_queries, d_kv_all, strips = attend_back(
        queries, self_kv, d_attended, self_totals, TOK, 0, classes, near, tiles
    )
    feed_parts, d_queries, d_kv_all, strips = lax.optimization_barrier(
        (feed_parts, d_queries, d_kv_all, strips)
    )
    wide, tall = (
        mine + jnp.concatenate([inner, outer], axis=1) for mine, inner, outer in feed_parts
    )
    grad_table = matmul(bias_sums(strips), bucket_hot.astype(F32)).T.reshape(8, 4, HEADS)
    grad_gains = jnp.stack([grad_norm_two, grad_norm_three]).reshape(2, 8, rows)
    grad_small = jnp.concatenate(
        [
            jnp.zeros((8, 1, 128), F32),
            jnp.pad(jnp.transpose(grad_gains, (1, 0, 2)), ((0, 0), (0, 0), (0, 128 - rows))),
            jnp.pad(grad_table, ((0, 0), (0, 9), (0, 128 - HEADS))),
        ],
        axis=1,
    )
    done = finish(
        [
            cross_attended, normed_two, attended, normed_one,
            cross_branch, d_cross_queries, self_branch, d_queries,
            wide, tall,
            d_kv_all.reshape(8, 2, 2, TOK, D),
            d_cross_kv_all.reshape(8, 2, 2, ENC, D),
        ],
        [
            states,
            kv_one,
            kv_two,
            transposed_right(d_queries, query_one),
            d_mid_one,
            decoder_in[0],
            norm_one,
            grad_small,
        ],
        3,
    )
    early, late, extras, grad_decoder, grad_encoder = done
    (
        grad_out_two, grad_query_two, grad_out_one, grad_query_one,
        grad_key_two, grad_value_two, grad_key_one, grad_value_one,
        grad_gate, grad_up, grad_down,
    ) = unpack(early, late)
    return (
        block_out[None],
        grad_decoder[None],
        grad_encoder[None],
        extras[0, :rows],
        grad_query_one,
        grad_key_one,
        grad_value_one,
        grad_out_one,
        extras[3:7, :HEADS],
        extras[1, :rows],
        grad_query_two,
        grad_key_two,
        grad_value_two,
        grad_out_two,
        extras[2, :rows],
        grad_gate,
        grad_up,
        grad_down,
    )


def solution(mesh):
    tokens = P("fsdp", "ctx", None)
    matrix = P("fsdp", None)
    vector = P("fsdp")
    weights = (
        (vector,) + (matrix,) * 5 + (vector,) + (matrix,) * 4 + (vector,) + (matrix,) * 3
    )
    return jax.shard_map(
        body,
        mesh=mesh,
        in_specs=(tokens,) * 3 + (P(), P()) + weights,
        out_specs=(tokens,) * 3 + weights,
        check_vma=False,
    )
```

```python
import functools

import jax
import jax.numpy as jnp
from jax import lax
from jax.experimental import pallas as pl
from jax.experimental.pallas import tpu as pltpu
from jax.sharding import PartitionSpec as P

D = 768
FF = 2048
HEADS = 12
HEAD_DIM = 64
PAIRS = HEADS // 2
N_CTX = 16
TOK = 128
ENC = 64
HALF = 64
REACH = 128
BF = jnp.bfloat16
F32 = jnp.float32
MIB = 1024 * 1024


def ctx_place():
    me = lax.axis_index("ctx")
    core = me % 2
    high = (me // 2) % 2
    y = me // 4
    return me, core, high, y


def slot_of(y, shift, high, core):
    return ((y + shift) % 4) * 4 + 2 * high + core


def split_heads(block):
    lane = lax.broadcasted_iota(jnp.int32, block.shape, 1)
    nothing = jnp.zeros_like(block)
    return jnp.concatenate(
        [jnp.where(lane < HEAD_DIM, block, nothing), jnp.where(lane < HEAD_DIM, nothing, block)],
        axis=0,
    )


def join_heads(transposed):
    row = lax.broadcasted_iota(jnp.int32, (2 * HEAD_DIM, TOK), 0)
    return jnp.where(row < HEAD_DIM, transposed[:, :TOK], transposed[:, TOK:]).T


def contract(left, right, dims):
    return lax.dot_general(left, right, (dims, ((), ())), preferred_element_type=F32)


def key_chunk(ref, j):
    if ref.shape[2] == 2 * HALF:
        return ref[j, 0]
    return ref[pl.ds(2 * j, 2), 0].reshape(2 * HALF, 2 * HEAD_DIM)


def bias_chunk(class_ref, tile_ref, j, first=0):
    lane = lax.broadcasted_iota(jnp.int32, (HALF, TOK), 1)
    rows = []
    for half in range(2):
        spot = 2 * j + half
        near = class_ref[0, spot]
        far = class_ref[1, spot]
        rows.append(
            jnp.concatenate(
                [
                    jnp.where(lane < HALF, tile_ref[first + head, near], tile_ref[first + head, far])
                    for head in range(2)
                ],
                axis=1,
            )
        )
    return jnp.concatenate(rows, axis=0)


def fold(values, join):
    return join(values.reshape(-1, 8, values.shape[-1]), axis=0)


def attend_pair(queries, keys, values, bias, score_ref, share_ref, chunks):
    queries = split_heads(queries)
    highest = None
    for j in range(chunks):
        scores = contract(keys(j), queries, ((1,), (1,)))
        if bias is not None:
            scores = scores + bias(j)
        score_ref[j] = scores
        top = fold(scores, jnp.max)
        highest = top if highest is None else jnp.maximum(highest, top)
    highest = jnp.max(highest, axis=0, keepdims=True)
    summed = jnp.zeros((8, 2 * TOK), F32)
    for j in range(chunks):
        raised = jnp.exp(score_ref[j] - highest)
        summed = summed + fold(raised, jnp.sum)
        share_ref[j] = raised.astype(BF)
    summed = jnp.sum(summed, axis=0, keepdims=True)
    gathered = jnp.concatenate([values(j) for j in range(chunks)], axis=0)
    mixed = contract(gathered, share_ref[:chunks].reshape(-1, 2 * TOK), ((0,), (0,)))
    return join_heads(mixed / summed).astype(BF), highest + jnp.log(summed)


def attend_pairs(first, last, kv_ref, query_ref, out_ref, total_ref, score_ref, share_ref, bias=None):
    rows = kv_ref.shape[2]
    chunks = N_CTX * rows // TOK

    def step(pair, carry):
        cut = pl.ds(pl.multiple_of(pair * TOK, TOK), TOK)

        def chunk(part, j):
            if rows == TOK:
                return kv_ref[j, part, :, cut]
            return kv_ref[2 * j : 2 * j + 2, part, :, cut].reshape(TOK, TOK)

        mixed, total = attend_pair(
            query_ref[:, cut],
            functools.partial(chunk, 0),
            functools.partial(chunk, 1),
            None if bias is None else functools.partial(bias, pair),
            score_ref,
            share_ref,
            chunks,
        )
        out_ref[:, cut] = mixed
        total_ref[pair] = jnp.broadcast_to(total, (8, 2 * TOK))
        return carry

    lax.fori_loop(first, last, step, 0)


def strip_hot():
    shape = (REACH, 3 * TOK)
    spot = lax.broadcasted_iota(jnp.int32, shape, 1)
    distance = jnp.clip(HALF * (spot // TOK) + spot % TOK - (HALF - 1), 0, REACH - 1)
    return (distance == lax.broadcasted_iota(jnp.int32, shape, 0)).astype(BF)


def index_tables(me, pairs_ref, class_ref, near_ref):
    own = pairs_ref[me]
    for half in range(2):
        query = 31 - own if half else own
        spots = [jnp.int32(-1)] * 3
        for block in range(32):
            pair = pairs_ref[block // 2]
            key = 31 - pair if block % 2 else pair
            gap = query - key
            class_ref[half, block] = jnp.where(gap < 0, 4, jnp.minimum(gap, 3))
            for near in range(3):
                spots[near] = jnp.where(gap == near, block, spots[near])
        for near in range(3):
            near_ref[half, near] = spots[near]


def build_tiles(bias_rows, strips, tile_ref):
    lane = lax.broadcasted_iota(jnp.int32, (HALF, TOK), 1)
    key = lax.broadcasted_iota(jnp.int32, (HALF, TOK), 0)
    row = jnp.where(lane < HALF, lane, lane - HALF)
    for head in range(HEADS):
        for gap in range(3):
            strip = strips[head : head + 1, gap * TOK : gap * TOK + TOK]
            turned = pltpu.roll(
                jnp.broadcast_to(strip, (HALF, TOK)), 65, 1, stride=1, stride_axis=0
            )
            tile = jnp.where(lane < HALF, turned, pltpu.roll(turned, HALF, 1))
            if gap == 0:
                tile = jnp.where(key > row, -1e30, tile)
            tile_ref[head, gap] = tile
        tile_ref[head, 3] = jnp.broadcast_to(bias_rows[head : head + 1, REACH - 1 :], (HALF, TOK))
        tile_ref[head, 4] = jnp.full((HALF, TOK), -1e30, F32)


def torus_place():
    me, core, high, y = ctx_place()
    shard = lax.axis_index("fsdp")
    return me, core, high, y, shard // 4, shard % 4


def hop(src, dst, send_sem, recv_sem, ctx, fsdp):
    return pltpu.make_async_remote_copy(
        src_ref=src,
        dst_ref=dst,
        send_sem=send_sem,
        recv_sem=recv_sem,
        device_id={"ctx": ctx, "fsdp": fsdp},
    )


def greet_all(devices):
    barrier = pltpu.get_barrier_semaphore()
    for ctx, fsdp in devices:
        pl.semaphore_signal(barrier, inc=1, device_id={"ctx": ctx, "fsdp": fsdp})
    pl.semaphore_wait(barrier, len(devices))


ROOT = (2.0 / 3.141592653589793) ** 0.5
PACKS = ((0, 1), (2, 3), (4, 5, 6, 7), (8, 9), (10,))


def front_kernel(*refs):
    sources = refs[:11]
    small_ref, token_ref, state_ref, upstream_ref, bucket_ref, pairs_ref = refs[11:17]
    results = refs[17:20]
    (
        gain_out, normed_out, query_out, tile_ref, attended_ref, total_ref, mid_one_ref,
        normed_two_ref, cross_query_ref, cross_attended_ref, cross_total_ref,
        block_ref, d_mid_ref, branch_ref, d_cross_ref, gain_grad_ref,
        wide_mine, wide_inner, wide_outer, tall_mine, tall_inner, tall_outer,
        class_ref, near_ref, self_result, cross_result,
    ) = refs[20:46]
    targets = refs[46:51]
    (
        self_out_ref, cross_out_ref, landing, self_ref, cross_ref, score_ref, share_ref,
        feed_left, feed_right, slope_ref, turned, turned_hidden,
        send_sem, x_sem, z_sem, core_sem,
        fill_sem, small_sem, self_sem, cross_sem, feed_sem, local_sem,
    ) = refs[51:]
    me, core, high, y, low, x = torus_place()
    shard = low * 4 + x
    sibling = (slot_of(y, 0, high, 1 - core), shard)
    inside = (me, (1 - low) * 4 + x)
    outside = (slot_of(y, 0, 1 - high, core), (1 - low) * 4 + x)
    across = slot_of(y, 0, 1 - high, core)
    ahead, behind = (slot_of(y, shift, high, core) for shift in (1, 3))
    others = [low * 4 + (x + shift) % 4 for shift in (1, 2, 3)]
    peers = [(shard + shift) % 8 for shift in range(1, 8)]
    greet_all(
        [sibling, outside, (across, shard), (ahead, shard), (behind, shard)]
        + [(me, peer) for peer in peers]
    )
    sends = []

    def send(src, dst, recv_sem, device):
        copy = hop(src, dst, send_sem.at[len(sends)], recv_sem, *device)
        copy.start()
        sends.append(copy)

    def arrived(ref, recv_sem):
        hop(ref, ref, send_sem.at[0], recv_sem, *sibling).wait_recv()

    def bring(src, dst, sem):
        copy = pltpu.make_async_copy(src, dst, sem)
        copy.start()
        return copy


    def part(k, owner, whose, side=None):
        ref = targets[k]
        count = ref.shape[1] // 2
        start = pl.multiple_of(whose * count, 16)
        if side is None:
            return ref.at[owner, pl.ds(start, count), :]
        width = ref.shape[2] // 2
        return ref.at[owner, pl.ds(start, count), pl.ds(side * width, width)]

    def fill(k):
        copies = []
        start = 0
        for source in PACKS[k]:
            width = sources[source].shape[1]
            copies.append(
                bring(
                    sources[source],
                    targets[k].at[shard, :, pl.ds(start, width)],
                    fill_sem.at[source],
                )
            )
            start += width
        return copies

    def send_own(k):
        for copy in fills[k]:
            copy.wait()
        for spot in (1, 0, 2):
            block = part(k, shard, core)
            send(block, block, x_sem.at[k, spot], (me, others[spot]))
        for side, device in enumerate((inside, outside)):
            piece = part(k, shard, core, side)
            send(piece, piece, z_sem.at[k, 3, side], device)


    def pass_x(k):
        for spot in (0, 2, 1):
            owner = low * 4 + (x + 3 - spot) % 4
            block = part(k, owner, core)
            arrived(block, x_sem.at[k, spot])
            for side, device in enumerate((inside, outside)):
                piece = part(k, owner, core, side)
                send(piece, piece, z_sem.at[k, spot, side], device)
            send(block, block, core_sem.at[k, spot], sibling)

    def pass_z(k):
        for spot in (3, 0, 2, 1):
            owner = (1 - low) * 4 + (x + 3 - spot) % 4
            for side in range(2):
                piece = part(k, owner, core, side)
                arrived(piece, z_sem.at[k, spot, side])
                send(piece, piece, core_sem.at[k, 3 + 2 * spot + side], sibling)

    def complete(k):
        for spot in range(3):
            owner = low * 4 + (x + 3 - spot) % 4
            arrived(part(k, owner, 1 - core), core_sem.at[k, spot])
        for spot in range(4):
            owner = (1 - low) * 4 + (x + 3 - spot) % 4
            for side in range(2):
                arrived(part(k, owner, 1 - core, side), core_sem.at[k, 3 + 2 * spot + side])


    def kv_start(src, out, sems):
        send(src, out.at[me], sems.at[me, 0], (across, shard))
        send(src, out.at[me], sems.at[me, 0], (ahead, shard))
        send(src, out.at[me], sems.at[me, 0], (behind, shard))
        send(src, out.at[me], sems.at[me, 0], sibling)

    def kv_across(out, sems):
        block = out.at[across]
        arrived(block, sems.at[across, 0])
        send(block, block, sems.at[across, 0], (ahead, shard))
        send(block, block, sems.at[across, 0], (behind, shard))
        send(block, block, sems.at[across, 0], sibling)

    def kv_near(out, sems, flip):
        half = 1 - high if flip else high
        slot = slot_of(y, 1, half, core)
        block = out.at[slot]
        arrived(block, sems.at[slot, 0])
        send(block.at[0], block.at[0], sems.at[slot, 0], (behind, shard))
        send(block, block, sems.at[slot, 0], sibling)
        slot = slot_of(y, 3, half, core)
        block = out.at[slot]
        arrived(block, sems.at[slot, 0])
        send(block.at[1], block.at[1], sems.at[slot, 1], (ahead, shard))
        send(block, block, sems.at[slot, 0], sibling)

    def kv_far(out, sems, flip):
        slot = slot_of(y, 2, 1 - high if flip else high, core)
        for part in range(2):
            arrived(out.at[slot, part], sems.at[slot, part])
        send(out.at[slot], out.at[slot], sems.at[slot, 0], sibling)

    def kv_complete(out, sems):
        for shift in range(4):
            for half in range(2):
                slot = slot_of(y, shift, half, 1 - core)
                arrived(out.at[slot], sems.at[slot, 0])

    fills = [fill(k) for k in range(5)]
    own_small = bring(small_ref, landing.at[shard], local_sem.at[0])
    for spot, peer in enumerate(peers):
        send(small_ref, landing.at[shard], small_sem.at[spot], (me, peer))
    send_own(0)
    send_own(1)
    own_small.wait()
    for spot in range(7):
        arrived(landing.at[(shard + 7 - spot) % 8], small_sem.at[spot])
    gains = landing[...].astype(F32)
    gain = [
        jnp.concatenate([gains[owner, k : k + 1, :96] for owner in range(8)], axis=1)
        for k in range(3)
    ]
    for k in range(3):
        gain_out[k : k + 1, :] = gain[k]
    tokens = token_ref[...].astype(F32)
    normed = rms_scaled(tokens, gain[0])
    normed_out[...] = normed
    pass_x(0)
    send_own(2)
    pass_z(0)
    pass_x(1)
    send_own(3)
    complete(0)
    exits = [bring(targets[0], results[0], local_sem.at[1])]
    for half in range(2):
        weight = targets[0][:, :, half * D : half * D + D].reshape(D, D)
        self_ref[half] = matmul(normed, weight).astype(BF)
    kv_start(self_ref, self_out_ref, self_sem)
    own_self = bring(self_ref, self_out_ref.at[me], local_sem.at[2])
    pass_z(1)
    complete(1)
    exits.append(bring(targets[1], results[1], local_sem.at[4]))
    for half in range(2):
        weight = targets[1][:, :, half * D : half * D + D].reshape(D, D)
        cross_ref[half] = matmul(state_ref[...], weight).astype(BF)
    kv_start(cross_ref, cross_out_ref, cross_sem)
    own_cross = bring(cross_ref, cross_out_ref.at[me], local_sem.at[3])
    index_tables(me, pairs_ref, class_ref, near_ref)
    slab = lax.broadcasted_iota(jnp.int32, (128, REACH), 0)
    place = slab % 16 - 3
    wanted = jnp.where((place >= 0) & (place < 4), 4 * (slab // 16) + place, -1)
    hot = jnp.where(wanted == bucket_ref[...], 1.0, 0.0).astype(BF)
    bias_rows = contract(landing[...].reshape(128, 128), hot, ((0,), (0,)))[:16]
    build_tiles(bias_rows, matmul(bias_rows.astype(BF), strip_hot()), tile_ref)
    kv_across(self_out_ref, self_sem)
    pass_x(2)
    send_own(4)
    kv_near(self_out_ref, self_sem, False)
    pass_z(2)
    kv_across(cross_out_ref, cross_sem)
    kv_near(self_out_ref, self_sem, True)
    pass_x(3)
    complete(2)
    exits.append(bring(targets[2], results[2], local_sem.at[5]))

    def square(k):
        return targets[2][:, :, k * D : k * D + D].reshape(D, D)

    query_out[...] = matmul(normed, square(0)).astype(BF)
    kv_far(self_out_ref, self_sem, False)
    kv_far(self_out_ref, self_sem, True)
    kv_near(cross_out_ref, cross_sem, False)
    own_self.wait()
    own_cross.wait()
    kv_complete(self_out_ref, self_sem)
    exits.append(bring(self_out_ref, self_result, local_sem.at[6]))

    def attend_self(first, last):
        attend_pairs(
            first, last, self_out_ref, query_out, attended_ref, total_ref, score_ref, share_ref,
            lambda pair, j: bias_chunk(class_ref, tile_ref, j, 2 * pair),
        )

    def attend_cross(first, last):
        attend_pairs(
            first, last, cross_out_ref, cross_query_ref, cross_attended_ref, cross_total_ref,
            score_ref, share_ref,
        )

    attend_self(0, 2)
    pass_x(4)
    kv_near(cross_out_ref, cross_sem, True)
    kv_far(cross_out_ref, cross_sem, False)
    attend_self(2, 4)
    pass_z(3)
    kv_far(cross_out_ref, cross_sem, True)
    attend_self(4, 6)
    mid_one = tokens + matmul(attended_ref[...], square(1))
    mid_one_ref[...] = mid_one
    normed_two = rms_scaled(mid_one, gain[1])
    normed_two_ref[...] = normed_two
    cross_query_ref[...] = matmul(normed_two, square(2)).astype(BF)
    pass_z(4)
    kv_complete(cross_out_ref, cross_sem)
    exits.append(bring(cross_out_ref, cross_result, local_sem.at[7]))
    attend_cross(0, 3)
    complete(3)
    attend_cross(3, 6)
    complete(4)
    mid_two = mid_one_ref[...] + matmul(cross_attended_ref[...], square(3))


    normed_three = rms_scaled(mid_two, gain[2])
    upstream = upstream_ref[...]
    near_rows, far_rows = pl.ds(0, TOK), pl.ds(TOK, TOK)
    feed_left[near_rows, :D] = normed_three
    for piece in range(4):
        start = piece * 512
        gate = matmul(normed_three, targets[3][:, :, start : start + 512].reshape(D, 512))
        up = matmul(normed_three, targets[3][:, :, FF + start : FF + start + 512].reshape(D, 512))
        gate = gate.astype(BF).astype(F32)
        up = up.astype(BF).astype(F32)
        square_gate = gate * gate
        curve = jnp.tanh(ROOT * (gate + 0.044715 * gate * square_gate))
        raised = 0.5 * gate * (1.0 + curve)
        steep = 0.5 * (1.0 + curve) + 0.5 * gate * (1.0 - curve * curve) * (
            ROOT * (1.0 + 3.0 * 0.044715 * square_gate)
        )
        d_hidden = contract(
            upstream, targets[4][2 * piece : 2 * piece + 2].reshape(512, D), ((1,), (1,))
        )
        feed_left[near_rows, D + start : D + start + 512] = (raised * up).astype(BF)
        slope_ref[0, :, start : start + 512] = (d_hidden * up * steep).astype(BF)
        slope_ref[1, :, start : start + 512] = (d_hidden * raised).astype(BF)
    half = D // 2
    near_half = pl.ds(pl.multiple_of(core * half, 128), half)
    far_half = pl.ds(pl.multiple_of((1 - core) * half, 128), half)
    swaps = []
    for index, (src, dst) in enumerate(
        (
            (feed_left.at[near_rows], feed_left.at[far_rows]),
            (slope_ref.at[1 - core], feed_right.at[far_rows, pl.ds(0, FF)]),
            (upstream_ref.at[:, far_half], feed_right.at[far_rows, pl.ds(FF, half)]),
        )
    ):
        copy = hop(src, dst, feed_sem.at[0, index], feed_sem.at[1, index], *sibling)
        copy.start()
        swaps.append(copy)
    feed_right[near_rows, :FF] = slope_ref[core]
    feed_right[near_rows, FF:] = upstream_ref[:, near_half]
    block_ref[...] = mid_two + matmul(feed_left[near_rows, D:], targets[4][...].reshape(FF, D))
    grad = contract(slope_ref[0], targets[3][:, :, :FF].reshape(D, FF), ((1,), (1,)))
    grad = grad + contract(slope_ref[1], targets[3][:, :, FF:].reshape(D, FF), ((1,), (1,)))
    inverse = lax.rsqrt(jnp.mean(mid_two * mid_two, axis=-1, keepdims=True) + 1e-06)
    gain_grad_ref[...] = jnp.sum(mid_two * inverse * grad, axis=0, keepdims=True)
    scaled = gain[2] * grad
    mixed = jnp.mean(mid_two * scaled, axis=-1, keepdims=True)
    d_mid_two = upstream.astype(F32) + (
        inverse * scaled - mid_two * (inverse * inverse * inverse * mixed)
    )
    d_mid_ref[...] = d_mid_two
    branch_ref[...] = d_mid_two.astype(BF)
    d_cross_ref[...] = contract(d_mid_two.astype(BF), square(3), ((1,), (1,))).astype(BF)
    for copy in swaps:
        copy.wait_recv()
    turned[...] = feed_left[:, :D].T.reshape(8, 96, 2 * TOK)
    turned_hidden[...] = feed_left[:, D:].T.reshape(8, FF // 8, 2 * TOK)
    for group in range(2):
        owners = pl.ds(4 * ((1 - low + group) % 2), 4)
        left = turned[owners].reshape(4 * 96, 2 * TOK)
        for piece in range(4):
            cut = slice(piece * 512, piece * 512 + 512)
            part = matmul(left, feed_right[:, cut]).astype(BF).reshape(4, 96, 512)
            if group:
                wide_mine[:, :, cut] = part
            else:
                wide_inner[:, :, cut] = part[:, :48]
                wide_outer[:, :, cut] = part[:, 48:]
        left = turned_hidden[owners].reshape(4 * FF // 8, 2 * TOK)
        part = matmul(left, feed_right[:, FF:]).astype(BF).reshape(4, FF // 8, half)
        if group:
            tall_mine[...] = part
        else:
            tall_inner[...] = part[:, :128]
            tall_outer[...] = part[:, 128:]
    for copy in sends + swaps:
        copy.wait_send()
    for copy in exits:
        copy.wait()


def front(weights, others, collective_id):
    dma = pltpu.SemaphoreType.DMA
    packs = [
        (8, weights[group[0]].shape[0], sum(weights[k].shape[1] for k in group)) for group in PACKS
    ]
    anywhere = pl.BlockSpec(memory_space=pl.ANY)
    inside = pl.BlockSpec(memory_space=pltpu.VMEM)
    scalars = pl.BlockSpec(memory_space=pltpu.SMEM)
    return pl.pallas_call(
        front_kernel,
        out_shape=[jax.ShapeDtypeStruct(pack, BF) for pack in packs[:3]]
        + [
            jax.ShapeDtypeStruct((3, D), F32),
            jax.ShapeDtypeStruct((TOK, D), BF),
            jax.ShapeDtypeStruct((TOK, D), BF),
            jax.ShapeDtypeStruct((HEADS, 5, HALF, TOK), F32),
            jax.ShapeDtypeStruct((TOK, D), BF),
            jax.ShapeDtypeStruct((PAIRS, 8, 2 * TOK), F32),
            jax.ShapeDtypeStruct((TOK, D), F32),
            jax.ShapeDtypeStruct((TOK, D), BF),
            jax.ShapeDtypeStruct((TOK, D), BF),
            jax.ShapeDtypeStruct((TOK, D), BF),
            jax.ShapeDtypeStruct((PAIRS, 8, 2 * TOK), F32),
            jax.ShapeDtypeStruct((TOK, D), F32),
            jax.ShapeDtypeStruct((TOK, D), F32),
            jax.ShapeDtypeStruct((TOK, D), BF),
            jax.ShapeDtypeStruct((TOK, D), BF),
            jax.ShapeDtypeStruct((1, D), F32),
            jax.ShapeDtypeStruct((4, 96, FF), BF),
            jax.ShapeDtypeStruct((4, 48, FF), BF),
            jax.ShapeDtypeStruct((4, 48, FF), BF),
            jax.ShapeDtypeStruct((4, 256, D // 2), BF),
            jax.ShapeDtypeStruct((4, 128, D // 2), BF),
            jax.ShapeDtypeStruct((4, 128, D // 2), BF),
            jax.ShapeDtypeStruct((2, 32), jnp.int32),
            jax.ShapeDtypeStruct((2, 3), jnp.int32),
            jax.ShapeDtypeStruct((N_CTX, 2, TOK, D), BF),
            jax.ShapeDtypeStruct((N_CTX, 2, ENC, D), BF),
        ],
        in_specs=[anywhere] * 12 + [inside] * 4 + [scalars],
        out_specs=[anywhere] * 3 + [inside] * 22 + [scalars] * 2 + [anywhere] * 2,
        scratch_shapes=[pltpu.VMEM(pack, BF) for pack in packs]
        + [
            pltpu.VMEM((N_CTX, 2, TOK, D), BF),
            pltpu.VMEM((N_CTX, 2, ENC, D), BF),
            pltpu.VMEM((8, 16, 128), BF),
            pltpu.VMEM((2, TOK, D), BF),
            pltpu.VMEM((2, ENC, D), BF),
            pltpu.VMEM((N_CTX, TOK, 2 * TOK), F32),
            pltpu.VMEM((N_CTX, TOK, 2 * TOK), BF),
            pltpu.VMEM((2 * TOK, D + FF), BF),
            pltpu.VMEM((2 * TOK, FF + D // 2), BF),
            pltpu.VMEM((2, TOK, FF), BF),
            pltpu.VMEM((8, 96, 2 * TOK), BF),
            pltpu.VMEM((8, FF // 8, 2 * TOK), BF),
            dma((5 * 22 + 7 + 2 * 18,)),
            dma((5, 3)),
            dma((5, 4, 2)),
            dma((5, 11)),
            dma((11,)),
            dma((7,)),
            dma((N_CTX, 2)),
            dma((N_CTX, 2)),
            dma((2, 3)),
            dma((8,)),
        ],
        compiler_params=pltpu.CompilerParams(
            collective_id=collective_id, has_side_effects=True, vmem_limit_bytes=60 * MIB
        ),
        name="front",
    )(*weights, *others)


PIECE = 96
WIDTHS = (D // 2, D // 2, D // 2, D // 2, D, D, FF)
SPAN = sum(WIDTHS)
DOWN = len(WIDTHS)
CHUNKS = DOWN + 1
CROSS_KV, SELF_KV, WIDE = 4, 5, 6
LEFT = (D,) * 4
RIGHT = (D // 2,) * 4


def finish_kernel(*refs):
    lefts = refs[:4]
    rights = refs[4:8]
    wide_refs, down_refs = refs[8:11], refs[11:14]
    dkv_ref, dckv_ref, square_ref = refs[14:17]
    state_ref, kv_ref, ckv_ref, dq_ref, dmid_ref, token_ref, gain_ref, small_ref = refs[17:25]
    early_out, late_out, small_out, decoder_ref, encoder_ref = refs[25:30]
    (
        left_all, right_all, turned, turned_one, turned_state, state_all, s_right, c_right,
        kept, from_z, from_x, via_x, d_z, d_x, d_via,
        s_kept, s_core, s_row, s_via, s_stage, s_high, s_fin,
        c_kept, c_core, c_row, c_via, c_stage, c_high, c_fin,
        small_f32, sm_own, sm_core, sm_z, sm_x, sm_ctx, sm_total,
        packed, from_ctx, land, late_packed, late_from, late_land,
        wide_add, down_add, query_ref, bring_sem,
        s_sem, c_sem, fill_sem, act_send, act_recv, late_send, late_recv, z_send, z_recv,
        x_send, x_recv, ctx_send, ctx_recv, pass_send, pass_recv, sm_send, sm_recv, local_sem,
    ) = refs[30:]
    me, core, high, y, low, x = torus_place()
    shard = low * 4 + x
    rank = y * 2 + high
    sibling = (slot_of(y, 0, high, 1 - core), shard)
    inside = (me, (1 - low) * 4 + x)
    outside = (slot_of(y, 0, 1 - high, core), (1 - low) * 4 + x)
    across = (slot_of(y, 0, 1 - high, core), shard)
    others = [low * 4 + (x + shift) % 4 for shift in (1, 2, 3)]
    ahead = (slot_of(y, 1, high, core), shard)
    behind = (slot_of(y, 3, high, core), shard)
    shifts = [(dy, dz) for dy in range(4) for dz in range(2)][1:]
    mates = [((y + dy) % 4) * 2 + (high + dz) % 2 for dy, dz in shifts]
    greet_all(
        [sibling, inside, outside]
        + [(me, other) for other in others]
        + [(mate * 2 + core, shard) for mate in mates]
    )
    sends = []

    def go(src, dst, send_sem, recv_sem, device):
        copy = hop(src, dst, send_sem, recv_sem, *device)
        copy.start()
        sends.append(copy)
        return copy

    def bring(src, dst, sem):
        copy = pltpu.make_async_copy(src, dst, sem)
        copy.start()
        return copy


    def rows_start(source, held, arrived, sem):
        over = []
        local = []
        for spot, shift in enumerate((2, 1, 3, 0)):
            pair = pl.ds(((y + shift) % 4) * 2, 2)
            block = pl.ds(2 * spot, 2)
            over.append(
                go(
                    source.at[pair, 1 - core], arrived.at[block],
                    sem.at[0, spot], sem.at[1, spot], sibling,
                )
            )
            local.append(bring(source.at[pair, core], held.at[block], sem.at[4, spot]))
        return over, local


    def rows_send(copies, held, arrived, via, row, sem):
        over, local = copies
        onward = []
        for spot in range(4):
            local[spot].wait()
            over[spot].wait_recv()
            for block in (2 * spot, 2 * spot + 1):
                for part in range(2):
                    held[block, part] = held[block, part] + arrived[block, part]
            if spot == 0:
                first = go(held.at[0], via.at[0], sem.at[2, 0], sem.at[3, 0], ahead)
                second = go(held.at[1], via.at[1], sem.at[2, 1], sem.at[3, 1], behind)
            elif spot == 1:
                onward.append(go(held.at[3], row.at[0, 1], sem.at[2, 2], sem.at[3, 2], ahead))
            elif spot == 2:
                onward.append(go(held.at[4], row.at[1, 0], sem.at[2, 3], sem.at[3, 3], behind))
        return first, second, onward

    def rows_via(state, held, via, row, sem):
        first, second, onward = state
        first.wait_recv()
        for part in range(2):
            held[2, part] = held[2, part] + via[0, part]
        onward.append(go(held.at[2], row.at[0, 0], sem.at[2, 4], sem.at[3, 4], ahead))
        second.wait_recv()
        for part in range(2):
            held[5, part] = held[5, part] + via[1, part]
        onward.append(go(held.at[5], row.at[1, 1], sem.at[2, 5], sem.at[3, 5], behind))
        return onward

    def rows_total(held, row, half, part):
        return (
            held[6 + half, part].astype(F32)
            + row[0, half, part].astype(F32)
            + row[1, half, part].astype(F32)
        )

    def rows_across(onward, held, row, stage, landing, sem):
        for copy in onward:
            copy.wait_recv()
        for part in range(2):
            stage[part] = rows_total(held, row, 1 - high, part).astype(BF)
        return go(stage, landing, sem.at[2, 6], sem.at[3, 6], across)

    def rows_sum(last, held, row, landing, final, right, which):
        totals = [rows_total(held, row, high, part) for part in range(2)]
        last.wait_recv()
        for part in range(2):
            final[part] = (totals[part] + landing[part].astype(F32)).astype(BF)
        count = final.shape[1]
        copy = go(
            final.at[1 - core], right.at[pl.ds(count, count)],
            late_send.at[which], late_recv.at[which], sibling,
        )
        right[:count] = final[core]
        return copy


    starts = [sum(WIDTHS[:k]) for k in range(len(WIDTHS))]
    left_starts = [sum(LEFT[:k]) for k in range(4)]
    right_starts = [sum(RIGHT[:k]) for k in range(4)]
    acts = {}
    over_z, over_via, over_x = {}, {}, {}
    column_ahead = (me, low * 4 + (x + 1) % 4)
    column_behind = (me, low * 4 + (x + 3) % 4)

    def buffers(k):
        if k == DOWN:
            return d_z, d_x, d_via, pl.ds(0, D // 2)
        return from_z, from_x, via_x, pl.ds(starts[k], WIDTHS[k])

    def acts_start(index):
        left = pl.ds(left_starts[index], LEFT[index])
        right = pl.ds(right_starts[index], RIGHT[index])
        near = pl.ds(pl.multiple_of(core * RIGHT[index], 128), RIGHT[index])
        far = pl.ds(pl.multiple_of((1 - core) * RIGHT[index], 128), RIGHT[index])
        mine = pl.ds(0, TOK)
        theirs = pl.ds(TOK, TOK)
        acts[index] = (
            bring(lefts[index], left_all.at[mine, left], fill_sem.at[index, 0]),
            bring(rights[index].at[:, near], right_all.at[mine, right], fill_sem.at[index, 1]),
            go(
                lefts[index], left_all.at[theirs, left],
                act_send.at[index, 0], act_recv.at[index, 0], sibling,
            ),
            go(
                rights[index].at[:, far], right_all.at[theirs, right],
                act_send.at[index, 1], act_recv.at[index, 1], sibling,
            ),
        )

    def multiply(k, left_ref, right):
        landing, _, _, cut = buffers(k)
        for group in range(2):
            owners = pl.ds(4 * ((1 - low + group) % 2), 4)
            left = left_ref[owners].reshape(4 * PIECE, right.shape[0])
            kept[owners, :, cut] = (
                contract(left, right, ((1,), (0,))).astype(BF).reshape(4, PIECE, WIDTHS[k])
            )
            if group == 0:
                half = PIECE // 2
                over_z[k] = [
                    go(
                        kept.at[owners, pl.ds(side * half, half), cut],
                        landing.at[:, pl.ds(side * half, half), cut],
                        z_send.at[k, side],
                        z_recv.at[k, side],
                        device,
                    )
                    for side, device in enumerate((inside, outside))
                ]

    def make(index):
        near_left, near_right, far_left, far_right = acts[index]
        near_left.wait()
        near_right.wait()
        far_left.wait_recv()
        far_right.wait_recv()
        left = left_all[:, left_starts[index] : left_starts[index] + LEFT[index]].T
        right = right_all[:, right_starts[index] : right_starts[index] + RIGHT[index]]
        target = turned_one if index == 3 else turned
        target[...] = left.reshape(8, PIECE, 2 * TOK)
        multiply(index, target, right)

    def step_z(k):
        landing, _, _, cut = buffers(k)
        for copy in over_z[k]:
            copy.wait_recv()
        for column in range(4):
            landing[column, :, cut] = landing[column, :, cut] + kept[4 * low + column, :, cut]
        send_x(k)


    def send_x(k):
        landing, spread, via, cut = buffers(k)
        half = landing.shape[1] // 2
        upper, lower = pl.ds(0, half), pl.ds(half, half)
        away, front_column, back_column = (x + 2) % 4, (x + 1) % 4, (x + 3) % 4
        over_via[k] = (
            go(
                landing.at[away, upper, cut], via.at[0, :, cut],
                x_send.at[k, 0], x_recv.at[k, 0], column_ahead,
            ),
            go(
                landing.at[away, lower, cut], via.at[1, :, cut],
                x_send.at[k, 1], x_recv.at[k, 1], column_behind,
            ),
        )
        over_x[k] = [
            go(
                landing.at[front_column, lower, cut], spread.at[0, lower, cut],
                x_send.at[k, 2], x_recv.at[k, 2], column_ahead,
            ),
            go(
                landing.at[back_column, upper, cut], spread.at[1, upper, cut],
                x_send.at[k, 3], x_recv.at[k, 3], column_behind,
            ),
        ]

    def step_via(k):
        landing, spread, via, cut = buffers(k)
        half = landing.shape[1] // 2
        upper, lower = pl.ds(0, half), pl.ds(half, half)
        front_column, back_column = (x + 1) % 4, (x + 3) % 4
        over_via[k][0].wait_recv()
        landing[front_column, upper, cut] = landing[front_column, upper, cut] + via[0, :, cut]
        over_x[k].append(
            go(
                landing.at[front_column, upper, cut], spread.at[0, upper, cut],
                x_send.at[k, 4], x_recv.at[k, 4], column_ahead,
            )
        )
        over_via[k][1].wait_recv()
        landing[back_column, lower, cut] = landing[back_column, lower, cut] + via[1, :, cut]
        over_x[k].append(
            go(
                landing.at[back_column, lower, cut], spread.at[1, lower, cut],
                x_send.at[k, 5], x_recv.at[k, 5], column_behind,
            )
        )

    def step_x(k):
        landing, spread, _, cut = buffers(k)
        for copy in over_x[k]:
            copy.wait_recv()
        total = landing[x, :, cut].astype(F32)
        for spot in range(2):
            total = total + spread[spot, :, cut].astype(F32)
        total = total.astype(BF)
        half = D // 2
        if k == WIDE:
            for piece in range(8):
                packed[piece, :PIECE, :256] = total[:, piece * 256 : piece * 256 + 256]
        elif k == DOWN:
            for piece in range(8):
                for part in range(3):
                    packed[piece, part * 32 : part * 32 + 32, 256:] = total[
                        piece * 32 : piece * 32 + 32, part * 128 : part * 128 + 128
                    ]
        else:
            middle = PIECE // 2
            for upper in range(2):
                rows = total[upper * middle : upper * middle + middle, :]
                if k == CROSS_KV or k == SELF_KV:
                    for piece in range(2):
                        late_packed[(0 if k == CROSS_KV else 4) + 2 * piece + upper] = rows[
                            :, piece * half : piece * half + half
                        ]
                else:
                    packed[2 * k + upper, PIECE:, :] = rows


    def mate_device(mate):
        return (mate * 2 + core, shard)

    def ctx_start(which, source, landing):
        return [
            go(
                source.at[mate], landing.at[spot],
                ctx_send.at[which, spot], ctx_recv.at[which, spot], mate_device(mate),
            )
            for spot, mate in enumerate(mates)
        ]

    def ctx_sum(which, over, source, landing, final):
        total = source[rank].astype(F32)
        for spot in range(7):
            over[spot].wait_recv()
            total = total + landing[spot].astype(F32)
        final[rank, core] = total.astype(BF)
        own = final.at[rank, core]
        for spot, mate in enumerate(mates):
            go(own, own, ctx_send.at[which, 7 + spot], ctx_recv.at[which, 7 + rank], mate_device(mate))
        go(own, own, pass_send.at[which, 7], pass_recv.at[which, rank], sibling)

    def landed(ref, recv_sem):
        hop(ref, ref, pass_send.at[0, 0], recv_sem, *sibling).wait_recv()

    def ctx_pass(which, final):
        for spot, mate in enumerate(mates):
            block = final.at[mate, core]
            landed(block, ctx_recv.at[which, 7 + mate])
            go(block, block, pass_send.at[which, spot], pass_recv.at[which, mate], sibling)

    def ctx_done(which, final):
        for mate in [rank] + mates:
            landed(final.at[mate, 1 - core], pass_recv.at[which, mate])

    wide_cut = pl.ds(starts[WIDE], FF)
    down_copies = [bring(down_refs[0], d_z, bring_sem.at[0])] + [
        bring(down_refs[1 + side], down_add.at[side], bring_sem.at[1 + side]) for side in range(2)
    ]
    wide_copies = [bring(wide_refs[0], from_z.at[:, :, wide_cut], bring_sem.at[3])] + [
        bring(wide_refs[1 + side], wide_add.at[side], bring_sem.at[4 + side]) for side in range(2)
    ]
    s_copies = rows_start(dkv_ref, s_kept, s_core, s_sem)
    c_copies = rows_start(dckv_ref, c_kept, c_core, c_sem)
    for index in range(4):
        acts_start(index)
    state_near = bring(state_ref, state_all.at[pl.ds(0, ENC)], local_sem.at[0])
    state_far = go(
        state_ref, state_all.at[pl.ds(ENC, ENC)], late_send.at[2], late_recv.at[2], sibling
    )
    query_copy = bring(square_ref.at[:, :, pl.ds(0, D)], query_ref, bring_sem.at[6])
    for copy in down_copies:
        copy.wait()
    for side in range(2):
        for column in range(4):
            rows = slice(side * 128, side * 128 + 128)
            d_z[column, rows, :] = d_z[column, rows, :] + down_add[side, column]
    send_x(DOWN)
    for copy in wide_copies:
        copy.wait()
    for side in range(2):
        for column in range(4):
            rows = slice(side * 48, side * 48 + 48)
            from_z[column, rows, wide_cut] = from_z[column, rows, wide_cut] + wide_add[side, column]
    send_x(WIDE)
    s_state = rows_send(s_copies, s_kept, s_core, s_via, s_row, s_sem)
    make(0)
    make(1)
    s_onward = rows_via(s_state, s_kept, s_via, s_row, s_sem)
    c_state = rows_send(c_copies, c_kept, c_core, c_via, c_row, c_sem)
    make(2)
    make(3)
    step_via(DOWN)
    step_via(WIDE)
    for k in range(4):
        step_z(k)
    state_near.wait()
    state_far.wait_recv()
    turned_state[...] = state_all[...].T.reshape(8, PIECE, 2 * ENC)
    s_last = rows_across(s_onward, s_kept, s_row, s_stage, s_high, s_sem)
    c_onward = rows_via(c_state, c_kept, c_via, c_row, c_sem)
    for k in range(4):
        step_via(k)
    step_x(DOWN)
    step_x(WIDE)
    s_far = rows_sum(s_last, s_kept, s_row, s_high, s_fin, s_right, 0)
    for k in range(4):
        step_x(k)
    early = ctx_start(0, packed, from_ctx)
    s_far.wait_recv()
    multiply(SELF_KV, turned_one, s_right[...])
    c_last = rows_across(c_onward, c_kept, c_row, c_stage, c_high, c_sem)
    tokens = token_ref[...].astype(F32)
    d_kv = jnp.concatenate([s_fin[0], s_fin[1]], axis=1)
    query_copy.wait()
    grad = contract(dq_ref[...], query_ref[...].reshape(D, D), ((1,), (1,)))
    grad = grad + contract(d_kv, kv_ref[...], ((1,), (1,)))
    inverse = lax.rsqrt(jnp.mean(tokens * tokens, axis=-1, keepdims=True) + 1e-06)
    small_f32[...] = small_ref[...]
    line = jnp.sum(tokens * inverse * grad, axis=0, keepdims=True)
    for owner in range(8):
        small_f32[owner, 0:1, :96] = line[:, owner * 96 : owner * 96 + 96]
    sm_own[...] = small_f32[...].astype(BF)
    sm_over = go(sm_own, sm_core, sm_send.at[0], sm_recv.at[0], sibling)
    c_far = rows_sum(c_last, c_kept, c_row, c_high, c_fin, c_right, 1)
    c_far.wait_recv()
    multiply(CROSS_KV, turned_state, c_right[...])
    step_z(SELF_KV)
    sm_over.wait_recv()
    sm_own_sum = (sm_own[...].astype(F32) + sm_core[...].astype(F32)).astype(BF)
    sm_over.wait_send()
    sm_own[...] = sm_own_sum
    sm_inside = go(
        sm_own.at[pl.ds(4 * (1 - low), 4)], sm_z, sm_send.at[1], sm_recv.at[1], inside
    )
    ctx_sum(0, early, packed, from_ctx, land)
    step_z(CROSS_KV)
    step_via(SELF_KV)
    sm_inside.wait_recv()
    for column in range(4):
        sm_z[column] = sm_z[column] + sm_own[4 * low + column]
    sm_row = [
        go(
            sm_z.at[(x + spot + 1) % 4], sm_x.at[spot],
            sm_send.at[2 + spot], sm_recv.at[2 + spot], (me, others[spot]),
        )
        for spot in range(3)
    ]
    step_via(CROSS_KV)
    scaled = gain_ref[...] * grad
    mixed = jnp.mean(tokens * scaled, axis=-1, keepdims=True)
    decoder_ref[...] = (
        dmid_ref[...] + inverse * scaled - tokens * (inverse * inverse * inverse * mixed)
    )
    step_x(SELF_KV)
    step_x(CROSS_KV)
    late = ctx_start(1, late_packed, late_from)
    sm_sum = sm_z[x].astype(F32)
    for spot in range(3):
        sm_row[spot].wait_recv()
        sm_sum = sm_sum + sm_x[spot].astype(F32)
    sm_total[...] = sm_sum.astype(BF)
    sm_mates = [
        go(sm_total, sm_ctx.at[spot], sm_send.at[5 + spot], sm_recv.at[5 + spot], mate_device(mate))
        for spot, mate in enumerate(mates)
    ]
    ctx_pass(0, land)
    ctx_sum(1, late, late_packed, late_from, late_land)
    d_ckv = jnp.concatenate([c_fin[0], c_fin[1]], axis=1)
    encoder_ref[...] = contract(d_ckv, ckv_ref[...], ((1,), (1,)))
    sm_sum = sm_total[...].astype(F32)
    for spot in range(7):
        sm_mates[spot].wait_recv()
        sm_sum = sm_sum + sm_ctx[spot].astype(F32)
    small_out[...] = sm_sum
    ctx_done(0, land)
    early_out[...] = land[...]
    ctx_pass(1, late_land)
    ctx_done(1, late_land)
    late_out[...] = late_land[...]
    for copy in sends:
        if copy is not sm_over:
            copy.wait_send()


def unpack_kernel(early, late, *refs):
    square_refs = refs[:8]
    gate_ref, up_ref, down_ref = refs[8:]
    half = D // 2
    middle = PIECE // 2
    for side in range(2):
        columns = slice(side * half, side * half + half)
        for upper in range(2):
            rows = slice(upper * middle, upper * middle + middle)
            for k in range(4):
                square_refs[k][rows, columns] = early[2 * k + upper, side, PIECE:, :].astype(F32)
            for k in range(2):
                for piece in range(2):
                    square_refs[4 + 2 * k + side][rows, piece * half : piece * half + half] = late[
                        4 * k + 2 * piece + upper, side
                    ].astype(F32)
        target = up_ref if side else gate_ref
        for piece in range(8):
            target[:, piece * 256 : piece * 256 + 256] = early[piece, side, :PIECE, :256].astype(F32)
            for part in range(3):
                down_ref[
                    piece * 32 : piece * 32 + 32,
                    side * half + part * 128 : side * half + part * 128 + 128,
                ] = early[piece, side, part * 32 : part * 32 + 32, 256:].astype(F32)


def unpack(early, late):
    outs = (
        [jax.ShapeDtypeStruct((PIECE, D), F32)] * 8
        + [jax.ShapeDtypeStruct((PIECE, FF), F32)] * 2
        + [jax.ShapeDtypeStruct((FF // 8, D), F32)]
    )
    return pl.pallas_call(
        unpack_kernel,
        out_shape=outs,
        in_specs=[pl.BlockSpec(memory_space=pltpu.VMEM)] * 2,
        out_specs=[pl.BlockSpec(memory_space=pltpu.VMEM)] * len(outs),
        compiler_params=pltpu.CompilerParams(vmem_limit_bytes=24 * MIB),
        name="unpack",
    )(early, late)


def finish(far, near, collective_id):
    dma = pltpu.SemaphoreType.DMA

    def rows(count):
        return [
            pltpu.VMEM((8, 2, count, D), BF),
            pltpu.VMEM((8, 2, count, D), BF),
            pltpu.VMEM((2, 2, 2, count, D), BF),
            pltpu.VMEM((2, 2, count, D), BF),
            pltpu.VMEM((2, count, D), BF),
            pltpu.VMEM((2, count, D), BF),
            pltpu.VMEM((2, count, D), BF),
        ]

    outs = [
        jax.ShapeDtypeStruct((8, 2, 3 * PIECE // 2, D // 2), BF),
        jax.ShapeDtypeStruct((8, 2, PIECE // 2, D // 2), BF),
        jax.ShapeDtypeStruct((16, 128), F32),
        jax.ShapeDtypeStruct((TOK, D), F32),
        jax.ShapeDtypeStruct((ENC, D), F32),
    ]
    return pl.pallas_call(
        finish_kernel,
        out_shape=outs,
        in_specs=[pl.BlockSpec(memory_space=pl.ANY)] * len(far)
        + [pl.BlockSpec(memory_space=pltpu.VMEM)] * len(near),
        out_specs=[pl.BlockSpec(memory_space=pltpu.VMEM)] * len(outs),
        scratch_shapes=[
            pltpu.VMEM((2 * TOK, sum(LEFT)), BF),
            pltpu.VMEM((2 * TOK, sum(RIGHT)), BF),
            pltpu.VMEM((8, PIECE, 2 * TOK), BF),
            pltpu.VMEM((8, PIECE, 2 * TOK), BF),
            pltpu.VMEM((8, PIECE, 2 * ENC), BF),
            pltpu.VMEM((2 * ENC, D), BF),
            pltpu.VMEM((2 * TOK, D), BF),
            pltpu.VMEM((2 * ENC, D), BF),
            pltpu.VMEM((8, PIECE, SPAN - FF), BF),
            pltpu.VMEM((4, PIECE, SPAN), BF),
            pltpu.VMEM((2, PIECE, SPAN), BF),
            pltpu.VMEM((2, PIECE // 2, SPAN), BF),
            pltpu.VMEM((4, FF // 8, D // 2), BF),
            pltpu.VMEM((2, FF // 8, D // 2), BF),
            pltpu.VMEM((2, FF // 16, D // 2), BF),
        ]
        + rows(TOK)
        + rows(ENC)
        + [
            pltpu.VMEM((8, 16, 128), F32),
            pltpu.VMEM((8, 16, 128), BF),
            pltpu.VMEM((8, 16, 128), BF),
            pltpu.VMEM((4, 16, 128), BF),
            pltpu.VMEM((3, 16, 128), BF),
            pltpu.VMEM((7, 16, 128), BF),
            pltpu.VMEM((16, 128), BF),
            pltpu.VMEM((8, 3 * PIECE // 2, D // 2), BF),
            pltpu.VMEM((7, 3 * PIECE // 2, D // 2), BF),
            pltpu.VMEM((8, 2, 3 * PIECE // 2, D // 2), BF),
            pltpu.VMEM((8, PIECE // 2, D // 2), BF),
            pltpu.VMEM((7, PIECE // 2, D // 2), BF),
            pltpu.VMEM((8, 2, PIECE // 2, D // 2), BF),
            pltpu.VMEM((2, 4, PIECE // 2, FF), BF),
            pltpu.VMEM((2, 4, FF // 16, D // 2), BF),
            pltpu.VMEM((8, PIECE, D), BF),
            dma((7,)),
            dma((5, 7)),
            dma((5, 7)),
            dma((4, 2)),
            dma((4, 2)),
            dma((4, 2)),
            dma((3,)),
            dma((3,)),
            dma((CHUNKS, 2)),
            dma((CHUNKS, 2)),
            dma((CHUNKS, 6)),
            dma((CHUNKS, 6)),
            dma((2, 14)),
            dma((2, 15)),
            dma((2, 8)),
            dma((2, 8)),
            dma((12,)),
            dma((12,)),
            dma((3,)),
        ],
        compiler_params=pltpu.CompilerParams(
            collective_id=collective_id, has_side_effects=True, vmem_limit_bytes=62 * MIB
        ),
        name="finish_gradients",
    )(*far, *near)


def backward_kernel(biased, *refs):
    if biased:
        class_ref, near_ref, q_ref, k_ref, v_ref, g_ref, total_ref, tile_ref = refs[:8]
        dq_ref, dkv_ref, strip_ref, share_ref, slope_ref, share_low, slope_low = refs[8:]
    else:
        q_ref, k_ref, v_ref, g_ref, total_ref = refs[:5]
        dq_ref, dkv_ref, share_ref, slope_ref, share_low, slope_low = refs[5:]
    chunks = share_ref.shape[0]
    queries = split_heads(q_ref[...])
    grads = split_heads(g_ref[...])
    totals = total_ref[0, 0:1]
    inner = jnp.zeros((8, 2 * TOK), F32)
    for j in range(chunks):
        scores = contract(key_chunk(k_ref, j), queries, ((1,), (1,)))
        if biased:
            scores = scores + bias_chunk(class_ref, tile_ref, j)
        shares = jnp.exp(scores - totals)
        slopes = contract(key_chunk(v_ref, j), grads, ((1,), (1,)))
        inner = inner + fold(shares * slopes, jnp.sum)
        share_ref[j] = shares
        slope_ref[j] = slopes
        share_low[j] = shares.astype(BF)
    inner = jnp.sum(inner, axis=0, keepdims=True)
    for j in range(chunks):
        grad = share_ref[j] * (slope_ref[j] - inner)
        if biased:
            slope_ref[j] = grad
        slope_low[j] = grad.astype(BF)
    keys = jnp.concatenate([key_chunk(k_ref, j) for j in range(chunks)], axis=0)
    low = slope_low[...].reshape(-1, 2 * TOK)
    dq_ref[...] = join_heads(contract(keys, low, ((0,), (0,)))).astype(BF)
    shape = dkv_ref.shape
    block = (shape[0], shape[2], shape[3])
    dkv_ref[:, 0] = contract(low, queries, ((1,), (0,))).astype(BF).reshape(block)
    dkv_ref[:, 1] = (
        contract(share_low[...].reshape(-1, 2 * TOK), grads, ((1,), (0,))).astype(BF).reshape(block)
    )
    if biased:
        lane = lax.broadcasted_iota(jnp.int32, (HALF, TOK), 1)
        for gap in range(3):
            pieces = []
            for half in range(2):
                spot = near_ref[half, gap]
                held = slope_ref[jnp.maximum(spot, 0) // 2, pl.ds(
                    pl.multiple_of((jnp.maximum(spot, 0) % 2) * HALF, HALF), HALF)]
                pieces.append(jnp.where(spot >= 0, held, jnp.zeros_like(held)))
            for head in range(2):
                cut = slice(head * TOK, (head + 1) * TOK)
                strip_ref[head, gap] = jnp.where(lane < HALF, pieces[0][:, cut], pieces[1][:, cut])


def pair_columns(pair):
    return (0, pair)


def kv_spec(rows, row_block, part):
    return pl.BlockSpec(
        (N_CTX, 1, rows, 2 * HEAD_DIM), lambda pair: (0, part, row_block, pair)
    )


SMEM_SPEC = pl.BlockSpec(memory_space=pltpu.SMEM)
TILE_SPEC = pl.BlockSpec((2, 5, HALF, TOK), lambda pair: (pair, 0, 0, 0))
TOTAL_SPEC = pl.BlockSpec((1, 8, 2 * TOK), lambda pair: (pair, 0, 0))
ROW_SPEC = pl.BlockSpec((TOK, 2 * HEAD_DIM), pair_columns)
LOCAL = pltpu.CompilerParams(vmem_limit_bytes=48 * MIB)


def attend_back(queries, gathered, grads, totals, rows, row_block, classes=None, near=None, tiles=None):
    biased = classes is not None
    chunks = N_CTX * rows // TOK
    specs = [ROW_SPEC, kv_spec(rows, row_block, 0), kv_spec(rows, row_block, 1), ROW_SPEC, TOTAL_SPEC]
    operands = [queries, gathered, gathered, grads, totals]
    out_specs = [
        ROW_SPEC,
        pl.BlockSpec((N_CTX, 2, rows, 2 * HEAD_DIM), lambda pair: (0, 0, 0, pair)),
    ]
    out_shape = [
        jax.ShapeDtypeStruct((TOK, D), BF),
        jax.ShapeDtypeStruct((N_CTX, 2, rows, D), BF),
    ]
    if biased:
        specs = [SMEM_SPEC, SMEM_SPEC] + specs + [TILE_SPEC]
        operands = [classes, near] + operands + [tiles]
        out_specs.append(pl.BlockSpec((2, 3, HALF, TOK), lambda pair: (pair, 0, 0, 0)))
        out_shape.append(jax.ShapeDtypeStruct((HEADS, 3, HALF, TOK), F32))
    return pl.pallas_call(
        functools.partial(backward_kernel, biased),
        grid=(PAIRS,),
        in_specs=specs,
        out_specs=out_specs,
        out_shape=out_shape,
        scratch_shapes=[
            pltpu.VMEM((chunks, TOK, 2 * TOK), F32),
            pltpu.VMEM((chunks, TOK, 2 * TOK), F32),
            pltpu.VMEM((chunks, TOK, 2 * TOK), BF),
            pltpu.VMEM((chunks, TOK, 2 * TOK), BF),
        ],
        compiler_params=LOCAL,
        cost_estimate=pl.CostEstimate(flops=1000, bytes_accessed=1000, transcendentals=0),
        name="attend_self_back" if biased else "attend_cross_back",
    )(*operands)


def matmul(left, right):
    return jnp.dot(left, right, preferred_element_type=F32)


def transposed_left(left, right):
    return contract(left, right, ((0,), (0,)))


def transposed_right(left, right):
    return contract(left, right, ((1,), (1,)))


def rms_scaled(values, gain):
    inverse = lax.rsqrt(jnp.mean(values * values, axis=-1, keepdims=True) + 1e-06)
    return (values * inverse * gain).astype(BF)


def rms_back(values, gain, grad):
    inverse = lax.rsqrt(jnp.mean(values * values, axis=-1, keepdims=True) + 1e-06)
    scaled = gain * grad
    mixed = jnp.mean(values * scaled, axis=-1, keepdims=True)
    grad_values = inverse * scaled - values * (inverse * inverse * inverse * mixed)
    return grad_values, jnp.sum(values * inverse * grad, axis=0)


def near_hot():
    shape = (REACH, 3 * HALF * HALF)
    spot = lax.broadcasted_iota(jnp.int32, shape, 1)
    gap = spot // (HALF * HALF)
    key = (spot // HALF) % HALF
    row = spot % HALF
    distance = jnp.clip(HALF * gap + row - key, 0, REACH - 1)
    return (distance == lax.broadcasted_iota(jnp.int32, shape, 0)).astype(BF)


def bias_sums(strips):
    tiles = (strips[..., :HALF] + strips[..., HALF:]).reshape(HEADS, -1)
    high = tiles.astype(BF)
    low = (tiles - high.astype(F32)).astype(BF)
    hot = near_hot()
    sums = transposed_right(high, hot) + transposed_right(low, hot)
    far = -jnp.sum(sums[:, :-1], axis=1, keepdims=True)
    return jnp.concatenate([sums[:, :-1], far], axis=1)


def swap(values, move):
    perm = []
    for ctx in range(N_CTX):
        for shard in range(8):
            there, owner = move(ctx, shard)
            perm.append((ctx * 8 + shard, there * 8 + owner))
    return lax.ppermute(values, ("ctx", "fsdp"), perm)


def over_z(mine, upper, lower):
    inner = swap(upper, lambda ctx, shard: (ctx, (shard + 4) % 8))
    outer = swap(lower, lambda ctx, shard: (ctx ^ 2, (shard + 4) % 8))
    return mine, inner, outer


def body(
    decoder_in,
    encoder_states,
    out_grad,
    block_pairs,
    bucket_table,
    gain_self,
    self_query,
    self_key,
    self_value,
    self_out,
    position_bias,
    gain_cross,
    cross_query,
    cross_key,
    cross_value,
    cross_out,
    gain_feed,
    feed_gate,
    feed_up,
    feed_down,
):
    me = lax.axis_index("ctx")
    rows = self_query.shape[0]
    small = jnp.concatenate(
        [
            jnp.pad(jnp.stack([gain_self, gain_cross, gain_feed]), ((0, 0), (0, 128 - rows))),
            jnp.pad(position_bias, ((0, 9), (0, 128 - HEADS))),
        ],
        axis=0,
    )
    (
        kv_one, kv_two, square, gains, normed_one, queries, tiles, attended, self_totals, mid_one,
        normed_two, cross_queries, cross_attended, cross_totals, block_out, d_mid_two,
        cross_branch, d_cross_attended, grad_norm_three, *feed_parts, classes, near, self_kv,
        cross_kv,
    ) = front(
        [
            self_key, self_value, cross_key, cross_value,
            self_query, self_out, cross_query, cross_out,
            feed_gate, feed_up, feed_down,
        ],
        [
            small, decoder_in[0], encoder_states[0], out_grad[0], bucket_table[None, :], block_pairs,
        ],
        0,
    )
    kv_one = kv_one.reshape(D, 2 * D)
    kv_two = kv_two.reshape(D, 2 * D)
    out_one, query_two = (square.reshape(D, 4 * D)[:, k * D : k * D + D] for k in (1, 2))
    norm_one, norm_two = gains[0:1], gains[1:2]
    bucket_hot = (bucket_table[:, None] == jnp.arange(32, dtype=jnp.int32)[None, :]).astype(BF)
    tokens = decoder_in[0].astype(F32)
    states = encoder_states[0]
    upstream = out_grad[0]
    feed_parts = [over_z(*feed_parts[:3]), over_z(*feed_parts[3:])]
    d_cross_queries, d_cross_kv_all = attend_back(
        cross_queries, cross_kv, d_cross_attended, cross_totals, ENC, 0
    )
    d_normed_two = transposed_right(d_cross_queries, query_two)
    part_two, grad_norm_two = rms_back(mid_one, norm_two, d_normed_two)
    d_mid_one = d_mid_two + part_two
    self_branch = d_mid_one.astype(BF)
    d_attended = transposed_right(self_branch, out_one).astype(BF)
    feed_parts[1], d_attended = lax.optimization_barrier((feed_parts[1], d_attended))
    d_queries, d_kv_all, strips = attend_back(
        queries, self_kv, d_attended, self_totals, TOK, 0, classes, near, tiles
    )
    feed_parts, d_queries, d_kv_all, strips = lax.optimization_barrier(
        (feed_parts, d_queries, d_kv_all, strips)
    )
    grad_table = matmul(bias_sums(strips), bucket_hot.astype(F32)).T.reshape(8, 4, HEADS)
    grad_gains = jnp.stack([grad_norm_two, grad_norm_three[0]]).reshape(2, 8, rows)
    grad_small = jnp.concatenate(
        [
            jnp.zeros((8, 1, 128), F32),
            jnp.pad(jnp.transpose(grad_gains, (1, 0, 2)), ((0, 0), (0, 0), (0, 128 - rows))),
            jnp.pad(grad_table, ((0, 0), (0, 9), (0, 128 - HEADS))),
        ],
        axis=1,
    )
    done = finish(
        [
            cross_attended, normed_two, attended, normed_one,
            cross_branch, d_cross_queries, self_branch, d_queries,
            *feed_parts[0],
            *feed_parts[1],
            d_kv_all.reshape(8, 2, 2, TOK, D),
            d_cross_kv_all.reshape(8, 2, 2, ENC, D),
            square,
        ],
        [
            states,
            kv_one,
            kv_two,
            d_queries,
            d_mid_one,
            decoder_in[0],
            norm_one,
            grad_small,
        ],
        3,
    )
    early, late, extras, grad_decoder, grad_encoder = done
    (
        grad_out_two, grad_query_two, grad_out_one, grad_query_one,
        grad_key_two, grad_value_two, grad_key_one, grad_value_one,
        grad_gate, grad_up, grad_down,
    ) = unpack(early, late)
    return (
        block_out[None],
        grad_decoder[None],
        grad_encoder[None],
        extras[0, :rows],
        grad_query_one,
        grad_key_one,
        grad_value_one,
        grad_out_one,
        extras[3:7, :HEADS],
        extras[1, :rows],
        grad_query_two,
        grad_key_two,
        grad_value_two,
        grad_out_two,
        extras[2, :rows],
        grad_gate,
        grad_up,
        grad_down,
    )


def solution(mesh):
    tokens = P("fsdp", "ctx", None)
    matrix = P("fsdp", None)
    vector = P("fsdp")
    weights = (
        (vector,) + (matrix,) * 5 + (vector,) + (matrix,) * 4 + (vector,) + (matrix,) * 3
    )
    return jax.shard_map(
        body,
        mesh=mesh,
        in_specs=(tokens,) * 3 + (P(), P()) + weights,
        out_specs=(tokens,) * 3 + weights,
        check_vma=False,
    )
```

```python
import functools

import jax
import jax.numpy as jnp
from jax import lax
from jax.experimental import pallas as pl
from jax.experimental.pallas import tpu as pltpu
from jax.sharding import PartitionSpec as P

D = 768
FF = 2048
HEADS = 12
HEAD_DIM = 64
PAIRS = HEADS // 2
N_CTX = 16
TOK = 128
ENC = 64
HALF = 64
REACH = 128
BF = jnp.bfloat16
F32 = jnp.float32
MIB = 1024 * 1024


def ctx_place():
    me = lax.axis_index("ctx")
    core = me % 2
    high = (me // 2) % 2
    y = me // 4
    return me, core, high, y


def slot_of(y, shift, high, core):
    return ((y + shift) % 4) * 4 + 2 * high + core


def split_heads(block):
    lane = lax.broadcasted_iota(jnp.int32, block.shape, 1)
    nothing = jnp.zeros_like(block)
    return jnp.concatenate(
        [jnp.where(lane < HEAD_DIM, block, nothing), jnp.where(lane < HEAD_DIM, nothing, block)],
        axis=0,
    )


def join_heads(transposed):
    row = lax.broadcasted_iota(jnp.int32, (2 * HEAD_DIM, TOK), 0)
    return jnp.where(row < HEAD_DIM, transposed[:, :TOK], transposed[:, TOK:]).T


def contract(left, right, dims):
    return lax.dot_general(left, right, (dims, ((), ())), preferred_element_type=F32)


def key_chunk(ref, j):
    if ref.shape[2] == 2 * HALF:
        return ref[j, 0]
    return ref[pl.ds(2 * j, 2), 0].reshape(2 * HALF, 2 * HEAD_DIM)


def bias_chunk(class_ref, tile_ref, j, first=0):
    lane = lax.broadcasted_iota(jnp.int32, (HALF, TOK), 1)
    rows = []
    for half in range(2):
        spot = 2 * j + half
        near = class_ref[0, spot]
        far = class_ref[1, spot]
        rows.append(
            jnp.concatenate(
                [
                    jnp.where(lane < HALF, tile_ref[first + head, near], tile_ref[first + head, far])
                    for head in range(2)
                ],
                axis=1,
            )
        )
    return jnp.concatenate(rows, axis=0)


def fold(values, join):
    return join(values.reshape(-1, 8, values.shape[-1]), axis=0)


def attend_pair(queries, keys, values, bias, score_ref, share_ref, chunks):
    queries = split_heads(queries)
    highest = None
    for j in range(chunks):
        scores = contract(keys(j), queries, ((1,), (1,)))
        if bias is not None:
            scores = scores + bias(j)
        score_ref[j] = scores
        top = fold(scores, jnp.max)
        highest = top if highest is None else jnp.maximum(highest, top)
    highest = jnp.max(highest, axis=0, keepdims=True)
    summed = jnp.zeros((8, 2 * TOK), F32)
    for j in range(chunks):
        raised = jnp.exp(score_ref[j] - highest)
        summed = summed + fold(raised, jnp.sum)
        share_ref[j] = raised.astype(BF)
    summed = jnp.sum(summed, axis=0, keepdims=True)
    gathered = jnp.concatenate([values(j) for j in range(chunks)], axis=0)
    mixed = contract(gathered, share_ref[:chunks].reshape(-1, 2 * TOK), ((0,), (0,)))
    return join_heads(mixed / summed).astype(BF), highest + jnp.log(summed)


def attend_pairs(first, last, kv_ref, query_ref, out_ref, total_ref, score_ref, share_ref, bias=None):
    rows = kv_ref.shape[2]
    chunks = N_CTX * rows // TOK

    def step(pair, carry):
        cut = pl.ds(pl.multiple_of(pair * TOK, TOK), TOK)

        def chunk(part, j):
            if rows == TOK:
                return kv_ref[j, part, :, cut]
            return kv_ref[2 * j : 2 * j + 2, part, :, cut].reshape(TOK, TOK)

        mixed, total = attend_pair(
            query_ref[:, cut],
            functools.partial(chunk, 0),
            functools.partial(chunk, 1),
            None if bias is None else functools.partial(bias, pair),
            score_ref,
            share_ref,
            chunks,
        )
        out_ref[:, cut] = mixed
        total_ref[pair] = jnp.broadcast_to(total, (8, 2 * TOK))
        return carry

    lax.fori_loop(first, last, step, 0)


def strip_hot():
    shape = (REACH, 3 * TOK)
    spot = lax.broadcasted_iota(jnp.int32, shape, 1)
    distance = jnp.clip(HALF * (spot // TOK) + spot % TOK - (HALF - 1), 0, REACH - 1)
    return (distance == lax.broadcasted_iota(jnp.int32, shape, 0)).astype(BF)


def index_tables(me, pairs_ref, class_ref, near_ref):
    own = pairs_ref[me]
    for half in range(2):
        query = 31 - own if half else own
        spots = [jnp.int32(-1)] * 3
        for block in range(32):
            pair = pairs_ref[block // 2]
            key = 31 - pair if block % 2 else pair
            gap = query - key
            class_ref[half, block] = jnp.where(gap < 0, 4, jnp.minimum(gap, 3))
            for near in range(3):
                spots[near] = jnp.where(gap == near, block, spots[near])
        for near in range(3):
            near_ref[half, near] = spots[near]


def build_tiles(bias_rows, strips, tile_ref):
    lane = lax.broadcasted_iota(jnp.int32, (HALF, TOK), 1)
    key = lax.broadcasted_iota(jnp.int32, (HALF, TOK), 0)
    row = jnp.where(lane < HALF, lane, lane - HALF)
    for head in range(HEADS):
        for gap in range(3):
            strip = strips[head : head + 1, gap * TOK : gap * TOK + TOK]
            turned = pltpu.roll(
                jnp.broadcast_to(strip, (HALF, TOK)), 65, 1, stride=1, stride_axis=0
            )
            tile = jnp.where(lane < HALF, turned, pltpu.roll(turned, HALF, 1))
            if gap == 0:
                tile = jnp.where(key > row, -1e30, tile)
            tile_ref[head, gap] = tile
        tile_ref[head, 3] = jnp.broadcast_to(bias_rows[head : head + 1, REACH - 1 :], (HALF, TOK))
        tile_ref[head, 4] = jnp.full((HALF, TOK), -1e30, F32)


def torus_place():
    me, core, high, y = ctx_place()
    shard = lax.axis_index("fsdp")
    return me, core, high, y, shard // 4, shard % 4


def hop(src, dst, send_sem, recv_sem, ctx, fsdp):
    return pltpu.make_async_remote_copy(
        src_ref=src,
        dst_ref=dst,
        send_sem=send_sem,
        recv_sem=recv_sem,
        device_id={"ctx": ctx, "fsdp": fsdp},
    )


def greet_all(devices):
    barrier = pltpu.get_barrier_semaphore()
    for ctx, fsdp in devices:
        pl.semaphore_signal(barrier, inc=1, device_id={"ctx": ctx, "fsdp": fsdp})
    pl.semaphore_wait(barrier, len(devices))


Z_FIRST = 4
ROOT = (2.0 / 3.141592653589793) ** 0.5
PACKS = ((0, 1), (2, 3), (4, 5, 6, 7), (8, 9), (10,))


def front_kernel(*refs):
    sources = refs[:11]
    small_ref, token_ref, state_ref, upstream_ref, bucket_ref, pairs_ref = refs[11:17]
    results = refs[17:20]
    (
        gain_out, normed_out, query_out, tile_result, attended_ref, total_ref, mid_one_ref,
        normed_two_ref, cross_query_ref, cross_attended_ref, cross_total_ref,
        block_ref, d_mid_ref, branch_ref, d_cross_ref, gain_grad_ref,
        wide_mine_out, wide_inner_out, wide_outer_out, tall_mine_out, tall_inner_out, tall_outer_out,
        class_ref, near_ref, self_result, cross_result,
    ) = refs[20:46]
    targets = refs[46:51]
    (
        self_out_ref, cross_out_ref, landing, self_ref, cross_ref, score_ref, share_ref,
        feed_left, feed_right, slope_ref, turned, turned_hidden, tile_ref,
        wide_mine, wide_inner, wide_outer, tall_mine, tall_inner, tall_outer,
        send_sem, x_sem, z_sem, core_sem,
        fill_sem, small_sem, self_sem, cross_sem, feed_sem, local_sem,
    ) = refs[51:]
    me, core, high, y, low, x = torus_place()
    shard = low * 4 + x
    sibling = (slot_of(y, 0, high, 1 - core), shard)
    inside = (me, (1 - low) * 4 + x)
    outside = (slot_of(y, 0, 1 - high, core), (1 - low) * 4 + x)
    across = slot_of(y, 0, 1 - high, core)
    ahead, behind = (slot_of(y, shift, high, core) for shift in (1, 3))
    others = [low * 4 + (x + shift) % 4 for shift in (1, 2, 3)]
    peers = [(shard + shift) % 8 for shift in range(1, 8)]
    greet_all(
        [sibling, outside, (across, shard), (ahead, shard), (behind, shard)]
        + [(me, peer) for peer in peers]
    )
    sends = []

    def send(src, dst, recv_sem, device):
        copy = hop(src, dst, send_sem.at[len(sends)], recv_sem, *device)
        copy.start()
        sends.append(copy)

    def arrived(ref, recv_sem):
        hop(ref, ref, send_sem.at[0], recv_sem, *sibling).wait_recv()

    def bring(src, dst, sem):
        copy = pltpu.make_async_copy(src, dst, sem)
        copy.start()
        return copy


    def part(k, owner, whose, side=None):
        ref = targets[k]
        count = ref.shape[1] // 2
        start = pl.multiple_of(whose * count, 16)
        if side is None:
            return ref.at[owner, pl.ds(start, count), :]
        width = ref.shape[2] // 2
        return ref.at[owner, pl.ds(start, count), pl.ds(side * width, width)]

    def fill(k):
        copies = []
        start = 0
        for source in PACKS[k]:
            width = sources[source].shape[1]
            copies.append(
                bring(
                    sources[source],
                    targets[k].at[shard, :, pl.ds(start, width)],
                    fill_sem.at[source],
                )
            )
            start += width
        return copies

    def send_own(k):
        for copy in fills[k]:
            copy.wait()
        for spot in (1, 0, 2):
            block = part(k, shard, core)
            send(block, block, x_sem.at[k, spot], (me, others[spot]))
        for side, device in enumerate((inside, outside)):
            piece = part(k, shard, core, side)
            send(piece, piece, z_sem.at[k, 3, side], device)


    def pass_x(k):
        for spot in (0, 2, 1):
            owner = low * 4 + (x + 3 - spot) % 4
            block = part(k, owner, core)
            arrived(block, x_sem.at[k, spot])
            if k != Z_FIRST:
                for side, device in enumerate((inside, outside)):
                    piece = part(k, owner, core, side)
                    send(piece, piece, z_sem.at[k, spot, side], device)
            send(block, block, core_sem.at[k, spot], sibling)

    def pass_z(k):
        for spot in (3, 0, 2, 1):
            owner = (1 - low) * 4 + (x + 3 - spot) % 4
            for side in range(2):
                piece = part(k, owner, core, side)
                arrived(piece, z_sem.at[k, spot, side])
                if k == Z_FIRST and spot == 3:
                    for onward in (1, 0, 2):
                        send(piece, piece, z_sem.at[k, onward, side], (me, others[onward]))
                send(piece, piece, core_sem.at[k, 3 + 2 * spot + side], sibling)

    def complete(k):
        for spot in range(3):
            owner = low * 4 + (x + 3 - spot) % 4
            arrived(part(k, owner, 1 - core), core_sem.at[k, spot])
        for spot in range(4):
            owner = (1 - low) * 4 + (x + 3 - spot) % 4
            for side in range(2):
                arrived(part(k, owner, 1 - core, side), core_sem.at[k, 3 + 2 * spot + side])


    def kv_start(src, out, sems):
        send(src, out.at[me], sems.at[me, 0], (across, shard))
        send(src, out.at[me], sems.at[me, 0], (ahead, shard))
        send(src, out.at[me], sems.at[me, 0], (behind, shard))
        send(src, out.at[me], sems.at[me, 0], sibling)

    def kv_across(out, sems):
        block = out.at[across]
        arrived(block, sems.at[across, 0])
        send(block, block, sems.at[across, 0], (ahead, shard))
        send(block, block, sems.at[across, 0], (behind, shard))
        send(block, block, sems.at[across, 0], sibling)

    def kv_near(out, sems, flip):
        half = 1 - high if flip else high
        slot = slot_of(y, 1, half, core)
        block = out.at[slot]
        arrived(block, sems.at[slot, 0])
        send(block.at[0], block.at[0], sems.at[slot, 0], (behind, shard))
        send(block, block, sems.at[slot, 0], sibling)
        slot = slot_of(y, 3, half, core)
        block = out.at[slot]
        arrived(block, sems.at[slot, 0])
        send(block.at[1], block.at[1], sems.at[slot, 1], (ahead, shard))
        send(block, block, sems.at[slot, 0], sibling)

    def kv_far(out, sems, flip):
        slot = slot_of(y, 2, 1 - high if flip else high, core)
        for part in range(2):
            arrived(out.at[slot, part], sems.at[slot, part])
        send(out.at[slot], out.at[slot], sems.at[slot, 0], sibling)

    def kv_complete(out, sems):
        for shift in range(4):
            for half in range(2):
                slot = slot_of(y, shift, half, 1 - core)
                arrived(out.at[slot], sems.at[slot, 0])

    fills = [fill(k) for k in range(5)]
    own_small = bring(small_ref, landing.at[shard], local_sem.at[0])
    for spot, peer in enumerate(peers):
        send(small_ref, landing.at[shard], small_sem.at[spot], (me, peer))
    send_own(0)
    send_own(1)
    own_small.wait()
    for spot in range(7):
        arrived(landing.at[(shard + 7 - spot) % 8], small_sem.at[spot])
    gains = landing[...].astype(F32)
    gain = [
        jnp.concatenate([gains[owner, k : k + 1, :96] for owner in range(8)], axis=1)
        for k in range(3)
    ]
    for k in range(3):
        gain_out[k : k + 1, :] = gain[k]
    tokens = token_ref[...].astype(F32)
    normed = rms_scaled(tokens, gain[0])
    normed_out[...] = normed
    pass_x(0)
    send_own(2)
    pass_z(0)
    pass_x(1)
    send_own(3)
    complete(0)
    exits = [bring(targets[0], results[0], local_sem.at[1])]
    for half in range(2):
        weight = targets[0][:, :, half * D : half * D + D].reshape(D, D)
        self_ref[half] = matmul(normed, weight).astype(BF)
    kv_start(self_ref, self_out_ref, self_sem)
    own_self = bring(self_ref, self_out_ref.at[me], local_sem.at[2])
    pass_z(1)
    complete(1)
    exits.append(bring(targets[1], results[1], local_sem.at[4]))
    for half in range(2):
        weight = targets[1][:, :, half * D : half * D + D].reshape(D, D)
        cross_ref[half] = matmul(state_ref[...], weight).astype(BF)
    kv_start(cross_ref, cross_out_ref, cross_sem)
    own_cross = bring(cross_ref, cross_out_ref.at[me], local_sem.at[3])
    index_tables(me, pairs_ref, class_ref, near_ref)
    slab = lax.broadcasted_iota(jnp.int32, (128, REACH), 0)
    place = slab % 16 - 3
    wanted = jnp.where((place >= 0) & (place < 4), 4 * (slab // 16) + place, -1)
    hot = jnp.where(wanted == bucket_ref[...], 1.0, 0.0).astype(BF)
    bias_rows = contract(landing[...].reshape(128, 128), hot, ((0,), (0,)))[:16]
    build_tiles(bias_rows, matmul(bias_rows.astype(BF), strip_hot()), tile_ref)
    exits.append(bring(tile_ref, tile_result, local_sem.at[8]))
    kv_across(self_out_ref, self_sem)
    pass_x(2)
    send_own(4)
    kv_near(self_out_ref, self_sem, False)
    pass_z(2)
    kv_across(cross_out_ref, cross_sem)
    kv_near(self_out_ref, self_sem, True)
    pass_x(3)
    complete(2)
    exits.append(bring(targets[2], results[2], local_sem.at[5]))

    def square(k):
        return targets[2][:, :, k * D : k * D + D].reshape(D, D)

    query_out[...] = matmul(normed, square(0)).astype(BF)
    kv_far(self_out_ref, self_sem, False)
    kv_far(self_out_ref, self_sem, True)
    kv_near(cross_out_ref, cross_sem, False)
    own_self.wait()
    own_cross.wait()
    kv_complete(self_out_ref, self_sem)
    exits.append(bring(self_out_ref, self_result, local_sem.at[6]))

    def attend_self(first, last):
        attend_pairs(
            first, last, self_out_ref, query_out, attended_ref, total_ref, score_ref, share_ref,
            lambda pair, j: bias_chunk(class_ref, tile_ref, j, 2 * pair),
        )

    def attend_cross(first, last):
        attend_pairs(
            first, last, cross_out_ref, cross_query_ref, cross_attended_ref, cross_total_ref,
            score_ref, share_ref,
        )

    attend_self(0, 2)
    pass_x(4)
    kv_near(cross_out_ref, cross_sem, True)
    kv_far(cross_out_ref, cross_sem, False)
    attend_self(2, 4)
    pass_z(3)
    kv_far(cross_out_ref, cross_sem, True)
    attend_self(4, 6)
    mid_one = tokens + matmul(attended_ref[...], square(1))
    mid_one_ref[...] = mid_one
    normed_two = rms_scaled(mid_one, gain[1])
    normed_two_ref[...] = normed_two
    cross_query_ref[...] = matmul(normed_two, square(2)).astype(BF)
    pass_z(4)
    kv_complete(cross_out_ref, cross_sem)
    exits.append(bring(cross_out_ref, cross_result, local_sem.at[7]))
    attend_cross(0, 3)
    complete(3)
    attend_cross(3, 6)
    complete(4)
    mid_two = mid_one_ref[...] + matmul(cross_attended_ref[...], square(3))


    normed_three = rms_scaled(mid_two, gain[2])
    upstream = upstream_ref[...]
    near_rows, far_rows = pl.ds(0, TOK), pl.ds(TOK, TOK)
    feed_left[near_rows, :D] = normed_three
    for piece in range(4):
        start = piece * 512
        gate = matmul(normed_three, targets[3][:, :, start : start + 512].reshape(D, 512))
        up = matmul(normed_three, targets[3][:, :, FF + start : FF + start + 512].reshape(D, 512))
        gate = gate.astype(BF).astype(F32)
        up = up.astype(BF).astype(F32)
        square_gate = gate * gate
        curve = jnp.tanh(ROOT * (gate + 0.044715 * gate * square_gate))
        raised = 0.5 * gate * (1.0 + curve)
        steep = 0.5 * (1.0 + curve) + 0.5 * gate * (1.0 - curve * curve) * (
            ROOT * (1.0 + 3.0 * 0.044715 * square_gate)
        )
        d_hidden = contract(
            upstream, targets[4][2 * piece : 2 * piece + 2].reshape(512, D), ((1,), (1,))
        )
        feed_left[near_rows, D + start : D + start + 512] = (raised * up).astype(BF)
        slope_ref[0, :, start : start + 512] = (d_hidden * up * steep).astype(BF)
        slope_ref[1, :, start : start + 512] = (d_hidden * raised).astype(BF)
    half = D // 2
    near_half = pl.ds(pl.multiple_of(core * half, 128), half)
    far_half = pl.ds(pl.multiple_of((1 - core) * half, 128), half)
    swaps = []
    for index, (src, dst) in enumerate(
        (
            (feed_left.at[near_rows], feed_left.at[far_rows]),
            (slope_ref.at[1 - core], feed_right.at[far_rows, pl.ds(0, FF)]),
            (upstream_ref.at[:, far_half], feed_right.at[far_rows, pl.ds(FF, half)]),
        )
    ):
        copy = hop(src, dst, feed_sem.at[0, index], feed_sem.at[1, index], *sibling)
        copy.start()
        swaps.append(copy)
    feed_right[near_rows, :FF] = slope_ref[core]
    feed_right[near_rows, FF:] = upstream_ref[:, near_half]
    block_ref[...] = mid_two + matmul(feed_left[near_rows, D:], targets[4][...].reshape(FF, D))
    grad = contract(slope_ref[0], targets[3][:, :, :FF].reshape(D, FF), ((1,), (1,)))
    grad = grad + contract(slope_ref[1], targets[3][:, :, FF:].reshape(D, FF), ((1,), (1,)))
    inverse = lax.rsqrt(jnp.mean(mid_two * mid_two, axis=-1, keepdims=True) + 1e-06)
    gain_grad_ref[...] = jnp.sum(mid_two * inverse * grad, axis=0, keepdims=True)
    scaled = gain[2] * grad
    mixed = jnp.mean(mid_two * scaled, axis=-1, keepdims=True)
    d_mid_two = upstream.astype(F32) + (
        inverse * scaled - mid_two * (inverse * inverse * inverse * mixed)
    )
    d_mid_ref[...] = d_mid_two
    branch_ref[...] = d_mid_two.astype(BF)
    d_cross_ref[...] = contract(d_mid_two.astype(BF), square(3), ((1,), (1,))).astype(BF)
    for copy in swaps:
        copy.wait_recv()
    turned[...] = feed_left[:, :D].T.reshape(8, 96, 2 * TOK)
    turned_hidden[...] = feed_left[:, D:].T.reshape(8, FF // 8, 2 * TOK)
    for group in range(2):
        owners = pl.ds(4 * ((1 - low + group) % 2), 4)
        left = turned[owners].reshape(4 * 96, 2 * TOK)
        for piece in range(4):
            cut = slice(piece * 512, piece * 512 + 512)
            part = matmul(left, feed_right[:, cut]).astype(BF).reshape(4, 96, 512)
            if group:
                wide_mine[:, :, cut] = part
            else:
                wide_inner[:, :, cut] = part[:, :48]
                wide_outer[:, :, cut] = part[:, 48:]
        if group:
            exits.append(bring(wide_mine, wide_mine_out, local_sem.at[9]))
        else:
            exits.append(bring(wide_inner, wide_inner_out, local_sem.at[10]))
            exits.append(bring(wide_outer, wide_outer_out, local_sem.at[11]))
        left = turned_hidden[owners].reshape(4 * FF // 8, 2 * TOK)
        part = matmul(left, feed_right[:, FF:]).astype(BF).reshape(4, FF // 8, half)
        if group:
            tall_mine[...] = part
            exits.append(bring(tall_mine, tall_mine_out, local_sem.at[12]))
        else:
            tall_inner[...] = part[:, :128]
            tall_outer[...] = part[:, 128:]
            exits.append(bring(tall_inner, tall_inner_out, local_sem.at[13]))
            exits.append(bring(tall_outer, tall_outer_out, local_sem.at[14]))
    for copy in sends + swaps:
        copy.wait_send()
    for copy in exits:
        copy.wait()


def front(weights, others, collective_id):
    dma = pltpu.SemaphoreType.DMA
    packs = [
        (8, weights[group[0]].shape[0], sum(weights[k].shape[1] for k in group)) for group in PACKS
    ]
    anywhere = pl.BlockSpec(memory_space=pl.ANY)
    inside = pl.BlockSpec(memory_space=pltpu.VMEM)
    scalars = pl.BlockSpec(memory_space=pltpu.SMEM)
    return pl.pallas_call(
        front_kernel,
        out_shape=[jax.ShapeDtypeStruct(pack, BF) for pack in packs[:3]]
        + [
            jax.ShapeDtypeStruct((3, D), F32),
            jax.ShapeDtypeStruct((TOK, D), BF),
            jax.ShapeDtypeStruct((TOK, D), BF),
            jax.ShapeDtypeStruct((HEADS, 5, HALF, TOK), F32),
            jax.ShapeDtypeStruct((TOK, D), BF),
            jax.ShapeDtypeStruct((PAIRS, 8, 2 * TOK), F32),
            jax.ShapeDtypeStruct((TOK, D), F32),
            jax.ShapeDtypeStruct((TOK, D), BF),
            jax.ShapeDtypeStruct((TOK, D), BF),
            jax.ShapeDtypeStruct((TOK, D), BF),
            jax.ShapeDtypeStruct((PAIRS, 8, 2 * TOK), F32),
            jax.ShapeDtypeStruct((TOK, D), F32),
            jax.ShapeDtypeStruct((TOK, D), F32),
            jax.ShapeDtypeStruct((TOK, D), BF),
            jax.ShapeDtypeStruct((TOK, D), BF),
            jax.ShapeDtypeStruct((1, D), F32),
            jax.ShapeDtypeStruct((4, 96, FF), BF),
            jax.ShapeDtypeStruct((4, 48, FF), BF),
            jax.ShapeDtypeStruct((4, 48, FF), BF),
            jax.ShapeDtypeStruct((4, 256, D // 2), BF),
            jax.ShapeDtypeStruct((4, 128, D // 2), BF),
            jax.ShapeDtypeStruct((4, 128, D // 2), BF),
            jax.ShapeDtypeStruct((2, 32), jnp.int32),
            jax.ShapeDtypeStruct((2, 3), jnp.int32),
            jax.ShapeDtypeStruct((N_CTX, 2, TOK, D), BF),
            jax.ShapeDtypeStruct((N_CTX, 2, ENC, D), BF),
        ],
        in_specs=[anywhere] * 12 + [inside] * 4 + [scalars],
        out_specs=[anywhere] * 3
        + [inside] * 3
        + [anywhere]
        + [inside] * 12
        + [anywhere] * 6
        + [scalars] * 2
        + [anywhere] * 2,
        scratch_shapes=[pltpu.VMEM(pack, BF) for pack in packs]
        + [
            pltpu.VMEM((N_CTX, 2, TOK, D), BF),
            pltpu.VMEM((N_CTX, 2, ENC, D), BF),
            pltpu.VMEM((8, 16, 128), BF),
            pltpu.VMEM((2, TOK, D), BF),
            pltpu.VMEM((2, ENC, D), BF),
            pltpu.VMEM((N_CTX, TOK, 2 * TOK), F32),
            pltpu.VMEM((N_CTX, TOK, 2 * TOK), BF),
            pltpu.VMEM((2 * TOK, D + FF), BF),
            pltpu.VMEM((2 * TOK, FF + D // 2), BF),
            pltpu.VMEM((2, TOK, FF), BF),
            pltpu.VMEM((8, 96, 2 * TOK), BF),
            pltpu.VMEM((8, FF // 8, 2 * TOK), BF),
            pltpu.VMEM((HEADS, 5, HALF, TOK), F32),
            pltpu.VMEM((4, 96, FF), BF),
            pltpu.VMEM((4, 48, FF), BF),
            pltpu.VMEM((4, 48, FF), BF),
            pltpu.VMEM((4, 256, D // 2), BF),
            pltpu.VMEM((4, 128, D // 2), BF),
            pltpu.VMEM((4, 128, D // 2), BF),
            dma((5 * 22 + 7 + 2 * 18,)),
            dma((5, 3)),
            dma((5, 4, 2)),
            dma((5, 11)),
            dma((11,)),
            dma((7,)),
            dma((N_CTX, 2)),
            dma((N_CTX, 2)),
            dma((2, 3)),
            dma((15,)),
        ],
        compiler_params=pltpu.CompilerParams(
            collective_id=collective_id, has_side_effects=True, vmem_limit_bytes=60 * MIB
        ),
        name="front",
    )(*weights, *others)


PIECE = 96
WIDTHS = (D // 2, D // 2, D // 2, D // 2, D, D, FF)
SPAN = sum(WIDTHS)
DOWN = len(WIDTHS)
CHUNKS = DOWN + 1
CROSS_KV, SELF_KV, WIDE = 4, 5, 6
LEFT = (D,) * 4
RIGHT = (D // 2,) * 4


def finish_kernel(*refs):
    lefts = refs[:4]
    rights = refs[4:8]
    wide_refs, down_refs = refs[8:11], refs[11:14]
    dkv_ref, dckv_ref, square_ref = refs[14:17]
    kv_source, ckv_source, state_ref, dq_ref, dmid_ref, token_ref, gain_ref, small_ref = refs[17:25]
    early_out, late_out, small_out, decoder_ref, encoder_ref = refs[25:30]
    (
        left_all, right_all, turned, turned_one, turned_state, state_all, s_right, c_right,
        kept, from_z, from_x, via_x, d_z, d_x, d_via,
        s_kept, s_core, s_row, s_via, s_stage, s_high, s_fin,
        c_kept, c_core, c_row, c_via, c_stage, c_high, c_fin,
        small_f32, sm_own, sm_core, sm_z, sm_x, sm_ctx, sm_total,
        packed, from_ctx, land, late_packed, late_from, late_land,
        wide_add, down_add, query_ref, kv_ref, ckv_ref, bring_sem,
        s_sem, c_sem, fill_sem, act_send, act_recv, late_send, late_recv, z_send, z_recv,
        x_send, x_recv, ctx_send, ctx_recv, pass_send, pass_recv, sm_send, sm_recv, local_sem,
    ) = refs[30:]
    me, core, high, y, low, x = torus_place()
    shard = low * 4 + x
    rank = y * 2 + high
    sibling = (slot_of(y, 0, high, 1 - core), shard)
    inside = (me, (1 - low) * 4 + x)
    outside = (slot_of(y, 0, 1 - high, core), (1 - low) * 4 + x)
    across = (slot_of(y, 0, 1 - high, core), shard)
    others = [low * 4 + (x + shift) % 4 for shift in (1, 2, 3)]
    ahead = (slot_of(y, 1, high, core), shard)
    behind = (slot_of(y, 3, high, core), shard)
    shifts = [(dy, dz) for dy in range(4) for dz in range(2)][1:]
    mates = [((y + dy) % 4) * 2 + (high + dz) % 2 for dy, dz in shifts]
    greet_all(
        [sibling, inside, outside]
        + [(me, other) for other in others]
        + [(mate * 2 + core, shard) for mate in mates]
    )
    sends = []

    def go(src, dst, send_sem, recv_sem, device):
        copy = hop(src, dst, send_sem, recv_sem, *device)
        copy.start()
        sends.append(copy)
        return copy

    def bring(src, dst, sem):
        copy = pltpu.make_async_copy(src, dst, sem)
        copy.start()
        return copy


    def rows_start(source, held, arrived, sem):
        over = []
        local = []
        for spot, shift in enumerate((2, 1, 3, 0)):
            pair = pl.ds(((y + shift) % 4) * 2, 2)
            block = pl.ds(2 * spot, 2)
            over.append(
                go(
                    source.at[pair, 1 - core], arrived.at[block],
                    sem.at[0, spot], sem.at[1, spot], sibling,
                )
            )
            local.append(bring(source.at[pair, core], held.at[block], sem.at[4, spot]))
        return over, local


    def rows_send(copies, held, arrived, via, row, sem):
        over, local = copies
        onward = []
        for spot in range(4):
            local[spot].wait()
            over[spot].wait_recv()
            for block in (2 * spot, 2 * spot + 1):
                for part in range(2):
                    held[block, part] = held[block, part] + arrived[block, part]
            if spot == 0:
                first = go(held.at[0], via.at[0], sem.at[2, 0], sem.at[3, 0], ahead)
                second = go(held.at[1], via.at[1], sem.at[2, 1], sem.at[3, 1], behind)
            elif spot == 1:
                onward.append(go(held.at[3], row.at[0, 1], sem.at[2, 2], sem.at[3, 2], ahead))
            elif spot == 2:
                onward.append(go(held.at[4], row.at[1, 0], sem.at[2, 3], sem.at[3, 3], behind))
        return first, second, onward

    def rows_via(state, held, via, row, sem):
        first, second, onward = state
        first.wait_recv()
        for part in range(2):
            held[2, part] = held[2, part] + via[0, part]
        onward.append(go(held.at[2], row.at[0, 0], sem.at[2, 4], sem.at[3, 4], ahead))
        second.wait_recv()
        for part in range(2):
            held[5, part] = held[5, part] + via[1, part]
        onward.append(go(held.at[5], row.at[1, 1], sem.at[2, 5], sem.at[3, 5], behind))
        return onward

    def rows_total(held, row, half, part):
        return (
            held[6 + half, part].astype(F32)
            + row[0, half, part].astype(F32)
            + row[1, half, part].astype(F32)
        )

    def rows_across(onward, held, row, stage, landing, sem):
        for copy in onward:
            copy.wait_recv()
        for part in range(2):
            stage[part] = rows_total(held, row, 1 - high, part).astype(BF)
        return go(stage, landing, sem.at[2, 6], sem.at[3, 6], across)

    def rows_sum(last, held, row, landing, final, right, which):
        totals = [rows_total(held, row, high, part) for part in range(2)]
        last.wait_recv()
        for part in range(2):
            final[part] = (totals[part] + landing[part].astype(F32)).astype(BF)
        count = final.shape[1]
        copy = go(
            final.at[1 - core], right.at[pl.ds(count, count)],
            late_send.at[which], late_recv.at[which], sibling,
        )
        right[:count] = final[core]
        return copy


    starts = [sum(WIDTHS[:k]) for k in range(len(WIDTHS))]
    left_starts = [sum(LEFT[:k]) for k in range(4)]
    right_starts = [sum(RIGHT[:k]) for k in range(4)]
    acts = {}
    over_z, over_via, over_x = {}, {}, {}
    column_ahead = (me, low * 4 + (x + 1) % 4)
    column_behind = (me, low * 4 + (x + 3) % 4)

    def buffers(k):
        if k == DOWN:
            return d_z, d_x, d_via, pl.ds(0, D // 2)
        return from_z, from_x, via_x, pl.ds(starts[k], WIDTHS[k])

    def acts_start(index):
        left = pl.ds(left_starts[index], LEFT[index])
        right = pl.ds(right_starts[index], RIGHT[index])
        near = pl.ds(pl.multiple_of(core * RIGHT[index], 128), RIGHT[index])
        far = pl.ds(pl.multiple_of((1 - core) * RIGHT[index], 128), RIGHT[index])
        mine = pl.ds(0, TOK)
        theirs = pl.ds(TOK, TOK)
        acts[index] = (
            bring(lefts[index], left_all.at[mine, left], fill_sem.at[index, 0]),
            bring(rights[index].at[:, near], right_all.at[mine, right], fill_sem.at[index, 1]),
            go(
                lefts[index], left_all.at[theirs, left],
                act_send.at[index, 0], act_recv.at[index, 0], sibling,
            ),
            go(
                rights[index].at[:, far], right_all.at[theirs, right],
                act_send.at[index, 1], act_recv.at[index, 1], sibling,
            ),
        )

    def multiply(k, left_ref, right):
        landing, _, _, cut = buffers(k)
        for group in range(2):
            owners = pl.ds(4 * ((1 - low + group) % 2), 4)
            left = left_ref[owners].reshape(4 * PIECE, right.shape[0])
            kept[owners, :, cut] = (
                contract(left, right, ((1,), (0,))).astype(BF).reshape(4, PIECE, WIDTHS[k])
            )
            if group == 0:
                half = PIECE // 2
                over_z[k] = [
                    go(
                        kept.at[owners, pl.ds(side * half, half), cut],
                        landing.at[:, pl.ds(side * half, half), cut],
                        z_send.at[k, side],
                        z_recv.at[k, side],
                        device,
                    )
                    for side, device in enumerate((inside, outside))
                ]

    def make(index):
        near_left, near_right, far_left, far_right = acts[index]
        near_left.wait()
        near_right.wait()
        far_left.wait_recv()
        far_right.wait_recv()
        left = left_all[:, left_starts[index] : left_starts[index] + LEFT[index]].T
        right = right_all[:, right_starts[index] : right_starts[index] + RIGHT[index]]
        target = turned_one if index == 3 else turned
        target[...] = left.reshape(8, PIECE, 2 * TOK)
        multiply(index, target, right)

    def step_z(k):
        landing, _, _, cut = buffers(k)
        for copy in over_z[k]:
            copy.wait_recv()
        for column in range(4):
            landing[column, :, cut] = landing[column, :, cut] + kept[4 * low + column, :, cut]
        send_x(k)


    def send_x(k):
        landing, spread, via, cut = buffers(k)
        half = landing.shape[1] // 2
        upper, lower = pl.ds(0, half), pl.ds(half, half)
        away, front_column, back_column = (x + 2) % 4, (x + 1) % 4, (x + 3) % 4
        over_via[k] = (
            go(
                landing.at[away, upper, cut], via.at[0, :, cut],
                x_send.at[k, 0], x_recv.at[k, 0], column_ahead,
            ),
            go(
                landing.at[away, lower, cut], via.at[1, :, cut],
                x_send.at[k, 1], x_recv.at[k, 1], column_behind,
            ),
        )
        over_x[k] = [
            go(
                landing.at[front_column, lower, cut], spread.at[0, lower, cut],
                x_send.at[k, 2], x_recv.at[k, 2], column_ahead,
            ),
            go(
                landing.at[back_column, upper, cut], spread.at[1, upper, cut],
                x_send.at[k, 3], x_recv.at[k, 3], column_behind,
            ),
        ]

    def step_via(k):
        landing, spread, via, cut = buffers(k)
        half = landing.shape[1] // 2
        upper, lower = pl.ds(0, half), pl.ds(half, half)
        front_column, back_column = (x + 1) % 4, (x + 3) % 4
        over_via[k][0].wait_recv()
        landing[front_column, upper, cut] = landing[front_column, upper, cut] + via[0, :, cut]
        over_x[k].append(
            go(
                landing.at[front_column, upper, cut], spread.at[0, upper, cut],
                x_send.at[k, 4], x_recv.at[k, 4], column_ahead,
            )
        )
        over_via[k][1].wait_recv()
        landing[back_column, lower, cut] = landing[back_column, lower, cut] + via[1, :, cut]
        over_x[k].append(
            go(
                landing.at[back_column, lower, cut], spread.at[1, lower, cut],
                x_send.at[k, 5], x_recv.at[k, 5], column_behind,
            )
        )

    def step_x(k):
        landing, spread, _, cut = buffers(k)
        for copy in over_x[k]:
            copy.wait_recv()
        total = landing[x, :, cut].astype(F32)
        for spot in range(2):
            total = total + spread[spot, :, cut].astype(F32)
        total = total.astype(BF)
        half = D // 2
        if k == WIDE:
            for piece in range(8):
                packed[piece, :PIECE, :256] = total[:, piece * 256 : piece * 256 + 256]
        elif k == DOWN:
            for piece in range(8):
                for part in range(3):
                    packed[piece, part * 32 : part * 32 + 32, 256:] = total[
                        piece * 32 : piece * 32 + 32, part * 128 : part * 128 + 128
                    ]
        else:
            middle = PIECE // 2
            for upper in range(2):
                rows = total[upper * middle : upper * middle + middle, :]
                if k == CROSS_KV or k == SELF_KV:
                    for piece in range(2):
                        late_packed[(0 if k == CROSS_KV else 4) + 2 * piece + upper] = rows[
                            :, piece * half : piece * half + half
                        ]
                else:
                    packed[2 * k + upper, PIECE:, :] = rows


    def mate_device(mate):
        return (mate * 2 + core, shard)

    def ctx_start(which, source, landing):
        return [
            go(
                source.at[mate], landing.at[spot],
                ctx_send.at[which, spot], ctx_recv.at[which, spot], mate_device(mate),
            )
            for spot, mate in enumerate(mates)
        ]

    def ctx_sum(which, over, source, landing, final):
        total = source[rank].astype(F32)
        for spot in range(7):
            over[spot].wait_recv()
            total = total + landing[spot].astype(F32)
        final[rank, core] = total.astype(BF)
        own = final.at[rank, core]
        for spot, mate in enumerate(mates):
            go(own, own, ctx_send.at[which, 7 + spot], ctx_recv.at[which, 7 + rank], mate_device(mate))
        go(own, own, pass_send.at[which, 7], pass_recv.at[which, rank], sibling)

    def landed(ref, recv_sem):
        hop(ref, ref, pass_send.at[0, 0], recv_sem, *sibling).wait_recv()

    def ctx_pass(which, final):
        for spot, mate in enumerate(mates):
            block = final.at[mate, core]
            landed(block, ctx_recv.at[which, 7 + mate])
            go(block, block, pass_send.at[which, spot], pass_recv.at[which, mate], sibling)

    def ctx_done(which, final):
        for mate in [rank] + mates:
            landed(final.at[mate, 1 - core], pass_recv.at[which, mate])

    wide_cut = pl.ds(starts[WIDE], FF)
    down_copies = [bring(down_refs[0], d_z, bring_sem.at[0])] + [
        bring(down_refs[1 + side], down_add.at[side], bring_sem.at[1 + side]) for side in range(2)
    ]
    wide_copies = [bring(wide_refs[0], from_z.at[:, :, wide_cut], bring_sem.at[3])] + [
        bring(wide_refs[1 + side], wide_add.at[side], bring_sem.at[4 + side]) for side in range(2)
    ]
    s_copies = rows_start(dkv_ref, s_kept, s_core, s_sem)
    c_copies = rows_start(dckv_ref, c_kept, c_core, c_sem)
    for index in range(4):
        acts_start(index)
    state_near = bring(state_ref, state_all.at[pl.ds(0, ENC)], local_sem.at[0])
    state_far = go(
        state_ref, state_all.at[pl.ds(ENC, ENC)], late_send.at[2], late_recv.at[2], sibling
    )
    kv_copy = bring(kv_source, kv_ref, bring_sem.at[7])
    ckv_copy = bring(ckv_source, ckv_ref, bring_sem.at[8])
    query_copy = bring(square_ref.at[:, :, pl.ds(0, D)], query_ref, bring_sem.at[6])
    for copy in down_copies:
        copy.wait()
    for side in range(2):
        for column in range(4):
            rows = slice(side * 128, side * 128 + 128)
            d_z[column, rows, :] = d_z[column, rows, :] + down_add[side, column]
    send_x(DOWN)
    for copy in wide_copies:
        copy.wait()
    for side in range(2):
        for column in range(4):
            rows = slice(side * 48, side * 48 + 48)
            from_z[column, rows, wide_cut] = from_z[column, rows, wide_cut] + wide_add[side, column]
    send_x(WIDE)
    s_state = rows_send(s_copies, s_kept, s_core, s_via, s_row, s_sem)
    make(0)
    make(1)
    s_onward = rows_via(s_state, s_kept, s_via, s_row, s_sem)
    c_state = rows_send(c_copies, c_kept, c_core, c_via, c_row, c_sem)
    step_via(DOWN)
    step_via(WIDE)
    state_near.wait()
    state_far.wait_recv()
    turned_state[...] = state_all[...].T.reshape(8, PIECE, 2 * ENC)
    s_last = rows_across(s_onward, s_kept, s_row, s_stage, s_high, s_sem)
    make(2)
    make(3)
    c_onward = rows_via(c_state, c_kept, c_via, c_row, c_sem)
    step_z(0)
    step_z(1)
    s_far = rows_sum(s_last, s_kept, s_row, s_high, s_fin, s_right, 0)
    step_x(DOWN)
    s_far.wait_recv()
    multiply(SELF_KV, turned_one, s_right[...])
    step_z(2)
    step_z(3)
    step_via(0)
    step_via(1)
    step_x(WIDE)
    c_last = rows_across(c_onward, c_kept, c_row, c_stage, c_high, c_sem)
    step_via(2)
    step_via(3)
    tokens = token_ref[...].astype(F32)
    d_kv = jnp.concatenate([s_fin[0], s_fin[1]], axis=1)
    query_copy.wait()
    kv_copy.wait()
    grad = contract(dq_ref[...], query_ref[...].reshape(D, D), ((1,), (1,)))
    grad = grad + contract(d_kv, kv_ref[...], ((1,), (1,)))
    inverse = lax.rsqrt(jnp.mean(tokens * tokens, axis=-1, keepdims=True) + 1e-06)
    small_f32[...] = small_ref[...]
    line = jnp.sum(tokens * inverse * grad, axis=0, keepdims=True)
    for owner in range(8):
        small_f32[owner, 0:1, :96] = line[:, owner * 96 : owner * 96 + 96]
    sm_own[...] = small_f32[...].astype(BF)
    sm_over = go(sm_own, sm_core, sm_send.at[0], sm_recv.at[0], sibling)
    c_far = rows_sum(c_last, c_kept, c_row, c_high, c_fin, c_right, 1)
    for k in range(4):
        step_x(k)
    early = ctx_start(0, packed, from_ctx)
    c_far.wait_recv()
    multiply(CROSS_KV, turned_state, c_right[...])
    step_z(SELF_KV)
    sm_over.wait_recv()
    sm_own_sum = (sm_own[...].astype(F32) + sm_core[...].astype(F32)).astype(BF)
    sm_over.wait_send()
    sm_own[...] = sm_own_sum
    sm_inside = go(
        sm_own.at[pl.ds(4 * (1 - low), 4)], sm_z, sm_send.at[1], sm_recv.at[1], inside
    )
    ctx_sum(0, early, packed, from_ctx, land)
    step_z(CROSS_KV)
    step_via(SELF_KV)
    sm_inside.wait_recv()
    for column in range(4):
        sm_z[column] = sm_z[column] + sm_own[4 * low + column]
    sm_row = [
        go(
            sm_z.at[(x + spot + 1) % 4], sm_x.at[spot],
            sm_send.at[2 + spot], sm_recv.at[2 + spot], (me, others[spot]),
        )
        for spot in range(3)
    ]
    step_via(CROSS_KV)
    scaled = gain_ref[...] * grad
    mixed = jnp.mean(tokens * scaled, axis=-1, keepdims=True)
    decoder_ref[...] = (
        dmid_ref[...] + inverse * scaled - tokens * (inverse * inverse * inverse * mixed)
    )
    step_x(SELF_KV)
    step_x(CROSS_KV)
    late = ctx_start(1, late_packed, late_from)
    sm_sum = sm_z[x].astype(F32)
    for spot in range(3):
        sm_row[spot].wait_recv()
        sm_sum = sm_sum + sm_x[spot].astype(F32)
    sm_total[...] = sm_sum.astype(BF)
    sm_mates = [
        go(sm_total, sm_ctx.at[spot], sm_send.at[5 + spot], sm_recv.at[5 + spot], mate_device(mate))
        for spot, mate in enumerate(mates)
    ]
    ctx_pass(0, land)
    ctx_sum(1, late, late_packed, late_from, late_land)
    d_ckv = jnp.concatenate([c_fin[0], c_fin[1]], axis=1)
    ckv_copy.wait()
    encoder_ref[...] = contract(d_ckv, ckv_ref[...], ((1,), (1,)))
    sm_sum = sm_total[...].astype(F32)
    for spot in range(7):
        sm_mates[spot].wait_recv()
        sm_sum = sm_sum + sm_ctx[spot].astype(F32)
    small_out[...] = sm_sum
    ctx_done(0, land)
    early_exit = bring(land, early_out, bring_sem.at[9])
    ctx_pass(1, late_land)
    ctx_done(1, late_land)
    late_exit = bring(late_land, late_out, bring_sem.at[10])
    early_exit.wait()
    late_exit.wait()
    for copy in sends:
        if copy is not sm_over:
            copy.wait_send()


def unpack_kernel(early, late, *refs):
    for source, target in zip(refs[:3], refs[14:]):
        target[...] = source[...]
    square_refs = refs[3:11]
    gate_ref, up_ref, down_ref = refs[11:14]
    half = D // 2
    middle = PIECE // 2
    for side in range(2):
        columns = slice(side * half, side * half + half)
        for upper in range(2):
            rows = slice(upper * middle, upper * middle + middle)
            for k in range(4):
                square_refs[k][rows, columns] = early[2 * k + upper, side, PIECE:, :].astype(F32)
            for k in range(2):
                for piece in range(2):
                    square_refs[4 + 2 * k + side][rows, piece * half : piece * half + half] = late[
                        4 * k + 2 * piece + upper, side
                    ].astype(F32)
        target = up_ref if side else gate_ref
        for piece in range(8):
            target[:, piece * 256 : piece * 256 + 256] = early[piece, side, :PIECE, :256].astype(F32)
            for part in range(3):
                down_ref[
                    piece * 32 : piece * 32 + 32,
                    side * half + part * 128 : side * half + part * 128 + 128,
                ] = early[piece, side, part * 32 : part * 32 + 32, 256:].astype(F32)


def unpack(early, late, *whole):
    outs = (
        [jax.ShapeDtypeStruct((PIECE, D), F32)] * 8
        + [jax.ShapeDtypeStruct((PIECE, FF), F32)] * 2
        + [jax.ShapeDtypeStruct((FF // 8, D), F32)]
        + [jax.ShapeDtypeStruct(part.shape, F32) for part in whole]
    )
    return pl.pallas_call(
        unpack_kernel,
        out_shape=outs,
        in_specs=[pl.BlockSpec(memory_space=pltpu.VMEM)] * (2 + len(whole)),
        out_specs=[pl.BlockSpec(memory_space=pltpu.VMEM)] * len(outs),
        compiler_params=pltpu.CompilerParams(vmem_limit_bytes=24 * MIB),
        name="unpack",
    )(early, late, *whole)


def finish(far, near, collective_id):
    dma = pltpu.SemaphoreType.DMA

    def rows(count):
        return [
            pltpu.VMEM((8, 2, count, D), BF),
            pltpu.VMEM((8, 2, count, D), BF),
            pltpu.VMEM((2, 2, 2, count, D), BF),
            pltpu.VMEM((2, 2, count, D), BF),
            pltpu.VMEM((2, count, D), BF),
            pltpu.VMEM((2, count, D), BF),
            pltpu.VMEM((2, count, D), BF),
        ]

    outs = [
        jax.ShapeDtypeStruct((8, 2, 3 * PIECE // 2, D // 2), BF),
        jax.ShapeDtypeStruct((8, 2, PIECE // 2, D // 2), BF),
        jax.ShapeDtypeStruct((16, 128), F32),
        jax.ShapeDtypeStruct((TOK, D), F32),
        jax.ShapeDtypeStruct((ENC, D), F32),
    ]
    return pl.pallas_call(
        finish_kernel,
        out_shape=outs,
        in_specs=[pl.BlockSpec(memory_space=pl.ANY)] * len(far)
        + [pl.BlockSpec(memory_space=pltpu.VMEM)] * len(near),
        out_specs=[pl.BlockSpec(memory_space=pl.ANY)] * 2
        + [pl.BlockSpec(memory_space=pltpu.VMEM)] * 3,
        scratch_shapes=[
            pltpu.VMEM((2 * TOK, sum(LEFT)), BF),
            pltpu.VMEM((2 * TOK, sum(RIGHT)), BF),
            pltpu.VMEM((8, PIECE, 2 * TOK), BF),
            pltpu.VMEM((8, PIECE, 2 * TOK), BF),
            pltpu.VMEM((8, PIECE, 2 * ENC), BF),
            pltpu.VMEM((2 * ENC, D), BF),
            pltpu.VMEM((2 * TOK, D), BF),
            pltpu.VMEM((2 * ENC, D), BF),
            pltpu.VMEM((8, PIECE, SPAN - FF), BF),
            pltpu.VMEM((4, PIECE, SPAN), BF),
            pltpu.VMEM((2, PIECE, SPAN), BF),
            pltpu.VMEM((2, PIECE // 2, SPAN), BF),
            pltpu.VMEM((4, FF // 8, D // 2), BF),
            pltpu.VMEM((2, FF // 8, D // 2), BF),
            pltpu.VMEM((2, FF // 16, D // 2), BF),
        ]
        + rows(TOK)
        + rows(ENC)
        + [
            pltpu.VMEM((8, 16, 128), F32),
            pltpu.VMEM((8, 16, 128), BF),
            pltpu.VMEM((8, 16, 128), BF),
            pltpu.VMEM((4, 16, 128), BF),
            pltpu.VMEM((3, 16, 128), BF),
            pltpu.VMEM((7, 16, 128), BF),
            pltpu.VMEM((16, 128), BF),
            pltpu.VMEM((8, 3 * PIECE // 2, D // 2), BF),
            pltpu.VMEM((7, 3 * PIECE // 2, D // 2), BF),
            pltpu.VMEM((8, 2, 3 * PIECE // 2, D // 2), BF),
            pltpu.VMEM((8, PIECE // 2, D // 2), BF),
            pltpu.VMEM((7, PIECE // 2, D // 2), BF),
            pltpu.VMEM((8, 2, PIECE // 2, D // 2), BF),
            pltpu.VMEM((2, 4, PIECE // 2, FF), BF),
            pltpu.VMEM((2, 4, FF // 16, D // 2), BF),
            pltpu.VMEM((8, PIECE, D), BF),
            pltpu.VMEM((D, 2 * D), BF),
            pltpu.VMEM((D, 2 * D), BF),
            dma((11,)),
            dma((5, 7)),
            dma((5, 7)),
            dma((4, 2)),
            dma((4, 2)),
            dma((4, 2)),
            dma((3,)),
            dma((3,)),
            dma((CHUNKS, 2)),
            dma((CHUNKS, 2)),
            dma((CHUNKS, 6)),
            dma((CHUNKS, 6)),
            dma((2, 14)),
            dma((2, 15)),
            dma((2, 8)),
            dma((2, 8)),
            dma((12,)),
            dma((12,)),
            dma((3,)),
        ],
        compiler_params=pltpu.CompilerParams(
            collective_id=collective_id, has_side_effects=True, vmem_limit_bytes=62 * MIB
        ),
        name="finish_gradients",
    )(*far, *near)


def backward_kernel(biased, *refs):
    if biased:
        class_ref, near_ref, q_ref, k_ref, v_ref, g_ref, total_ref, tile_ref = refs[:8]
        dq_ref, dkv_ref, strip_ref, share_ref, slope_ref, share_low, slope_low = refs[8:]
    else:
        q_ref, k_ref, v_ref, g_ref, total_ref = refs[:5]
        dq_ref, dkv_ref, share_ref, slope_ref, share_low, slope_low = refs[5:]
    chunks = share_ref.shape[0]
    queries = split_heads(q_ref[...])
    grads = split_heads(g_ref[...])
    totals = total_ref[0, 0:1]
    inner = jnp.zeros((8, 2 * TOK), F32)
    for j in range(chunks):
        scores = contract(key_chunk(k_ref, j), queries, ((1,), (1,)))
        if biased:
            scores = scores + bias_chunk(class_ref, tile_ref, j)
        shares = jnp.exp(scores - totals)
        slopes = contract(key_chunk(v_ref, j), grads, ((1,), (1,)))
        inner = inner + fold(shares * slopes, jnp.sum)
        share_ref[j] = shares
        slope_ref[j] = slopes
        share_low[j] = shares.astype(BF)
    inner = jnp.sum(inner, axis=0, keepdims=True)
    for j in range(chunks):
        grad = share_ref[j] * (slope_ref[j] - inner)
        if biased:
            slope_ref[j] = grad
        slope_low[j] = grad.astype(BF)
    keys = jnp.concatenate([key_chunk(k_ref, j) for j in range(chunks)], axis=0)
    low = slope_low[...].reshape(-1, 2 * TOK)
    dq_ref[...] = join_heads(contract(keys, low, ((0,), (0,)))).astype(BF)
    shape = dkv_ref.shape
    block = (shape[0], shape[2], shape[3])
    dkv_ref[:, 0] = contract(low, queries, ((1,), (0,))).astype(BF).reshape(block)
    dkv_ref[:, 1] = (
        contract(share_low[...].reshape(-1, 2 * TOK), grads, ((1,), (0,))).astype(BF).reshape(block)
    )
    if biased:
        lane = lax.broadcasted_iota(jnp.int32, (HALF, TOK), 1)
        for gap in range(3):
            pieces = []
            for half in range(2):
                spot = near_ref[half, gap]
                held = slope_ref[jnp.maximum(spot, 0) // 2, pl.ds(
                    pl.multiple_of((jnp.maximum(spot, 0) % 2) * HALF, HALF), HALF)]
                pieces.append(jnp.where(spot >= 0, held, jnp.zeros_like(held)))
            for head in range(2):
                cut = slice(head * TOK, (head + 1) * TOK)
                strip_ref[head, gap] = jnp.where(lane < HALF, pieces[0][:, cut], pieces[1][:, cut])


def pair_columns(pair):
    return (0, pair)


def kv_spec(rows, row_block, part):
    return pl.BlockSpec(
        (N_CTX, 1, rows, 2 * HEAD_DIM), lambda pair: (0, part, row_block, pair)
    )


SMEM_SPEC = pl.BlockSpec(memory_space=pltpu.SMEM)
TILE_SPEC = pl.BlockSpec((2, 5, HALF, TOK), lambda pair: (pair, 0, 0, 0))
TOTAL_SPEC = pl.BlockSpec((1, 8, 2 * TOK), lambda pair: (pair, 0, 0))
ROW_SPEC = pl.BlockSpec((TOK, 2 * HEAD_DIM), pair_columns)
LOCAL = pltpu.CompilerParams(vmem_limit_bytes=48 * MIB)


def attend_back(queries, gathered, grads, totals, rows, row_block, classes=None, near=None, tiles=None):
    biased = classes is not None
    chunks = N_CTX * rows // TOK
    specs = [ROW_SPEC, kv_spec(rows, row_block, 0), kv_spec(rows, row_block, 1), ROW_SPEC, TOTAL_SPEC]
    operands = [queries, gathered, gathered, grads, totals]
    out_specs = [
        ROW_SPEC,
        pl.BlockSpec((N_CTX, 2, rows, 2 * HEAD_DIM), lambda pair: (0, 0, 0, pair)),
    ]
    out_shape = [
        jax.ShapeDtypeStruct((TOK, D), BF),
        jax.ShapeDtypeStruct((N_CTX, 2, rows, D), BF),
    ]
    if biased:
        specs = [SMEM_SPEC, SMEM_SPEC] + specs + [TILE_SPEC]
        operands = [classes, near] + operands + [tiles]
        out_specs.append(pl.BlockSpec((2, 3, HALF, TOK), lambda pair: (pair, 0, 0, 0)))
        out_shape.append(jax.ShapeDtypeStruct((HEADS, 3, HALF, TOK), F32))
    return pl.pallas_call(
        functools.partial(backward_kernel, biased),
        grid=(PAIRS,),
        in_specs=specs,
        out_specs=out_specs,
        out_shape=out_shape,
        scratch_shapes=[
            pltpu.VMEM((chunks, TOK, 2 * TOK), F32),
            pltpu.VMEM((chunks, TOK, 2 * TOK), F32),
            pltpu.VMEM((chunks, TOK, 2 * TOK), BF),
            pltpu.VMEM((chunks, TOK, 2 * TOK), BF),
        ],
        compiler_params=LOCAL,
        cost_estimate=pl.CostEstimate(flops=1000, bytes_accessed=1000, transcendentals=0),
        name="attend_self_back" if biased else "attend_cross_back",
    )(*operands)


def matmul(left, right):
    return jnp.dot(left, right, preferred_element_type=F32)


def transposed_left(left, right):
    return contract(left, right, ((0,), (0,)))


def transposed_right(left, right):
    return contract(left, right, ((1,), (1,)))


def rms_scaled(values, gain):
    inverse = lax.rsqrt(jnp.mean(values * values, axis=-1, keepdims=True) + 1e-06)
    return (values * inverse * gain).astype(BF)


def rms_back(values, gain, grad):
    inverse = lax.rsqrt(jnp.mean(values * values, axis=-1, keepdims=True) + 1e-06)
    scaled = gain * grad
    mixed = jnp.mean(values * scaled, axis=-1, keepdims=True)
    grad_values = inverse * scaled - values * (inverse * inverse * inverse * mixed)
    return grad_values, jnp.sum(values * inverse * grad, axis=0)


def near_hot():
    shape = (REACH, 3 * HALF * HALF)
    spot = lax.broadcasted_iota(jnp.int32, shape, 1)
    gap = spot // (HALF * HALF)
    key = (spot // HALF) % HALF
    row = spot % HALF
    distance = jnp.clip(HALF * gap + row - key, 0, REACH - 1)
    return (distance == lax.broadcasted_iota(jnp.int32, shape, 0)).astype(BF)


def bias_sums(strips):
    tiles = (strips[..., :HALF] + strips[..., HALF:]).reshape(HEADS, -1)
    high = tiles.astype(BF)
    low = (tiles - high.astype(F32)).astype(BF)
    hot = near_hot()
    sums = transposed_right(high, hot) + transposed_right(low, hot)
    far = -jnp.sum(sums[:, :-1], axis=1, keepdims=True)
    return jnp.concatenate([sums[:, :-1], far], axis=1)


def swap(values, move):
    perm = []
    for ctx in range(N_CTX):
        for shard in range(8):
            there, owner = move(ctx, shard)
            perm.append((ctx * 8 + shard, there * 8 + owner))
    return lax.ppermute(values, ("ctx", "fsdp"), perm)


def over_z(mine, upper, lower):
    inner = swap(upper, lambda ctx, shard: (ctx, (shard + 4) % 8))
    outer = swap(lower, lambda ctx, shard: (ctx ^ 2, (shard + 4) % 8))
    return mine, inner, outer


def body(
    decoder_in,
    encoder_states,
    out_grad,
    block_pairs,
    bucket_table,
    gain_self,
    self_query,
    self_key,
    self_value,
    self_out,
    position_bias,
    gain_cross,
    cross_query,
    cross_key,
    cross_value,
    cross_out,
    gain_feed,
    feed_gate,
    feed_up,
    feed_down,
):
    me = lax.axis_index("ctx")
    rows = self_query.shape[0]
    small = jnp.concatenate(
        [
            jnp.pad(jnp.stack([gain_self, gain_cross, gain_feed]), ((0, 0), (0, 128 - rows))),
            jnp.pad(position_bias, ((0, 9), (0, 128 - HEADS))),
        ],
        axis=0,
    )
    (
        kv_one, kv_two, square, gains, normed_one, queries, tiles, attended, self_totals, mid_one,
        normed_two, cross_queries, cross_attended, cross_totals, block_out, d_mid_two,
        cross_branch, d_cross_attended, grad_norm_three, *feed_parts, classes, near, self_kv,
        cross_kv,
    ) = front(
        [
            self_key, self_value, cross_key, cross_value,
            self_query, self_out, cross_query, cross_out,
            feed_gate, feed_up, feed_down,
        ],
        [
            small, decoder_in[0], encoder_states[0], out_grad[0], bucket_table[None, :], block_pairs,
        ],
        0,
    )
    kv_one = kv_one.reshape(D, 2 * D)
    kv_two = kv_two.reshape(D, 2 * D)
    out_one, query_two = (square.reshape(D, 4 * D)[:, k * D : k * D + D] for k in (1, 2))
    norm_one, norm_two = gains[0:1], gains[1:2]
    bucket_hot = (bucket_table[:, None] == jnp.arange(32, dtype=jnp.int32)[None, :]).astype(BF)
    tokens = decoder_in[0].astype(F32)
    states = encoder_states[0]
    upstream = out_grad[0]
    feed_parts = [over_z(*feed_parts[:3]), over_z(*feed_parts[3:])]
    d_cross_queries, d_cross_kv_all = attend_back(
        cross_queries, cross_kv, d_cross_attended, cross_totals, ENC, 0
    )
    d_normed_two = transposed_right(d_cross_queries, query_two)
    part_two, grad_norm_two = rms_back(mid_one, norm_two, d_normed_two)
    d_mid_one = d_mid_two + part_two
    self_branch = d_mid_one.astype(BF)
    d_attended = transposed_right(self_branch, out_one).astype(BF)
    feed_parts[1], d_attended = lax.optimization_barrier((feed_parts[1], d_attended))
    d_queries, d_kv_all, strips = attend_back(
        queries, self_kv, d_attended, self_totals, TOK, 0, classes, near, tiles
    )
    feed_parts, d_queries, d_kv_all, strips = lax.optimization_barrier(
        (feed_parts, d_queries, d_kv_all, strips)
    )
    grad_table = matmul(bias_sums(strips), bucket_hot.astype(F32)).T.reshape(8, 4, HEADS)
    grad_gains = jnp.stack([grad_norm_two, grad_norm_three[0]]).reshape(2, 8, rows)
    grad_small = jnp.concatenate(
        [
            jnp.zeros((8, 1, 128), F32),
            jnp.pad(jnp.transpose(grad_gains, (1, 0, 2)), ((0, 0), (0, 0), (0, 128 - rows))),
            jnp.pad(grad_table, ((0, 0), (0, 9), (0, 128 - HEADS))),
        ],
        axis=1,
    )
    done = finish(
        [
            cross_attended, normed_two, attended, normed_one,
            cross_branch, d_cross_queries, self_branch, d_queries,
            *feed_parts[0],
            *feed_parts[1],
            d_kv_all.reshape(8, 2, 2, TOK, D),
            d_cross_kv_all.reshape(8, 2, 2, ENC, D),
            square,
            kv_one,
            kv_two,
        ],
        [
            states,
            d_queries,
            d_mid_one,
            decoder_in[0],
            norm_one,
            grad_small,
        ],
        3,
    )
    early, late, extras, grad_decoder, grad_encoder = done
    (
        grad_out_two, grad_query_two, grad_out_one, grad_query_one,
        grad_key_two, grad_value_two, grad_key_one, grad_value_one,
        grad_gate, grad_up, grad_down, block_out, grad_decoder, grad_encoder,
    ) = unpack(early, late, block_out, grad_decoder, grad_encoder)
    return (
        block_out[None],
        grad_decoder[None],
        grad_encoder[None],
        extras[0, :rows],
        grad_query_one,
        grad_key_one,
        grad_value_one,
        grad_out_one,
        extras[3:7, :HEADS],
        extras[1, :rows],
        grad_query_two,
        grad_key_two,
        grad_value_two,
        grad_out_two,
        extras[2, :rows],
        grad_gate,
        grad_up,
        grad_down,
    )


def solution(mesh):
    tokens = P("fsdp", "ctx", None)
    matrix = P("fsdp", None)
    vector = P("fsdp")
    weights = (
        (vector,) + (matrix,) * 5 + (vector,) + (matrix,) * 4 + (vector,) + (matrix,) * 3
    )
    return jax.shard_map(
        body,
        mesh=mesh,
        in_specs=(tokens,) * 3 + (P(), P()) + weights,
        out_specs=(tokens,) * 3 + weights,
        check_vma=False,
    )
```

```python
import functools

import jax
import jax.numpy as jnp
from jax import lax
from jax.experimental import pallas as pl
from jax.experimental.pallas import tpu as pltpu
from jax.sharding import PartitionSpec as P

D = 768
FF = 2048
HEADS = 12
HEAD_DIM = 64
PAIRS = HEADS // 2
N_CTX = 16
TOK = 128
ENC = 64
HALF = 64
REACH = 128
BF = jnp.bfloat16
F32 = jnp.float32
MIB = 1024 * 1024


def ctx_place():
    me = lax.axis_index("ctx")
    core = me % 2
    high = (me // 2) % 2
    y = me // 4
    return me, core, high, y


def slot_of(y, shift, high, core):
    return ((y + shift) % 4) * 4 + 2 * high + core


def split_heads(block):
    lane = lax.broadcasted_iota(jnp.int32, block.shape, 1)
    nothing = jnp.zeros_like(block)
    return jnp.concatenate(
        [jnp.where(lane < HEAD_DIM, block, nothing), jnp.where(lane < HEAD_DIM, nothing, block)],
        axis=0,
    )


def join_heads(transposed):
    row = lax.broadcasted_iota(jnp.int32, (2 * HEAD_DIM, TOK), 0)
    return jnp.where(row < HEAD_DIM, transposed[:, :TOK], transposed[:, TOK:]).T


def contract(left, right, dims):
    return lax.dot_general(left, right, (dims, ((), ())), preferred_element_type=F32)


def key_chunk(ref, j):
    if ref.shape[2] == 2 * HALF:
        return ref[j, 0]
    return ref[pl.ds(2 * j, 2), 0].reshape(2 * HALF, 2 * HEAD_DIM)


def bias_chunk(class_ref, tile_ref, j, first=0):
    lane = lax.broadcasted_iota(jnp.int32, (HALF, TOK), 1)
    rows = []
    for half in range(2):
        spot = 2 * j + half
        near = class_ref[0, spot]
        far = class_ref[1, spot]
        rows.append(
            jnp.concatenate(
                [
                    jnp.where(lane < HALF, tile_ref[first + head, near], tile_ref[first + head, far])
                    for head in range(2)
                ],
                axis=1,
            )
        )
    return jnp.concatenate(rows, axis=0)


def fold(values, join):
    return join(values.reshape(-1, 8, values.shape[-1]), axis=0)


def attend_pair(queries, keys, values, bias, score_ref, share_ref, chunks):
    queries = split_heads(queries)
    highest = None
    for j in range(chunks):
        scores = contract(keys(j), queries, ((1,), (1,)))
        if bias is not None:
            scores = scores + bias(j)
        score_ref[j] = scores
        top = fold(scores, jnp.max)
        highest = top if highest is None else jnp.maximum(highest, top)
    highest = jnp.max(highest, axis=0, keepdims=True)
    summed = jnp.zeros((8, 2 * TOK), F32)
    for j in range(chunks):
        raised = jnp.exp(score_ref[j] - highest)
        summed = summed + fold(raised, jnp.sum)
        share_ref[j] = raised.astype(BF)
    summed = jnp.sum(summed, axis=0, keepdims=True)
    gathered = jnp.concatenate([values(j) for j in range(chunks)], axis=0)
    mixed = contract(gathered, share_ref[:chunks].reshape(-1, 2 * TOK), ((0,), (0,)))
    return join_heads(mixed / summed).astype(BF), highest + jnp.log(summed)


def attend_pairs(first, last, kv_ref, query_ref, out_ref, total_ref, score_ref, share_ref, bias=None):
    rows = kv_ref.shape[2]
    chunks = N_CTX * rows // TOK

    def step(pair, carry):
        cut = pl.ds(pl.multiple_of(pair * TOK, TOK), TOK)

        def chunk(part, j):
            if rows == TOK:
                return kv_ref[j, part, :, cut]
            return kv_ref[2 * j : 2 * j + 2, part, :, cut].reshape(TOK, TOK)

        mixed, total = attend_pair(
            query_ref[:, cut],
            functools.partial(chunk, 0),
            functools.partial(chunk, 1),
            None if bias is None else functools.partial(bias, pair),
            score_ref,
            share_ref,
            chunks,
        )
        out_ref[:, cut] = mixed
        total_ref[pair] = jnp.broadcast_to(total, (8, 2 * TOK))
        return carry

    lax.fori_loop(first, last, step, 0)


def strip_hot():
    shape = (REACH, 3 * TOK)
    spot = lax.broadcasted_iota(jnp.int32, shape, 1)
    distance = jnp.clip(HALF * (spot // TOK) + spot % TOK - (HALF - 1), 0, REACH - 1)
    return (distance == lax.broadcasted_iota(jnp.int32, shape, 0)).astype(BF)


def index_tables(me, pairs_ref, class_ref, near_ref):
    own = pairs_ref[me]
    for half in range(2):
        query = 31 - own if half else own
        spots = [jnp.int32(-1)] * 3
        for block in range(32):
            pair = pairs_ref[block // 2]
            key = 31 - pair if block % 2 else pair
            gap = query - key
            class_ref[half, block] = jnp.where(gap < 0, 4, jnp.minimum(gap, 3))
            for near in range(3):
                spots[near] = jnp.where(gap == near, block, spots[near])
        for near in range(3):
            near_ref[half, near] = spots[near]


def build_tiles(bias_rows, strips, tile_ref):
    lane = lax.broadcasted_iota(jnp.int32, (HALF, TOK), 1)
    key = lax.broadcasted_iota(jnp.int32, (HALF, TOK), 0)
    row = jnp.where(lane < HALF, lane, lane - HALF)
    for head in range(HEADS):
        for gap in range(3):
            strip = strips[head : head + 1, gap * TOK : gap * TOK + TOK]
            turned = pltpu.roll(
                jnp.broadcast_to(strip, (HALF, TOK)), 65, 1, stride=1, stride_axis=0
            )
            tile = jnp.where(lane < HALF, turned, pltpu.roll(turned, HALF, 1))
            if gap == 0:
                tile = jnp.where(key > row, -1e30, tile)
            tile_ref[head, gap] = tile
        tile_ref[head, 3] = jnp.broadcast_to(bias_rows[head : head + 1, REACH - 1 :], (HALF, TOK))
        tile_ref[head, 4] = jnp.full((HALF, TOK), -1e30, F32)


def torus_place():
    me, core, high, y = ctx_place()
    shard = lax.axis_index("fsdp")
    return me, core, high, y, shard // 4, shard % 4


def hop(src, dst, send_sem, recv_sem, ctx, fsdp):
    return pltpu.make_async_remote_copy(
        src_ref=src,
        dst_ref=dst,
        send_sem=send_sem,
        recv_sem=recv_sem,
        device_id={"ctx": ctx, "fsdp": fsdp},
    )


def greet_all(devices):
    barrier = pltpu.get_barrier_semaphore()
    for ctx, fsdp in devices:
        pl.semaphore_signal(barrier, inc=1, device_id={"ctx": ctx, "fsdp": fsdp})
    pl.semaphore_wait(barrier, len(devices))


ROOT = (2.0 / 3.141592653589793) ** 0.5
PACKS = ((0, 1), (2, 3), (4, 5, 6, 7), (8, 9), (10,))


def front_kernel(*refs):
    sources = refs[:11]
    small_ref, token_ref, state_ref, upstream_ref, bucket_ref, pairs_ref = refs[11:17]
    results = refs[17:20]
    (
        gain_out, normed_out, query_out, tile_result, attended_ref, total_ref, mid_one_ref,
        normed_two_ref, cross_query_ref, cross_attended_ref, cross_total_ref,
        block_ref, d_mid_ref, branch_ref, d_cross_ref, gain_grad_ref,
        wide_mine_out, wide_inner_out, wide_outer_out, tall_mine_out, tall_inner_out, tall_outer_out,
        class_ref, near_ref, self_result, cross_result,
    ) = refs[20:46]
    targets = refs[46:51]
    (
        self_out_ref, cross_out_ref, landing, self_ref, cross_ref, score_ref, share_ref,
        feed_left, feed_right, slope_ref, turned, turned_hidden, tile_ref,
        wide_mine, wide_inner, wide_outer, tall_mine, tall_inner, tall_outer,
        send_sem, x_sem, z_sem, core_sem,
        fill_sem, small_sem, self_sem, cross_sem, feed_sem, local_sem,
    ) = refs[51:]
    me, core, high, y, low, x = torus_place()
    shard = low * 4 + x
    sibling = (slot_of(y, 0, high, 1 - core), shard)
    inside = (me, (1 - low) * 4 + x)
    outside = (slot_of(y, 0, 1 - high, core), (1 - low) * 4 + x)
    across = slot_of(y, 0, 1 - high, core)
    ahead, behind = (slot_of(y, shift, high, core) for shift in (1, 3))
    others = [low * 4 + (x + shift) % 4 for shift in (1, 2, 3)]
    peers = [(shard + shift) % 8 for shift in range(1, 8)]
    greet_all(
        [sibling, outside, (across, shard), (ahead, shard), (behind, shard)]
        + [(me, peer) for peer in peers]
    )
    sends = []

    def send(src, dst, recv_sem, device):
        copy = hop(src, dst, send_sem.at[len(sends)], recv_sem, *device)
        copy.start()
        sends.append(copy)

    def arrived(ref, recv_sem):
        hop(ref, ref, send_sem.at[0], recv_sem, *sibling).wait_recv()

    def bring(src, dst, sem):
        copy = pltpu.make_async_copy(src, dst, sem)
        copy.start()
        return copy


    def part(k, owner, whose, side=None):
        ref = targets[k]
        count = ref.shape[1] // 2
        start = pl.multiple_of(whose * count, 16)
        if side is None:
            return ref.at[owner, pl.ds(start, count), :]
        width = ref.shape[2] // 2
        return ref.at[owner, pl.ds(start, count), pl.ds(side * width, width)]

    def fill(k):
        copies = []
        start = 0
        for source in PACKS[k]:
            width = sources[source].shape[1]
            copies.append(
                bring(
                    sources[source],
                    targets[k].at[shard, :, pl.ds(start, width)],
                    fill_sem.at[source],
                )
            )
            start += width
        return copies

    def send_own(k):
        for copy in fills[k]:
            copy.wait()
        for spot in (1, 0, 2):
            block = part(k, shard, core)
            send(block, block, x_sem.at[k, spot], (me, others[spot]))
        for side, device in enumerate((inside, outside)):
            piece = part(k, shard, core, side)
            send(piece, piece, z_sem.at[k, 3, side], device)


    def pass_x(k):
        for spot in (0, 2, 1):
            owner = low * 4 + (x + 3 - spot) % 4
            block = part(k, owner, core)
            arrived(block, x_sem.at[k, spot])
            for side, device in enumerate((inside, outside)):
                piece = part(k, owner, core, side)
                send(piece, piece, z_sem.at[k, spot, side], device)
            send(block, block, core_sem.at[k, spot], sibling)

    def pass_z(k):
        for spot in (3, 0, 2, 1):
            owner = (1 - low) * 4 + (x + 3 - spot) % 4
            for side in range(2):
                piece = part(k, owner, core, side)
                arrived(piece, z_sem.at[k, spot, side])
                send(piece, piece, core_sem.at[k, 3 + 2 * spot + side], sibling)

    def complete(k):
        for spot in range(3):
            owner = low * 4 + (x + 3 - spot) % 4
            arrived(part(k, owner, 1 - core), core_sem.at[k, spot])
        for spot in range(4):
            owner = (1 - low) * 4 + (x + 3 - spot) % 4
            for side in range(2):
                arrived(part(k, owner, 1 - core, side), core_sem.at[k, 3 + 2 * spot + side])


    def kv_start(src, out, sems):
        send(src, out.at[me], sems.at[me, 0], (across, shard))
        send(src, out.at[me], sems.at[me, 0], (ahead, shard))
        send(src, out.at[me], sems.at[me, 0], (behind, shard))
        send(src, out.at[me], sems.at[me, 0], sibling)

    def kv_across(out, sems):
        block = out.at[across]
        arrived(block, sems.at[across, 0])
        send(block, block, sems.at[across, 0], (ahead, shard))
        send(block, block, sems.at[across, 0], (behind, shard))
        send(block, block, sems.at[across, 0], sibling)

    def kv_near(out, sems, flip):
        half = 1 - high if flip else high
        slot = slot_of(y, 1, half, core)
        block = out.at[slot]
        arrived(block, sems.at[slot, 0])
        send(block.at[0], block.at[0], sems.at[slot, 0], (behind, shard))
        send(block, block, sems.at[slot, 0], sibling)
        slot = slot_of(y, 3, half, core)
        block = out.at[slot]
        arrived(block, sems.at[slot, 0])
        send(block.at[1], block.at[1], sems.at[slot, 1], (ahead, shard))
        send(block, block, sems.at[slot, 0], sibling)

    def kv_far(out, sems, flip):
        slot = slot_of(y, 2, 1 - high if flip else high, core)
        for part in range(2):
            arrived(out.at[slot, part], sems.at[slot, part])
        send(out.at[slot], out.at[slot], sems.at[slot, 0], sibling)

    def kv_complete(out, sems):
        for shift in range(4):
            for half in range(2):
                slot = slot_of(y, shift, half, 1 - core)
                arrived(out.at[slot], sems.at[slot, 0])

    fills = [fill(k) for k in range(5)]
    own_small = bring(small_ref, landing.at[shard], local_sem.at[0])
    for spot, peer in enumerate(peers):
        send(small_ref, landing.at[shard], small_sem.at[spot], (me, peer))
    send_own(0)
    send_own(1)
    own_small.wait()
    for spot in range(7):
        arrived(landing.at[(shard + 7 - spot) % 8], small_sem.at[spot])
    gains = landing[...].astype(F32)
    gain = [
        jnp.concatenate([gains[owner, k : k + 1, :96] for owner in range(8)], axis=1)
        for k in range(3)
    ]
    for k in range(3):
        gain_out[k : k + 1, :] = gain[k]
    tokens = token_ref[...].astype(F32)
    normed = rms_scaled(tokens, gain[0])
    normed_out[...] = normed
    pass_x(0)
    send_own(2)
    pass_z(0)
    pass_x(1)
    send_own(3)
    complete(0)
    exits = [bring(targets[0], results[0], local_sem.at[1])]
    for half in range(2):
        weight = targets[0][:, :, half * D : half * D + D].reshape(D, D)
        self_ref[half] = matmul(normed, weight).astype(BF)
    kv_start(self_ref, self_out_ref, self_sem)
    own_self = bring(self_ref, self_out_ref.at[me], local_sem.at[2])
    pass_z(1)
    send_own(4)
    complete(1)
    exits.append(bring(targets[1], results[1], local_sem.at[4]))
    for half in range(2):
        weight = targets[1][:, :, half * D : half * D + D].reshape(D, D)
        cross_ref[half] = matmul(state_ref[...], weight).astype(BF)
    kv_start(cross_ref, cross_out_ref, cross_sem)
    own_cross = bring(cross_ref, cross_out_ref.at[me], local_sem.at[3])
    index_tables(me, pairs_ref, class_ref, near_ref)
    slab = lax.broadcasted_iota(jnp.int32, (128, REACH), 0)
    place = slab % 16 - 3
    wanted = jnp.where((place >= 0) & (place < 4), 4 * (slab // 16) + place, -1)
    hot = jnp.where(wanted == bucket_ref[...], 1.0, 0.0).astype(BF)
    bias_rows = contract(landing[...].reshape(128, 128), hot, ((0,), (0,)))[:16]
    build_tiles(bias_rows, matmul(bias_rows.astype(BF), strip_hot()), tile_ref)
    exits.append(bring(tile_ref, tile_result, local_sem.at[8]))
    kv_across(self_out_ref, self_sem)
    pass_x(2)
    kv_near(self_out_ref, self_sem, False)
    pass_z(2)
    kv_across(cross_out_ref, cross_sem)
    kv_near(self_out_ref, self_sem, True)
    pass_x(3)
    complete(2)
    exits.append(bring(targets[2], results[2], local_sem.at[5]))

    def square(k):
        return targets[2][:, :, k * D : k * D + D].reshape(D, D)

    query_out[...] = matmul(normed, square(0)).astype(BF)
    kv_far(self_out_ref, self_sem, False)
    kv_far(self_out_ref, self_sem, True)
    kv_near(cross_out_ref, cross_sem, False)
    own_self.wait()
    own_cross.wait()
    kv_complete(self_out_ref, self_sem)
    exits.append(bring(self_out_ref, self_result, local_sem.at[6]))

    def attend_self(first, last):
        attend_pairs(
            first, last, self_out_ref, query_out, attended_ref, total_ref, score_ref, share_ref,
            lambda pair, j: bias_chunk(class_ref, tile_ref, j, 2 * pair),
        )

    def attend_cross(first, last):
        attend_pairs(
            first, last, cross_out_ref, cross_query_ref, cross_attended_ref, cross_total_ref,
            score_ref, share_ref,
        )

    attend_self(0, 2)
    pass_x(4)
    kv_near(cross_out_ref, cross_sem, True)
    kv_far(cross_out_ref, cross_sem, False)
    attend_self(2, 4)
    pass_z(3)
    kv_far(cross_out_ref, cross_sem, True)
    attend_self(4, 6)
    mid_one = tokens + matmul(attended_ref[...], square(1))
    mid_one_ref[...] = mid_one
    normed_two = rms_scaled(mid_one, gain[1])
    normed_two_ref[...] = normed_two
    cross_query_ref[...] = matmul(normed_two, square(2)).astype(BF)
    kv_complete(cross_out_ref, cross_sem)
    exits.append(bring(cross_out_ref, cross_result, local_sem.at[7]))
    attend_cross(0, 3)
    pass_z(4)
    attend_cross(3, 6)
    complete(3)
    mid_two = mid_one_ref[...] + matmul(cross_attended_ref[...], square(3))


    normed_three = rms_scaled(mid_two, gain[2])
    upstream = upstream_ref[...]
    near_rows, far_rows = pl.ds(0, TOK), pl.ds(TOK, TOK)
    feed_left[near_rows, :D] = normed_three
    for piece in range(4):
        start = piece * 512
        gate = matmul(normed_three, targets[3][:, :, start : start + 512].reshape(D, 512))
        up = matmul(normed_three, targets[3][:, :, FF + start : FF + start + 512].reshape(D, 512))
        gate = gate.astype(BF).astype(F32)
        up = up.astype(BF).astype(F32)
        square_gate = gate * gate
        curve = jnp.tanh(ROOT * (gate + 0.044715 * gate * square_gate))
        raised = 0.5 * gate * (1.0 + curve)
        steep = 0.5 * (1.0 + curve) + 0.5 * gate * (1.0 - curve * curve) * (
            ROOT * (1.0 + 3.0 * 0.044715 * square_gate)
        )
        feed_left[near_rows, D + start : D + start + 512] = (raised * up).astype(BF)
        for side in range(2):
            cut = slice(side * 256, side * 256 + 256)
            score_ref[2 * piece + side] = (up * steep)[:, cut]
            score_ref[8 + 2 * piece + side] = raised[:, cut]
    complete(4)
    for piece in range(8):
        start = piece * 256
        d_hidden = contract(upstream, targets[4][piece], ((1,), (1,)))
        slope_ref[0, :, start : start + 256] = (d_hidden * score_ref[piece]).astype(BF)
        slope_ref[1, :, start : start + 256] = (d_hidden * score_ref[8 + piece]).astype(BF)
    half = D // 2
    near_half = pl.ds(pl.multiple_of(core * half, 128), half)
    far_half = pl.ds(pl.multiple_of((1 - core) * half, 128), half)
    swaps = []
    for index, (src, dst) in enumerate(
        (
            (feed_left.at[near_rows], feed_left.at[far_rows]),
            (slope_ref.at[1 - core], feed_right.at[far_rows, pl.ds(0, FF)]),
            (upstream_ref.at[:, far_half], feed_right.at[far_rows, pl.ds(FF, half)]),
        )
    ):
        copy = hop(src, dst, feed_sem.at[0, index], feed_sem.at[1, index], *sibling)
        copy.start()
        swaps.append(copy)
    feed_right[near_rows, :FF] = slope_ref[core]
    feed_right[near_rows, FF:] = upstream_ref[:, near_half]
    block_ref[...] = mid_two + matmul(feed_left[near_rows, D:], targets[4][...].reshape(FF, D))
    grad = contract(slope_ref[0], targets[3][:, :, :FF].reshape(D, FF), ((1,), (1,)))
    grad = grad + contract(slope_ref[1], targets[3][:, :, FF:].reshape(D, FF), ((1,), (1,)))
    inverse = lax.rsqrt(jnp.mean(mid_two * mid_two, axis=-1, keepdims=True) + 1e-06)
    gain_grad_ref[...] = jnp.sum(mid_two * inverse * grad, axis=0, keepdims=True)
    scaled = gain[2] * grad
    mixed = jnp.mean(mid_two * scaled, axis=-1, keepdims=True)
    d_mid_two = upstream.astype(F32) + (
        inverse * scaled - mid_two * (inverse * inverse * inverse * mixed)
    )
    d_mid_ref[...] = d_mid_two
    branch_ref[...] = d_mid_two.astype(BF)
    d_cross_ref[...] = contract(d_mid_two.astype(BF), square(3), ((1,), (1,))).astype(BF)
    for copy in swaps:
        copy.wait_recv()
    turned[...] = feed_left[:, :D].T.reshape(8, 96, 2 * TOK)
    turned_hidden[...] = feed_left[:, D:].T.reshape(8, FF // 8, 2 * TOK)
    for group in range(2):
        owners = pl.ds(4 * ((1 - low + group) % 2), 4)
        left = turned[owners].reshape(4 * 96, 2 * TOK)
        for piece in range(4):
            cut = slice(piece * 512, piece * 512 + 512)
            part = matmul(left, feed_right[:, cut]).astype(BF).reshape(4, 96, 512)
            if group:
                wide_mine[:, :, cut] = part
            else:
                wide_inner[:, :, cut] = part[:, :48]
                wide_outer[:, :, cut] = part[:, 48:]
        if group:
            exits.append(bring(wide_mine, wide_mine_out, local_sem.at[9]))
        else:
            exits.append(bring(wide_inner, wide_inner_out, local_sem.at[10]))
            exits.append(bring(wide_outer, wide_outer_out, local_sem.at[11]))
        left = turned_hidden[owners].reshape(4 * FF // 8, 2 * TOK)
        part = matmul(left, feed_right[:, FF:]).astype(BF).reshape(4, FF // 8, half)
        if group:
            tall_mine[...] = part
            exits.append(bring(tall_mine, tall_mine_out, local_sem.at[12]))
        else:
            tall_inner[...] = part[:, :128]
            tall_outer[...] = part[:, 128:]
            exits.append(bring(tall_inner, tall_inner_out, local_sem.at[13]))
            exits.append(bring(tall_outer, tall_outer_out, local_sem.at[14]))
    for copy in sends + swaps:
        copy.wait_send()
    for copy in exits:
        copy.wait()


def front(weights, others, collective_id):
    dma = pltpu.SemaphoreType.DMA
    packs = [
        (8, weights[group[0]].shape[0], sum(weights[k].shape[1] for k in group)) for group in PACKS
    ]
    anywhere = pl.BlockSpec(memory_space=pl.ANY)
    inside = pl.BlockSpec(memory_space=pltpu.VMEM)
    scalars = pl.BlockSpec(memory_space=pltpu.SMEM)
    return pl.pallas_call(
        front_kernel,
        out_shape=[jax.ShapeDtypeStruct(pack, BF) for pack in packs[:3]]
        + [
            jax.ShapeDtypeStruct((3, D), F32),
            jax.ShapeDtypeStruct((TOK, D), BF),
            jax.ShapeDtypeStruct((TOK, D), BF),
            jax.ShapeDtypeStruct((HEADS, 5, HALF, TOK), F32),
            jax.ShapeDtypeStruct((TOK, D), BF),
            jax.ShapeDtypeStruct((PAIRS, 8, 2 * TOK), F32),
            jax.ShapeDtypeStruct((TOK, D), F32),
            jax.ShapeDtypeStruct((TOK, D), BF),
            jax.ShapeDtypeStruct((TOK, D), BF),
            jax.ShapeDtypeStruct((TOK, D), BF),
            jax.ShapeDtypeStruct((PAIRS, 8, 2 * TOK), F32),
            jax.ShapeDtypeStruct((TOK, D), F32),
            jax.ShapeDtypeStruct((TOK, D), F32),
            jax.ShapeDtypeStruct((TOK, D), BF),
            jax.ShapeDtypeStruct((TOK, D), BF),
            jax.ShapeDtypeStruct((1, D), F32),
            jax.ShapeDtypeStruct((4, 96, FF), BF),
            jax.ShapeDtypeStruct((4, 48, FF), BF),
            jax.ShapeDtypeStruct((4, 48, FF), BF),
            jax.ShapeDtypeStruct((4, 256, D // 2), BF),
            jax.ShapeDtypeStruct((4, 128, D // 2), BF),
            jax.ShapeDtypeStruct((4, 128, D // 2), BF),
            jax.ShapeDtypeStruct((2, 32), jnp.int32),
            jax.ShapeDtypeStruct((2, 3), jnp.int32),
            jax.ShapeDtypeStruct((N_CTX, 2, TOK, D), BF),
            jax.ShapeDtypeStruct((N_CTX, 2, ENC, D), BF),
        ],
        in_specs=[anywhere] * 12 + [inside] * 4 + [scalars],
        out_specs=[anywhere] * 3
        + [inside] * 3
        + [anywhere]
        + [inside] * 12
        + [anywhere] * 6
        + [scalars] * 2
        + [anywhere] * 2,
        scratch_shapes=[pltpu.VMEM(pack, BF) for pack in packs]
        + [
            pltpu.VMEM((N_CTX, 2, TOK, D), BF),
            pltpu.VMEM((N_CTX, 2, ENC, D), BF),
            pltpu.VMEM((8, 16, 128), BF),
            pltpu.VMEM((2, TOK, D), BF),
            pltpu.VMEM((2, ENC, D), BF),
            pltpu.VMEM((N_CTX, TOK, 2 * TOK), F32),
            pltpu.VMEM((N_CTX, TOK, 2 * TOK), BF),
            pltpu.VMEM((2 * TOK, D + FF), BF),
            pltpu.VMEM((2 * TOK, FF + D // 2), BF),
            pltpu.VMEM((2, TOK, FF), BF),
            pltpu.VMEM((8, 96, 2 * TOK), BF),
            pltpu.VMEM((8, FF // 8, 2 * TOK), BF),
            pltpu.VMEM((HEADS, 5, HALF, TOK), F32),
            pltpu.VMEM((4, 96, FF), BF),
            pltpu.VMEM((4, 48, FF), BF),
            pltpu.VMEM((4, 48, FF), BF),
            pltpu.VMEM((4, 256, D // 2), BF),
            pltpu.VMEM((4, 128, D // 2), BF),
            pltpu.VMEM((4, 128, D // 2), BF),
            dma((5 * 22 + 7 + 2 * 18,)),
            dma((5, 3)),
            dma((5, 4, 2)),
            dma((5, 11)),
            dma((11,)),
            dma((7,)),
            dma((N_CTX, 2)),
            dma((N_CTX, 2)),
            dma((2, 3)),
            dma((15,)),
        ],
        compiler_params=pltpu.CompilerParams(
            collective_id=collective_id, has_side_effects=True, vmem_limit_bytes=60 * MIB
        ),
        name="front",
    )(*weights, *others)


PIECE = 96
WIDTHS = (D // 2, D // 2, D // 2, D // 2, D, D, FF)
SPAN = sum(WIDTHS)
DOWN = len(WIDTHS)
CHUNKS = DOWN + 1
CROSS_KV, SELF_KV, WIDE = 4, 5, 6
LEFT = (D,) * 4
RIGHT = (D // 2,) * 4


def finish_kernel(*refs):
    lefts = refs[:4]
    rights = refs[4:8]
    wide_refs, down_refs = refs[8:11], refs[11:14]
    dkv_ref, dckv_ref, square_ref = refs[14:17]
    kv_source, ckv_source, state_ref, dq_ref, dmid_ref, token_ref, gain_ref, small_ref = refs[17:25]
    early_out, late_out, small_out, decoder_ref, encoder_ref = refs[25:30]
    (
        left_all, right_all, turned, turned_one, turned_state, state_all, s_right, c_right,
        kept, from_z, from_x, via_x, d_z, d_x, d_via,
        s_kept, s_core, s_row, s_via, s_stage, s_high, s_fin,
        c_kept, c_core, c_row, c_via, c_stage, c_high, c_fin,
        small_f32, sm_own, sm_core, sm_z, sm_x, sm_ctx, sm_total,
        packed, from_ctx, land, late_packed, late_from, late_land,
        wide_add, down_add, query_ref, kv_ref, ckv_ref, bring_sem,
        s_sem, c_sem, fill_sem, act_send, act_recv, late_send, late_recv, z_send, z_recv,
        x_send, x_recv, ctx_send, ctx_recv, pass_send, pass_recv, sm_send, sm_recv, local_sem,
    ) = refs[30:]
    me, core, high, y, low, x = torus_place()
    shard = low * 4 + x
    rank = y * 2 + high
    sibling = (slot_of(y, 0, high, 1 - core), shard)
    inside = (me, (1 - low) * 4 + x)
    outside = (slot_of(y, 0, 1 - high, core), (1 - low) * 4 + x)
    across = (slot_of(y, 0, 1 - high, core), shard)
    others = [low * 4 + (x + shift) % 4 for shift in (1, 2, 3)]
    ahead = (slot_of(y, 1, high, core), shard)
    behind = (slot_of(y, 3, high, core), shard)
    shifts = [(dy, dz) for dy in range(4) for dz in range(2)][1:]
    mates = [((y + dy) % 4) * 2 + (high + dz) % 2 for dy, dz in shifts]
    greet_all(
        [sibling, inside, outside]
        + [(me, other) for other in others]
        + [(mate * 2 + core, shard) for mate in mates]
    )
    sends = []

    def go(src, dst, send_sem, recv_sem, device):
        copy = hop(src, dst, send_sem, recv_sem, *device)
        copy.start()
        sends.append(copy)
        return copy

    def bring(src, dst, sem):
        copy = pltpu.make_async_copy(src, dst, sem)
        copy.start()
        return copy


    def rows_start(source, held, arrived, sem):
        over = []
        local = []
        for spot, shift in enumerate((2, 1, 3, 0)):
            pair = pl.ds(((y + shift) % 4) * 2, 2)
            block = pl.ds(2 * spot, 2)
            over.append(
                go(
                    source.at[pair, 1 - core], arrived.at[block],
                    sem.at[0, spot], sem.at[1, spot], sibling,
                )
            )
            local.append(bring(source.at[pair, core], held.at[block], sem.at[4, spot]))
        return over, local


    def rows_send(copies, held, arrived, via, row, sem):
        over, local = copies
        onward = []
        for spot in range(4):
            local[spot].wait()
            over[spot].wait_recv()
            for block in (2 * spot, 2 * spot + 1):
                for part in range(2):
                    held[block, part] = held[block, part] + arrived[block, part]
            if spot == 0:
                first = go(held.at[0], via.at[0], sem.at[2, 0], sem.at[3, 0], ahead)
                second = go(held.at[1], via.at[1], sem.at[2, 1], sem.at[3, 1], behind)
            elif spot == 1:
                onward.append(go(held.at[3], row.at[0, 1], sem.at[2, 2], sem.at[3, 2], ahead))
            elif spot == 2:
                onward.append(go(held.at[4], row.at[1, 0], sem.at[2, 3], sem.at[3, 3], behind))
        return first, second, onward

    def rows_via(state, held, via, row, sem):
        first, second, onward = state
        first.wait_recv()
        for part in range(2):
            held[2, part] = held[2, part] + via[0, part]
        onward.append(go(held.at[2], row.at[0, 0], sem.at[2, 4], sem.at[3, 4], ahead))
        second.wait_recv()
        for part in range(2):
            held[5, part] = held[5, part] + via[1, part]
        onward.append(go(held.at[5], row.at[1, 1], sem.at[2, 5], sem.at[3, 5], behind))
        return onward

    def rows_total(held, row, half, part):
        return (
            held[6 + half, part].astype(F32)
            + row[0, half, part].astype(F32)
            + row[1, half, part].astype(F32)
        )

    def rows_across(onward, held, row, stage, landing, sem):
        for copy in onward:
            copy.wait_recv()
        for part in range(2):
            stage[part] = rows_total(held, row, 1 - high, part).astype(BF)
        return go(stage, landing, sem.at[2, 6], sem.at[3, 6], across)

    def rows_sum(last, held, row, landing, final, right, which):
        totals = [rows_total(held, row, high, part) for part in range(2)]
        last.wait_recv()
        for part in range(2):
            final[part] = (totals[part] + landing[part].astype(F32)).astype(BF)
        count = final.shape[1]
        copy = go(
            final.at[1 - core], right.at[pl.ds(count, count)],
            late_send.at[which], late_recv.at[which], sibling,
        )
        right[:count] = final[core]
        return copy


    starts = [sum(WIDTHS[:k]) for k in range(len(WIDTHS))]
    left_starts = [sum(LEFT[:k]) for k in range(4)]
    right_starts = [sum(RIGHT[:k]) for k in range(4)]
    acts = {}
    over_z, over_via, over_x = {}, {}, {}
    column_ahead = (me, low * 4 + (x + 1) % 4)
    column_behind = (me, low * 4 + (x + 3) % 4)

    def buffers(k):
        if k == DOWN:
            return d_z, d_x, d_via, pl.ds(0, D // 2)
        return from_z, from_x, via_x, pl.ds(starts[k], WIDTHS[k])

    def acts_start(index):
        left = pl.ds(left_starts[index], LEFT[index])
        right = pl.ds(right_starts[index], RIGHT[index])
        near = pl.ds(pl.multiple_of(core * RIGHT[index], 128), RIGHT[index])
        far = pl.ds(pl.multiple_of((1 - core) * RIGHT[index], 128), RIGHT[index])
        mine = pl.ds(0, TOK)
        theirs = pl.ds(TOK, TOK)
        acts[index] = (
            bring(lefts[index], left_all.at[mine, left], fill_sem.at[index, 0]),
            bring(rights[index].at[:, near], right_all.at[mine, right], fill_sem.at[index, 1]),
            go(
                lefts[index], left_all.at[theirs, left],
                act_send.at[index, 0], act_recv.at[index, 0], sibling,
            ),
            go(
                rights[index].at[:, far], right_all.at[theirs, right],
                act_send.at[index, 1], act_recv.at[index, 1], sibling,
            ),
        )

    def multiply(k, left_ref, right):
        landing, _, _, cut = buffers(k)
        for group in range(2):
            owners = pl.ds(4 * ((1 - low + group) % 2), 4)
            left = left_ref[owners].reshape(4 * PIECE, right.shape[0])
            kept[owners, :, cut] = (
                contract(left, right, ((1,), (0,))).astype(BF).reshape(4, PIECE, WIDTHS[k])
            )
            if group == 0:
                half = PIECE // 2
                over_z[k] = [
                    go(
                        kept.at[owners, pl.ds(side * half, half), cut],
                        landing.at[:, pl.ds(side * half, half), cut],
                        z_send.at[k, side],
                        z_recv.at[k, side],
                        device,
                    )
                    for side, device in enumerate((inside, outside))
                ]

    def make(index):
        near_left, near_right, far_left, far_right = acts[index]
        near_left.wait()
        near_right.wait()
        far_left.wait_recv()
        far_right.wait_recv()
        left = left_all[:, left_starts[index] : left_starts[index] + LEFT[index]].T
        right = right_all[:, right_starts[index] : right_starts[index] + RIGHT[index]]
        target = turned_one if index == 3 else turned
        target[...] = left.reshape(8, PIECE, 2 * TOK)
        multiply(index, target, right)

    def step_z(k):
        landing, _, _, cut = buffers(k)
        for copy in over_z[k]:
            copy.wait_recv()
        for column in range(4):
            landing[column, :, cut] = landing[column, :, cut] + kept[4 * low + column, :, cut]
        send_x(k)


    def send_x(k):
        landing, spread, via, cut = buffers(k)
        half = landing.shape[1] // 2
        upper, lower = pl.ds(0, half), pl.ds(half, half)
        away, front_column, back_column = (x + 2) % 4, (x + 1) % 4, (x + 3) % 4
        over_via[k] = (
            go(
                landing.at[away, upper, cut], via.at[0, :, cut],
                x_send.at[k, 0], x_recv.at[k, 0], column_ahead,
            ),
            go(
                landing.at[away, lower, cut], via.at[1, :, cut],
                x_send.at[k, 1], x_recv.at[k, 1], column_behind,
            ),
        )
        over_x[k] = [
            go(
                landing.at[front_column, lower, cut], spread.at[0, lower, cut],
                x_send.at[k, 2], x_recv.at[k, 2], column_ahead,
            ),
            go(
                landing.at[back_column, upper, cut], spread.at[1, upper, cut],
                x_send.at[k, 3], x_recv.at[k, 3], column_behind,
            ),
        ]

    def step_via(k):
        landing, spread, via, cut = buffers(k)
        half = landing.shape[1] // 2
        upper, lower = pl.ds(0, half), pl.ds(half, half)
        front_column, back_column = (x + 1) % 4, (x + 3) % 4
        over_via[k][0].wait_recv()
        landing[front_column, upper, cut] = landing[front_column, upper, cut] + via[0, :, cut]
        over_x[k].append(
            go(
                landing.at[front_column, upper, cut], spread.at[0, upper, cut],
                x_send.at[k, 4], x_recv.at[k, 4], column_ahead,
            )
        )
        over_via[k][1].wait_recv()
        landing[back_column, lower, cut] = landing[back_column, lower, cut] + via[1, :, cut]
        over_x[k].append(
            go(
                landing.at[back_column, lower, cut], spread.at[1, lower, cut],
                x_send.at[k, 5], x_recv.at[k, 5], column_behind,
            )
        )

    def step_x(k):
        landing, spread, _, cut = buffers(k)
        for copy in over_x[k]:
            copy.wait_recv()
        total = landing[x, :, cut].astype(F32)
        for spot in range(2):
            total = total + spread[spot, :, cut].astype(F32)
        total = total.astype(BF)
        half = D // 2
        if k == WIDE:
            for piece in range(8):
                packed[piece, :PIECE, :256] = total[:, piece * 256 : piece * 256 + 256]
        elif k == DOWN:
            for piece in range(8):
                for part in range(3):
                    packed[piece, part * 32 : part * 32 + 32, 256:] = total[
                        piece * 32 : piece * 32 + 32, part * 128 : part * 128 + 128
                    ]
        else:
            middle = PIECE // 2
            for upper in range(2):
                rows = total[upper * middle : upper * middle + middle, :]
                if k == CROSS_KV or k == SELF_KV:
                    for piece in range(2):
                        late_packed[(0 if k == CROSS_KV else 4) + 2 * piece + upper] = rows[
                            :, piece * half : piece * half + half
                        ]
                else:
                    packed[2 * k + upper, PIECE:, :] = rows


    def mate_device(mate):
        return (mate * 2 + core, shard)

    def ctx_start(which, source, landing):
        return [
            go(
                source.at[mate], landing.at[spot],
                ctx_send.at[which, spot], ctx_recv.at[which, spot], mate_device(mate),
            )
            for spot, mate in enumerate(mates)
        ]

    def ctx_sum(which, over, source, landing, final):
        total = source[rank].astype(F32)
        for spot in range(7):
            over[spot].wait_recv()
            total = total + landing[spot].astype(F32)
        final[rank, core] = total.astype(BF)
        own = final.at[rank, core]
        for spot, mate in enumerate(mates):
            go(own, own, ctx_send.at[which, 7 + spot], ctx_recv.at[which, 7 + rank], mate_device(mate))
        go(own, own, pass_send.at[which, 7], pass_recv.at[which, rank], sibling)

    def landed(ref, recv_sem):
        hop(ref, ref, pass_send.at[0, 0], recv_sem, *sibling).wait_recv()

    def ctx_pass(which, final):
        for spot, mate in enumerate(mates):
            block = final.at[mate, core]
            landed(block, ctx_recv.at[which, 7 + mate])
            go(block, block, pass_send.at[which, spot], pass_recv.at[which, mate], sibling)

    def ctx_done(which, final):
        for mate in [rank] + mates:
            landed(final.at[mate, 1 - core], pass_recv.at[which, mate])

    wide_cut = pl.ds(starts[WIDE], FF)
    down_copies = [bring(down_refs[0], d_z, bring_sem.at[0])] + [
        bring(down_refs[1 + side], down_add.at[side], bring_sem.at[1 + side]) for side in range(2)
    ]
    wide_copies = [bring(wide_refs[0], from_z.at[:, :, wide_cut], bring_sem.at[3])] + [
        bring(wide_refs[1 + side], wide_add.at[side], bring_sem.at[4 + side]) for side in range(2)
    ]
    s_copies = rows_start(dkv_ref, s_kept, s_core, s_sem)
    c_copies = rows_start(dckv_ref, c_kept, c_core, c_sem)
    for index in range(4):
        acts_start(index)
    state_near = bring(state_ref, state_all.at[pl.ds(0, ENC)], local_sem.at[0])
    state_far = go(
        state_ref, state_all.at[pl.ds(ENC, ENC)], late_send.at[2], late_recv.at[2], sibling
    )
    kv_copy = bring(kv_source, kv_ref, bring_sem.at[7])
    ckv_copy = bring(ckv_source, ckv_ref, bring_sem.at[8])
    query_copy = bring(square_ref.at[:, :, pl.ds(0, D)], query_ref, bring_sem.at[6])
    for copy in down_copies:
        copy.wait()
    for side in range(2):
        for column in range(4):
            rows = slice(side * 128, side * 128 + 128)
            d_z[column, rows, :] = d_z[column, rows, :] + down_add[side, column]
    send_x(DOWN)
    for copy in wide_copies:
        copy.wait()
    for side in range(2):
        for column in range(4):
            rows = slice(side * 48, side * 48 + 48)
            from_z[column, rows, wide_cut] = from_z[column, rows, wide_cut] + wide_add[side, column]
    send_x(WIDE)
    s_state = rows_send(s_copies, s_kept, s_core, s_via, s_row, s_sem)
    make(0)
    make(1)
    s_onward = rows_via(s_state, s_kept, s_via, s_row, s_sem)
    c_state = rows_send(c_copies, c_kept, c_core, c_via, c_row, c_sem)
    make(2)
    make(3)
    step_via(DOWN)
    step_via(WIDE)
    for k in range(4):
        step_z(k)
    state_near.wait()
    state_far.wait_recv()
    turned_state[...] = state_all[...].T.reshape(8, PIECE, 2 * ENC)
    s_last = rows_across(s_onward, s_kept, s_row, s_stage, s_high, s_sem)
    c_onward = rows_via(c_state, c_kept, c_via, c_row, c_sem)
    for k in range(4):
        step_via(k)
    step_x(DOWN)
    step_x(WIDE)
    s_far = rows_sum(s_last, s_kept, s_row, s_high, s_fin, s_right, 0)
    for k in range(4):
        step_x(k)
    early = ctx_start(0, packed, from_ctx)
    s_far.wait_recv()
    multiply(SELF_KV, turned_one, s_right[...])
    c_last = rows_across(c_onward, c_kept, c_row, c_stage, c_high, c_sem)
    tokens = token_ref[...].astype(F32)
    d_kv = jnp.concatenate([s_fin[0], s_fin[1]], axis=1)
    query_copy.wait()
    kv_copy.wait()
    grad = contract(dq_ref[...], query_ref[...].reshape(D, D), ((1,), (1,)))
    grad = grad + contract(d_kv, kv_ref[...], ((1,), (1,)))
    inverse = lax.rsqrt(jnp.mean(tokens * tokens, axis=-1, keepdims=True) + 1e-06)
    small_f32[...] = small_ref[...]
    line = jnp.sum(tokens * inverse * grad, axis=0, keepdims=True)
    for owner in range(8):
        small_f32[owner, 0:1, :96] = line[:, owner * 96 : owner * 96 + 96]
    sm_own[...] = small_f32[...].astype(BF)
    sm_over = go(sm_own, sm_core, sm_send.at[0], sm_recv.at[0], sibling)
    c_far = rows_sum(c_last, c_kept, c_row, c_high, c_fin, c_right, 1)
    c_far.wait_recv()
    multiply(CROSS_KV, turned_state, c_right[...])
    step_z(SELF_KV)
    sm_over.wait_recv()
    sm_own_sum = (sm_own[...].astype(F32) + sm_core[...].astype(F32)).astype(BF)
    sm_over.wait_send()
    sm_own[...] = sm_own_sum
    sm_inside = go(
        sm_own.at[pl.ds(4 * (1 - low), 4)], sm_z, sm_send.at[1], sm_recv.at[1], inside
    )
    ctx_sum(0, early, packed, from_ctx, land)
    step_z(CROSS_KV)
    step_via(SELF_KV)
    sm_inside.wait_recv()
    for column in range(4):
        sm_z[column] = sm_z[column] + sm_own[4 * low + column]
    sm_row = [
        go(
            sm_z.at[(x + spot + 1) % 4], sm_x.at[spot],
            sm_send.at[2 + spot], sm_recv.at[2 + spot], (me, others[spot]),
        )
        for spot in range(3)
    ]
    step_via(CROSS_KV)
    scaled = gain_ref[...] * grad
    mixed = jnp.mean(tokens * scaled, axis=-1, keepdims=True)
    decoder_ref[...] = (
        dmid_ref[...] + inverse * scaled - tokens * (inverse * inverse * inverse * mixed)
    )
    step_x(SELF_KV)
    step_x(CROSS_KV)
    late = ctx_start(1, late_packed, late_from)
    sm_sum = sm_z[x].astype(F32)
    for spot in range(3):
        sm_row[spot].wait_recv()
        sm_sum = sm_sum + sm_x[spot].astype(F32)
    sm_total[...] = sm_sum.astype(BF)
    sm_mates = [
        go(sm_total, sm_ctx.at[spot], sm_send.at[5 + spot], sm_recv.at[5 + spot], mate_device(mate))
        for spot, mate in enumerate(mates)
    ]
    ctx_pass(0, land)
    ctx_sum(1, late, late_packed, late_from, late_land)
    d_ckv = jnp.concatenate([c_fin[0], c_fin[1]], axis=1)
    ckv_copy.wait()
    encoder_ref[...] = contract(d_ckv, ckv_ref[...], ((1,), (1,)))
    sm_sum = sm_total[...].astype(F32)
    for spot in range(7):
        sm_mates[spot].wait_recv()
        sm_sum = sm_sum + sm_ctx[spot].astype(F32)
    small_out[...] = sm_sum
    ctx_done(0, land)
    early_exit = bring(land, early_out, bring_sem.at[9])
    ctx_pass(1, late_land)
    ctx_done(1, late_land)
    late_exit = bring(late_land, late_out, bring_sem.at[10])
    early_exit.wait()
    late_exit.wait()
    for copy in sends:
        if copy is not sm_over:
            copy.wait_send()


def unpack_kernel(early, late, *refs):
    for source, target in zip(refs[:3], refs[14:]):
        target[...] = source[...]
    square_refs = refs[3:11]
    gate_ref, up_ref, down_ref = refs[11:14]
    half = D // 2
    middle = PIECE // 2
    for side in range(2):
        columns = slice(side * half, side * half + half)
        for upper in range(2):
            rows = slice(upper * middle, upper * middle + middle)
            for k in range(4):
                square_refs[k][rows, columns] = early[2 * k + upper, side, PIECE:, :].astype(F32)
            for k in range(2):
                for piece in range(2):
                    square_refs[4 + 2 * k + side][rows, piece * half : piece * half + half] = late[
                        4 * k + 2 * piece + upper, side
                    ].astype(F32)
        target = up_ref if side else gate_ref
        for piece in range(8):
            target[:, piece * 256 : piece * 256 + 256] = early[piece, side, :PIECE, :256].astype(F32)
            for part in range(3):
                down_ref[
                    piece * 32 : piece * 32 + 32,
                    side * half + part * 128 : side * half + part * 128 + 128,
                ] = early[piece, side, part * 32 : part * 32 + 32, 256:].astype(F32)


def unpack(early, late, *whole):
    outs = (
        [jax.ShapeDtypeStruct((PIECE, D), F32)] * 8
        + [jax.ShapeDtypeStruct((PIECE, FF), F32)] * 2
        + [jax.ShapeDtypeStruct((FF // 8, D), F32)]
        + [jax.ShapeDtypeStruct(part.shape, F32) for part in whole]
    )
    return pl.pallas_call(
        unpack_kernel,
        out_shape=outs,
        in_specs=[pl.BlockSpec(memory_space=pltpu.VMEM)] * (2 + len(whole)),
        out_specs=[pl.BlockSpec(memory_space=pltpu.VMEM)] * len(outs),
        compiler_params=pltpu.CompilerParams(vmem_limit_bytes=24 * MIB),
        name="unpack",
    )(early, late, *whole)


def finish(far, near, collective_id):
    dma = pltpu.SemaphoreType.DMA

    def rows(count):
        return [
            pltpu.VMEM((8, 2, count, D), BF),
            pltpu.VMEM((8, 2, count, D), BF),
            pltpu.VMEM((2, 2, 2, count, D), BF),
            pltpu.VMEM((2, 2, count, D), BF),
            pltpu.VMEM((2, count, D), BF),
            pltpu.VMEM((2, count, D), BF),
            pltpu.VMEM((2, count, D), BF),
        ]

    outs = [
        jax.ShapeDtypeStruct((8, 2, 3 * PIECE // 2, D // 2), BF),
        jax.ShapeDtypeStruct((8, 2, PIECE // 2, D // 2), BF),
        jax.ShapeDtypeStruct((16, 128), F32),
        jax.ShapeDtypeStruct((TOK, D), F32),
        jax.ShapeDtypeStruct((ENC, D), F32),
    ]
    return pl.pallas_call(
        finish_kernel,
        out_shape=outs,
        in_specs=[pl.BlockSpec(memory_space=pl.ANY)] * len(far)
        + [pl.BlockSpec(memory_space=pltpu.VMEM)] * len(near),
        out_specs=[pl.BlockSpec(memory_space=pl.ANY)] * 2
        + [pl.BlockSpec(memory_space=pltpu.VMEM)] * 3,
        scratch_shapes=[
            pltpu.VMEM((2 * TOK, sum(LEFT)), BF),
            pltpu.VMEM((2 * TOK, sum(RIGHT)), BF),
            pltpu.VMEM((8, PIECE, 2 * TOK), BF),
            pltpu.VMEM((8, PIECE, 2 * TOK), BF),
            pltpu.VMEM((8, PIECE, 2 * ENC), BF),
            pltpu.VMEM((2 * ENC, D), BF),
            pltpu.VMEM((2 * TOK, D), BF),
            pltpu.VMEM((2 * ENC, D), BF),
            pltpu.VMEM((8, PIECE, SPAN - FF), BF),
            pltpu.VMEM((4, PIECE, SPAN), BF),
            pltpu.VMEM((2, PIECE, SPAN), BF),
            pltpu.VMEM((2, PIECE // 2, SPAN), BF),
            pltpu.VMEM((4, FF // 8, D // 2), BF),
            pltpu.VMEM((2, FF // 8, D // 2), BF),
            pltpu.VMEM((2, FF // 16, D // 2), BF),
        ]
        + rows(TOK)
        + rows(ENC)
        + [
            pltpu.VMEM((8, 16, 128), F32),
            pltpu.VMEM((8, 16, 128), BF),
            pltpu.VMEM((8, 16, 128), BF),
            pltpu.VMEM((4, 16, 128), BF),
            pltpu.VMEM((3, 16, 128), BF),
            pltpu.VMEM((7, 16, 128), BF),
            pltpu.VMEM((16, 128), BF),
            pltpu.VMEM((8, 3 * PIECE // 2, D // 2), BF),
            pltpu.VMEM((7, 3 * PIECE // 2, D // 2), BF),
            pltpu.VMEM((8, 2, 3 * PIECE // 2, D // 2), BF),
            pltpu.VMEM((8, PIECE // 2, D // 2), BF),
            pltpu.VMEM((7, PIECE // 2, D // 2), BF),
            pltpu.VMEM((8, 2, PIECE // 2, D // 2), BF),
            pltpu.VMEM((2, 4, PIECE // 2, FF), BF),
            pltpu.VMEM((2, 4, FF // 16, D // 2), BF),
            pltpu.VMEM((8, PIECE, D), BF),
            pltpu.VMEM((D, 2 * D), BF),
            pltpu.VMEM((D, 2 * D), BF),
            dma((11,)),
            dma((5, 7)),
            dma((5, 7)),
            dma((4, 2)),
            dma((4, 2)),
            dma((4, 2)),
            dma((3,)),
            dma((3,)),
            dma((CHUNKS, 2)),
            dma((CHUNKS, 2)),
            dma((CHUNKS, 6)),
            dma((CHUNKS, 6)),
            dma((2, 14)),
            dma((2, 15)),
            dma((2, 8)),
            dma((2, 8)),
            dma((12,)),
            dma((12,)),
            dma((3,)),
        ],
        compiler_params=pltpu.CompilerParams(
            collective_id=collective_id, has_side_effects=True, vmem_limit_bytes=62 * MIB
        ),
        name="finish_gradients",
    )(*far, *near)


def backward_kernel(biased, *refs):
    if biased:
        class_ref, near_ref, q_ref, k_ref, v_ref, g_ref, total_ref, tile_ref = refs[:8]
        dq_ref, dkv_ref, strip_ref, share_ref, slope_ref, share_low, slope_low = refs[8:]
    else:
        q_ref, k_ref, v_ref, g_ref, total_ref = refs[:5]
        dq_ref, dkv_ref, share_ref, slope_ref, share_low, slope_low = refs[5:]
    chunks = share_ref.shape[0]
    queries = split_heads(q_ref[...])
    grads = split_heads(g_ref[...])
    totals = total_ref[0, 0:1]
    inner = jnp.zeros((8, 2 * TOK), F32)
    for j in range(chunks):
        scores = contract(key_chunk(k_ref, j), queries, ((1,), (1,)))
        if biased:
            scores = scores + bias_chunk(class_ref, tile_ref, j)
        shares = jnp.exp(scores - totals)
        slopes = contract(key_chunk(v_ref, j), grads, ((1,), (1,)))
        inner = inner + fold(shares * slopes, jnp.sum)
        share_ref[j] = shares
        slope_ref[j] = slopes
        share_low[j] = shares.astype(BF)
    inner = jnp.sum(inner, axis=0, keepdims=True)
    for j in range(chunks):
        grad = share_ref[j] * (slope_ref[j] - inner)
        if biased:
            slope_ref[j] = grad
        slope_low[j] = grad.astype(BF)
    keys = jnp.concatenate([key_chunk(k_ref, j) for j in range(chunks)], axis=0)
    low = slope_low[...].reshape(-1, 2 * TOK)
    dq_ref[...] = join_heads(contract(keys, low, ((0,), (0,)))).astype(BF)
    shape = dkv_ref.shape
    block = (shape[0], shape[2], shape[3])
    dkv_ref[:, 0] = contract(low, queries, ((1,), (0,))).astype(BF).reshape(block)
    dkv_ref[:, 1] = (
        contract(share_low[...].reshape(-1, 2 * TOK), grads, ((1,), (0,))).astype(BF).reshape(block)
    )
    if biased:
        lane = lax.broadcasted_iota(jnp.int32, (HALF, TOK), 1)
        for gap in range(3):
            pieces = []
            for half in range(2):
                spot = near_ref[half, gap]
                held = slope_ref[jnp.maximum(spot, 0) // 2, pl.ds(
                    pl.multiple_of((jnp.maximum(spot, 0) % 2) * HALF, HALF), HALF)]
                pieces.append(jnp.where(spot >= 0, held, jnp.zeros_like(held)))
            for head in range(2):
                cut = slice(head * TOK, (head + 1) * TOK)
                strip_ref[head, gap] = jnp.where(lane < HALF, pieces[0][:, cut], pieces[1][:, cut])


def pair_columns(pair):
    return (0, pair)


def kv_spec(rows, row_block, part):
    return pl.BlockSpec(
        (N_CTX, 1, rows, 2 * HEAD_DIM), lambda pair: (0, part, row_block, pair)
    )


SMEM_SPEC = pl.BlockSpec(memory_space=pltpu.SMEM)
TILE_SPEC = pl.BlockSpec((2, 5, HALF, TOK), lambda pair: (pair, 0, 0, 0))
TOTAL_SPEC = pl.BlockSpec((1, 8, 2 * TOK), lambda pair: (pair, 0, 0))
ROW_SPEC = pl.BlockSpec((TOK, 2 * HEAD_DIM), pair_columns)
LOCAL = pltpu.CompilerParams(vmem_limit_bytes=48 * MIB)


def attend_back(queries, gathered, grads, totals, rows, row_block, classes=None, near=None, tiles=None):
    biased = classes is not None
    chunks = N_CTX * rows // TOK
    specs = [ROW_SPEC, kv_spec(rows, row_block, 0), kv_spec(rows, row_block, 1), ROW_SPEC, TOTAL_SPEC]
    operands = [queries, gathered, gathered, grads, totals]
    out_specs = [
        ROW_SPEC,
        pl.BlockSpec((N_CTX, 2, rows, 2 * HEAD_DIM), lambda pair: (0, 0, 0, pair)),
    ]
    out_shape = [
        jax.ShapeDtypeStruct((TOK, D), BF),
        jax.ShapeDtypeStruct((N_CTX, 2, rows, D), BF),
    ]
    if biased:
        specs = [SMEM_SPEC, SMEM_SPEC] + specs + [TILE_SPEC]
        operands = [classes, near] + operands + [tiles]
        out_specs.append(pl.BlockSpec((2, 3, HALF, TOK), lambda pair: (pair, 0, 0, 0)))
        out_shape.append(jax.ShapeDtypeStruct((HEADS, 3, HALF, TOK), F32))
    return pl.pallas_call(
        functools.partial(backward_kernel, biased),
        grid=(PAIRS,),
        in_specs=specs,
        out_specs=out_specs,
        out_shape=out_shape,
        scratch_shapes=[
            pltpu.VMEM((chunks, TOK, 2 * TOK), F32),
            pltpu.VMEM((chunks, TOK, 2 * TOK), F32),
            pltpu.VMEM((chunks, TOK, 2 * TOK), BF),
            pltpu.VMEM((chunks, TOK, 2 * TOK), BF),
        ],
        compiler_params=LOCAL,
        cost_estimate=pl.CostEstimate(flops=1000, bytes_accessed=1000, transcendentals=0),
        name="attend_self_back" if biased else "attend_cross_back",
    )(*operands)


def matmul(left, right):
    return jnp.dot(left, right, preferred_element_type=F32)


def transposed_left(left, right):
    return contract(left, right, ((0,), (0,)))


def transposed_right(left, right):
    return contract(left, right, ((1,), (1,)))


def rms_scaled(values, gain):
    inverse = lax.rsqrt(jnp.mean(values * values, axis=-1, keepdims=True) + 1e-06)
    return (values * inverse * gain).astype(BF)


def rms_back(values, gain, grad):
    inverse = lax.rsqrt(jnp.mean(values * values, axis=-1, keepdims=True) + 1e-06)
    scaled = gain * grad
    mixed = jnp.mean(values * scaled, axis=-1, keepdims=True)
    grad_values = inverse * scaled - values * (inverse * inverse * inverse * mixed)
    return grad_values, jnp.sum(values * inverse * grad, axis=0)


def near_hot():
    shape = (REACH, 3 * HALF * HALF)
    spot = lax.broadcasted_iota(jnp.int32, shape, 1)
    gap = spot // (HALF * HALF)
    key = (spot // HALF) % HALF
    row = spot % HALF
    distance = jnp.clip(HALF * gap + row - key, 0, REACH - 1)
    return (distance == lax.broadcasted_iota(jnp.int32, shape, 0)).astype(BF)


def bias_sums(strips):
    tiles = (strips[..., :HALF] + strips[..., HALF:]).reshape(HEADS, -1)
    high = tiles.astype(BF)
    low = (tiles - high.astype(F32)).astype(BF)
    hot = near_hot()
    sums = transposed_right(high, hot) + transposed_right(low, hot)
    far = -jnp.sum(sums[:, :-1], axis=1, keepdims=True)
    return jnp.concatenate([sums[:, :-1], far], axis=1)


def swap(values, move):
    perm = []
    for ctx in range(N_CTX):
        for shard in range(8):
            there, owner = move(ctx, shard)
            perm.append((ctx * 8 + shard, there * 8 + owner))
    return lax.ppermute(values, ("ctx", "fsdp"), perm)


def over_z(mine, upper, lower):
    inner = swap(upper, lambda ctx, shard: (ctx, (shard + 4) % 8))
    outer = swap(lower, lambda ctx, shard: (ctx ^ 2, (shard + 4) % 8))
    return mine, inner, outer


def body(
    decoder_in,
    encoder_states,
    out_grad,
    block_pairs,
    bucket_table,
    gain_self,
    self_query,
    self_key,
    self_value,
    self_out,
    position_bias,
    gain_cross,
    cross_query,
    cross_key,
    cross_value,
    cross_out,
    gain_feed,
    feed_gate,
    feed_up,
    feed_down,
):
    me = lax.axis_index("ctx")
    rows = self_query.shape[0]
    small = jnp.concatenate(
        [
            jnp.pad(jnp.stack([gain_self, gain_cross, gain_feed]), ((0, 0), (0, 128 - rows))),
            jnp.pad(position_bias, ((0, 9), (0, 128 - HEADS))),
        ],
        axis=0,
    )
    (
        kv_one, kv_two, square, gains, normed_one, queries, tiles, attended, self_totals, mid_one,
        normed_two, cross_queries, cross_attended, cross_totals, block_out, d_mid_two,
        cross_branch, d_cross_attended, grad_norm_three, *feed_parts, classes, near, self_kv,
        cross_kv,
    ) = front(
        [
            self_key, self_value, cross_key, cross_value,
            self_query, self_out, cross_query, cross_out,
            feed_gate, feed_up, feed_down,
        ],
        [
            small, decoder_in[0], encoder_states[0], out_grad[0], bucket_table[None, :], block_pairs,
        ],
        0,
    )
    kv_one = kv_one.reshape(D, 2 * D)
    kv_two = kv_two.reshape(D, 2 * D)
    out_one, query_two = (square.reshape(D, 4 * D)[:, k * D : k * D + D] for k in (1, 2))
    norm_one, norm_two = gains[0:1], gains[1:2]
    bucket_hot = (bucket_table[:, None] == jnp.arange(32, dtype=jnp.int32)[None, :]).astype(BF)
    tokens = decoder_in[0].astype(F32)
    states = encoder_states[0]
    upstream = out_grad[0]
    feed_parts = [over_z(*feed_parts[:3]), over_z(*feed_parts[3:])]
    d_cross_queries, d_cross_kv_all = attend_back(
        cross_queries, cross_kv, d_cross_attended, cross_totals, ENC, 0
    )
    d_normed_two = transposed_right(d_cross_queries, query_two)
    part_two, grad_norm_two = rms_back(mid_one, norm_two, d_normed_two)
    d_mid_one = d_mid_two + part_two
    self_branch = d_mid_one.astype(BF)
    d_attended = transposed_right(self_branch, out_one).astype(BF)
    feed_parts[1], d_attended = lax.optimization_barrier((feed_parts[1], d_attended))
    d_queries, d_kv_all, strips = attend_back(
        queries, self_kv, d_attended, self_totals, TOK, 0, classes, near, tiles
    )
    feed_parts, d_queries, d_kv_all, strips = lax.optimization_barrier(
        (feed_parts, d_queries, d_kv_all, strips)
    )
    grad_table = matmul(bias_sums(strips), bucket_hot.astype(F32)).T.reshape(8, 4, HEADS)
    grad_gains = jnp.stack([grad_norm_two, grad_norm_three[0]]).reshape(2, 8, rows)
    grad_small = jnp.concatenate(
        [
            jnp.zeros((8, 1, 128), F32),
            jnp.pad(jnp.transpose(grad_gains, (1, 0, 2)), ((0, 0), (0, 0), (0, 128 - rows))),
            jnp.pad(grad_table, ((0, 0), (0, 9), (0, 128 - HEADS))),
        ],
        axis=1,
    )
    done = finish(
        [
            cross_attended, normed_two, attended, normed_one,
            cross_branch, d_cross_queries, self_branch, d_queries,
            *feed_parts[0],
            *feed_parts[1],
            d_kv_all.reshape(8, 2, 2, TOK, D),
            d_cross_kv_all.reshape(8, 2, 2, ENC, D),
            square,
            kv_one,
            kv_two,
        ],
        [
            states,
            d_queries,
            d_mid_one,
            decoder_in[0],
            norm_one,
            grad_small,
        ],
        3,
    )
    early, late, extras, grad_decoder, grad_encoder = done
    (
        grad_out_two, grad_query_two, grad_out_one, grad_query_one,
        grad_key_two, grad_value_two, grad_key_one, grad_value_one,
        grad_gate, grad_up, grad_down, block_out, grad_decoder, grad_encoder,
    ) = unpack(early, late, block_out, grad_decoder, grad_encoder)
    return (
        block_out[None],
        grad_decoder[None],
        grad_encoder[None],
        extras[0, :rows],
        grad_query_one,
        grad_key_one,
        grad_value_one,
        grad_out_one,
        extras[3:7, :HEADS],
        extras[1, :rows],
        grad_query_two,
        grad_key_two,
        grad_value_two,
        grad_out_two,
        extras[2, :rows],
        grad_gate,
        grad_up,
        grad_down,
    )


def solution(mesh):
    tokens = P("fsdp", "ctx", None)
    matrix = P("fsdp", None)
    vector = P("fsdp")
    weights = (
        (vector,) + (matrix,) * 5 + (vector,) + (matrix,) * 4 + (vector,) + (matrix,) * 3
    )
    return jax.shard_map(
        body,
        mesh=mesh,
        in_specs=(tokens,) * 3 + (P(), P()) + weights,
        out_specs=(tokens,) * 3 + weights,
        check_vma=False,
    )
```

```python
import functools

import jax
import jax.numpy as jnp
from jax import lax
from jax.experimental import pallas as pl
from jax.experimental.pallas import tpu as pltpu
from jax.sharding import PartitionSpec as P

D = 768
FF = 2048
HEADS = 12
HEAD_DIM = 64
PAIRS = HEADS // 2
N_CTX = 16
TOK = 128
ENC = 64
HALF = 64
REACH = 128
BF = jnp.bfloat16
F32 = jnp.float32
MIB = 1024 * 1024


def ctx_place():
    me = lax.axis_index("ctx")
    core = me % 2
    high = (me // 2) % 2
    y = me // 4
    return me, core, high, y


def slot_of(y, shift, high, core):
    return ((y + shift) % 4) * 4 + 2 * high + core


def split_heads(block):
    lane = lax.broadcasted_iota(jnp.int32, block.shape, 1)
    nothing = jnp.zeros_like(block)
    return jnp.concatenate(
        [jnp.where(lane < HEAD_DIM, block, nothing), jnp.where(lane < HEAD_DIM, nothing, block)],
        axis=0,
    )


def join_heads(transposed):
    row = lax.broadcasted_iota(jnp.int32, (2 * HEAD_DIM, TOK), 0)
    return jnp.where(row < HEAD_DIM, transposed[:, :TOK], transposed[:, TOK:]).T


def contract(left, right, dims):
    return lax.dot_general(left, right, (dims, ((), ())), preferred_element_type=F32)


def key_chunk(ref, j):
    if ref.shape[2] == 2 * HALF:
        return ref[j, 0]
    return ref[pl.ds(2 * j, 2), 0].reshape(2 * HALF, 2 * HEAD_DIM)


def bias_chunk(class_ref, tile_ref, j, first=0):
    lane = lax.broadcasted_iota(jnp.int32, (HALF, TOK), 1)
    rows = []
    for half in range(2):
        spot = 2 * j + half
        near = class_ref[0, spot]
        far = class_ref[1, spot]
        rows.append(
            jnp.concatenate(
                [
                    jnp.where(lane < HALF, tile_ref[first + head, near], tile_ref[first + head, far])
                    for head in range(2)
                ],
                axis=1,
            )
        )
    return jnp.concatenate(rows, axis=0)


def fold(values, join):
    return join(values.reshape(-1, 8, values.shape[-1]), axis=0)


def attend_pair(queries, keys, values, bias, score_ref, share_ref, chunks):
    queries = split_heads(queries)
    highest = None
    for j in range(chunks):
        scores = contract(keys(j), queries, ((1,), (1,)))
        if bias is not None:
            scores = scores + bias(j)
        score_ref[j] = scores
        top = fold(scores, jnp.max)
        highest = top if highest is None else jnp.maximum(highest, top)
    highest = jnp.max(highest, axis=0, keepdims=True)
    summed = jnp.zeros((8, 2 * TOK), F32)
    for j in range(chunks):
        raised = jnp.exp(score_ref[j] - highest)
        summed = summed + fold(raised, jnp.sum)
        share_ref[j] = raised.astype(BF)
    summed = jnp.sum(summed, axis=0, keepdims=True)
    gathered = jnp.concatenate([values(j) for j in range(chunks)], axis=0)
    mixed = contract(gathered, share_ref[:chunks].reshape(-1, 2 * TOK), ((0,), (0,)))
    return join_heads(mixed / summed).astype(BF), highest + jnp.log(summed)


def attend_pairs(first, last, kv_ref, query_ref, out_ref, total_ref, score_ref, share_ref, bias=None):
    rows = kv_ref.shape[2]
    chunks = N_CTX * rows // TOK

    def step(pair, carry):
        cut = pl.ds(pl.multiple_of(pair * TOK, TOK), TOK)

        def chunk(part, j):
            if rows == TOK:
                return kv_ref[j, part, :, cut]
            return kv_ref[2 * j : 2 * j + 2, part, :, cut].reshape(TOK, TOK)

        mixed, total = attend_pair(
            query_ref[:, cut],
            functools.partial(chunk, 0),
            functools.partial(chunk, 1),
            None if bias is None else functools.partial(bias, pair),
            score_ref,
            share_ref,
            chunks,
        )
        out_ref[:, cut] = mixed
        total_ref[pair] = jnp.broadcast_to(total, (8, 2 * TOK))
        return carry

    lax.fori_loop(first, last, step, 0)


def strip_hot():
    shape = (REACH, 3 * TOK)
    spot = lax.broadcasted_iota(jnp.int32, shape, 1)
    distance = jnp.clip(HALF * (spot // TOK) + spot % TOK - (HALF - 1), 0, REACH - 1)
    return (distance == lax.broadcasted_iota(jnp.int32, shape, 0)).astype(BF)


def index_tables(me, pairs_ref, class_ref, near_ref):
    own = pairs_ref[me]
    for half in range(2):
        query = 31 - own if half else own
        spots = [jnp.int32(-1)] * 3
        for block in range(32):
            pair = pairs_ref[block // 2]
            key = 31 - pair if block % 2 else pair
            gap = query - key
            class_ref[half, block] = jnp.where(gap < 0, 4, jnp.minimum(gap, 3))
            for near in range(3):
                spots[near] = jnp.where(gap == near, block, spots[near])
        for near in range(3):
            near_ref[half, near] = spots[near]


def build_tiles(bias_rows, strips, tile_ref):
    lane = lax.broadcasted_iota(jnp.int32, (HALF, TOK), 1)
    key = lax.broadcasted_iota(jnp.int32, (HALF, TOK), 0)
    row = jnp.where(lane < HALF, lane, lane - HALF)
    for head in range(HEADS):
        for gap in range(3):
            strip = strips[head : head + 1, gap * TOK : gap * TOK + TOK]
            turned = pltpu.roll(
                jnp.broadcast_to(strip, (HALF, TOK)), 65, 1, stride=1, stride_axis=0
            )
            tile = jnp.where(lane < HALF, turned, pltpu.roll(turned, HALF, 1))
            if gap == 0:
                tile = jnp.where(key > row, -1e30, tile)
            tile_ref[head, gap] = tile
        tile_ref[head, 3] = jnp.broadcast_to(bias_rows[head : head + 1, REACH - 1 :], (HALF, TOK))
        tile_ref[head, 4] = jnp.full((HALF, TOK), -1e30, F32)


def torus_place():
    me, core, high, y = ctx_place()
    shard = lax.axis_index("fsdp")
    return me, core, high, y, shard // 4, shard % 4


def hop(src, dst, send_sem, recv_sem, ctx, fsdp):
    return pltpu.make_async_remote_copy(
        src_ref=src,
        dst_ref=dst,
        send_sem=send_sem,
        recv_sem=recv_sem,
        device_id={"ctx": ctx, "fsdp": fsdp},
    )


def greet_all(devices):
    barrier = pltpu.get_barrier_semaphore()
    for ctx, fsdp in devices:
        pl.semaphore_signal(barrier, inc=1, device_id={"ctx": ctx, "fsdp": fsdp})
    pl.semaphore_wait(barrier, len(devices))


ROOT = (2.0 / 3.141592653589793) ** 0.5
PACKS = ((0, 1), (2, 3), (4, 5, 6, 7), (8, 9), (10,))


def front_kernel(*refs):
    sources = refs[:11]
    small_ref, token_ref, state_ref, upstream_ref, bucket_ref, pairs_ref = refs[11:17]
    results = refs[17:20]
    (
        gain_out, normed_out, query_out, tile_result, attended_ref, total_ref, mid_one_ref,
        normed_two_ref, cross_query_ref, cross_attended_ref, cross_total_ref,
        block_ref, d_mid_ref, branch_ref, d_cross_ref, gain_grad_ref,
        wide_mine_out, wide_inner_out, wide_outer_out, tall_mine_out, tall_inner_out, tall_outer_out,
        class_ref, near_ref, self_result, cross_result,
    ) = refs[20:46]
    targets = refs[46:51]
    (
        self_out_ref, cross_out_ref, landing, self_ref, cross_ref, score_ref, share_ref,
        feed_left, feed_right, slope_ref, turned, turned_hidden, tile_ref,
        wide_mine, wide_inner, wide_outer, tall_mine, tall_inner, tall_outer,
        send_sem, x_sem, z_sem, core_sem,
        fill_sem, small_sem, self_sem, cross_sem, feed_sem, local_sem,
    ) = refs[51:]
    me, core, high, y, low, x = torus_place()
    shard = low * 4 + x
    sibling = (slot_of(y, 0, high, 1 - core), shard)
    inside = (me, (1 - low) * 4 + x)
    outside = (slot_of(y, 0, 1 - high, core), (1 - low) * 4 + x)
    across = slot_of(y, 0, 1 - high, core)
    ahead, behind = (slot_of(y, shift, high, core) for shift in (1, 3))
    others = [low * 4 + (x + shift) % 4 for shift in (1, 2, 3)]
    peers = [(shard + shift) % 8 for shift in range(1, 8)]
    greet_all(
        [sibling, outside, (across, shard), (ahead, shard), (behind, shard)]
        + [(me, peer) for peer in peers]
    )
    sends = []

    def send(src, dst, recv_sem, device):
        copy = hop(src, dst, send_sem.at[len(sends)], recv_sem, *device)
        copy.start()
        sends.append(copy)

    def arrived(ref, recv_sem):
        hop(ref, ref, send_sem.at[0], recv_sem, *sibling).wait_recv()

    def bring(src, dst, sem):
        copy = pltpu.make_async_copy(src, dst, sem)
        copy.start()
        return copy


    def part(k, owner, whose, side=None):
        ref = targets[k]
        count = ref.shape[1] // 2
        start = pl.multiple_of(whose * count, 16)
        if side is None:
            return ref.at[owner, pl.ds(start, count), :]
        width = ref.shape[2] // 2
        return ref.at[owner, pl.ds(start, count), pl.ds(side * width, width)]

    def fill(k):
        copies = []
        start = 0
        for source in PACKS[k]:
            width = sources[source].shape[1]
            copies.append(
                bring(
                    sources[source],
                    targets[k].at[shard, :, pl.ds(start, width)],
                    fill_sem.at[source],
                )
            )
            start += width
        return copies

    def send_own(k):
        for copy in fills[k]:
            copy.wait()
        for spot in (1, 0, 2):
            block = part(k, shard, core)
            send(block, block, x_sem.at[k, spot], (me, others[spot]))
        for side, device in enumerate((inside, outside)):
            piece = part(k, shard, core, side)
            send(piece, piece, z_sem.at[k, 3, side], device)


    def pass_x(k):
        for spot in (0, 2, 1):
            owner = low * 4 + (x + 3 - spot) % 4
            block = part(k, owner, core)
            arrived(block, x_sem.at[k, spot])
            for side, device in enumerate((inside, outside)):
                piece = part(k, owner, core, side)
                send(piece, piece, z_sem.at[k, spot, side], device)
            send(block, block, core_sem.at[k, spot], sibling)

    def pass_z(k):
        for spot in (3, 0, 2, 1):
            owner = (1 - low) * 4 + (x + 3 - spot) % 4
            for side in range(2):
                piece = part(k, owner, core, side)
                arrived(piece, z_sem.at[k, spot, side])
                send(piece, piece, core_sem.at[k, 3 + 2 * spot + side], sibling)

    def complete(k):
        for spot in range(3):
            owner = low * 4 + (x + 3 - spot) % 4
            arrived(part(k, owner, 1 - core), core_sem.at[k, spot])
        for spot in range(4):
            owner = (1 - low) * 4 + (x + 3 - spot) % 4
            for side in range(2):
                arrived(part(k, owner, 1 - core, side), core_sem.at[k, 3 + 2 * spot + side])


    def kv_start(src, out, sems):
        send(src, out.at[me], sems.at[me, 0], (across, shard))
        send(src, out.at[me], sems.at[me, 0], (ahead, shard))
        send(src, out.at[me], sems.at[me, 0], (behind, shard))
        send(src, out.at[me], sems.at[me, 0], sibling)

    def kv_across(out, sems):
        block = out.at[across]
        arrived(block, sems.at[across, 0])
        send(block, block, sems.at[across, 0], (ahead, shard))
        send(block, block, sems.at[across, 0], (behind, shard))
        send(block, block, sems.at[across, 0], sibling)

    def kv_near(out, sems, flip):
        half = 1 - high if flip else high
        slot = slot_of(y, 1, half, core)
        block = out.at[slot]
        arrived(block, sems.at[slot, 0])
        send(block.at[0], block.at[0], sems.at[slot, 0], (behind, shard))
        send(block, block, sems.at[slot, 0], sibling)
        slot = slot_of(y, 3, half, core)
        block = out.at[slot]
        arrived(block, sems.at[slot, 0])
        send(block.at[1], block.at[1], sems.at[slot, 1], (ahead, shard))
        send(block, block, sems.at[slot, 0], sibling)

    def kv_far(out, sems, flip):
        slot = slot_of(y, 2, 1 - high if flip else high, core)
        for part in range(2):
            arrived(out.at[slot, part], sems.at[slot, part])
        send(out.at[slot], out.at[slot], sems.at[slot, 0], sibling)

    def kv_complete(out, sems):
        for shift in range(4):
            for half in range(2):
                slot = slot_of(y, shift, half, 1 - core)
                arrived(out.at[slot], sems.at[slot, 0])

    fills = [fill(k) for k in range(5)]
    own_small = bring(small_ref, landing.at[shard], local_sem.at[0])
    for spot, peer in enumerate(peers):
        send(small_ref, landing.at[shard], small_sem.at[spot], (me, peer))
    send_own(0)
    send_own(1)
    own_small.wait()
    for spot in range(7):
        arrived(landing.at[(shard + 7 - spot) % 8], small_sem.at[spot])
    gains = landing[...].astype(F32)
    gain = [
        jnp.concatenate([gains[owner, k : k + 1, :96] for owner in range(8)], axis=1)
        for k in range(3)
    ]
    for k in range(3):
        gain_out[k : k + 1, :] = gain[k]
    tokens = token_ref[...].astype(F32)
    normed = rms_scaled(tokens, gain[0])
    normed_out[...] = normed
    pass_x(0)
    send_own(2)
    pass_z(0)
    pass_x(1)
    send_own(3)
    complete(0)
    exits = [bring(targets[0], results[0], local_sem.at[1])]
    for half in range(2):
        weight = targets[0][:, :, half * D : half * D + D].reshape(D, D)
        self_ref[half] = matmul(normed, weight).astype(BF)
    kv_start(self_ref, self_out_ref, self_sem)
    own_self = bring(self_ref, self_out_ref.at[me], local_sem.at[2])
    pass_z(1)
    send_own(4)
    complete(1)
    exits.append(bring(targets[1], results[1], local_sem.at[4]))
    for half in range(2):
        weight = targets[1][:, :, half * D : half * D + D].reshape(D, D)
        cross_ref[half] = matmul(state_ref[...], weight).astype(BF)
    kv_start(cross_ref, cross_out_ref, cross_sem)
    own_cross = bring(cross_ref, cross_out_ref.at[me], local_sem.at[3])
    index_tables(me, pairs_ref, class_ref, near_ref)
    slab = lax.broadcasted_iota(jnp.int32, (128, REACH), 0)
    place = slab % 16 - 3
    wanted = jnp.where((place >= 0) & (place < 4), 4 * (slab // 16) + place, -1)
    hot = jnp.where(wanted == bucket_ref[...], 1.0, 0.0).astype(BF)
    bias_rows = contract(landing[...].reshape(128, 128), hot, ((0,), (0,)))[:16]
    build_tiles(bias_rows, matmul(bias_rows.astype(BF), strip_hot()), tile_ref)
    exits.append(bring(tile_ref, tile_result, local_sem.at[8]))
    kv_across(self_out_ref, self_sem)
    pass_x(2)
    kv_near(self_out_ref, self_sem, False)
    pass_z(2)
    kv_across(cross_out_ref, cross_sem)
    kv_near(self_out_ref, self_sem, True)
    pass_x(3)
    complete(2)
    exits.append(bring(targets[2], results[2], local_sem.at[5]))

    def square(k):
        return targets[2][:, :, k * D : k * D + D].reshape(D, D)

    query_out[...] = matmul(normed, square(0)).astype(BF)
    kv_far(self_out_ref, self_sem, False)
    kv_far(self_out_ref, self_sem, True)
    kv_near(cross_out_ref, cross_sem, False)
    own_self.wait()
    own_cross.wait()
    kv_complete(self_out_ref, self_sem)
    exits.append(bring(self_out_ref, self_result, local_sem.at[6]))

    def attend_self(first, last):
        attend_pairs(
            first, last, self_out_ref, query_out, attended_ref, total_ref, score_ref, share_ref,
            lambda pair, j: bias_chunk(class_ref, tile_ref, j, 2 * pair),
        )

    def attend_cross(first, last):
        attend_pairs(
            first, last, cross_out_ref, cross_query_ref, cross_attended_ref, cross_total_ref,
            score_ref, share_ref,
        )

    attend_self(0, 2)
    pass_x(4)
    kv_near(cross_out_ref, cross_sem, True)
    kv_far(cross_out_ref, cross_sem, False)
    attend_self(2, 4)
    pass_z(3)
    kv_far(cross_out_ref, cross_sem, True)
    attend_self(4, 6)
    mid_one = tokens + matmul(attended_ref[...], square(1))
    mid_one_ref[...] = mid_one
    normed_two = rms_scaled(mid_one, gain[1])
    normed_two_ref[...] = normed_two
    cross_query_ref[...] = matmul(normed_two, square(2)).astype(BF)
    kv_complete(cross_out_ref, cross_sem)
    exits.append(bring(cross_out_ref, cross_result, local_sem.at[7]))
    attend_cross(0, 3)
    pass_z(4)
    attend_cross(3, 6)
    complete(3)
    mid_two = mid_one_ref[...] + matmul(cross_attended_ref[...], square(3))


    normed_three = rms_scaled(mid_two, gain[2])
    upstream = upstream_ref[...]
    near_rows, far_rows = pl.ds(0, TOK), pl.ds(TOK, TOK)
    feed_left[near_rows, :D] = normed_three
    for piece in range(4):
        start = piece * 512
        gate = matmul(normed_three, targets[3][:, :, start : start + 512].reshape(D, 512))
        up = matmul(normed_three, targets[3][:, :, FF + start : FF + start + 512].reshape(D, 512))
        gate = gate.astype(BF).astype(F32)
        up = up.astype(BF).astype(F32)
        square_gate = gate * gate
        curve = jnp.tanh(ROOT * (gate + 0.044715 * gate * square_gate))
        raised = 0.5 * gate * (1.0 + curve)
        steep = 0.5 * (1.0 + curve) + 0.5 * gate * (1.0 - curve * curve) * (
            ROOT * (1.0 + 3.0 * 0.044715 * square_gate)
        )
        feed_left[near_rows, D + start : D + start + 512] = (raised * up).astype(BF)
        for side in range(2):
            cut = slice(side * 256, side * 256 + 256)
            score_ref[2 * piece + side] = (up * steep)[:, cut]
            score_ref[8 + 2 * piece + side] = raised[:, cut]
    complete(4)
    for piece in range(8):
        start = piece * 256
        d_hidden = contract(upstream, targets[4][piece], ((1,), (1,)))
        slope_ref[0, :, start : start + 256] = (d_hidden * score_ref[piece]).astype(BF)
        slope_ref[1, :, start : start + 256] = (d_hidden * score_ref[8 + piece]).astype(BF)
    half = D // 2
    near_half = pl.ds(pl.multiple_of(core * half, 128), half)
    far_half = pl.ds(pl.multiple_of((1 - core) * half, 128), half)
    swaps = []
    for index, (src, dst) in enumerate(
        (
            (feed_left.at[near_rows], feed_left.at[far_rows]),
            (slope_ref.at[1 - core], feed_right.at[far_rows, pl.ds(0, FF)]),
            (upstream_ref.at[:, far_half], feed_right.at[far_rows, pl.ds(FF, half)]),
        )
    ):
        copy = hop(src, dst, feed_sem.at[0, index], feed_sem.at[1, index], *sibling)
        copy.start()
        swaps.append(copy)
    feed_right[near_rows, :FF] = slope_ref[core]
    feed_right[near_rows, FF:] = upstream_ref[:, near_half]
    block_ref[...] = mid_two + matmul(feed_left[near_rows, D:], targets[4][...].reshape(FF, D))
    grad = contract(slope_ref[0], targets[3][:, :, :FF].reshape(D, FF), ((1,), (1,)))
    grad = grad + contract(slope_ref[1], targets[3][:, :, FF:].reshape(D, FF), ((1,), (1,)))
    inverse = lax.rsqrt(jnp.mean(mid_two * mid_two, axis=-1, keepdims=True) + 1e-06)
    gain_grad_ref[...] = jnp.sum(mid_two * inverse * grad, axis=0, keepdims=True)
    scaled = gain[2] * grad
    mixed = jnp.mean(mid_two * scaled, axis=-1, keepdims=True)
    d_mid_two = upstream.astype(F32) + (
        inverse * scaled - mid_two * (inverse * inverse * inverse * mixed)
    )
    d_mid_ref[...] = d_mid_two
    branch_ref[...] = d_mid_two.astype(BF)
    d_cross_ref[...] = contract(d_mid_two.astype(BF), square(3), ((1,), (1,))).astype(BF)
    for copy in swaps:
        copy.wait_recv()
    turned[...] = feed_left[:, :D].T.reshape(8, 96, 2 * TOK)
    turned_hidden[...] = feed_left[:, D:].T.reshape(8, FF // 8, 2 * TOK)
    for group in range(2):
        owners = pl.ds(4 * ((1 - low + group) % 2), 4)
        left = turned[owners].reshape(4 * 96, 2 * TOK)
        for piece in range(4):
            cut = slice(piece * 512, piece * 512 + 512)
            part = matmul(left, feed_right[:, cut]).astype(BF).reshape(4, 96, 512)
            if group:
                wide_mine[:, :, cut] = part
            else:
                wide_inner[:, :, cut] = part[:, :48]
                wide_outer[:, :, cut] = part[:, 48:]
        if group:
            exits.append(bring(wide_mine, wide_mine_out, local_sem.at[9]))
        else:
            exits.append(bring(wide_inner, wide_inner_out, local_sem.at[10]))
            exits.append(bring(wide_outer, wide_outer_out, local_sem.at[11]))
        left = turned_hidden[owners].reshape(4 * FF // 8, 2 * TOK)
        part = matmul(left, feed_right[:, FF:]).astype(BF).reshape(4, FF // 8, half)
        if group:
            tall_mine[...] = part
            exits.append(bring(tall_mine, tall_mine_out, local_sem.at[12]))
        else:
            tall_inner[...] = part[:, :128]
            tall_outer[...] = part[:, 128:]
            exits.append(bring(tall_inner, tall_inner_out, local_sem.at[13]))
            exits.append(bring(tall_outer, tall_outer_out, local_sem.at[14]))
    for copy in sends + swaps:
        copy.wait_send()
    for copy in exits:
        copy.wait()


def front(weights, others, collective_id):
    dma = pltpu.SemaphoreType.DMA
    packs = [
        (8, weights[group[0]].shape[0], sum(weights[k].shape[1] for k in group)) for group in PACKS
    ]
    anywhere = pl.BlockSpec(memory_space=pl.ANY)
    inside = pl.BlockSpec(memory_space=pltpu.VMEM)
    scalars = pl.BlockSpec(memory_space=pltpu.SMEM)
    return pl.pallas_call(
        front_kernel,
        out_shape=[jax.ShapeDtypeStruct(pack, BF) for pack in packs[:3]]
        + [
            jax.ShapeDtypeStruct((3, D), F32),
            jax.ShapeDtypeStruct((TOK, D), BF),
            jax.ShapeDtypeStruct((TOK, D), BF),
            jax.ShapeDtypeStruct((HEADS, 5, HALF, TOK), F32),
            jax.ShapeDtypeStruct((TOK, D), BF),
            jax.ShapeDtypeStruct((PAIRS, 8, 2 * TOK), F32),
            jax.ShapeDtypeStruct((TOK, D), F32),
            jax.ShapeDtypeStruct((TOK, D), BF),
            jax.ShapeDtypeStruct((TOK, D), BF),
            jax.ShapeDtypeStruct((TOK, D), BF),
            jax.ShapeDtypeStruct((PAIRS, 8, 2 * TOK), F32),
            jax.ShapeDtypeStruct((TOK, D), F32),
            jax.ShapeDtypeStruct((TOK, D), F32),
            jax.ShapeDtypeStruct((TOK, D), BF),
            jax.ShapeDtypeStruct((TOK, D), BF),
            jax.ShapeDtypeStruct((1, D), F32),
            jax.ShapeDtypeStruct((4, 96, FF), BF),
            jax.ShapeDtypeStruct((4, 48, FF), BF),
            jax.ShapeDtypeStruct((4, 48, FF), BF),
            jax.ShapeDtypeStruct((4, 256, D // 2), BF),
            jax.ShapeDtypeStruct((4, 128, D // 2), BF),
            jax.ShapeDtypeStruct((4, 128, D // 2), BF),
            jax.ShapeDtypeStruct((2, 32), jnp.int32),
            jax.ShapeDtypeStruct((2, 3), jnp.int32),
            jax.ShapeDtypeStruct((N_CTX, 2, TOK, D), BF),
            jax.ShapeDtypeStruct((N_CTX, 2, ENC, D), BF),
        ],
        in_specs=[anywhere] * 12 + [inside] * 4 + [scalars],
        out_specs=[anywhere] * 3
        + [inside] * 3
        + [anywhere]
        + [inside] * 12
        + [anywhere] * 6
        + [scalars] * 2
        + [anywhere] * 2,
        scratch_shapes=[pltpu.VMEM(pack, BF) for pack in packs]
        + [
            pltpu.VMEM((N_CTX, 2, TOK, D), BF),
            pltpu.VMEM((N_CTX, 2, ENC, D), BF),
            pltpu.VMEM((8, 16, 128), BF),
            pltpu.VMEM((2, TOK, D), BF),
            pltpu.VMEM((2, ENC, D), BF),
            pltpu.VMEM((N_CTX, TOK, 2 * TOK), F32),
            pltpu.VMEM((N_CTX, TOK, 2 * TOK), BF),
            pltpu.VMEM((2 * TOK, D + FF), BF),
            pltpu.VMEM((2 * TOK, FF + D // 2), BF),
            pltpu.VMEM((2, TOK, FF), BF),
            pltpu.VMEM((8, 96, 2 * TOK), BF),
            pltpu.VMEM((8, FF // 8, 2 * TOK), BF),
            pltpu.VMEM((HEADS, 5, HALF, TOK), F32),
            pltpu.VMEM((4, 96, FF), BF),
            pltpu.VMEM((4, 48, FF), BF),
            pltpu.VMEM((4, 48, FF), BF),
            pltpu.VMEM((4, 256, D // 2), BF),
            pltpu.VMEM((4, 128, D // 2), BF),
            pltpu.VMEM((4, 128, D // 2), BF),
            dma((5 * 22 + 7 + 2 * 18,)),
            dma((5, 3)),
            dma((5, 4, 2)),
            dma((5, 11)),
            dma((11,)),
            dma((7,)),
            dma((N_CTX, 2)),
            dma((N_CTX, 2)),
            dma((2, 3)),
            dma((15,)),
        ],
        compiler_params=pltpu.CompilerParams(
            collective_id=collective_id, has_side_effects=True, vmem_limit_bytes=60 * MIB
        ),
        name="front",
    )(*weights, *others)


PIECE = 96
WIDTHS = (D // 2, D // 2, D // 2, D // 2, D, D, FF)
SPAN = sum(WIDTHS)
DOWN = len(WIDTHS)
CHUNKS = DOWN + 1
CROSS_KV, SELF_KV, WIDE = 4, 5, 6
LEFT = (D,) * 4
RIGHT = (D // 2,) * 4


def finish_kernel(*refs):
    lefts = refs[:4]
    rights = refs[4:8]
    wide_refs, down_refs = refs[8:11], refs[11:14]
    dkv_ref, dckv_ref, square_ref = refs[14:17]
    kv_source, ckv_source, state_ref, dq_ref, dmid_ref, token_ref, gain_ref, small_ref = refs[17:25]
    early_out, late_out, small_out, decoder_ref, encoder_ref = refs[25:30]
    (
        left_all, right_all, turned, turned_one, turned_state, state_all, s_right, c_right,
        kept, from_z, from_x, via_x, d_z, d_x, d_via,
        s_kept, s_core, s_row, s_via, s_stage, s_high, s_fin,
        c_kept, c_core, c_row, c_via, c_stage, c_high, c_fin,
        small_f32, sm_own, sm_core, sm_z, sm_x, sm_ctx, sm_total,
        packed, from_ctx, land, late_packed, late_from, late_land,
        wide_add, down_add, query_ref, kv_ref, ckv_ref, bring_sem,
        s_sem, c_sem, fill_sem, act_send, act_recv, late_send, late_recv, z_send, z_recv,
        x_send, x_recv, ctx_send, ctx_recv, pass_send, pass_recv, sm_send, sm_recv, local_sem,
    ) = refs[30:]
    me, core, high, y, low, x = torus_place()
    shard = low * 4 + x
    rank = y * 2 + high
    sibling = (slot_of(y, 0, high, 1 - core), shard)
    inside = (me, (1 - low) * 4 + x)
    outside = (slot_of(y, 0, 1 - high, core), (1 - low) * 4 + x)
    across = (slot_of(y, 0, 1 - high, core), shard)
    others = [low * 4 + (x + shift) % 4 for shift in (1, 2, 3)]
    ahead = (slot_of(y, 1, high, core), shard)
    behind = (slot_of(y, 3, high, core), shard)
    shifts = [(dy, dz) for dy in range(4) for dz in range(2)][1:]
    mates = [((y + dy) % 4) * 2 + (high + dz) % 2 for dy, dz in shifts]
    greet_all(
        [sibling, inside, outside]
        + [(me, other) for other in others]
        + [(mate * 2 + core, shard) for mate in mates]
    )
    sends = []

    def go(src, dst, send_sem, recv_sem, device):
        copy = hop(src, dst, send_sem, recv_sem, *device)
        copy.start()
        sends.append(copy)
        return copy

    def bring(src, dst, sem):
        copy = pltpu.make_async_copy(src, dst, sem)
        copy.start()
        return copy


    def rows_start(source, held, arrived, sem):
        over = []
        local = []
        for spot, shift in enumerate((2, 1, 3, 0)):
            pair = pl.ds(((y + shift) % 4) * 2, 2)
            block = pl.ds(2 * spot, 2)
            over.append(
                go(
                    source.at[pair, 1 - core], arrived.at[block],
                    sem.at[0, spot], sem.at[1, spot], sibling,
                )
            )
            local.append(bring(source.at[pair, core], held.at[block], sem.at[4, spot]))
        return over, local


    def rows_send(copies, held, arrived, via, row, sem):
        over, local = copies
        onward = []
        for spot in range(4):
            local[spot].wait()
            over[spot].wait_recv()
            for block in (2 * spot, 2 * spot + 1):
                for part in range(2):
                    held[block, part] = held[block, part] + arrived[block, part]
            if spot == 0:
                first = go(held.at[0], via.at[0], sem.at[2, 0], sem.at[3, 0], ahead)
                second = go(held.at[1], via.at[1], sem.at[2, 1], sem.at[3, 1], behind)
            elif spot == 1:
                onward.append(go(held.at[3], row.at[0, 1], sem.at[2, 2], sem.at[3, 2], ahead))
            elif spot == 2:
                onward.append(go(held.at[4], row.at[1, 0], sem.at[2, 3], sem.at[3, 3], behind))
        return first, second, onward

    def rows_via(state, held, via, row, sem):
        first, second, onward = state
        first.wait_recv()
        for part in range(2):
            held[2, part] = held[2, part] + via[0, part]
        onward.append(go(held.at[2], row.at[0, 0], sem.at[2, 4], sem.at[3, 4], ahead))
        second.wait_recv()
        for part in range(2):
            held[5, part] = held[5, part] + via[1, part]
        onward.append(go(held.at[5], row.at[1, 1], sem.at[2, 5], sem.at[3, 5], behind))
        return onward

    def rows_total(held, row, half, part):
        return (
            held[6 + half, part].astype(F32)
            + row[0, half, part].astype(F32)
            + row[1, half, part].astype(F32)
        )

    def rows_across(onward, held, row, stage, landing, sem):
        for copy in onward:
            copy.wait_recv()
        for part in range(2):
            stage[part] = rows_total(held, row, 1 - high, part).astype(BF)
        return go(stage, landing, sem.at[2, 6], sem.at[3, 6], across)

    def rows_sum(last, held, row, landing, final, right, which):
        totals = [rows_total(held, row, high, part) for part in range(2)]
        last.wait_recv()
        for part in range(2):
            final[part] = (totals[part] + landing[part].astype(F32)).astype(BF)
        count = final.shape[1]
        copy = go(
            final.at[1 - core], right.at[pl.ds(count, count)],
            late_send.at[which], late_recv.at[which], sibling,
        )
        right[:count] = final[core]
        return copy


    starts = [sum(WIDTHS[:k]) for k in range(len(WIDTHS))]
    left_starts = [sum(LEFT[:k]) for k in range(4)]
    right_starts = [sum(RIGHT[:k]) for k in range(4)]
    acts = {}
    over_z, over_via, over_x = {}, {}, {}
    column_ahead = (me, low * 4 + (x + 1) % 4)
    column_behind = (me, low * 4 + (x + 3) % 4)

    def buffers(k):
        if k == DOWN:
            return d_z, d_x, d_via, pl.ds(0, D // 2)
        return from_z, from_x, via_x, pl.ds(starts[k], WIDTHS[k])

    def acts_start(index):
        left = pl.ds(left_starts[index], LEFT[index])
        right = pl.ds(right_starts[index], RIGHT[index])
        near = pl.ds(pl.multiple_of(core * RIGHT[index], 128), RIGHT[index])
        far = pl.ds(pl.multiple_of((1 - core) * RIGHT[index], 128), RIGHT[index])
        mine = pl.ds(0, TOK)
        theirs = pl.ds(TOK, TOK)
        acts[index] = (
            bring(lefts[index], left_all.at[mine, left], fill_sem.at[index, 0]),
            bring(rights[index].at[:, near], right_all.at[mine, right], fill_sem.at[index, 1]),
            go(
                lefts[index], left_all.at[theirs, left],
                act_send.at[index, 0], act_recv.at[index, 0], sibling,
            ),
            go(
                rights[index].at[:, far], right_all.at[theirs, right],
                act_send.at[index, 1], act_recv.at[index, 1], sibling,
            ),
        )

    def multiply(k, left_ref, right):
        landing, _, _, cut = buffers(k)
        for group in range(2):
            owners = pl.ds(4 * ((1 - low + group) % 2), 4)
            left = left_ref[owners].reshape(4 * PIECE, right.shape[0])
            kept[owners, :, cut] = (
                contract(left, right, ((1,), (0,))).astype(BF).reshape(4, PIECE, WIDTHS[k])
            )
            if group == 0:
                half = PIECE // 2
                over_z[k] = [
                    go(
                        kept.at[owners, pl.ds(side * half, half), cut],
                        landing.at[:, pl.ds(side * half, half), cut],
                        z_send.at[k, side],
                        z_recv.at[k, side],
                        device,
                    )
                    for side, device in enumerate((inside, outside))
                ]

    def make(index):
        near_left, near_right, far_left, far_right = acts[index]
        near_left.wait()
        near_right.wait()
        far_left.wait_recv()
        far_right.wait_recv()
        left = left_all[:, left_starts[index] : left_starts[index] + LEFT[index]].T
        right = right_all[:, right_starts[index] : right_starts[index] + RIGHT[index]]
        target = turned_one if index == 3 else turned
        target[...] = left.reshape(8, PIECE, 2 * TOK)
        multiply(index, target, right)

    def step_z(k):
        landing, _, _, cut = buffers(k)
        for copy in over_z[k]:
            copy.wait_recv()
        for column in range(4):
            landing[column, :, cut] = landing[column, :, cut] + kept[4 * low + column, :, cut]
        send_x(k)


    def send_x(k):
        landing, spread, via, cut = buffers(k)
        half = landing.shape[1] // 2
        upper, lower = pl.ds(0, half), pl.ds(half, half)
        away, front_column, back_column = (x + 2) % 4, (x + 1) % 4, (x + 3) % 4
        over_via[k] = (
            go(
                landing.at[away, upper, cut], via.at[0, :, cut],
                x_send.at[k, 0], x_recv.at[k, 0], column_ahead,
            ),
            go(
                landing.at[away, lower, cut], via.at[1, :, cut],
                x_send.at[k, 1], x_recv.at[k, 1], column_behind,
            ),
        )
        over_x[k] = [
            go(
                landing.at[front_column, lower, cut], spread.at[0, lower, cut],
                x_send.at[k, 2], x_recv.at[k, 2], column_ahead,
            ),
            go(
                landing.at[back_column, upper, cut], spread.at[1, upper, cut],
                x_send.at[k, 3], x_recv.at[k, 3], column_behind,
            ),
        ]

    def step_via(k):
        landing, spread, via, cut = buffers(k)
        half = landing.shape[1] // 2
        upper, lower = pl.ds(0, half), pl.ds(half, half)
        front_column, back_column = (x + 1) % 4, (x + 3) % 4
        over_via[k][0].wait_recv()
        landing[front_column, upper, cut] = landing[front_column, upper, cut] + via[0, :, cut]
        over_x[k].append(
            go(
                landing.at[front_column, upper, cut], spread.at[0, upper, cut],
                x_send.at[k, 4], x_recv.at[k, 4], column_ahead,
            )
        )
        over_via[k][1].wait_recv()
        landing[back_column, lower, cut] = landing[back_column, lower, cut] + via[1, :, cut]
        over_x[k].append(
            go(
                landing.at[back_column, lower, cut], spread.at[1, lower, cut],
                x_send.at[k, 5], x_recv.at[k, 5], column_behind,
            )
        )

    def step_x(k):
        landing, spread, _, cut = buffers(k)
        for copy in over_x[k]:
            copy.wait_recv()
        total = landing[x, :, cut].astype(F32)
        for spot in range(2):
            total = total + spread[spot, :, cut].astype(F32)
        total = total.astype(BF)
        half = D // 2
        if k == WIDE:
            for piece in range(8):
                packed[piece, :PIECE, :256] = total[:, piece * 256 : piece * 256 + 256]
        elif k == DOWN:
            for piece in range(8):
                for part in range(3):
                    packed[piece, part * 32 : part * 32 + 32, 256:] = total[
                        piece * 32 : piece * 32 + 32, part * 128 : part * 128 + 128
                    ]
        else:
            middle = PIECE // 2
            for upper in range(2):
                rows = total[upper * middle : upper * middle + middle, :]
                if k == CROSS_KV or k == SELF_KV:
                    for piece in range(2):
                        late_packed[(0 if k == CROSS_KV else 4) + 2 * piece + upper] = rows[
                            :, piece * half : piece * half + half
                        ]
                else:
                    packed[2 * k + upper, PIECE:, :] = rows


    def mate_device(mate):
        return (mate * 2 + core, shard)

    def ctx_start(which, source, landing):
        return [
            go(
                source.at[mate], landing.at[spot],
                ctx_send.at[which, spot], ctx_recv.at[which, spot], mate_device(mate),
            )
            for spot, mate in enumerate(mates)
        ]

    def ctx_sum(which, over, source, landing, final):
        total = source[rank].astype(F32)
        for spot in range(7):
            over[spot].wait_recv()
            total = total + landing[spot].astype(F32)
        final[rank, core] = total.astype(BF)
        own = final.at[rank, core]
        for spot, mate in enumerate(mates):
            go(own, own, ctx_send.at[which, 7 + spot], ctx_recv.at[which, 7 + rank], mate_device(mate))
        go(own, own, pass_send.at[which, 7], pass_recv.at[which, rank], sibling)

    def landed(ref, recv_sem):
        hop(ref, ref, pass_send.at[0, 0], recv_sem, *sibling).wait_recv()

    def ctx_pass(which, final):
        for spot, mate in enumerate(mates):
            block = final.at[mate, core]
            landed(block, ctx_recv.at[which, 7 + mate])
            go(block, block, pass_send.at[which, spot], pass_recv.at[which, mate], sibling)

    def ctx_done(which, final):
        for mate in [rank] + mates:
            landed(final.at[mate, 1 - core], pass_recv.at[which, mate])

    wide_cut = pl.ds(starts[WIDE], FF)
    down_copies = [bring(down_refs[0], d_z, bring_sem.at[0])] + [
        bring(down_refs[1 + side], down_add.at[side], bring_sem.at[1 + side]) for side in range(2)
    ]
    wide_copies = [bring(wide_refs[0], from_z.at[:, :, wide_cut], bring_sem.at[3])] + [
        bring(wide_refs[1 + side], wide_add.at[side], bring_sem.at[4 + side]) for side in range(2)
    ]
    s_copies = rows_start(dkv_ref, s_kept, s_core, s_sem)
    c_copies = rows_start(dckv_ref, c_kept, c_core, c_sem)
    for index in range(4):
        acts_start(index)
    state_near = bring(state_ref, state_all.at[pl.ds(0, ENC)], local_sem.at[0])
    state_far = go(
        state_ref, state_all.at[pl.ds(ENC, ENC)], late_send.at[2], late_recv.at[2], sibling
    )
    kv_copy = bring(kv_source, kv_ref, bring_sem.at[7])
    ckv_copy = bring(ckv_source, ckv_ref, bring_sem.at[8])
    query_copy = bring(square_ref.at[:, :, pl.ds(0, D)], query_ref, bring_sem.at[6])
    for copy in down_copies:
        copy.wait()
    for side in range(2):
        for column in range(4):
            rows = slice(side * 128, side * 128 + 128)
            d_z[column, rows, :] = d_z[column, rows, :] + down_add[side, column]
    send_x(DOWN)
    for copy in wide_copies:
        copy.wait()
    for side in range(2):
        for column in range(4):
            rows = slice(side * 48, side * 48 + 48)
            from_z[column, rows, wide_cut] = from_z[column, rows, wide_cut] + wide_add[side, column]
    send_x(WIDE)
    s_state = rows_send(s_copies, s_kept, s_core, s_via, s_row, s_sem)
    make(0)
    make(1)
    s_onward = rows_via(s_state, s_kept, s_via, s_row, s_sem)
    c_state = rows_send(c_copies, c_kept, c_core, c_via, c_row, c_sem)
    make(2)
    make(3)
    step_via(DOWN)
    step_via(WIDE)
    for k in range(4):
        step_z(k)
    state_near.wait()
    state_far.wait_recv()
    turned_state[...] = state_all[...].T.reshape(8, PIECE, 2 * ENC)
    s_last = rows_across(s_onward, s_kept, s_row, s_stage, s_high, s_sem)
    c_onward = rows_via(c_state, c_kept, c_via, c_row, c_sem)
    for k in range(4):
        step_via(k)
    step_x(DOWN)
    step_x(WIDE)
    s_far = rows_sum(s_last, s_kept, s_row, s_high, s_fin, s_right, 0)
    for k in range(4):
        step_x(k)
    early = ctx_start(0, packed, from_ctx)
    s_far.wait_recv()
    multiply(SELF_KV, turned_one, s_right[...])
    c_last = rows_across(c_onward, c_kept, c_row, c_stage, c_high, c_sem)
    tokens = token_ref[...].astype(F32)
    d_kv = jnp.concatenate([s_fin[0], s_fin[1]], axis=1)
    query_copy.wait()
    kv_copy.wait()
    grad = contract(dq_ref[...], query_ref[...].reshape(D, D), ((1,), (1,)))
    grad = grad + contract(d_kv, kv_ref[...], ((1,), (1,)))
    inverse = lax.rsqrt(jnp.mean(tokens * tokens, axis=-1, keepdims=True) + 1e-06)
    small_f32[...] = small_ref[...]
    line = jnp.sum(tokens * inverse * grad, axis=0, keepdims=True)
    for owner in range(8):
        small_f32[owner, 0:1, :96] = line[:, owner * 96 : owner * 96 + 96]
    sm_own[...] = small_f32[...].astype(BF)
    sm_over = go(sm_own, sm_core, sm_send.at[0], sm_recv.at[0], sibling)
    c_far = rows_sum(c_last, c_kept, c_row, c_high, c_fin, c_right, 1)
    c_far.wait_recv()
    multiply(CROSS_KV, turned_state, c_right[...])
    step_z(SELF_KV)
    sm_over.wait_recv()
    sm_own_sum = (sm_own[...].astype(F32) + sm_core[...].astype(F32)).astype(BF)
    sm_over.wait_send()
    sm_own[...] = sm_own_sum
    sm_inside = go(
        sm_own.at[pl.ds(4 * (1 - low), 4)], sm_z, sm_send.at[1], sm_recv.at[1], inside
    )
    ctx_sum(0, early, packed, from_ctx, land)
    step_z(CROSS_KV)
    step_via(SELF_KV)
    sm_inside.wait_recv()
    for column in range(4):
        sm_z[column] = sm_z[column] + sm_own[4 * low + column]
    sm_row = [
        go(
            sm_z.at[(x + spot + 1) % 4], sm_x.at[spot],
            sm_send.at[2 + spot], sm_recv.at[2 + spot], (me, others[spot]),
        )
        for spot in range(3)
    ]
    step_via(CROSS_KV)
    scaled = gain_ref[...] * grad
    mixed = jnp.mean(tokens * scaled, axis=-1, keepdims=True)
    decoder_ref[...] = (
        dmid_ref[...] + inverse * scaled - tokens * (inverse * inverse * inverse * mixed)
    )
    step_x(SELF_KV)
    step_x(CROSS_KV)
    late = ctx_start(1, late_packed, late_from)
    sm_sum = sm_z[x].astype(F32)
    for spot in range(3):
        sm_row[spot].wait_recv()
        sm_sum = sm_sum + sm_x[spot].astype(F32)
    sm_total[...] = sm_sum.astype(BF)
    sm_mates = [
        go(sm_total, sm_ctx.at[spot], sm_send.at[5 + spot], sm_recv.at[5 + spot], mate_device(mate))
        for spot, mate in enumerate(mates)
    ]
    ctx_pass(0, land)
    ctx_sum(1, late, late_packed, late_from, late_land)
    d_ckv = jnp.concatenate([c_fin[0], c_fin[1]], axis=1)
    ckv_copy.wait()
    encoder_ref[...] = contract(d_ckv, ckv_ref[...], ((1,), (1,)))
    sm_sum = sm_total[...].astype(F32)
    for spot in range(7):
        sm_mates[spot].wait_recv()
        sm_sum = sm_sum + sm_ctx[spot].astype(F32)
    small_out[...] = sm_sum
    ctx_done(0, land)
    early_exit = bring(land, early_out, bring_sem.at[9])
    ctx_pass(1, late_land)
    ctx_done(1, late_land)
    late_exit = bring(late_land, late_out, bring_sem.at[10])
    early_exit.wait()
    late_exit.wait()
    for copy in sends:
        if copy is not sm_over:
            copy.wait_send()


def unpack_kernel(early, late, *refs):
    for source, target in zip(refs[:3], refs[14:]):
        target[...] = source[...]
    square_refs = refs[3:11]
    gate_ref, up_ref, down_ref = refs[11:14]
    half = D // 2
    middle = PIECE // 2
    for side in range(2):
        columns = slice(side * half, side * half + half)
        for upper in range(2):
            rows = slice(upper * middle, upper * middle + middle)
            for k in range(4):
                square_refs[k][rows, columns] = early[2 * k + upper, side, PIECE:, :].astype(F32)
            for k in range(2):
                for piece in range(2):
                    square_refs[4 + 2 * k + side][rows, piece * half : piece * half + half] = late[
                        4 * k + 2 * piece + upper, side
                    ].astype(F32)
        target = up_ref if side else gate_ref
        for piece in range(8):
            target[:, piece * 256 : piece * 256 + 256] = early[piece, side, :PIECE, :256].astype(F32)
            for part in range(3):
                down_ref[
                    piece * 32 : piece * 32 + 32,
                    side * half + part * 128 : side * half + part * 128 + 128,
                ] = early[piece, side, part * 32 : part * 32 + 32, 256:].astype(F32)


def unpack(early, late, *whole):
    outs = (
        [jax.ShapeDtypeStruct((PIECE, D), F32)] * 8
        + [jax.ShapeDtypeStruct((PIECE, FF), F32)] * 2
        + [jax.ShapeDtypeStruct((FF // 8, D), F32)]
        + [jax.ShapeDtypeStruct(part.shape, F32) for part in whole]
    )
    return pl.pallas_call(
        unpack_kernel,
        out_shape=outs,
        in_specs=[pl.BlockSpec(memory_space=pltpu.VMEM)] * (2 + len(whole)),
        out_specs=[pl.BlockSpec(memory_space=pltpu.VMEM)] * len(outs),
        compiler_params=pltpu.CompilerParams(vmem_limit_bytes=62 * MIB),
        name="unpack",
    )(early, late, *whole)


def finish(far, near, collective_id):
    dma = pltpu.SemaphoreType.DMA

    def rows(count):
        return [
            pltpu.VMEM((8, 2, count, D), BF),
            pltpu.VMEM((8, 2, count, D), BF),
            pltpu.VMEM((2, 2, 2, count, D), BF),
            pltpu.VMEM((2, 2, count, D), BF),
            pltpu.VMEM((2, count, D), BF),
            pltpu.VMEM((2, count, D), BF),
            pltpu.VMEM((2, count, D), BF),
        ]

    outs = [
        jax.ShapeDtypeStruct((8, 2, 3 * PIECE // 2, D // 2), BF),
        jax.ShapeDtypeStruct((8, 2, PIECE // 2, D // 2), BF),
        jax.ShapeDtypeStruct((16, 128), F32),
        jax.ShapeDtypeStruct((TOK, D), F32),
        jax.ShapeDtypeStruct((ENC, D), F32),
    ]
    return pl.pallas_call(
        finish_kernel,
        out_shape=outs,
        in_specs=[pl.BlockSpec(memory_space=pl.ANY)] * len(far)
        + [pl.BlockSpec(memory_space=pltpu.VMEM)] * len(near),
        out_specs=[pl.BlockSpec(memory_space=pl.ANY)] * 2
        + [pl.BlockSpec(memory_space=pltpu.VMEM)] * 3,
        scratch_shapes=[
            pltpu.VMEM((2 * TOK, sum(LEFT)), BF),
            pltpu.VMEM((2 * TOK, sum(RIGHT)), BF),
            pltpu.VMEM((8, PIECE, 2 * TOK), BF),
            pltpu.VMEM((8, PIECE, 2 * TOK), BF),
            pltpu.VMEM((8, PIECE, 2 * ENC), BF),
            pltpu.VMEM((2 * ENC, D), BF),
            pltpu.VMEM((2 * TOK, D), BF),
            pltpu.VMEM((2 * ENC, D), BF),
            pltpu.VMEM((8, PIECE, SPAN - FF), BF),
            pltpu.VMEM((4, PIECE, SPAN), BF),
            pltpu.VMEM((2, PIECE, SPAN), BF),
            pltpu.VMEM((2, PIECE // 2, SPAN), BF),
            pltpu.VMEM((4, FF // 8, D // 2), BF),
            pltpu.VMEM((2, FF // 8, D // 2), BF),
            pltpu.VMEM((2, FF // 16, D // 2), BF),
        ]
        + rows(TOK)
        + rows(ENC)
        + [
            pltpu.VMEM((8, 16, 128), F32),
            pltpu.VMEM((8, 16, 128), BF),
            pltpu.VMEM((8, 16, 128), BF),
            pltpu.VMEM((4, 16, 128), BF),
            pltpu.VMEM((3, 16, 128), BF),
            pltpu.VMEM((7, 16, 128), BF),
            pltpu.VMEM((16, 128), BF),
            pltpu.VMEM((8, 3 * PIECE // 2, D // 2), BF),
            pltpu.VMEM((7, 3 * PIECE // 2, D // 2), BF),
            pltpu.VMEM((8, 2, 3 * PIECE // 2, D // 2), BF),
            pltpu.VMEM((8, PIECE // 2, D // 2), BF),
            pltpu.VMEM((7, PIECE // 2, D // 2), BF),
            pltpu.VMEM((8, 2, PIECE // 2, D // 2), BF),
            pltpu.VMEM((2, 4, PIECE // 2, FF), BF),
            pltpu.VMEM((2, 4, FF // 16, D // 2), BF),
            pltpu.VMEM((8, PIECE, D), BF),
            pltpu.VMEM((D, 2 * D), BF),
            pltpu.VMEM((D, 2 * D), BF),
            dma((11,)),
            dma((5, 7)),
            dma((5, 7)),
            dma((4, 2)),
            dma((4, 2)),
            dma((4, 2)),
            dma((3,)),
            dma((3,)),
            dma((CHUNKS, 2)),
            dma((CHUNKS, 2)),
            dma((CHUNKS, 6)),
            dma((CHUNKS, 6)),
            dma((2, 14)),
            dma((2, 15)),
            dma((2, 8)),
            dma((2, 8)),
            dma((12,)),
            dma((12,)),
            dma((3,)),
        ],
        compiler_params=pltpu.CompilerParams(
            collective_id=collective_id, has_side_effects=True, vmem_limit_bytes=62 * MIB
        ),
        name="finish_gradients",
    )(*far, *near)


def backward_kernel(biased, *refs):
    if biased:
        class_ref, near_ref, q_ref, k_ref, v_ref, g_ref, total_ref, tile_ref = refs[:8]
        dq_ref, dkv_ref, strip_ref, share_ref, slope_ref, share_low, slope_low = refs[8:]
    else:
        q_ref, k_ref, v_ref, g_ref, total_ref = refs[:5]
        dq_ref, dkv_ref, share_ref, slope_ref, share_low, slope_low = refs[5:]
    chunks = share_ref.shape[0]
    queries = split_heads(q_ref[...])
    grads = split_heads(g_ref[...])
    totals = total_ref[0, 0:1]
    inner = jnp.zeros((8, 2 * TOK), F32)
    for j in range(chunks):
        scores = contract(key_chunk(k_ref, j), queries, ((1,), (1,)))
        if biased:
            scores = scores + bias_chunk(class_ref, tile_ref, j)
        shares = jnp.exp(scores - totals)
        slopes = contract(key_chunk(v_ref, j), grads, ((1,), (1,)))
        inner = inner + fold(shares * slopes, jnp.sum)
        share_ref[j] = shares
        slope_ref[j] = slopes
        share_low[j] = shares.astype(BF)
    inner = jnp.sum(inner, axis=0, keepdims=True)
    for j in range(chunks):
        grad = share_ref[j] * (slope_ref[j] - inner)
        if biased:
            slope_ref[j] = grad
        slope_low[j] = grad.astype(BF)
    keys = jnp.concatenate([key_chunk(k_ref, j) for j in range(chunks)], axis=0)
    low = slope_low[...].reshape(-1, 2 * TOK)
    dq_ref[...] = join_heads(contract(keys, low, ((0,), (0,)))).astype(BF)
    shape = dkv_ref.shape
    block = (shape[0], shape[2], shape[3])
    dkv_ref[:, 0] = contract(low, queries, ((1,), (0,))).astype(BF).reshape(block)
    dkv_ref[:, 1] = (
        contract(share_low[...].reshape(-1, 2 * TOK), grads, ((1,), (0,))).astype(BF).reshape(block)
    )
    if biased:
        lane = lax.broadcasted_iota(jnp.int32, (HALF, TOK), 1)
        for gap in range(3):
            pieces = []
            for half in range(2):
                spot = near_ref[half, gap]
                held = slope_ref[jnp.maximum(spot, 0) // 2, pl.ds(
                    pl.multiple_of((jnp.maximum(spot, 0) % 2) * HALF, HALF), HALF)]
                pieces.append(jnp.where(spot >= 0, held, jnp.zeros_like(held)))
            for head in range(2):
                cut = slice(head * TOK, (head + 1) * TOK)
                strip_ref[head, gap] = jnp.where(lane < HALF, pieces[0][:, cut], pieces[1][:, cut])


def pair_columns(pair):
    return (0, pair)


def kv_spec(rows, row_block, part):
    return pl.BlockSpec(
        (N_CTX, 1, rows, 2 * HEAD_DIM), lambda pair: (0, part, row_block, pair)
    )


SMEM_SPEC = pl.BlockSpec(memory_space=pltpu.SMEM)
TILE_SPEC = pl.BlockSpec((2, 5, HALF, TOK), lambda pair: (pair, 0, 0, 0))
TOTAL_SPEC = pl.BlockSpec((1, 8, 2 * TOK), lambda pair: (pair, 0, 0))
ROW_SPEC = pl.BlockSpec((TOK, 2 * HEAD_DIM), pair_columns)
LOCAL = pltpu.CompilerParams(vmem_limit_bytes=62 * MIB)


def attend_back(queries, gathered, grads, totals, rows, row_block, classes=None, near=None, tiles=None):
    biased = classes is not None
    chunks = N_CTX * rows // TOK
    specs = [ROW_SPEC, kv_spec(rows, row_block, 0), kv_spec(rows, row_block, 1), ROW_SPEC, TOTAL_SPEC]
    operands = [queries, gathered, gathered, grads, totals]
    out_specs = [
        ROW_SPEC,
        pl.BlockSpec((N_CTX, 2, rows, 2 * HEAD_DIM), lambda pair: (0, 0, 0, pair)),
    ]
    out_shape = [
        jax.ShapeDtypeStruct((TOK, D), BF),
        jax.ShapeDtypeStruct((N_CTX, 2, rows, D), BF),
    ]
    if biased:
        specs = [SMEM_SPEC, SMEM_SPEC] + specs + [TILE_SPEC]
        operands = [classes, near] + operands + [tiles]
        out_specs.append(pl.BlockSpec((2, 3, HALF, TOK), lambda pair: (pair, 0, 0, 0)))
        out_shape.append(jax.ShapeDtypeStruct((HEADS, 3, HALF, TOK), F32))
    return pl.pallas_call(
        functools.partial(backward_kernel, biased),
        grid=(PAIRS,),
        in_specs=specs,
        out_specs=out_specs,
        out_shape=out_shape,
        scratch_shapes=[
            pltpu.VMEM((chunks, TOK, 2 * TOK), F32),
            pltpu.VMEM((chunks, TOK, 2 * TOK), F32),
            pltpu.VMEM((chunks, TOK, 2 * TOK), BF),
            pltpu.VMEM((chunks, TOK, 2 * TOK), BF),
        ],
        compiler_params=LOCAL,
        cost_estimate=pl.CostEstimate(flops=1000, bytes_accessed=1000, transcendentals=0),
        name="attend_self_back" if biased else "attend_cross_back",
    )(*operands)


def matmul(left, right):
    return jnp.dot(left, right, preferred_element_type=F32)


def transposed_left(left, right):
    return contract(left, right, ((0,), (0,)))


def transposed_right(left, right):
    return contract(left, right, ((1,), (1,)))


def rms_scaled(values, gain):
    inverse = lax.rsqrt(jnp.mean(values * values, axis=-1, keepdims=True) + 1e-06)
    return (values * inverse * gain).astype(BF)


def rms_back(values, gain, grad):
    inverse = lax.rsqrt(jnp.mean(values * values, axis=-1, keepdims=True) + 1e-06)
    scaled = gain * grad
    mixed = jnp.mean(values * scaled, axis=-1, keepdims=True)
    grad_values = inverse * scaled - values * (inverse * inverse * inverse * mixed)
    return grad_values, jnp.sum(values * inverse * grad, axis=0)


def near_hot():
    shape = (REACH, 3 * HALF * HALF)
    spot = lax.broadcasted_iota(jnp.int32, shape, 1)
    gap = spot // (HALF * HALF)
    key = (spot // HALF) % HALF
    row = spot % HALF
    distance = jnp.clip(HALF * gap + row - key, 0, REACH - 1)
    return (distance == lax.broadcasted_iota(jnp.int32, shape, 0)).astype(BF)


def bias_sums(strips):
    tiles = (strips[..., :HALF] + strips[..., HALF:]).reshape(HEADS, -1)
    high = tiles.astype(BF)
    low = (tiles - high.astype(F32)).astype(BF)
    hot = near_hot()
    sums = transposed_right(high, hot) + transposed_right(low, hot)
    far = -jnp.sum(sums[:, :-1], axis=1, keepdims=True)
    return jnp.concatenate([sums[:, :-1], far], axis=1)


def swap(values, move):
    perm = []
    for ctx in range(N_CTX):
        for shard in range(8):
            there, owner = move(ctx, shard)
            perm.append((ctx * 8 + shard, there * 8 + owner))
    return lax.ppermute(values, ("ctx", "fsdp"), perm)


def over_z(mine, upper, lower):
    inner = swap(upper, lambda ctx, shard: (ctx, (shard + 4) % 8))
    outer = swap(lower, lambda ctx, shard: (ctx ^ 2, (shard + 4) % 8))
    return mine, inner, outer


def body(
    decoder_in,
    encoder_states,
    out_grad,
    block_pairs,
    bucket_table,
    gain_self,
    self_query,
    self_key,
    self_value,
    self_out,
    position_bias,
    gain_cross,
    cross_query,
    cross_key,
    cross_value,
    cross_out,
    gain_feed,
    feed_gate,
    feed_up,
    feed_down,
):
    me = lax.axis_index("ctx")
    rows = self_query.shape[0]
    small = jnp.concatenate(
        [
            jnp.pad(jnp.stack([gain_self, gain_cross, gain_feed]), ((0, 0), (0, 128 - rows))),
            jnp.pad(position_bias, ((0, 9), (0, 128 - HEADS))),
        ],
        axis=0,
    )
    (
        kv_one, kv_two, square, gains, normed_one, queries, tiles, attended, self_totals, mid_one,
        normed_two, cross_queries, cross_attended, cross_totals, block_out, d_mid_two,
        cross_branch, d_cross_attended, grad_norm_three, *feed_parts, classes, near, self_kv,
        cross_kv,
    ) = front(
        [
            self_key, self_value, cross_key, cross_value,
            self_query, self_out, cross_query, cross_out,
            feed_gate, feed_up, feed_down,
        ],
        [
            small, decoder_in[0], encoder_states[0], out_grad[0], bucket_table[None, :], block_pairs,
        ],
        0,
    )
    kv_one = kv_one.reshape(D, 2 * D)
    kv_two = kv_two.reshape(D, 2 * D)
    out_one, query_two = (square.reshape(D, 4 * D)[:, k * D : k * D + D] for k in (1, 2))
    norm_one, norm_two = gains[0:1], gains[1:2]
    bucket_hot = (bucket_table[:, None] == jnp.arange(32, dtype=jnp.int32)[None, :]).astype(BF)
    tokens = decoder_in[0].astype(F32)
    states = encoder_states[0]
    upstream = out_grad[0]
    feed_parts = [over_z(*feed_parts[:3]), over_z(*feed_parts[3:])]
    d_cross_queries, d_cross_kv_all = attend_back(
        cross_queries, cross_kv, d_cross_attended, cross_totals, ENC, 0
    )
    d_normed_two = transposed_right(d_cross_queries, query_two)
    part_two, grad_norm_two = rms_back(mid_one, norm_two, d_normed_two)
    d_mid_one = d_mid_two + part_two
    self_branch = d_mid_one.astype(BF)
    d_attended = transposed_right(self_branch, out_one).astype(BF)
    feed_parts[1], d_attended = lax.optimization_barrier((feed_parts[1], d_attended))
    d_queries, d_kv_all, strips = attend_back(
        queries, self_kv, d_attended, self_totals, TOK, 0, classes, near, tiles
    )
    feed_parts, d_queries, d_kv_all, strips = lax.optimization_barrier(
        (feed_parts, d_queries, d_kv_all, strips)
    )
    grad_table = matmul(bias_sums(strips), bucket_hot.astype(F32)).T.reshape(8, 4, HEADS)
    grad_gains = jnp.stack([grad_norm_two, grad_norm_three[0]]).reshape(2, 8, rows)
    grad_small = jnp.concatenate(
        [
            jnp.zeros((8, 1, 128), F32),
            jnp.pad(jnp.transpose(grad_gains, (1, 0, 2)), ((0, 0), (0, 0), (0, 128 - rows))),
            jnp.pad(grad_table, ((0, 0), (0, 9), (0, 128 - HEADS))),
        ],
        axis=1,
    )
    done = finish(
        [
            cross_attended, normed_two, attended, normed_one,
            cross_branch, d_cross_queries, self_branch, d_queries,
            *feed_parts[0],
            *feed_parts[1],
            d_kv_all.reshape(8, 2, 2, TOK, D),
            d_cross_kv_all.reshape(8, 2, 2, ENC, D),
            square,
            kv_one,
            kv_two,
        ],
        [
            states,
            d_queries,
            d_mid_one,
            decoder_in[0],
            norm_one,
            grad_small,
        ],
        3,
    )
    early, late, extras, grad_decoder, grad_encoder = done
    (
        grad_out_two, grad_query_two, grad_out_one, grad_query_one,
        grad_key_two, grad_value_two, grad_key_one, grad_value_one,
        grad_gate, grad_up, grad_down, block_out, grad_decoder, grad_encoder,
    ) = unpack(early, late, block_out, grad_decoder, grad_encoder)
    return (
        block_out[None],
        grad_decoder[None],
        grad_encoder[None],
        extras[0, :rows],
        grad_query_one,
        grad_key_one,
        grad_value_one,
        grad_out_one,
        extras[3:7, :HEADS],
        extras[1, :rows],
        grad_query_two,
        grad_key_two,
        grad_value_two,
        grad_out_two,
        extras[2, :rows],
        grad_gate,
        grad_up,
        grad_down,
    )


def solution(mesh):
    tokens = P("fsdp", "ctx", None)
    matrix = P("fsdp", None)
    vector = P("fsdp")
    weights = (
        (vector,) + (matrix,) * 5 + (vector,) + (matrix,) * 4 + (vector,) + (matrix,) * 3
    )
    return jax.shard_map(
        body,
        mesh=mesh,
        in_specs=(tokens,) * 3 + (P(), P()) + weights,
        out_specs=(tokens,) * 3 + weights,
        check_vma=False,
    )
```
